32 devices in a mesh: dp: 16 (over z, y, x), chan: 2 (over core).
Axes of the slice: x: 2, y: 2, z: 4, core: 2. Of those that a mesh axis runs over, the one named last changes fastest.
Arguments:
- hidden_in: bfloat16 [6144, 384], P('dp'), may hold values from -6 to 6
- out_cot: bfloat16 [6144, 384], P('dp', 'chan'), may hold values from -6 to 6
- segment_ids: int32 [6144], P('dp'), may hold values from 0 to 2, as said below
- norm_gain: float32 [384], replicated
- in_weight: float32 [384, 2, 768], P(None, None, 'chan')
- out_weight: float32 [768, 384], P('chan'), may hold values from -0.21875 to 0.21875
- xproj_weight: float32 [2, 768, 56], P(None, 'chan'), may hold values from -0.21875 to 0.21875
- dtproj_weight: float32 [2, 24, 768], P(None, None, 'chan'), may hold values from -1.25 to 1.25
- conv_weight: float32 [2, 4, 768], P(None, None, 'chan'), may hold values from -3 to 3
- chan_params: float32 [2, 19, 768], P(None, None, 'chan')
- first_norm_gain: float32 [384], P('chan'), may hold values from -448 to 448
- first_in_weight: float32 [384, 2, 768], P(None, None, 'chan'), may hold values from -224 to 224
- first_out_weight: float32 [768, 384], P('chan'), may hold values from -320 to 320
- first_xproj_weight: float32 [2, 768, 56], P(None, 'chan'), may hold values from -448 to 448
- first_dtproj_weight: float32 [2, 24, 768], P(None, None, 'chan'), may hold values from -24 to 24
- first_conv_weight: float32 [2, 4, 768], P(None, None, 'chan'), may hold values from -128 to 128
- first_chan_params: float32 [2, 19, 768], P(None, None, 'chan'), may hold values from -128 to 128
- second_norm_gain: float32 [384], P('chan'), may hold values from 6144 to 24576
- second_in_weight: float32 [384, 2, 768], P(None, None, 'chan'), may hold values from 1536 to 6144
- second_out_weight: float32 [768, 384], P('chan'), may hold values from 3010.56 to 12042.24
- second_xproj_weight: float32 [2, 768, 56], P(None, 'chan'), may hold values from 6144 to 24576
- second_dtproj_weight: float32 [2, 24, 768], P(None, None, 'chan'), may hold values from 15.36 to 61.44
- second_conv_weight: float32 [2, 4, 768], P(None, None, 'chan'), may hold values from 552.96 to 2211.84
- second_chan_params: float32 [2, 19, 768], P(None, None, 'chan'), may hold values from 552.96 to 2211.84
Outputs:
- output: bfloat16 [6144, 384], P('dp', 'chan')
- input_grad: float32 [6144, 384], P('dp', 'chan')
- new_first_norm_gain: float32 [384], P('chan')
- new_second_norm_gain: float32 [384], P('chan')
- new_norm_gain: float32 [384], P('chan')
- copy_norm_gain: bfloat16 [384], P('chan')
- new_first_in_weight: float32 [384, 2, 768], P(None, None, 'chan')
- new_second_in_weight: float32 [384, 2, 768], P(None, None, 'chan')
- new_in_weight: float32 [384, 2, 768], P(None, None, 'chan')
- copy_in_weight: bfloat16 [384, 2, 768], P(None, None, 'chan')
- new_first_out_weight: float32 [768, 384], P('chan')
- new_second_out_weight: float32 [768, 384], P('chan')
- new_out_weight: float32 [768, 384], P('chan')
- copy_out_weight: bfloat16 [768, 384], P('chan')
- new_first_xproj_weight: float32 [2, 768, 56], P(None, 'chan')
- new_second_xproj_weight: float32 [2, 768, 56], P(None, 'chan')
- new_xproj_weight: float32 [2, 768, 56], P(None, 'chan')
- copy_xproj_weight: bfloat16 [2, 768, 56], P(None, 'chan')
- new_first_dtproj_weight: float32 [2, 24, 768], P(None, None, 'chan')
- new_second_dtproj_weight: float32 [2, 24, 768], P(None, None, 'chan')
- new_dtproj_weight: float32 [2, 24, 768], P(None, None, 'chan')
- copy_dtproj_weight: bfloat16 [2, 24, 768], P(None, None, 'chan')
- new_first_conv_weight: float32 [2, 4, 768], P(None, None, 'chan')
- new_second_conv_weight: float32 [2, 4, 768], P(None, None, 'chan')
- new_conv_weight: float32 [2, 4, 768], P(None, None, 'chan')
- copy_conv_weight: bfloat16 [2, 4, 768], P(None, None, 'chan')
- new_first_chan_params: float32 [2, 19, 768], P(None, None, 'chan')
- new_second_chan_params: float32 [2, 19, 768], P(None, None, 'chan')
- new_chan_params: float32 [2, 19, 768], P(None, None, 'chan')
- copy_chan_params: bfloat16 [2, 19, 768], P(None, None, 'chan')
- tensor_norms: float32 [7, 2], replicated
- step_stats: float32 [2, 768], P(None, 'chan')
The draws below stay inside these ranges and needn't reach their ends.
Inputs may be any that keep to these rules, and one draw needn't show every extreme that they name: `segment_ids`: each block of 384 tokens is a window over clips of 1, 2, 4 or 8 frames of 196 tokens laid end to end; its first and last pieces may be parts of longer clips. Within a block the ids start at 0 and rise by one at each new clip, every piece but the first and last holds a whole clip, and some block holds 3 pieces.
All inputs are finite; a program needn't handle non-finite values.
Results may differ from the reference program's by a relative error of at most 0.012.
The reference program's roundings to bfloat16 on the way count: a program that leaves them out, or rounds other values in their place, can miss the bound.
Values may be sent and summed in bfloat16 or wider, within the bound.
No kernel may reach another device: no remote copies, remote signals or barrier semaphores. Data moves between devices by JAX's collectives and lax.ppermute only.
A program may use at most 384 MiB of HBM per device.

```python
import math
import jax
import jax.numpy as jnp
from jax import lax

D = 384
E = 768
N = 16
R = 24
K = 4
TOK_DEV = 384
FRAME = 196
STEP = 4
TOKENS = 6144


def draw_segment_ids(key, part):
    key = jax.random.fold_in(key, 1)
    blocks = TOKENS // TOK_DEV
    clip_count = TOK_DEV // FRAME + 2
    keys = jax.random.split(key, 3)
    powers = jax.random.randint(keys[0], (blocks, clip_count), 0, 4)
    frame_table = jnp.array([1, 2, 4, 8], dtype=jnp.int32)
    lengths = FRAME * frame_table[powers]
    chosen = jax.random.randint(keys[2], (), 0, blocks)
    rows = jnp.arange(blocks, dtype=jnp.int32)
    is_chosen = rows == chosen
    later = jnp.where(is_chosen[:, None], FRAME, lengths[:, 1:])
    lengths = jnp.concatenate([lengths[:, :1], later], axis=1).astype(jnp.int32)
    phase = jax.random.randint(keys[1], (blocks,), 0, lengths[:, 0])
    phase = jnp.where(is_chosen, lengths[:, 0] - 1, phase).astype(jnp.int32)
    bounds = jnp.cumsum(lengths, axis=1)[:, :clip_count - 1] - phase[:, None]
    places = jnp.arange(TOK_DEV, dtype=jnp.int32)
    counted = jnp.sum((bounds[:, :, None] <= places[None, None, :]).astype(jnp.int32), axis=1)
    return counted.reshape(TOKENS).astype(jnp.int32)


def draw_norm_gain(key, part):
    key = jax.random.fold_in(key, 2)
    ramp = jnp.arange(D, dtype=jnp.float32) / D
    base = 0.6 + 1.2 * ramp
    noise = jax.random.uniform(key, (D,), jnp.float32, 0.85, 1.15)
    return base * noise


def draw_in_weight(key, part):
    key = jax.random.fold_in(key, 3)
    ramp = 0.6 + 1.2 * jnp.arange(E, dtype=jnp.float32) / E
    values = jax.random.normal(key, (D, 2, E), jnp.float32)
    return values * D ** (-0.5) * ramp[None, None, :]


def draw_chan_params(key, part):
    key = jax.random.fold_in(key, 4)
    keys = jax.random.split(key, 4)
    conv_bias = 0.3 * jax.random.normal(keys[0], (2, 1, E), jnp.float32)
    step_bias = jax.random.uniform(keys[1], (2, 1, E), jnp.float32, -4.5, -2.0)
    skip_gain = jax.random.uniform(keys[2], (2, 1, E), jnp.float32, 0.5, 1.5)
    log_rates = jax.random.uniform(keys[3], (2, N, E), jnp.float32, 0.0, 2.77)
    return jnp.concatenate([conv_bias, step_bias, skip_gain, log_rates], axis=1)


def levels(key, shape, shards, least, high):
    level, own = 1.0, jax.random.fold_in(key, 6)
    for dim, parts in shards:
        steps = jnp.exp(jax.random.uniform(jax.random.fold_in(own, dim), (parts,), jnp.float32, least / len(shards), high / len(shards)))
        level = level * jnp.repeat(steps, shape[dim] // parts).reshape([-1 if axis == dim else 1 for axis in range(len(shape))])
    return level


def scatter_about(rng, shape, width, most, shards=(), kind=jnp.bfloat16):
    values = jax.random.normal(rng, shape, jnp.float32) * width
    if len(shards) > 0:
        values = levels(rng, shape, shards, -0.22, 0.18) * values
    return jnp.clip(values, min=-most, max=most).astype(kind)


def setup_inputs(seed: int = 0) -> dict:
    streams_of = jax.random.split(jax.random.key(seed), 25)
    return {
        "hidden_in": scatter_about(streams_of[0], (TOKENS, D), 1.0, 6.0, ((0, 16),)),
        "out_cot": scatter_about(streams_of[1], (TOKENS, D), 1.0, 6.0, ((0, 16), (1, 2))),
        "segment_ids": draw_segment_ids(jax.random.fold_in(streams_of[24], 71), 0),
        "norm_gain": draw_norm_gain(jax.random.fold_in(streams_of[24], 71), 0),
        "in_weight": draw_in_weight(jax.random.fold_in(streams_of[24], 71), 0),
        "out_weight": scatter_about(streams_of[5], (E, D), E ** -0.5, 0.21875, ((0, 2),), jnp.float32),
        "xproj_weight": scatter_about(streams_of[6], (2, E, R + 2 * N), E ** -0.5, 0.21875, ((1, 2),), jnp.float32),
        "dtproj_weight": scatter_about(streams_of[7], (2, R, E), R ** -0.5, 1.25, ((2, 2),), jnp.float32),
        "conv_weight": scatter_about(streams_of[8], (2, K, E), K ** -0.5, 3.0, ((2, 2),), jnp.float32),
        "chan_params": draw_chan_params(jax.random.fold_in(streams_of[24], 71), 0),
        "first_norm_gain": scatter_about(streams_of[10], (D,), (TOKENS ** 0.5), 448.0, ((0, 2),), jnp.float32),
        "first_in_weight": scatter_about(streams_of[11], (D, 2, E), (0.5 * TOKENS ** 0.5), 224.0, ((2, 2),), jnp.float32),
        "first_out_weight": scatter_about(streams_of[12], (E, D), (0.7 * TOKENS ** 0.5), 320.0, ((0, 2),), jnp.float32),
        "first_xproj_weight": scatter_about(streams_of[13], (2, E, R + 2 * N), (TOKENS ** 0.5), 448.0, ((1, 2),), jnp.float32),
        "first_dtproj_weight": scatter_about(streams_of[14], (2, R, E), (0.05 * TOKENS ** 0.5), 24.0, ((2, 2),), jnp.float32),
        "first_conv_weight": scatter_about(streams_of[15], (2, K, E), (0.3 * TOKENS ** 0.5), 128.0, ((2, 2),), jnp.float32),
        "first_chan_params": scatter_about(streams_of[16], (2, 3 + N, E), (0.3 * TOKENS ** 0.5), 128.0, ((2, 2),), jnp.float32),
        "second_norm_gain": jnp.clip(jnp.exp(math.log(24576.0) - 1.3862944 * jax.random.uniform(streams_of[17], (D,), jnp.float32) ** levels(streams_of[17], (D,), ((0, 2),), -0.2, 0.2)), 6144.0, 24576.0),
        "second_in_weight": jnp.clip(jnp.exp(math.log(6144.0) - 1.3862944 * jax.random.uniform(streams_of[18], (D, 2, E), jnp.float32) ** levels(streams_of[18], (D, 2, E), ((2, 2),), -0.2, 0.2)), 1536.0, 6144.0),
        "second_out_weight": jnp.clip(jnp.exp(math.log(12042.24) - 1.3862944 * jax.random.uniform(streams_of[19], (E, D), jnp.float32) ** levels(streams_of[19], (E, D), ((0, 2),), -0.2, 0.2)), 3010.56, 12042.24),
        "second_xproj_weight": jnp.clip(jnp.exp(math.log(24576.0) - 1.3862944 * jax.random.uniform(streams_of[20], (2, E, R + 2 * N), jnp.float32) ** levels(streams_of[20], (2, E, R + 2 * N), ((1, 2),), -0.2, 0.2)), 6144.0, 24576.0),
        "second_dtproj_weight": jnp.clip(jnp.exp(math.log(61.44) - 1.3862944 * jax.random.uniform(streams_of[21], (2, R, E), jnp.float32) ** levels(streams_of[21], (2, R, E), ((2, 2),), -0.2, 0.2)), 15.36, 61.44),
        "second_conv_weight": jnp.clip(jnp.exp(math.log(2211.84) - 1.3862944 * jax.random.uniform(streams_of[22], (2, K, E), jnp.float32) ** levels(streams_of[22], (2, K, E), ((2, 2),), -0.2, 0.2)), 552.96, 2211.84),
        "second_chan_params": jnp.clip(jnp.exp(math.log(2211.84) - 1.3862944 * jax.random.uniform(streams_of[23], (2, 3 + N, E), jnp.float32) ** levels(streams_of[23], (2, 3 + N, E), ((2, 2),), -0.2, 0.2)), 552.96, 2211.84),
    }


@jax.custom_vjp
def low(v):
    return lax.optimization_barrier(v.astype(jnp.bfloat16)).astype(jnp.float32)

@jax.custom_vjp
def low_back(v):
    return v

def low_keep(v):
    return (low(v), None)

def low_pass(kept, grad):
    return (grad,)

def back_keep(v):
    return (v, None)

def back_low(kept, grad):
    return (low(grad),)
low.defvjp(low_keep, low_pass)
low_back.defvjp(back_keep, back_low)
precise = lax.Precision.HIGHEST
norm_eps = 1e-06
beta_one = 0.5
beta_two = 0.5
adam_eps = 1e-06
decay_rate = 0.01
learn_rate = 0.3

def matmul(left, right):
    return jnp.dot(left, right, precision=precise, preferred_element_type=jnp.float32)

def conv_taps(mixing, segment, kernel_taps, conv_bias):
    total = conv_bias + kernel_taps[0] * mixing
    for offset in range(1, kernel_taps.shape[0]):
        matched = (segment[offset:] == segment[:-offset]).astype(jnp.float32)
        mask_row = jnp.concatenate([jnp.zeros((offset,), jnp.float32), matched])
        shifted = jnp.concatenate([jnp.zeros((offset, mixing.shape[1]), jnp.float32), mixing[:-offset]], 0)
        total = total + kernel_taps[offset] * shifted * mask_row[:, None]
    return total

def selective(step_size, input_map, output_map, activation, decay_rates, keeping):

    def advance(carried, inputs_row):
        size_row, input_row, output_row, act_row, keep_row = inputs_row
        carried = jnp.exp(size_row[None, :] * decay_rates) * keep_row * carried + input_row[:, None] * (size_row * act_row)[None, :]
        return (carried, lax.optimization_barrier(jnp.sum(output_row[:, None] * carried, axis=0)))
    start = jnp.zeros(decay_rates.shape, jnp.float32)
    ignored, result = lax.scan(advance, start, (step_size, input_map, output_map, activation, keeping))
    return result

def branch_pass(mixing, segment, kernel_taps, branch_params, proj_x, proj_dt):
    keeping = jnp.concatenate([jnp.zeros((1,), jnp.float32), (segment[1:] == segment[:-1]).astype(jnp.float32)])
    conv_out = conv_taps(mixing, segment, kernel_taps, branch_params[0])
    activation = jax.nn.silu(conv_out)
    projection = low_back(matmul(low(activation), low(proj_x)))
    dt_low = projection[:, :R]
    input_map = projection[:, R:R + N]
    output_map = projection[:, R + N:]
    step_size = jax.nn.softplus(matmul(dt_low, proj_dt) + branch_params[1])
    decay_rates = -jnp.exp(branch_params[3:])
    scanned = selective(step_size, input_map, output_map, activation, decay_rates, keeping)
    return scanned + branch_params[2] * activation

def block_forward(source, gain, w_in, w_out, w_xproj, w_dtproj, w_conv, w_chan, segment):
    scale_inv = lax.rsqrt(lax.optimization_barrier(jnp.mean(source * source, axis=1, keepdims=True)) + norm_eps)
    normed = source * scale_inv * gain
    mixed = low_back(matmul(low(normed), low(w_in).reshape(D, 2 * E)))
    mixing = mixed[:, :E]
    gate_value = mixed[:, E:]
    forward_y = branch_pass(mixing, segment, w_conv[0], w_chan[0], w_xproj[0], w_dtproj[0])
    backward_y = jnp.flip(branch_pass(jnp.flip(mixing, 0), jnp.flip(segment, 0), w_conv[1], w_chan[1], w_xproj[1], w_dtproj[1]), 0)
    branch_out = (forward_y + backward_y) * jax.nn.silu(gate_value)
    return source + matmul(low(branch_out), low(w_out))

def lamb_update(weight, grad, first, second):
    first_new = beta_one * first + (1.0 - beta_one) * grad
    second_new = beta_two * second + (1.0 - beta_two) * grad * grad
    update = first_new / (1.0 - beta_one ** STEP) / (jnp.sqrt(second_new / (1.0 - beta_two ** STEP)) + adam_eps) + decay_rate * weight
    weight_norm = jnp.sqrt(jnp.sum(weight * weight))
    update_norm = jnp.sqrt(jnp.sum(update * update))
    moving = learn_rate * weight_norm / (update_norm + adam_eps) * update
    new_weight = weight - moving
    return (first_new, second_new, new_weight, new_weight.astype(jnp.bfloat16), weight_norm, update_norm, moving)

def reference(hidden_in, out_cot, segment_ids, norm_gain, in_weight, out_weight, xproj_weight, dtproj_weight, conv_weight, chan_params, first_norm_gain, first_in_weight, first_out_weight, first_xproj_weight, first_dtproj_weight, first_conv_weight, first_chan_params, second_norm_gain, second_in_weight, second_out_weight, second_xproj_weight, second_dtproj_weight, second_conv_weight, second_chan_params):
    weights = (norm_gain, in_weight, out_weight, xproj_weight, dtproj_weight, conv_weight, chan_params)
    blocks = TOKENS // TOK_DEV
    sources = hidden_in.astype(jnp.float32).reshape(blocks, TOK_DEV, D)
    cotangents = out_cot.astype(jnp.float32).reshape(blocks, TOK_DEV, D)
    segments = segment_ids.reshape(blocks, TOK_DEV)

    def one_block(totals, inputs_row):
        source, cotangent, segment = inputs_row

        def forward(source, gain, w_in, w_out, w_xproj, w_dtproj, w_conv, w_chan):
            return block_forward(source, gain, w_in, w_out, w_xproj, w_dtproj, w_conv, w_chan, segment)
        result, pullback = jax.vjp(forward, source, weights[0], weights[1], weights[2], weights[3], weights[4], weights[5], weights[6])
        grads = pullback(cotangent)
        totals = jax.tree.map(jnp.add, totals, tuple(grads[1:]))
        return (totals, (result.astype(jnp.bfloat16), grads[0]))
    start = tuple((jnp.zeros_like(tensor) for tensor in weights))
    totals, (outputs, input_grads) = lax.scan(one_block, start, (sources, cotangents, segments))
    firsts = (first_norm_gain, first_in_weight, first_out_weight, first_xproj_weight, first_dtproj_weight, first_conv_weight, first_chan_params)
    seconds = (second_norm_gain, second_in_weight, second_out_weight, second_xproj_weight, second_dtproj_weight, second_conv_weight, second_chan_params)
    results = [lamb_update(weights[place], totals[place], firsts[place], seconds[place]) for place in range(7)]
    tensor_norms = jnp.stack([jnp.stack([entry[4], entry[5]]) for entry in results])
    step_in = results[1][6]
    step_out = results[2][6]
    count = 3.0 * D
    step_mean = (lax.optimization_barrier(jnp.sum(step_in, axis=(0, 1))) + lax.optimization_barrier(jnp.sum(step_out, axis=1))) / count
    dev_in = step_in - step_mean
    dev_out = step_out - step_mean[:, None]
    step_var = (lax.optimization_barrier(jnp.sum(dev_in * dev_in, axis=(0, 1))) + lax.optimization_barrier(jnp.sum(dev_out * dev_out, axis=1))) / count
    step_stats = jnp.stack([step_mean, step_var])
    flat = []
    for entry in results:
        flat.extend([entry[0], entry[1], entry[2], entry[3]])
    return (outputs.reshape(TOKENS, D), input_grads.reshape(TOKENS, D), flat[0], flat[1], flat[2], flat[3], flat[4], flat[5], flat[6], flat[7], flat[8], flat[9], flat[10], flat[11], flat[12], flat[13], flat[14], flat[15], flat[16], flat[17], flat[18], flat[19], flat[20], flat[21], flat[22], flat[23], flat[24], flat[25], flat[26], flat[27], tensor_norms, step_stats)
```

```python
import functools

import jax
import jax.numpy as jnp
from jax import lax
from jax.experimental import pallas as pl
from jax.experimental.pallas import tpu as pltpu
from jax.sharding import PartitionSpec as P

STEP = 4
norm_eps = 1e-06
beta_one = 0.5
beta_two = 0.5
adam_eps = 1e-06
decay_rate = 0.01
learn_rate = 0.3
LOG2E = 1.4426950408889634
FAR = 1e30
FLOOR = -1e-26

f32 = jnp.float32
bf16 = jnp.bfloat16
HIGH = lax.Precision.HIGHEST
LANES = 128
ROWS = 16
MB = 1 << 20


def dot(left, right, dims, precision=None):
    return lax.dot_general(
        left, right, (dims, ((), ())), precision=precision, preferred_element_type=f32
    )


NN = ((1,), (0,))
TN = ((0,), (0,))
NT = ((1,), (1,))


def sigmoid(values):
    return 1.0 / (1.0 + jnp.exp(-values))


def silu_slope(values, sigma):
    return sigma * (1.0 + values * (1.0 - sigma))


def softplus(values):
    return jnp.maximum(values, 0.0) + jnp.log1p(jnp.exp(-jnp.abs(values)))


def wide(tile, times):
    return jnp.concatenate([tile] * times, axis=1)


def fold(values):
    total = values[0:8]
    for start in range(8, values.shape[0], 8):
        total = total + values[start : start + 8]
    return total


def shape(dims, dtype):
    return jax.ShapeDtypeStruct(dims, dtype)


def each_rows(length, body, carry=None, rows=ROWS):
    def step(index, held):
        return body(pl.multiple_of(index * rows, rows), held)

    return lax.fori_loop(0, length // rows, step, carry)


def front_kernel(
    hid, seg, gain, w_in, taps, params, w_xp,
    mix_out, gate_out, conv_out, part_out, norm_out, low_out, same_out,
    padded, sgpad,
):
    tokens, width = hid.shape
    chans = mix_out.shape[1]
    tiles = chans // LANES

    def normalise(start, held):
        source = hid[pl.ds(start, ROWS), :].astype(f32)
        scale = lax.rsqrt(jnp.sum(source * source, axis=1, keepdims=True) / width + norm_eps)
        norm_out[pl.ds(start, ROWS), :] = (source * scale * gain[...]).astype(bf16)
        return held

    each_rows(tokens, normalise, 0)
    for half in range(2):
        low_out[half] = w_in[:, half, :].astype(bf16)
    normed = norm_out[...]
    mixing = dot(normed, low_out[0], NN)
    mix_out[...] = mixing
    padded[0:8, :] = jnp.zeros((8, chans), f32)
    padded[pl.ds(8, tokens), :] = mixing
    padded[pl.ds(8 + tokens, 8), :] = jnp.zeros((8, chans), f32)
    gate_out[...] = dot(normed, low_out[1], NN)
    across = lax.broadcasted_iota(jnp.int32, (tokens, tokens), 0)
    along = lax.broadcasted_iota(jnp.int32, (tokens, tokens), 1)
    picked = jnp.where(across == along, seg[...].astype(f32), 0.0).astype(bf16)
    numbers = dot(picked, jnp.ones((tokens, LANES), bf16), NN)
    sgpad[0:8, :] = jnp.full((8, LANES), -1.0, f32)
    sgpad[pl.ds(8, tokens), :] = numbers
    sgpad[pl.ds(8 + tokens, 8), :] = jnp.full((8, LANES), -1.0, f32)
    width_taps = taps.shape[1]

    def convolve(start, held):
        window = padded[pl.ds(start, ROWS + 16), :]
        marks = sgpad[pl.ds(start, ROWS + 16), :]
        own = marks[8 : 8 + ROWS]
        base = window[8 : 8 + ROWS]
        for heading in range(2):
            total = params[0, heading : heading + 1, :] + taps[heading, 0:1, :] * base
            for offset in range(1, width_taps):
                begin = 8 - offset if heading == 0 else 8 + offset
                same = jnp.where(marks[begin : begin + ROWS] == own, 1.0, 0.0)
                if offset == 1:
                    same_out[heading, pl.ds(start, ROWS), :] = same
                moved = window[begin : begin + ROWS]
                total = total + taps[heading, offset : offset + 1, :] * moved * wide(same, tiles)
            conv_out[heading, pl.ds(start, ROWS), :] = total
        return held

    each_rows(tokens, convolve, 0)
    for heading in range(2):
        pre = conv_out[heading]
        act_low = (pre * sigmoid(pre)).astype(bf16)
        rows = w_xp.shape[1]
        part_out[heading * rows : (heading + 1) * rows, :] = dot(
            w_xp[heading].astype(bf16), act_low, NT
        )


SPAN = 64


def scan_kernel(
    own_part, far_part, conv_pre, gate, same, cot_own, cot_far, w_out, w_dt, params, core,
    grad_part, grad_act_out, gate_low_out, out_own, out_far, grad_out_w, grad_dt, grad_chan,
    proj, pre_step, grad_pre_all, grad_branch, step, far_step, inflow, result, through, decayed,
    grad_y, branch_low, maps_in, maps_out, states, picker, rates, rates2,
):
    tokens, chans = gate.shape
    tiles = chans // LANES
    rank = w_dt.shape[1]
    count = params.shape[0] - 3
    rows = rank + 2 * count
    blocks = tokens // LANES
    block_rows = LANES * count
    half_width = cot_own.shape[0]
    me = core[0]

    def cols(tile):
        return slice(tile * LANES, (tile + 1) * LANES)

    def base_of(heading, tile):
        return (heading * tiles + tile) * tokens

    def whole(ref, heading):
        return jnp.concatenate(
            [
                ref[base_of(heading, tile) : base_of(heading, tile) + tokens, :]
                for tile in range(tiles)
            ],
            axis=1,
        )

    proj[...] = own_part[...] + far_part[...]
    low_out = w_out[...].astype(bf16)
    low_cot = jnp.where(
        me == 0,
        jnp.concatenate([cot_own[...].astype(f32), cot_far[...].astype(f32)], 0),
        jnp.concatenate([cot_far[...].astype(f32), cot_own[...].astype(f32)], 0),
    ).astype(bf16)
    grad_branch[...] = dot(low_cot, low_out, ((0,), (1,)))
    for heading in range(2):
        for n in range(count):
            value = -jnp.exp(params[3 + n, heading : heading + 1, :])
            rates[heading, n : n + 1, :] = value
            rates2[heading, n : n + 1, :] = jnp.minimum(value * LOG2E, FLOOR)
        pre_step[heading] = (
            dot(proj[heading * rows : heading * rows + rank, :], w_dt[heading], TN, HIGH)
            + params[1, heading : heading + 1, :]
        )

    for tile in range(tiles):

        def prepare(start, held, tile=tile):
            here = pl.ds(start, SPAN)
            for heading in range(2):
                pre = conv_pre[heading, here, cols(tile)]
                act = pre * sigmoid(pre)
                size = softplus(pre_step[heading, here, cols(tile)])
                there = pl.ds(base_of(heading, tile) + start, SPAN)
                step[there, :] = size
                inflow[there, :] = size * act
                far_step[there, :] = jnp.where(same[heading, here, :] > 0.5, size, FAR)
            gated = gate[here, cols(tile)]
            grad_y[pl.ds(base_of(0, tile) + start, SPAN), :] = grad_branch[here, cols(tile)] * (
                gated * sigmoid(gated)
            )
            return held

        each_rows(tokens, prepare, 0, SPAN)

    picked = lax.broadcasted_iota(jnp.int32, (block_rows, LANES), 0) // count
    along = lax.broadcasted_iota(jnp.int32, (block_rows, LANES), 1)
    picker[...] = jnp.where(picked == along, 1.0, 0.0).astype(bf16)
    ones = jnp.ones((2 * LANES, LANES), bf16)
    for heading in range(2):
        for which, target in ((0, maps_in), (1, maps_out)):
            first = heading * rows + rank + which * count
            for block in range(blocks):
                tile = proj[first : first + count, cols(block)]
                high = tile.astype(bf16)
                rest = (tile - high.astype(f32)).astype(bf16)
                one = picker[...].reshape(LANES, count, LANES)
                spread = jnp.concatenate(
                    [
                        (one * high[None]).reshape(block_rows, LANES),
                        (one * rest[None]).reshape(block_rows, LANES),
                    ],
                    axis=1,
                )
                target[heading, block * block_rows : (block + 1) * block_rows, :] = dot(
                    spread, ones, NN
                )

    zero = jnp.zeros((count, chans), f32)
    blank = jnp.zeros((count, LANES), f32)
    states[0, 0:count, :] = zero
    states[1, tokens * count : (tokens + 1) * count, :] = zero
    group = 8
    pairs = [(heading, tile) for heading in range(2) for tile in range(tiles)]

    def row(ref, heading, tile, at):
        return ref[pl.ds(base_of(heading, tile) + at, 1), :]

    def forward(index, held):
        carried = list(held)
        for place in range(group):
            ahead = index * group + place
            for heading in range(2):
                at = ahead if heading == 0 else tokens - 1 - ahead
                slot = pl.multiple_of(at * count, count)
                kept = pl.multiple_of(slot + (count if heading == 0 else 0), count)
                enter = maps_in[heading, pl.ds(slot, count), :]
                leave = maps_out[heading, pl.ds(slot, count), :]
                for tile in range(tiles):
                    number = heading * tiles + tile
                    decay = jnp.exp2(
                        row(far_step, heading, tile, at) * rates2[heading, :, cols(tile)]
                    )
                    state = decay * carried[number] + enter * row(inflow, heading, tile, at)
                    carried[number] = state
                    result[pl.ds(base_of(heading, tile) + at, 1), :] = jnp.sum(
                        leave * state, axis=0, keepdims=True
                    )
                    states[heading, pl.ds(kept, count), cols(tile)] = state
        return tuple(carried)

    lax.fori_loop(0, tokens // group, forward, (blank,) * len(pairs))

    for tile in range(tiles):

        def finish_forward(start, held, tile=tile):
            here = pl.ds(start, SPAN)
            total = jnp.zeros((SPAN, LANES), f32)
            sums = []
            back = grad_y[pl.ds(base_of(0, tile) + start, SPAN), :]
            for heading in range(2):
                pre = conv_pre[heading, here, cols(tile)]
                act = pre * sigmoid(pre)
                total = total + result[pl.ds(base_of(heading, tile) + start, SPAN), :]
                total = total + params[2, heading : heading + 1, cols(tile)] * act
                sums.append(held[heading] + fold(back * act))
            gated = gate[here, cols(tile)]
            sigma = sigmoid(gated)
            branch_low[here, cols(tile)] = (total * (gated * sigma)).astype(bf16)
            gate_low_out[here, cols(tile)] = (
                grad_branch[here, cols(tile)] * total * silu_slope(gated, sigma)
            ).astype(bf16)
            return tuple(sums)

        skips = each_rows(tokens, finish_forward, (jnp.zeros((8, LANES), f32),) * 2, SPAN)
        for heading in range(2):
            grad_chan[2, heading : heading + 1, cols(tile)] = jnp.sum(
                skips[heading], axis=0, keepdims=True
            )
    branch = branch_low[...]
    sent = dot(low_out, branch, ((0,), (1,)))
    out_own[...] = jnp.where(me == 0, sent[:half_width], sent[half_width:])
    out_far[...] = jnp.where(me == 0, sent[half_width:], sent[:half_width])
    grad_w = dot(branch, low_cot, ((0,), (1,))).astype(bf16)
    for tile in range(grad_out_w.shape[0]):
        grad_out_w[tile] = grad_w[:, cols(tile)]

    def gather_map(heading, other, target_row):
        shift = count if heading == 0 else 0
        for block in range(blocks):
            begin = block * block_rows + shift
            left = states[heading, begin : begin + block_rows, :].astype(bf16)
            right = other[cols(block), :].astype(bf16)
            products = dot(left, right, NT) * picker[...].astype(f32)
            grad_part[target_row : target_row + count, cols(block)] = jnp.sum(
                products.reshape(LANES, count, LANES), axis=0
            )

    back_rows = whole(grad_y, 0)
    for heading in range(2):
        gather_map(heading, back_rows, heading * rows + rank + count)

    def backward(index, held):
        waiting = list(held[: len(pairs)])
        totals = list(held[len(pairs) :])
        for place in range(group):
            ahead = index * group + place
            for heading in range(2):
                at = tokens - 1 - ahead if heading == 0 else ahead
                slot = pl.multiple_of(at * count, count)
                after = pl.multiple_of((at + 1) * count, count)
                enter = maps_in[heading, pl.ds(slot, count), :]
                leave = maps_out[heading, pl.ds(slot, count), :]
                for tile in range(tiles):
                    number = heading * tiles + tile
                    decay = jnp.exp2(
                        row(far_step, heading, tile, at) * rates2[heading, :, cols(tile)]
                    )
                    grad = leave * row(grad_y, 0, tile, at) + waiting[number]
                    lead = decay * grad
                    waiting[number] = lead
                    before = states[
                        heading, pl.ds(slot if heading == 0 else after, count), cols(tile)
                    ]
                    slope = lead * before
                    here = pl.ds(base_of(heading, tile) + at, 1)
                    decayed[here, :] = jnp.sum(
                        slope * rates[heading, :, cols(tile)], axis=0, keepdims=True
                    )
                    through[here, :] = jnp.sum(grad * enter, axis=0, keepdims=True)
                    totals[number] = totals[number] + slope * row(step, heading, tile, at)
                    states[
                        heading, pl.ds(after if heading == 0 else slot, count), cols(tile)
                    ] = grad
        return tuple(waiting + totals)

    ends = lax.fori_loop(0, tokens // group, backward, (blank,) * (2 * len(pairs)))
    for number, (heading, tile) in enumerate(pairs):
        slopes = ends[len(pairs) + number] * rates[heading, :, cols(tile)]
        for n in range(count):
            grad_chan[3 + n, heading : heading + 1, cols(tile)] = slopes[n : n + 1]
    for heading in range(2):
        gather_map(heading, whole(inflow, heading), heading * rows + rank)

    for tile in range(tiles):

        def finish_backward(start, held, tile=tile):
            here = pl.ds(start, SPAN)
            sums = []
            back = grad_y[pl.ds(base_of(0, tile) + start, SPAN), :]
            for heading in range(2):
                there = pl.ds(base_of(heading, tile) + start, SPAN)
                pre = conv_pre[heading, here, cols(tile)]
                act = pre * sigmoid(pre)
                passed = through[there, :]
                grad_act_out[heading, here, cols(tile)] = (
                    passed * step[there, :] + back * params[2, heading : heading + 1, cols(tile)]
                )
                grad_pre = (decayed[there, :] + passed * act) * sigmoid(
                    pre_step[heading, here, cols(tile)]
                )
                grad_pre_all[heading, here, cols(tile)] = grad_pre
                sums.append(held[heading] + fold(grad_pre))
            return tuple(sums)

        biases = each_rows(tokens, finish_backward, (jnp.zeros((8, LANES), f32),) * 2, SPAN)
        for heading in range(2):
            grad_chan[1, heading : heading + 1, cols(tile)] = jnp.sum(
                biases[heading], axis=0, keepdims=True
            )
    for heading in range(2):
        grad_chan[0, heading : heading + 1, :] = jnp.zeros((1, chans), f32)
        grad_pre = grad_pre_all[heading]
        grad_dt[heading] = dot(
            proj[heading * rows : heading * rows + rank, :], grad_pre, NN, HIGH
        )
        grad_part[heading * rows : heading * rows + rank, :] = dot(
            w_dt[heading], grad_pre, NT, HIGH
        )


def back_kernel(
    own_part, far_part, grad_act, conv_pre, mixing, gate_low, normed, low_in, same_seg, w_xp, taps, hid, gain,
    grad_out_w, grad_dt, grad_chan, core,
    sums_out, in_own, in_far,
    padded, gpad, sgpad, mixed_low, small, act_low,
):
    tokens, width = hid.shape
    chans = mixing.shape[1]
    tiles = chans // LANES
    rows = w_xp.shape[1]
    width_taps = taps.shape[1]
    me = core[0]
    half_width = in_own.shape[0] - 8
    edge = jnp.zeros((8, chans), f32)
    padded[0:8, :] = edge
    padded[pl.ds(8 + tokens, 8), :] = edge
    padded[pl.ds(8, tokens), :] = mixing[...]
    gpad[0, 0:8, :] = edge
    gpad[1, 0:8, :] = edge
    gpad[0, pl.ds(8 + tokens, 8), :] = edge
    gpad[1, pl.ds(8 + tokens, 8), :] = edge
    sgpad[0:8, :] = jnp.full((8, LANES), -1.0, f32)
    sgpad[pl.ds(8 + tokens, 8), :] = jnp.full((8, LANES), -1.0, f32)
    across = lax.broadcasted_iota(jnp.int32, (tokens, tokens), 0)
    along = lax.broadcasted_iota(jnp.int32, (tokens, tokens), 1)
    picked = jnp.where(across == along, same_seg[...].astype(f32), 0.0).astype(bf16)
    sgpad[pl.ds(8, tokens), :] = dot(picked, jnp.ones((tokens, LANES), bf16), NN)

    parts = (own_part[...] + far_part[...]).astype(bf16)
    for heading in range(2):
        part = parts[heading * rows : (heading + 1) * rows, :]
        gpad[heading, pl.ds(8, tokens), :] = dot(part, w_xp[heading].astype(bf16), TN)

    blank = jnp.zeros((8, chans), f32)

    def through_conv(start, held):
        here = pl.ds(start, ROWS)
        window = padded[pl.ds(start, ROWS + 16), :]
        marks = sgpad[pl.ds(start, ROWS + 16), :]
        own = marks[8 : 8 + ROWS]
        base = window[8 : 8 + ROWS]
        sums = []
        for heading in range(2):
            pre = conv_pre[heading, here, :]
            sigma = sigmoid(pre)
            act_low[heading, here, :] = (pre * sigma).astype(bf16)
            inside = pl.ds(pl.multiple_of(start + 8, 8), ROWS)
            grad = (gpad[heading, inside, :] + grad_act[heading, here, :]) * silu_slope(pre, sigma)
            gpad[heading, inside, :] = grad
            sums.append(held[5 * heading] + fold(grad))
            sums.append(held[5 * heading + 1] + fold(grad * base))
            for offset in range(1, width_taps):
                begin = 8 - offset if heading == 0 else 8 + offset
                kept = jnp.where(marks[begin : begin + ROWS] == own, 1.0, 0.0)
                moved = window[begin : begin + ROWS]
                sums.append(held[5 * heading + 1 + offset] + fold(grad * moved * wide(kept, tiles)))
        return tuple(sums)

    sums = each_rows(tokens, through_conv, (blank,) * 10)
    small[...] = jnp.zeros(small.shape, f32)
    for heading in range(2):
        bias = jnp.sum(sums[5 * heading], axis=0, keepdims=True)
        for offset in range(width_taps):
            row = heading * width_taps + offset
            small[row : row + 1, :] = jnp.sum(sums[5 * heading + 1 + offset], axis=0, keepdims=True)
        for entry in range(grad_chan.shape[0]):
            row = 2 * width_taps + 2 * entry + heading
            small[row : row + 1, :] = (
                bias if entry == 0 else grad_chan[entry, heading : heading + 1, :]
            )

    def mixed(start, held):
        here = pl.ds(start, ROWS)
        marks = sgpad[pl.ds(start, ROWS + 16), :]
        own = marks[8 : 8 + ROWS]
        total = jnp.zeros((ROWS, chans), f32)
        for heading in range(2):
            window = gpad[heading, pl.ds(start, ROWS + 16), :]
            total = total + window[8 : 8 + ROWS] * taps[heading, 0:1, :]
            for offset in range(1, width_taps):
                begin = 8 + offset if heading == 0 else 8 - offset
                kept = jnp.where(marks[begin : begin + ROWS] == own, 1.0, 0.0)
                total = total + window[begin : begin + ROWS] * wide(kept, tiles) * taps[
                    heading, offset : offset + 1, :
                ]
        mixed_low[here, :] = total.astype(bf16)
        return held

    each_rows(tokens, mixed, 0)

    base_row = 0

    def put(values):
        nonlocal base_row
        for tile in range(values.shape[1] // LANES):
            sums_out[base_row : base_row + values.shape[0], :] = values[
                :, tile * LANES : (tile + 1) * LANES
            ].astype(bf16)
            base_row += values.shape[0]

    put(dot(normed[...], mixed_low[...], TN))
    put(dot(normed[...], gate_low[...], TN))
    for tile in range(tiles):
        sums_out[base_row : base_row + chans, :] = grad_out_w[tile]
        base_row += chans
    put(
        jnp.concatenate(
            [
                dot(parts[heading * rows : (heading + 1) * rows, :], act_low[heading], NN)
                for heading in range(2)
            ],
            axis=0,
        )
    )
    put(jnp.concatenate([grad_dt[0], grad_dt[1]], axis=0))

    partial = dot(mixed_low[...], low_in[0], NT) + dot(gate_low[...], low_in[1], NT)
    padded[pl.ds(8, tokens), :] = partial

    def gains(start, held):
        here = pl.ds(start, ROWS)
        source = hid[here, :].astype(f32)
        scale = lax.rsqrt(jnp.sum(source * source, axis=1, keepdims=True) / width + norm_eps)
        inside = pl.ds(pl.multiple_of(start + 8, 8), ROWS)
        grad = padded[inside, :]
        padded[inside, :] = grad * gain[...]
        return held + fold(grad * source * scale)

    gain_sum = each_rows(tokens, gains, jnp.zeros((8, width), f32))
    small[46:47, :] = jnp.sum(gain_sum, axis=0, keepdims=True)
    put(small[...])
    sums_out[base_row:, :] = jnp.zeros((sums_out.shape[0] - base_row, LANES), bf16)

    weighted = padded[pl.ds(8, tokens), :]
    products = weighted * hid[...].astype(f32)
    turned = weighted.T
    row_dot = dot(jnp.ones((8, width), f32), products, NT, HIGH)
    in_own[0:half_width, :] = jnp.where(me == 0, turned[:half_width], turned[half_width:])
    in_far[0:half_width, :] = jnp.where(me == 0, turned[half_width:], turned[:half_width])
    in_own[pl.ds(half_width, 8), :] = row_dot
    in_far[pl.ds(half_width, 8), :] = row_dot


def outputs_kernel(hid, cot_own, out_own, out_far, in_own, in_far, core, output, input_grad):
    width = hid.shape[1]
    half_width = cot_own.shape[0]
    me = core[0]
    source = hid[...].astype(f32).T
    scale = lax.rsqrt(jnp.sum(source * source, axis=0, keepdims=True) / width + norm_eps)
    own = jnp.where(me == 0, source[:half_width], source[half_width:])
    output[...] = (own + (out_own[...] + out_far[...])).astype(bf16)
    weighted = in_own[0:half_width, :] + in_far[0:half_width, :]
    row_dot = in_own[half_width : half_width + 1, :] + in_far[half_width : half_width + 1, :]
    input_grad[...] = (
        cot_own[...].astype(f32)
        + scale * weighted
        - own * (scale * scale * scale) * (row_dot / width)
    )


def lamb_moments(weight, grad, first, second):
    first_new = beta_one * first + (1.0 - beta_one) * grad
    second_new = beta_two * second + (1.0 - beta_two) * grad * grad
    update = (
        first_new
        / (1.0 - beta_one**STEP)
        / (jnp.sqrt(second_new / (1.0 - beta_two**STEP)) + adam_eps)
        + decay_rate * weight
    )
    return (first_new, second_new, update)


def moments_kernel(
    sums,
    w_in, w_out, w_xp, w_dt, w_cv, w_cp,
    a_in, a_out, a_xp, a_dt, a_cv, a_cp,
    b_in, b_out, b_xp, b_dt, b_cv, b_cp,
    x_in, x_out, x_xp, x_dt, x_cv, x_cp,
    y_in, y_out, y_xp, y_dt, y_cv, y_cp,
    u_in, u_out, u_xp, u_dt, u_cv, u_cp,
    norms, stats,
):
    width, _, chans = w_in.shape
    tiles = chans // LANES
    zero = jnp.zeros((8, chans), f32)
    norms[...] = jnp.zeros(norms.shape, f32)

    def note(place, weight_sq, update_sq):
        for row, values in ((place, weight_sq), (6 + place, update_sq)):
            total = jnp.sum(values, axis=0, keepdims=True)
            lanes = total[:, 0:LANES]
            for tile in range(1, values.shape[1] // LANES):
                lanes = lanes + total[:, tile * LANES : (tile + 1) * LANES]
            norms[row : row + 1, :] = lanes

    def fetch(base, stride, start, count, number):
        return jnp.concatenate(
            [sums[pl.ds(base + tile * stride + start, count), :].astype(f32) for tile in range(number)],
            axis=1,
        )

    held = (zero, zero)
    mean_rows = zero
    for half in range(2):

        def one_in(start, kept, half=half):
            here = pl.ds(start, ROWS)
            grad = fetch(half * tiles * width, width, start, ROWS, tiles)
            weight = w_in[here, half, :]
            first, second, update = lamb_moments(
                weight, grad, a_in[here, half, :], b_in[here, half, :]
            )
            x_in[here, half, :] = first
            y_in[here, half, :] = second
            u_in[half, here, :] = update
            return (
                kept[0] + fold(weight * weight),
                kept[1] + fold(update * update),
                kept[2] + fold(update),
            )

        got = each_rows(width, one_in, (held[0], held[1], mean_rows))
        held, mean_rows = (got[0], got[1]), got[2]
    note(0, *held)
    base = 2 * tiles * width
    in_sum = jnp.sum(mean_rows, axis=0, keepdims=True)
    in_mean = in_sum / (2 * width)

    def spread_in(start, kept):
        here = pl.ds(start, ROWS)
        for half in range(2):
            away = u_in[half, here, :] - in_mean
            kept = kept + fold(away * away)
        return kept

    in_dev = jnp.sum(each_rows(width, spread_in, zero), axis=0, keepdims=True)

    def one_out(start, kept):
        here = pl.ds(start, ROWS)
        grad = fetch(base, chans, start, ROWS, width // LANES)
        weight = w_out[here, :]
        first, second, update = lamb_moments(weight, grad, a_out[here, :], b_out[here, :])
        x_out[here, :] = first
        y_out[here, :] = second
        u_out[here, :] = update
        return (kept[0] + fold(weight * weight), kept[1] + fold(update * update))

    note(1, *each_rows(chans, one_out, (jnp.zeros((8, width), f32),) * 2))
    base += chans * (width // LANES)
    ones = jnp.ones((8, width), f32)
    out_all = u_out[...]
    out_mean = jnp.sum(out_all, axis=1, keepdims=True) / width
    away = out_all - out_mean
    out_sum = dot(ones, out_all, NT, HIGH)
    out_dev = dot(ones, away * away, NT, HIGH)
    stats[0:1, :] = in_mean
    stats[1:2, :] = in_dev
    stats[2:3, :] = out_sum[0:1] / width
    stats[3:4, :] = out_dev[0:1]
    stats[4:8, :] = jnp.zeros((4, chans), f32)

    def small(place, weight, grad, first, second, pads, x_ref, y_ref, u_ref, index):
        first_new, second_new, update = lamb_moments(weight, grad, first, second)
        x_ref[index] = first_new
        y_ref[index] = second_new
        u_ref[index] = update
        return (weight * weight, update * update)

    def rows_sum(values):
        return jnp.sum(values, axis=0, keepdims=True)

    rows = w_xp.shape[1]
    pair = [jnp.zeros((1, chans), f32)] * 2
    for heading in range(2):
        grad = fetch(base, 2 * rows, heading * rows, rows, tiles)
        got = small(2, w_xp[heading], grad, a_xp[heading], b_xp[heading], None, x_xp, y_xp, u_xp, heading)
        pair = [pair[0] + rows_sum(got[0]), pair[1] + rows_sum(got[1])]
    note(2, *pair)
    base += 2 * rows * tiles
    rank = w_dt.shape[1]
    grads = fetch(base, 2 * rank, 0, 2 * rank, tiles)
    pair = [jnp.zeros((1, chans), f32)] * 2
    for heading in range(2):
        grad = grads[heading * rank : (heading + 1) * rank]
        got = small(3, w_dt[heading], grad, a_dt[heading], b_dt[heading], None, x_dt, y_dt, u_dt, heading)
        pair = [pair[0] + rows_sum(got[0]), pair[1] + rows_sum(got[1])]
    note(3, *pair)
    base += 2 * rank * tiles
    grads = fetch(base, 48, 0, 48, tiles)
    taps = w_cv.shape[1]
    pair = [jnp.zeros((1, chans), f32)] * 2
    for heading in range(2):
        grad = grads[heading * taps : (heading + 1) * taps]
        got = small(4, w_cv[heading], grad, a_cv[heading], b_cv[heading], None, x_cv, y_cv, u_cv, heading)
        pair = [pair[0] + rows_sum(got[0]), pair[1] + rows_sum(got[1])]
    note(4, *pair)
    pair = [jnp.zeros((2, chans), f32)] * 2
    for entry in range(w_cp.shape[0]):
        row = 2 * taps + 2 * entry
        grad = grads[row : row + 2]
        got = small(5, w_cp[entry], grad, a_cp[entry], b_cp[entry], None, x_cp, y_cp, u_cp, entry)
        pair = [pair[0] + got[0], pair[1] + got[1]]
    note(5, *pair)
    for tile in range(tiles):
        norms[12 + tile : 13 + tile, :] = grads[46:47, tile * LANES : (tile + 1) * LANES]


def apply_kernel(
    norms_own, norms_far, stats,
    w_in, w_out, w_xp, w_dt, w_cv, w_cp,
    u_in, u_out, u_xp, u_dt, u_cv, u_cp,
    gain, gain_first, gain_second,
    n_in, c_in, n_out, c_out, n_xp, c_xp, n_dt, c_dt, n_cv, c_cv, n_cp, c_cp,
    g_first, g_second, g_new, g_copy, norms_out, stats_out,
):
    width, _, chans = w_in.shape
    totals = norms_own[...] + norms_far[...]
    gain_grad = jnp.concatenate([totals[12 + tile : 13 + tile, :] for tile in range(width // LANES)], axis=1)
    first, second, update = lamb_moments(
        gain[...], gain_grad, gain_first[...], gain_second[...]
    )
    sums = jnp.sum(totals, axis=1, keepdims=True)
    weight_sq = [jnp.sum(gain[...] * gain[...], axis=1, keepdims=True)] + [
        sums[place : place + 1] for place in range(6)
    ]
    update_sq = [jnp.sum(update * update, axis=1, keepdims=True)] + [
        sums[6 + place : 7 + place] for place in range(6)
    ]
    scales = []
    for place in range(7):
        weight_norm = jnp.sqrt(weight_sq[place])
        update_norm = jnp.sqrt(update_sq[place])
        scales.append(learn_rate * weight_norm / (update_norm + adam_eps))
        norms_out[0:1, place : place + 1] = weight_norm
        norms_out[1:2, place : place + 1] = update_norm
    fresh = gain[...] - scales[0] * update
    g_first[...] = first
    g_second[...] = second
    g_new[...] = fresh
    g_copy[...] = fresh.astype(bf16)

    def one_in(start, held):
        here = pl.ds(start, ROWS)
        for half in range(2):
            fresh = w_in[here, half, :] - scales[1] * u_in[half, here, :]
            n_in[here, half, :] = fresh
            c_in[here, half, :] = fresh.astype(bf16)
        return held

    each_rows(width, one_in, 0)

    def one_out(start, held):
        here = pl.ds(start, ROWS)
        fresh = w_out[here, :] - scales[2] * u_out[here, :]
        n_out[here, :] = fresh
        c_out[here, :] = fresh.astype(bf16)
        return held

    each_rows(chans, one_out, 0)
    for place, weight, change, fresh_ref, copy in (
        (3, w_xp, u_xp, n_xp, c_xp),
        (4, w_dt, u_dt, n_dt, c_dt),
        (5, w_cv, u_cv, n_cv, c_cv),
        (6, w_cp, u_cp, n_cp, c_cp),
    ):
        for index in range(weight.shape[0]):
            fresh = weight[index] - scales[place] * change[index]
            fresh_ref[index] = fresh
            copy[index] = fresh.astype(bf16)
    count_in = 2.0 * width
    count_out = 1.0 * width
    mean_in = scales[1] * stats[0:1, :]
    mean_out = scales[2] * stats[2:3, :]
    mean = (count_in * mean_in + count_out * mean_out) / (count_in + count_out)
    gap_in = mean_in - mean
    gap_out = mean_out - mean
    spread = (
        scales[1] * scales[1] * stats[1:2, :]
        + scales[2] * scales[2] * stats[3:4, :]
        + count_in * gap_in * gap_in
        + count_out * gap_out * gap_out
    ) / (count_in + count_out)
    stats_out[0:1, :] = mean
    stats_out[1:2, :] = spread


def call(kernel, outs, args, scratch=(), limit=32, scalars=0, flops=0):
    specs = [pl.BlockSpec(memory_space=pltpu.VMEM)] * (len(args) - scalars)
    specs += [pl.BlockSpec(memory_space=pltpu.SMEM)] * scalars
    return pl.pallas_call(
        kernel,
        out_shape=outs,
        in_specs=specs,
        out_specs=[pl.BlockSpec(memory_space=pltpu.VMEM)] * len(outs),
        scratch_shapes=list(scratch),
        compiler_params=pltpu.CompilerParams(vmem_limit_bytes=limit * MB),
        cost_estimate=pl.CostEstimate(flops=flops, bytes_accessed=8 * MB, transcendentals=0),
    )(*args)


def program(
    dp,
    hidden_in, out_cot, segment_ids,
    norm_gain, in_weight, out_weight, xproj_weight, dtproj_weight, conv_weight, chan_params,
    first_norm_gain, first_in_weight, first_out_weight, first_xproj_weight,
    first_dtproj_weight, first_conv_weight, first_chan_params,
    second_norm_gain, second_in_weight, second_out_weight, second_xproj_weight,
    second_dtproj_weight, second_conv_weight, second_chan_params,
):
    tokens, width = hidden_in.shape
    chans = in_weight.shape[2]
    half_width = first_norm_gain.shape[0]
    tiles = chans // LANES
    rank = dtproj_weight.shape[1]
    count = chan_params.shape[1] - 3
    rows = rank + 2 * count
    taps = conv_weight.shape[1]

    def swap(values):
        return lax.ppermute(values, "chan", [(0, 1), (1, 0)])

    me = lax.axis_index("chan")
    core = me.astype(jnp.int32).reshape(1)
    cot_own = out_cot.T
    cot_far = swap(cot_own)
    segments = segment_ids.reshape(1, tokens)
    gain = norm_gain.reshape(1, width)
    moments_own = jnp.stack([first_norm_gain, second_norm_gain])
    moments_far = swap(moments_own)
    moments_gain = jnp.where(
        me == 0,
        jnp.concatenate([moments_own, moments_far], 1),
        jnp.concatenate([moments_far, moments_own], 1),
    )

    def flip(values):
        return jnp.swapaxes(values, 1, 2)

    def turn(values):
        return jnp.swapaxes(values, 0, 1)

    w_xp = flip(xproj_weight)
    w_cp = turn(chan_params)
    square = (tokens, chans)

    mixing, gate, conv_pre, part, normed, low_in, same = call(
        front_kernel,
        [
            shape(square, f32), shape(square, f32), shape((2,) + square, f32),
            shape((2 * rows, tokens), f32), shape((tokens, width), bf16),
            shape((2, width, chans), bf16), shape((2, tokens, LANES), f32),
        ],
        [hidden_in, segments, gain, in_weight, conv_weight, w_cp, w_xp],
        [pltpu.VMEM((tokens + 16, chans), f32), pltpu.VMEM((tokens + 16, LANES), f32)],
    )
    part_far = swap(part)
    big = pltpu.VMEM((2,) + square, f32)
    flat = pltpu.VMEM((2 * tiles * tokens, LANES), f32)
    grad_part, grad_act, gate_low, out_own, out_send, grad_out_w, grad_dt, grad_chan = call(
        scan_kernel,
        [
            shape((2 * rows, tokens), f32), shape((2,) + square, f32), shape(square, bf16),
            shape((half_width, tokens), f32), shape((half_width, tokens), f32),
            shape((width // LANES, chans, LANES), bf16), shape((2, rank, chans), f32),
            shape((3 + count, 2, chans), f32),
        ],
        [part, part_far, conv_pre, gate, same, cot_own, cot_far, out_weight, dtproj_weight, w_cp, core],
        [
            pltpu.VMEM((2 * rows, tokens), f32), big, big, pltpu.VMEM(square, f32),
            flat, flat, flat, flat, flat, flat, pltpu.VMEM((tiles * tokens, LANES), f32),
            pltpu.VMEM(square, bf16),
            pltpu.VMEM((2, tokens * count, LANES), f32), pltpu.VMEM((2, tokens * count, LANES), f32),
            pltpu.VMEM((2, (tokens + 1) * count, chans), f32),
            pltpu.VMEM((LANES * count, LANES), bf16),
            pltpu.VMEM((2, count, chans), f32), pltpu.VMEM((2, count, chans), f32),
        ],
        limit=60, scalars=1,
    )
    grad_far = swap(grad_part)
    out_far = swap(out_send)
    total_rows = (
        2 * tiles * width + (width // LANES) * chans + tiles * (2 * rows + 2 * rank + 48)
    )
    chunk = -(-total_rows // (dp * 16)) * 16
    sums, in_own, in_send = call(
        back_kernel,
        [
            shape((dp * chunk, LANES), bf16),
            shape((half_width + 8, tokens), f32), shape((half_width + 8, tokens), f32),
        ],
        [
            grad_part, grad_far, grad_act, conv_pre, mixing, gate_low, normed, low_in, segments,
            w_xp, conv_weight, hidden_in, gain, grad_out_w, grad_dt, grad_chan, core,
        ],
        [
            pltpu.VMEM((tokens + 16, chans), f32), pltpu.VMEM((2, tokens + 16, chans), f32),
            pltpu.VMEM((tokens + 16, LANES), f32), pltpu.VMEM(square, bf16),
            pltpu.VMEM((48, chans), f32), pltpu.VMEM((2,) + square, bf16),
        ],
        scalars=1,
    )
    in_far = swap(in_send)
    gathered = lax.all_to_all(sums, "dp", 0, 0, tiled=True).reshape(dp, chunk, LANES)
    shard = jnp.sum(gathered.astype(f32), axis=0).astype(bf16)
    copies = jnp.broadcast_to(shard[None], (dp, chunk, LANES)).reshape(dp * chunk, LANES)
    totals = lax.all_to_all(copies, "dp", 0, 0, tiled=True)
    output, input_grad = call(
        outputs_kernel,
        [shape((half_width, tokens), bf16), shape((half_width, tokens), f32)],
        [hidden_in, cot_own, out_own, out_far, in_own, in_far, core],
        scalars=1,
    )

    weights = [in_weight, out_weight, w_xp, dtproj_weight, conv_weight, w_cp]
    firsts = [
        first_in_weight, first_out_weight, flip(first_xproj_weight), first_dtproj_weight,
        first_conv_weight, turn(first_chan_params),
    ]
    seconds = [
        second_in_weight, second_out_weight, flip(second_xproj_weight), second_dtproj_weight,
        second_conv_weight, turn(second_chan_params),
    ]
    same_shapes = [shape(tensor.shape, f32) for tensor in weights]
    update_shapes = [shape((2, width, chans), f32)] + same_shapes[1:]
    got = call(
        moments_kernel,
        same_shapes * 2 + update_shapes + [shape((16, LANES), f32), shape((8, chans), f32)],
        [totals, *weights, *firsts, *seconds],
    )
    new_first, new_second, updates = got[0:6], got[6:12], got[12:18]
    norms, stats = got[18], got[19]
    norms_far = swap(norms)
    pairs = []
    for tensor in weights:
        pairs += [shape(tensor.shape, f32), shape(tensor.shape, bf16)]
    done = call(
        apply_kernel,
        pairs
        + [shape((1, width), f32)] * 3
        + [shape((1, width), bf16), shape((2, 7), f32), shape((2, chans), f32)],
        [norms, norms_far, stats, *weights, *updates, gain, moments_gain[0:1], moments_gain[1:2]],
    )
    own_start = me * half_width

    def own(values):
        return lax.dynamic_slice_in_dim(values[0], own_start, half_width)

    flat = [own(done[12]), own(done[13]), own(done[14]), own(done[15])]
    for place in range(6):
        entry = [new_first[place], new_second[place], done[2 * place], done[2 * place + 1]]
        if place == 2:
            entry = [flip(tensor) for tensor in entry]
        if place == 5:
            entry = [turn(tensor) for tensor in entry]
        flat += entry
    return (output.T, input_grad.T, *flat, done[16].T, done[17])


def solution(mesh):
    rows = P("dp", None)
    cells = P("dp", "chan")
    last = P(None, None, "chan")
    first = P("chan", None)
    middle = P(None, "chan", None)
    tensors = (last, first, middle, last, last, last)
    outs = [cells, cells] + [P("chan")] * 4
    for spec in tensors:
        outs += [spec] * 4
    return jax.shard_map(
        functools.partial(program, mesh.shape["dp"]),
        mesh=mesh,
        in_specs=(rows, cells, P("dp"), P(), *tensors, P("chan"), *tensors, P("chan"), *tensors),
        out_specs=(*outs, P(), P(None, "chan")),
        check_vma=False,
    )
```

```python
import functools

import jax
import jax.numpy as jnp
from jax import lax
from jax.experimental import pallas as pl
from jax.experimental.pallas import tpu as pltpu
from jax.sharding import PartitionSpec as P

STEP = 4
norm_eps = 1e-06
beta_one = 0.5
beta_two = 0.5
adam_eps = 1e-06
decay_rate = 0.01
learn_rate = 0.3
LOG2E = 1.4426950408889634
FAR = 1e30
FLOOR = -1e-26

f32 = jnp.float32
bf16 = jnp.bfloat16
HIGH = lax.Precision.HIGHEST
LANES = 128
ROWS = 16
MB = 1 << 20


def dot(left, right, dims, precision=None):
    return lax.dot_general(
        left, right, (dims, ((), ())), precision=precision, preferred_element_type=f32
    )


NN = ((1,), (0,))
TN = ((0,), (0,))
NT = ((1,), (1,))


def sigmoid(values):
    return lax.logistic(values)


def silu_slope(values, sigma):
    return sigma * (1.0 + values * (1.0 - sigma))


def softplus(values):
    return jnp.maximum(values, 0.0) + jnp.log1p(jnp.exp(-jnp.abs(values)))


def wide(tile, times):
    return jnp.concatenate([tile] * times, axis=1)


def fold(values):
    total = values[0:8]
    for start in range(8, values.shape[0], 8):
        total = total + values[start : start + 8]
    return total


def shape(dims, dtype):
    return jax.ShapeDtypeStruct(dims, dtype)


def each_rows(length, body, carry=None, rows=ROWS):
    def step(index, held):
        return body(pl.multiple_of(index * rows, rows), held)

    return lax.fori_loop(0, length // rows, step, carry)


def spread_segments(numbers, tokens):
    across = lax.broadcasted_iota(jnp.int32, (tokens, tokens), 0)
    along = lax.broadcasted_iota(jnp.int32, (tokens, tokens), 1)
    row = numbers.astype(f32).reshape(1, tokens)
    picked = jnp.where(across == along, row, 0.0).astype(bf16)
    return dot(picked, jnp.ones((tokens, LANES), bf16), NN)


def front_kernel(
    hid, seg, gain, w_in, taps, params, w_xp,
    mix_out, gate_out, conv_out, part_out, norm_out, low_out, same_out,
    padded, sgpad,
    *, need, save,
):
    tokens, width = hid.shape
    chans = mix_out.shape[1]
    tiles = chans // LANES

    need(hid, gain)
    gain_row = gain[...].reshape(1, width)

    def normalise(start, held):
        source = hid[pl.ds(start, ROWS), :].astype(f32)
        scale = lax.rsqrt(jnp.sum(source * source, axis=1, keepdims=True) / width + norm_eps)
        norm_out[pl.ds(start, ROWS), :] = (source * scale * gain_row).astype(bf16)
        return held

    each_rows(tokens, normalise, 0)
    save(norm_out)
    need()
    for half in range(2):
        low_out[half] = w_in[:, half, :].astype(bf16)
    save(low_out)
    normed = norm_out[...]
    mixing = dot(normed, low_out[0], NN)
    mix_out[...] = mixing
    padded[0:8, :] = jnp.zeros((8, chans), f32)
    padded[pl.ds(8, tokens), :] = mixing
    padded[pl.ds(8 + tokens, 8), :] = jnp.zeros((8, chans), f32)
    save(mix_out)
    gate_out[...] = dot(normed, low_out[1], NN)
    save(gate_out)
    numbers = spread_segments(seg[...], tokens)
    sgpad[0:8, :] = jnp.full((8, LANES), -1.0, f32)
    sgpad[pl.ds(8, tokens), :] = numbers
    sgpad[pl.ds(8 + tokens, 8), :] = jnp.full((8, LANES), -1.0, f32)
    width_taps = taps.shape[1]

    def convolve(start, held):
        window = padded[pl.ds(start, ROWS + 16), :]
        marks = sgpad[pl.ds(start, ROWS + 16), :]
        own = marks[8 : 8 + ROWS]
        base = window[8 : 8 + ROWS]
        for heading in range(2):
            total = params[0, heading : heading + 1, :] + taps[heading, 0:1, :] * base
            for offset in range(1, width_taps):
                begin = 8 - offset if heading == 0 else 8 + offset
                same = jnp.where(marks[begin : begin + ROWS] == own, 1.0, 0.0)
                if offset == 1:
                    same_out[heading, pl.ds(start, ROWS), :] = same
                moved = window[begin : begin + ROWS]
                total = total + taps[heading, offset : offset + 1, :] * moved * wide(same, tiles)
            conv_out[heading, pl.ds(start, ROWS), :] = total
        return held

    each_rows(tokens, convolve, 0)
    save(conv_out, same_out)
    for heading in range(2):
        pre = conv_out[heading]
        act_low = (pre * sigmoid(pre)).astype(bf16)
        rows = w_xp.shape[1]
        part_out[heading * rows : (heading + 1) * rows, :] = dot(
            w_xp[heading].astype(bf16), act_low, NT
        )


SPAN = 64


class Sizes:
    def __init__(self, tokens, chans, count, rank):
        self.tokens, self.chans, self.count, self.rank = tokens, chans, count, rank
        self.tiles = chans // LANES
        self.blocks = tokens // LANES
        self.rows = rank + 2 * count
        self.block_rows = LANES * count
        self.pairs = [(heading, tile) for heading in range(2) for tile in range(self.tiles)]

    def base(self, heading, tile):
        return (heading * self.tiles + tile) * self.tokens

    def row(self, ref, heading, tile, at):
        return ref[pl.ds(self.base(heading, tile) + at, 1), :]

    def whole(self, ref, heading):
        starts = [self.base(heading, tile) for tile in range(self.tiles)]
        return jnp.concatenate([ref[start : start + self.tokens, :] for start in starts], axis=1)


def cols(tile):
    return slice(tile * LANES, (tile + 1) * LANES)


def split(values):
    high = values.astype(bf16)
    return high, (values - high.astype(f32)).astype(bf16)


def group_maps(target, tile, heading, count):
    groups = tile.shape[1] // count
    for group in range(groups):
        block, place = divmod(group * count, LANES)
        own = tile[:, cols(block)]
        if place:
            own = pltpu.roll(own, LANES - place, 1)
        target[heading, group] = own


def diagonal_maps(target, tile, heading, count):
    tokens = tile.shape[1]
    squared = count * count
    lane = lax.broadcasted_iota(jnp.int32, (count, squared), 1)
    row = lax.broadcasted_iota(jnp.int32, (count, squared), 0)
    repeat = jnp.where(lane % count == row, 1.0, 0.0).astype(bf16)
    token = lax.broadcasted_iota(jnp.int32, (tokens, squared), 0)
    place = lax.broadcasted_iota(jnp.int32, (tokens, squared), 1)
    mine = place // count == token % count
    for number, part in enumerate(split(tile)):
        spread = jnp.where(mine, dot(part, repeat, TN), 0.0).astype(bf16)
        target[heading, :, number] = spread.reshape(tokens // count, count, squared)


def weigh_states(left, maps):
    half = maps.shape[0] // 2
    got = dot(maps, left, NN)
    return got[:half] + got[half:]


def gather_states(left, right, count):
    products = dot(left, right, NT)
    lane = lax.broadcasted_iota(jnp.int32, (count, count), 1)
    total = products[0:count]
    for place in range(1, count):
        total = jnp.where(lane == place, products[place * count : (place + 1) * count], total)
    return total


def dot3(left, right, dims):
    (left_high, left_low), (right_high, right_low) = split(left), split(right)
    return dot(left_high, right_high, dims) + (
        dot(left_low, right_high, dims) + dot(left_high, right_low, dims)
    )


def scan_kernel(
    own_part, far_part, conv_pre, gate, same, cot_own, cot_far, w_out, w_dt, params, normed, core,
    grad_part, early, out_far, out_own, grad_act, grad_dt, grad_chan, gate_low,
    proj, pre_step, grad_branch, far_step, inflow, grad_y, grad_y_low, result, decayed, branch_low,
    maps, diagonal, gathered, states, low_one, low_two, rates, rates2, inflow_low,
    *, need, save,
):
    tokens, chans = gate.shape
    z = Sizes(tokens, chans, params.shape[0] - 3, w_dt.shape[1])
    count, rank, rows, tiles = z.count, z.rank, z.rows, z.tiles
    half_width = cot_own.shape[0]
    width = 2 * half_width
    me = core[0]
    groups = tokens // count

    proj[...] = own_part[...] + far_part[...]
    need(params, w_dt, w_out, cot_own)
    low_out = w_out[...].astype(bf16)
    low_cot = jnp.where(
        me == 0,
        jnp.concatenate([cot_own[...].astype(f32), cot_far[...].astype(f32)], 0),
        jnp.concatenate([cot_far[...].astype(f32), cot_own[...].astype(f32)], 0),
    ).astype(bf16)
    grad_branch[...] = dot(low_cot, low_out, ((0,), (1,)))
    for heading in range(2):
        for n in range(count):
            value = -jnp.exp(params[3 + n, heading : heading + 1, :])
            rates[heading, n : n + 1, :] = value
            rates2[heading, n : n + 1, :] = jnp.minimum(value * LOG2E, FLOOR)
        pre_step[heading] = (
            dot3(proj[heading * rows : heading * rows + rank, :], w_dt[heading], TN)
            + params[1, heading : heading + 1, :]
        )
        first = heading * rows + rank
        group_maps(maps, proj[first : first + count, :], heading, count)
        diagonal_maps(diagonal, proj[first + count : first + 2 * count, :], heading, count)

    need(conv_pre, gate, same)
    for tile in range(tiles):

        def prepare(start, held, tile=tile):
            here = pl.ds(start, SPAN)
            for heading in range(2):
                pre = conv_pre[heading, here, cols(tile)]
                act = pre * sigmoid(pre)
                size = softplus(pre_step[heading, here, cols(tile)])
                there = pl.ds(z.base(heading, tile) + start, SPAN)
                entering = size * act
                inflow[there, :] = entering
                inflow_low[heading, here, cols(tile)] = entering.astype(bf16)
                far_step[there, :] = jnp.where(same[heading, here, :] > 0.5, size, FAR)
            gated = gate[here, cols(tile)]
            back = grad_branch[here, cols(tile)] * (gated * sigmoid(gated))
            grad_y[pl.ds(z.base(0, tile) + start, SPAN), :] = back
            grad_y_low[here, cols(tile)] = back.astype(bf16)
            return held

        each_rows(tokens, prepare, 0, SPAN)

    blank = jnp.zeros((count, LANES), f32)
    states[0, 0:count, :] = jnp.zeros((count, chans), f32)
    states[1, tokens * count : (tokens + 1) * count, :] = jnp.zeros((count, chans), f32)
    low_one[...] = jnp.zeros(low_one.shape, bf16)
    low_two[...] = jnp.zeros(low_two.shape, bf16)

    def group_of(order, heading):
        return order if heading == 0 else groups - 1 - order

    def run_forward(order, carried, low):
        carried = list(carried)
        enters = [maps[heading, group_of(order, heading)] for heading in range(2)]
        for ahead in range(count):
            for heading in range(2):
                inner = ahead if heading == 0 else count - 1 - ahead
                at = group_of(order, heading) * count + inner
                kept = pl.multiple_of((at + (1 if heading == 0 else 0)) * count, count)
                enter = jnp.broadcast_to(enters[heading][:, inner : inner + 1], (count, LANES))
                for tile in range(tiles):
                    number = heading * tiles + tile
                    decay = jnp.exp2(z.row(far_step, heading, tile, at) * rates2[heading, :, cols(tile)])
                    state = decay * carried[number] + enter * z.row(inflow, heading, tile, at)
                    carried[number] = state
                    states[heading, pl.ds(kept, count), cols(tile)] = state
                    low[heading, inner * count : (inner + 1) * count, cols(tile)] = state.astype(bf16)
        return tuple(carried)

    def rows_of(group):
        return pl.ds(pl.multiple_of(group * count, count), count)

    def post_forward(order, low):
        for heading in range(2):
            group = group_of(order, heading)
            left = low[heading]
            gathered[heading, group] = gather_states(left, grad_y_low[rows_of(group), :], count)
            result[heading, rows_of(group), :] = weigh_states(
                left, diagonal[heading, group].reshape(2 * count, count * count)
            )

    def forward(index, carried):
        order = 2 * index
        post_forward(jnp.maximum(order - 1, 0), low_two.at[0])
        carried = run_forward(order, carried, low_one.at[0])
        post_forward(order, low_one.at[0])
        return run_forward(order + 1, carried, low_two.at[0])

    lax.fori_loop(0, groups // 2, forward, (blank,) * len(z.pairs))
    post_forward(groups - 1, low_two.at[0])

    def store_gathered(target_row, heading):
        for block in range(z.blocks):
            per = LANES // count
            pieces = [gathered[heading, block * per + place] for place in range(per)]
            grad_part[target_row : target_row + count, cols(block)] = jnp.concatenate(pieces, axis=1)

    for heading in range(2):
        first = heading * rows + rank
        store_gathered(first + count, heading)
        group_maps(maps, proj[first + count : first + 2 * count, :], heading, count)
        diagonal_maps(diagonal, proj[first : first + count, :], heading, count)

    for tile in range(tiles):

        def finish(start, held, tile=tile):
            here = pl.ds(start, SPAN)
            total = jnp.zeros((SPAN, LANES), f32)
            sums = []
            back = grad_y[pl.ds(z.base(0, tile) + start, SPAN), :]
            for heading in range(2):
                pre = conv_pre[heading, here, cols(tile)]
                act = pre * sigmoid(pre)
                total = total + result[heading, here, cols(tile)]
                total = total + params[2, heading : heading + 1, cols(tile)] * act
                sums.append(held[heading] + fold(back * act))
            gated = gate[here, cols(tile)]
            sigma = sigmoid(gated)
            branch_low[here, cols(tile)] = (total * (gated * sigma)).astype(bf16)
            gate_low[here, cols(tile)] = (
                grad_branch[here, cols(tile)] * total * silu_slope(gated, sigma)
            ).astype(bf16)
            return tuple(sums)

        skips = each_rows(tokens, finish, (jnp.zeros((8, LANES), f32),) * 2, SPAN)
        for heading in range(2):
            grad_chan[2, heading : heading + 1, cols(tile)] = jnp.sum(
                skips[heading], axis=0, keepdims=True
            )
    save(gate_low)
    need(normed)
    branch = branch_low[...]
    grad_w = dot(branch, low_cot, ((0,), (1,))).astype(bf16)
    for tile in range(width // LANES):
        early[tile * chans : (tile + 1) * chans, :] = grad_w[:, cols(tile)]
    base_row = chans * (width // LANES)
    grad_w = dot(normed[...], gate_low[...], TN).astype(bf16)
    for tile in range(tiles):
        early[base_row + tile * width : base_row + (tile + 1) * width, :] = grad_w[:, cols(tile)]
    base_row += tiles * width
    if early.shape[0] > base_row:
        early[base_row:, :] = jnp.zeros((early.shape[0] - base_row, LANES), bf16)
    sent = dot(low_out, branch, ((0,), (1,)))
    out_own[...] = jnp.where(me == 0, sent[:half_width], sent[half_width:])
    out_far[...] = jnp.where(me == 0, sent[half_width:], sent[:half_width])
    save(out_own)

    def run_backward(order, held, low, products):
        waiting = list(held[: len(z.pairs)])
        totals = list(held[len(z.pairs) :])
        leaves = [maps[heading, group_of(order, 1 - heading)] for heading in range(2)]
        for ahead in range(count):
            for heading in range(2):
                inner = ahead if heading == 1 else count - 1 - ahead
                at = group_of(order, 1 - heading) * count + inner
                prior = pl.multiple_of((at + (0 if heading == 0 else 1)) * count, count)
                leave = jnp.broadcast_to(leaves[heading][:, inner : inner + 1], (count, LANES))
                here = slice(inner * count, (inner + 1) * count)
                for tile in range(tiles):
                    number = heading * tiles + tile
                    size = z.row(far_step, heading, tile, at)
                    decay = jnp.exp2(size * rates2[heading, :, cols(tile)])
                    grad = leave * z.row(grad_y, 0, tile, at) + waiting[number]
                    lead = decay * grad
                    waiting[number] = lead
                    slope = lead * states[heading, pl.ds(prior, count), cols(tile)]
                    totals[number] = totals[number] + slope * size
                    products[heading, here, cols(tile)] = (slope * rates[heading, :, cols(tile)]).astype(bf16)
                    low[heading, here, cols(tile)] = grad.astype(bf16)
        return tuple(waiting + totals)

    lane = lax.broadcasted_iota(jnp.int32, (count, count * count), 1)
    row = lax.broadcasted_iota(jnp.int32, (count, count * count), 0)
    ones = jnp.where(lane // count == row, 1.0, 0.0).astype(bf16)

    def post_backward(order, low, products):
        for heading in range(2):
            group = group_of(order, 1 - heading)
            left = low[heading]
            gathered[heading, group] = gather_states(left, inflow_low[heading, rows_of(group), :], count)
            result[heading, rows_of(group), :] = weigh_states(
                left, diagonal[heading, group].reshape(2 * count, count * count)
            )
            decayed[heading, rows_of(group), :] = dot(ones, products[heading], NN)

    def backward(index, held):
        order = 2 * index
        post_backward(jnp.maximum(order - 1, 0), low_two.at[0], low_two.at[1])
        held = run_backward(order, held, low_one.at[0], low_one.at[1])
        post_backward(order, low_one.at[0], low_one.at[1])
        return run_backward(order + 1, held, low_two.at[0], low_two.at[1])

    held = lax.fori_loop(0, groups // 2, backward, (blank,) * (2 * len(z.pairs)))
    post_backward(groups - 1, low_two.at[0], low_two.at[1])
    for number, (heading, tile) in enumerate(z.pairs):
        slopes = held[len(z.pairs) + number] * rates[heading, :, cols(tile)]
        for n in range(count):
            grad_chan[3 + n, heading : heading + 1, cols(tile)] = slopes[n : n + 1]
    for heading in range(2):
        store_gathered(heading * rows + rank, heading)

    for tile in range(tiles):

        def close(start, held, tile=tile):
            here = pl.ds(start, SPAN)
            sums = []
            back = grad_y[pl.ds(z.base(0, tile) + start, SPAN), :]
            for heading in range(2):
                pre = conv_pre[heading, here, cols(tile)]
                act = pre * sigmoid(pre)
                passed = result[heading, here, cols(tile)]
                reach = pre_step[heading, here, cols(tile)]
                grad_act[heading, here, cols(tile)] = (
                    passed * softplus(reach) + back * params[2, heading : heading + 1, cols(tile)]
                )
                grad_pre = (decayed[heading, here, cols(tile)] + passed * act) * sigmoid(reach)
                pre_step[heading, here, cols(tile)] = grad_pre
                sums.append(held[heading] + fold(grad_pre))
            return tuple(sums)

        biases = each_rows(tokens, close, (jnp.zeros((8, LANES), f32),) * 2, SPAN)
        for heading in range(2):
            grad_chan[1, heading : heading + 1, cols(tile)] = jnp.sum(
                biases[heading], axis=0, keepdims=True
            )
    save(grad_act)
    for heading in range(2):
        grad_chan[0, heading : heading + 1, :] = jnp.zeros((1, chans), f32)
        grad_pre = pre_step[heading]
        grad_part[heading * rows : heading * rows + rank, :] = dot3(w_dt[heading], grad_pre, NT)
        grad_dt[heading] = dot3(proj[heading * rows : heading * rows + rank, :], grad_pre, NN)


def scan_call(args, sizes, early_rows, half_width, limit=52):
    z = sizes
    square = (z.tokens, z.chans)
    both = (2,) + square
    flat = pltpu.VMEM((2 * z.tiles * z.tokens, LANES), f32)
    groups = z.tokens // z.count
    squared = z.count * z.count
    return call(
        scan_kernel,
        at(
            "x", shape((2 * z.rows, z.tokens), f32), shape((early_rows, LANES), bf16),
            shape((half_width, z.tokens), f32),
        )
        + at(
            "h", shape((half_width, z.tokens), f32), shape(both, f32), shape((2, z.rank, z.chans), f32),
            shape((3 + z.count, 2, z.chans), f32), shape(square, bf16),
        ),
        args,
        [
            pltpu.VMEM((2 * z.rows, z.tokens), f32), pltpu.VMEM(both, f32), pltpu.VMEM(square, f32),
            flat, flat, pltpu.VMEM((z.tiles * z.tokens, LANES), f32), pltpu.VMEM(square, bf16),
            pltpu.VMEM(both, f32), pltpu.VMEM(both, f32), pltpu.VMEM(square, bf16),
            pltpu.VMEM((2, groups, z.count, LANES), f32),
            pltpu.VMEM((2, groups, 2, z.count, squared), bf16),
            pltpu.VMEM((2, groups, z.count, z.count), f32),
            pltpu.VMEM((2, (z.tokens + 1) * z.count, z.chans), f32),
            pltpu.VMEM((2, 2, squared, z.chans), bf16), pltpu.VMEM((2, 2, squared, z.chans), bf16),
            pltpu.VMEM((2, z.count, z.chans), f32), pltpu.VMEM((2, z.count, z.chans), f32),
            pltpu.VMEM(both, bf16),
        ],
        limit=limit, micros=30,
    )


def back_kernel(
    own_part, far_part, grad_act, conv_pre, mixing, gate_low, normed, low_in, seg, w_xp, taps, hid, gain,
    grad_dt, grad_chan, core,
    sums_out, in_own, in_far,
    padded, gpad, sgpad, mixed_low, small, act_low,
    *, need, save,
):
    tokens, width = hid.shape
    chans = mixing.shape[1]
    tiles = chans // LANES
    rows = w_xp.shape[1]
    width_taps = taps.shape[1]
    me = core[0]
    half_width = in_own.shape[0] - 8
    edge = jnp.zeros((8, chans), f32)
    padded[0:8, :] = edge
    padded[pl.ds(8 + tokens, 8), :] = edge
    gpad[0, 0:8, :] = edge
    gpad[1, 0:8, :] = edge
    gpad[0, pl.ds(8 + tokens, 8), :] = edge
    gpad[1, pl.ds(8 + tokens, 8), :] = edge
    sgpad[0:8, :] = jnp.full((8, LANES), -1.0, f32)
    sgpad[pl.ds(8 + tokens, 8), :] = jnp.full((8, LANES), -1.0, f32)
    need(seg, w_xp, mixing)
    padded[pl.ds(8, tokens), :] = mixing[...]
    sgpad[pl.ds(8, tokens), :] = spread_segments(seg[...], tokens)

    parts = (own_part[...] + far_part[...]).astype(bf16)
    for heading in range(2):
        part = parts[heading * rows : (heading + 1) * rows, :]
        gpad[heading, pl.ds(8, tokens), :] = dot(part, w_xp[heading].astype(bf16), TN)

    blank = jnp.zeros((8, chans), f32)
    need()

    def through_conv(start, held):
        here = pl.ds(start, ROWS)
        window = padded[pl.ds(start, ROWS + 16), :]
        marks = sgpad[pl.ds(start, ROWS + 16), :]
        own = marks[8 : 8 + ROWS]
        base = window[8 : 8 + ROWS]
        sums = []
        for heading in range(2):
            pre = conv_pre[heading, here, :]
            sigma = sigmoid(pre)
            act_low[heading, here, :] = (pre * sigma).astype(bf16)
            inside = pl.ds(pl.multiple_of(start + 8, 8), ROWS)
            grad = (gpad[heading, inside, :] + grad_act[heading, here, :]) * silu_slope(pre, sigma)
            gpad[heading, inside, :] = grad
            sums.append(held[5 * heading] + fold(grad))
            sums.append(held[5 * heading + 1] + fold(grad * base))
            for offset in range(1, width_taps):
                begin = 8 - offset if heading == 0 else 8 + offset
                kept = jnp.where(marks[begin : begin + ROWS] == own, 1.0, 0.0)
                moved = window[begin : begin + ROWS]
                sums.append(held[5 * heading + 1 + offset] + fold(grad * moved * wide(kept, tiles)))
        return tuple(sums)

    sums = each_rows(tokens, through_conv, (blank,) * 10)
    small[...] = jnp.zeros(small.shape, f32)
    for heading in range(2):
        bias = jnp.sum(sums[5 * heading], axis=0, keepdims=True)
        for offset in range(width_taps):
            row = heading * width_taps + offset
            small[row : row + 1, :] = jnp.sum(sums[5 * heading + 1 + offset], axis=0, keepdims=True)
        for entry in range(grad_chan.shape[0]):
            row = 2 * width_taps + 2 * entry + heading
            small[row : row + 1, :] = (
                bias
                if entry == 0
                else grad_chan[entry, heading : heading + 1, :]
            )

    def mixed(start, held):
        here = pl.ds(start, ROWS)
        marks = sgpad[pl.ds(start, ROWS + 16), :]
        own = marks[8 : 8 + ROWS]
        total = jnp.zeros((ROWS, chans), f32)
        for heading in range(2):
            window = gpad[heading, pl.ds(start, ROWS + 16), :]
            total = total + window[8 : 8 + ROWS] * taps[heading, 0:1, :]
            for offset in range(1, width_taps):
                begin = 8 + offset if heading == 0 else 8 - offset
                kept = jnp.where(marks[begin : begin + ROWS] == own, 1.0, 0.0)
                total = total + window[begin : begin + ROWS] * wide(kept, tiles) * taps[
                    heading, offset : offset + 1, :
                ]
        mixed_low[here, :] = total.astype(bf16)
        return held

    each_rows(tokens, mixed, 0)

    base_row = 0

    def put(values):
        nonlocal base_row
        for tile in range(values.shape[1] // LANES):
            sums_out[base_row : base_row + values.shape[0], :] = values[
                :, tile * LANES : (tile + 1) * LANES
            ].astype(bf16)
            base_row += values.shape[0]

    put(dot(normed[...], mixed_low[...], TN))
    put(
        jnp.concatenate(
            [
                dot(parts[heading * rows : (heading + 1) * rows, :], act_low[heading], NN)
                for heading in range(2)
            ],
            axis=0,
        )
    )
    put(jnp.concatenate([grad_dt[0], grad_dt[1]], axis=0))

    partial = dot(mixed_low[...], low_in[0], NT) + dot(gate_low[...], low_in[1], NT)
    padded[pl.ds(8, tokens), :] = partial

    gain_row = gain[...].reshape(1, width)

    def gains(start, held):
        here = pl.ds(start, ROWS)
        source = hid[here, :].astype(f32)
        scale = lax.rsqrt(jnp.sum(source * source, axis=1, keepdims=True) / width + norm_eps)
        inside = pl.ds(pl.multiple_of(start + 8, 8), ROWS)
        grad = padded[inside, :]
        padded[inside, :] = grad * gain_row
        return held + fold(grad * source * scale)

    gain_sum = each_rows(tokens, gains, jnp.zeros((8, width), f32))
    small[46:47, :] = jnp.sum(gain_sum, axis=0, keepdims=True)
    put(small[...])
    sums_out[base_row:, :] = jnp.zeros((sums_out.shape[0] - base_row, LANES), bf16)

    weighted = padded[pl.ds(8, tokens), :]
    products = weighted * hid[...].astype(f32)
    turned = weighted.T
    row_dot = dot(jnp.ones((8, width), f32), products, NT, HIGH)
    in_own[0:half_width, :] = jnp.where(me == 0, turned[:half_width], turned[half_width:])
    in_far[0:half_width, :] = jnp.where(me == 0, turned[half_width:], turned[:half_width])
    in_own[pl.ds(half_width, 8), :] = row_dot
    in_far[pl.ds(half_width, 8), :] = row_dot


def outputs_kernel(hid, cot_own, out_own, out_far, in_own, in_far, core, output, input_grad, *, need, save):
    width = hid.shape[1]
    half_width = cot_own.shape[0]
    me = core[0]
    need()
    source = hid[...].astype(f32).T
    scale = lax.rsqrt(jnp.sum(source * source, axis=0, keepdims=True) / width + norm_eps)
    own = jnp.where(me == 0, source[:half_width], source[half_width:])
    output[...] = (own + (out_own[...] + out_far[...])).astype(bf16)
    weighted = in_own[0:half_width, :] + in_far[0:half_width, :]
    save(output)
    row_dot = in_own[half_width : half_width + 1, :] + in_far[half_width : half_width + 1, :]
    input_grad[...] = (
        cot_own[...].astype(f32)
        + scale * weighted
        - own * (scale * scale * scale) * (row_dot / width)
    )


def lamb_moments(weight, grad, first, second):
    first_new = beta_one * first + (1.0 - beta_one) * grad
    second_new = beta_two * second + (1.0 - beta_two) * grad * grad
    update = (
        first_new
        / (1.0 - beta_one**STEP)
        / (jnp.sqrt(second_new / (1.0 - beta_two**STEP)) + adam_eps)
        + decay_rate * weight
    )
    return (first_new, second_new, update)


def rows_sum(values):
    return jnp.sum(values, axis=0, keepdims=True)


def lanes_sum(values):
    total = rows_sum(values)
    lanes = total[:, 0:LANES]
    for tile in range(1, values.shape[1] // LANES):
        lanes = lanes + total[:, cols(tile)]
    return lanes


def fetch(sums, base, stride, start, count, number):
    return jnp.concatenate(
        [sums[pl.ds(base + tile * stride + start, count), :].astype(f32) for tile in range(number)], axis=1
    )


def spread_of(update, mean, length):
    def step(start, kept):
        away = update[pl.ds(start, ROWS), :] - mean
        return kept + fold(away * away)

    return rows_sum(each_rows(length, step, jnp.zeros((8, update.shape[1]), f32)))


def half_update(half, sums, base, stride, weights, a_ref, b_ref, x_ref, y_ref, u_ref):
    length, _, chans = weights.shape
    zero = jnp.zeros((8, chans), f32)

    def step(start, kept):
        here = pl.ds(start, ROWS)
        grad = fetch(sums, base, stride, start, ROWS, chans // LANES)
        weight = weights[here, half, :]
        first, second, update = lamb_moments(weight, grad, a_ref[here, half, :], b_ref[here, half, :])
        x_ref[here, :] = first
        y_ref[here, :] = second
        u_ref[here, :] = update
        return (
            kept[0] + fold(weight * weight), kept[1] + fold(update * update), kept[2] + fold(update)
        )

    return each_rows(length, step, (zero, zero, zero))


def early_kernel(
    sums, w_in, a_in, b_in, w_out, a_out, b_out,
    x_out, y_out, x_gate, y_gate, u_gate, u_out, norms, stats,
    *, need, save,
):
    width, _, chans = w_in.shape
    tiles = width // LANES
    norms[...] = jnp.zeros(norms.shape, f32)
    zero = jnp.zeros((8, width), f32)
    need(w_out, a_out, b_out)

    def one_out(start, kept):
        here = pl.ds(start, ROWS)
        grad = fetch(sums, 0, chans, start, ROWS, tiles)
        weight = w_out[here, :]
        first, second, update = lamb_moments(weight, grad, a_out[here, :], b_out[here, :])
        x_out[here, :] = first
        y_out[here, :] = second
        u_out[here, :] = update
        return (kept[0] + fold(weight * weight), kept[1] + fold(update * update))

    weight_sq, update_sq = each_rows(chans, one_out, (zero, zero))
    norms[1:2, :] = lanes_sum(weight_sq)
    norms[7:8, :] = lanes_sum(update_sq)
    save(x_out, y_out, u_out)
    need()
    weight_sq, update_sq, total = half_update(
        1, sums, chans * tiles, width, w_in, a_in, b_in, x_gate, y_gate, u_gate
    )
    norms[0:1, :] = lanes_sum(weight_sq)
    norms[6:7, :] = lanes_sum(update_sq)
    save(x_gate, y_gate, u_gate)
    gate_mean = rows_sum(total) / width
    stats[0:1, :] = gate_mean
    stats[1:2, :] = spread_of(u_gate, gate_mean, width)
    ones = jnp.ones((8, width), f32)
    out_all = u_out[...]
    out_mean = jnp.sum(out_all, axis=1, keepdims=True) / width
    away = out_all - out_mean
    stats[2:3, :] = dot(ones, out_all, NT, HIGH)[0:1] / width
    stats[3:4, :] = dot(ones, away * away, NT, HIGH)[0:1]
    stats[4:8, :] = jnp.zeros((4, chans), f32)


def late_kernel(
    sums, x_gate, y_gate, early_norms, early_stats,
    w_in, a_in, b_in, w_xp, a_xp, b_xp, w_dt, a_dt, b_dt, w_cv, a_cv, b_cv, w_cp, a_cp, b_cp,
    x_in, y_in, x_xp, y_xp, x_dt, y_dt, x_cv, y_cv, x_cp, y_cp,
    u_mix, u_xp, u_dt, u_cv, u_cp, norms, stats,
    x_mix, y_mix,
    *, need, save,
):
    width, _, chans = w_in.shape
    tiles = chans // LANES
    need(early_norms, early_stats, w_in, a_in, b_in)
    norms[...] = early_norms[...]
    stats[...] = early_stats[...]
    weight_sq, update_sq, total = half_update(
        0, sums, 0, width, w_in, a_in, b_in, x_mix, y_mix, u_mix
    )
    save(u_mix)
    need()
    x_in[:, 0, :] = x_mix[...]
    x_in[:, 1, :] = x_gate[...]
    y_in[:, 0, :] = y_mix[...]
    y_in[:, 1, :] = y_gate[...]
    save(x_in, y_in)
    norms[0:1, :] += lanes_sum(weight_sq)
    norms[6:7, :] += lanes_sum(update_sq)
    mix_mean = rows_sum(total) / width
    stats[4:5, :] = mix_mean
    stats[5:6, :] = spread_of(u_mix, mix_mean, width)
    base = tiles * width

    def small(place, items, weight, a_ref, b_ref, x_ref, y_ref, u_ref):
        weight_sq, update_sq = jnp.zeros((1, LANES), f32), jnp.zeros((1, LANES), f32)
        for index, grad in enumerate(items):
            held = weight[index]
            first, second, update = lamb_moments(held, grad, a_ref[index], b_ref[index])
            x_ref[index] = first
            y_ref[index] = second
            u_ref[index] = update
            weight_sq = weight_sq + lanes_sum(held * held)
            update_sq = update_sq + lanes_sum(update * update)
        norms[place : place + 1, :] = weight_sq
        norms[6 + place : 7 + place, :] = update_sq

    rows = w_xp.shape[1]
    grads = fetch(sums, base, 2 * rows, 0, 2 * rows, tiles)
    small(2, [grads[:rows], grads[rows:]], w_xp, a_xp, b_xp, x_xp, y_xp, u_xp)
    base += 2 * rows * tiles
    rank = w_dt.shape[1]
    grads = fetch(sums, base, 2 * rank, 0, 2 * rank, tiles)
    small(3, [grads[:rank], grads[rank:]], w_dt, a_dt, b_dt, x_dt, y_dt, u_dt)
    base += 2 * rank * tiles
    grads = fetch(sums, base, 48, 0, 48, tiles)
    taps = w_cv.shape[1]
    small(4, [grads[:taps], grads[taps : 2 * taps]], w_cv, a_cv, b_cv, x_cv, y_cv, u_cv)
    entries = w_cp.shape[0]
    items = [grads[2 * (taps + entry) : 2 * (taps + entry) + 2] for entry in range(entries)]
    small(5, items, w_cp, a_cp, b_cp, x_cp, y_cp, u_cp)
    for tile in range(tiles):
        norms[12 + tile : 13 + tile, :] = grads[46:47, cols(tile)]


def apply_kernel(
    norms_own, norms_far, stats,
    w_in, w_out, w_xp, w_dt, w_cv, w_cp,
    u_mix, u_gate, u_out, u_xp, u_dt, u_cv, u_cp,
    gain, gain_first, gain_second, core,
    n_in, c_in, n_out, c_out, n_xp, c_xp, n_dt, c_dt, n_cv, c_cv, n_cp, c_cp,
    g_first, g_second, g_new, g_copy, norms_out, stats_out,
    *, need, save,
):
    width, _, chans = w_in.shape
    half_width = g_new.shape[0]
    me = core[0]
    need(norms_own, gain, stats)
    totals = norms_own[...] + norms_far[...]
    gain_grad = jnp.concatenate(
        [totals[12 + tile : 13 + tile, :] for tile in range(width // LANES)], axis=1
    )
    gain_row = gain[...].reshape(1, width)
    first, second, update = lamb_moments(gain_row, gain_grad, gain_first[...], gain_second[...])
    sums = jnp.sum(totals, axis=1, keepdims=True)
    weight_sq = [jnp.sum(gain_row * gain_row, axis=1, keepdims=True)] + [
        sums[place : place + 1] for place in range(6)
    ]
    update_sq = [jnp.sum(update * update, axis=1, keepdims=True)] + [
        sums[6 + place : 7 + place] for place in range(6)
    ]
    scales = []
    for place in range(7):
        weight_norm = jnp.sqrt(weight_sq[place])
        update_norm = jnp.sqrt(update_sq[place])
        scales.append(learn_rate * weight_norm / (update_norm + adam_eps))
        norms_out[0:1, place : place + 1] = weight_norm
        norms_out[1:2, place : place + 1] = update_norm
    fresh = gain_row - scales[0] * update

    def own(row):
        return jnp.where(me == 0, row[:, :half_width], row[:, half_width:]).reshape(half_width)

    g_first[...] = own(first)
    g_second[...] = own(second)
    g_new[...] = own(fresh)
    g_copy[...] = own(fresh).astype(bf16)

    need(w_in, u_mix, u_gate)

    def one_in(start, held):
        here = pl.ds(start, ROWS)
        for half, change in ((0, u_mix), (1, u_gate)):
            fresh = w_in[here, half, :] - scales[1] * change[here, :]
            n_in[here, half, :] = fresh
            c_in[here, half, :] = fresh.astype(bf16)
        return held

    each_rows(width, one_in, 0)
    save(n_in, c_in)
    need()

    def one_out(start, held):
        here = pl.ds(start, ROWS)
        fresh = w_out[here, :] - scales[2] * u_out[here, :]
        n_out[here, :] = fresh
        c_out[here, :] = fresh.astype(bf16)
        return held

    each_rows(chans, one_out, 0)
    save(n_out, c_out)
    for place, weight, change, fresh_ref, copy in (
        (3, w_xp, u_xp, n_xp, c_xp),
        (4, w_dt, u_dt, n_dt, c_dt),
        (5, w_cv, u_cv, n_cv, c_cv),
        (6, w_cp, u_cp, n_cp, c_cp),
    ):
        for index in range(weight.shape[0]):
            fresh = weight[index] - scales[place] * change[index]
            fresh_ref[index] = fresh
            copy[index] = fresh.astype(bf16)
    parts = [
        (scales[1], stats[4:5, :], stats[5:6, :]),
        (scales[1], stats[0:1, :], stats[1:2, :]),
        (scales[2], stats[2:3, :], stats[3:4, :]),
    ]
    means = [scale * part_mean for scale, part_mean, _ in parts]
    mean = (means[0] + means[1] + means[2]) / 3.0
    spread = jnp.zeros_like(mean)
    for (scale, _, squares), part_mean in zip(parts, means):
        gap = part_mean - mean
        spread = spread + scale * scale * squares + width * gap * gap
    stats_out[0:1, :] = mean
    stats_out[1:2, :] = spread / (3.0 * width)


def join_kernel(pieces, copies, *, need, save):
    total = pieces[0].astype(f32)
    for place in range(1, pieces.shape[0]):
        total = total + pieces[place].astype(f32)
    low = total.astype(bf16)
    for place in range(pieces.shape[0]):
        copies[place] = low


def send_pieces(values, dp):
    chunk = values.shape[0] // dp
    return lax.all_to_all(values, "dp", 0, 0, tiled=True).reshape(dp, chunk, LANES)


def join_pieces(pieces):
    copies = call(join_kernel, at("x", shape(pieces.shape, bf16)), at("x", pieces), limit=8)[0]
    return copies.reshape(-1, LANES)


def call(kernel, outs, args, scratch=(), limit=32, micros=1):
    given = [array for array, _ in args]
    kinds = [kind for _, kind in args]
    out_kinds = [kind for _, kind in outs]
    fetched = [place for place, kind in enumerate(kinds) if kind == "h"]
    stored = [place for place, kind in enumerate(out_kinds) if kind == "h"]
    staging = [pltpu.VMEM(given[place].shape, given[place].dtype) for place in fetched]
    staging += [pltpu.VMEM(outs[place][0].shape, outs[place][0].dtype) for place in stored]
    moves = max(1, len(staging))

    def body(*refs):
        ins = list(refs[: len(given)])
        results = list(refs[len(given) : len(given) + len(outs)])
        rest = refs[len(given) + len(outs) :]
        stage, sems, own = rest[: len(staging)], rest[len(staging)], rest[len(staging) + 1 :]
        loads, saves = {}, {}
        for number, place in enumerate(fetched):
            loads[id(stage[number])] = pltpu.make_async_copy(ins[place], stage[number], sems.at[number])
            ins[place] = stage[number]
        for load in loads.values():
            load.start()
        for number, place in enumerate(stored, len(fetched)):
            saves[id(stage[number])] = pltpu.make_async_copy(stage[number], results[place], sems.at[number])
            results[place] = stage[number]
        begun = []

        def need(*wanted):
            for key in [id(ref) for ref in wanted] or list(loads):
                if key in loads:
                    loads.pop(key).wait()

        def save(*ready):
            for key in [id(ref) for ref in ready] or list(saves):
                if key in saves:
                    begun.append(saves.pop(key))
                    begun[-1].start()

        kernel(*ins, *results, *own, need=need, save=save)
        need()
        save()
        for move in begun:
            move.wait()

    spaces = {"x": pltpu.VMEM, "h": pltpu.HBM, "m": pltpu.HBM, "s": pltpu.SMEM}
    placed = [
        pltpu.with_memory_space_constraint(array, pltpu.HBM) if kind in "hm" else array for array, kind in args
    ]
    return pl.pallas_call(
        body,
        out_shape=[pltpu.HBM(out.shape, out.dtype) if kind in "hm" else out for out, kind in outs],
        in_specs=[pl.BlockSpec(memory_space=spaces[kind]) for kind in kinds],
        out_specs=[pl.BlockSpec(memory_space=spaces[kind]) for kind in out_kinds],
        scratch_shapes=[*staging, pltpu.SemaphoreType.DMA((moves,)), *scratch],
        compiler_params=pltpu.CompilerParams(vmem_limit_bytes=limit * MB),
        cost_estimate=pl.CostEstimate(flops=micros * 10**9, bytes_accessed=MB, transcendentals=0),
    )(*placed)


def at(kind, *things):
    return [(thing, kind) for thing in things]


def program(
    dp,
    hidden_in, out_cot, segment_ids,
    norm_gain, in_weight, out_weight, xproj_weight, dtproj_weight, conv_weight, chan_params,
    first_norm_gain, first_in_weight, first_out_weight, first_xproj_weight,
    first_dtproj_weight, first_conv_weight, first_chan_params,
    second_norm_gain, second_in_weight, second_out_weight, second_xproj_weight,
    second_dtproj_weight, second_conv_weight, second_chan_params,
):
    tokens, width = hidden_in.shape
    chans = in_weight.shape[2]
    half_width = first_norm_gain.shape[0]
    tiles = chans // LANES
    rank = dtproj_weight.shape[1]
    count = chan_params.shape[1] - 3
    rows = rank + 2 * count
    taps = conv_weight.shape[1]

    def swap(values):
        return lax.ppermute(values, "chan", [(0, 1), (1, 0)])

    me = lax.axis_index("chan")
    core = me.astype(jnp.int32).reshape(1)
    cot_own = out_cot.T
    cot_far = swap(cot_own)
    moments_own = jnp.stack([first_norm_gain, second_norm_gain])
    moments_far = swap(moments_own)
    moments_gain = jnp.where(
        me == 0,
        jnp.concatenate([moments_own, moments_far], 1),
        jnp.concatenate([moments_far, moments_own], 1),
    )

    def flip(values):
        return jnp.swapaxes(values, 1, 2)

    def turn(values):
        return jnp.swapaxes(values, 0, 1)

    w_xp = flip(xproj_weight)
    w_cp = turn(chan_params)
    square = (tokens, chans)
    z = Sizes(tokens, chans, count, rank)
    smem = at("s", core)

    def padded_rows(amount):
        return -(-amount // (dp * 16)) * 16 * dp

    mixing, gate, conv_pre, part, normed, low_in, same = call(
        front_kernel,
        at("h", shape(square, f32), shape(square, f32), shape((2,) + square, f32))
        + at("x", shape((2 * rows, tokens), f32))
        + at(
            "h", shape((tokens, width), bf16), shape((2, width, chans), bf16),
            shape((2, tokens, LANES), f32),
        ),
        at("h", hidden_in, segment_ids, norm_gain, in_weight, conv_weight, w_cp, w_xp),
        [pltpu.VMEM((tokens + 16, chans), f32), pltpu.VMEM((tokens + 16, LANES), f32)],
        limit=16, micros=7,
    )
    part_far = swap(part)
    early_rows = padded_rows(tiles * width + (width // LANES) * chans)
    grad_part, early, out_send, out_own, grad_act, grad_dt, grad_chan, gate_low = scan_call(
        at("x", part, part_far) + at("h", conv_pre, gate, same, cot_own) + at("x", cot_far)
        + at("h", out_weight, dtproj_weight, w_cp, normed) + smem,
        z, early_rows, half_width,
    )
    early_pieces = send_pieces(early, dp)
    grad_far = swap(grad_part)
    early_sums = lax.all_to_all(join_pieces(early_pieces), "dp", 0, 0, tiled=True)
    out_far = swap(out_send)
    late_rows = padded_rows(tiles * (width + 2 * rows + 2 * rank + 48))
    late, in_own, in_send = call(
        back_kernel,
        at("x", shape((late_rows, LANES), bf16))
        + at("h", shape((half_width + 8, tokens), f32))
        + at("x", shape((half_width + 8, tokens), f32)),
        at("x", grad_part, grad_far)
        + at("h", grad_act, conv_pre, mixing, gate_low, normed, low_in)
        + at("h", segment_ids, w_xp, conv_weight, hidden_in, norm_gain, grad_dt, grad_chan)
        + smem,
        [
            pltpu.VMEM((tokens + 16, chans), f32), pltpu.VMEM((2, tokens + 16, chans), f32),
            pltpu.VMEM((tokens + 16, LANES), f32), pltpu.VMEM(square, bf16),
            pltpu.VMEM((48, chans), f32), pltpu.VMEM((2,) + square, bf16),
        ],
        limit=20, micros=8,
    )
    in_far = swap(in_send)
    late_pieces = send_pieces(late, dp)
    output, input_grad = call(
        outputs_kernel,
        at("h", shape((half_width, tokens), bf16), shape((half_width, tokens), f32)),
        at("h", hidden_in, cot_own, out_own) + at("x", out_far) + at("h", in_own) + at("x", in_far) + smem,
        limit=16, micros=3,
    )
    firsts = [first_xproj_weight, first_dtproj_weight, first_conv_weight, first_chan_params]
    seconds = [second_xproj_weight, second_dtproj_weight, second_conv_weight, second_chan_params]
    for group in (firsts, seconds):
        group[0], group[3] = flip(group[0]), turn(group[3])
    weights = [w_xp, dtproj_weight, conv_weight, w_cp]
    small = [tensor for trio in zip(weights, firsts, seconds) for tensor in trio]
    half = shape((width, chans), f32)
    whole_in, whole_out = shape(in_weight.shape, f32), shape(out_weight.shape, f32)
    x_out, y_out, x_gate, y_gate, u_gate, u_out, early_norms, early_stats = call(
        early_kernel,
        at(
            "h", whole_out, whole_out, half, half, half, whole_out, shape((16, LANES), f32),
            shape((8, chans), f32),
        ),
        at("x", early_sums)
        + at(
            "h", in_weight, first_in_weight, second_in_weight, out_weight, first_out_weight,
            second_out_weight,
        ),
        limit=24, micros=5,
    )
    late_sums = lax.all_to_all(join_pieces(late_pieces), "dp", 0, 0, tiled=True)
    shapes = [shape(tensor.shape, f32) for tensor in weights]
    late_outs = [whole_in, whole_in]
    for entry in shapes:
        late_outs += [entry, entry]
    got = call(
        late_kernel,
        at("h", *late_outs, half, *shapes)
        + at("x", shape((16, LANES), f32))
        + at("h", shape((8, chans), f32)),
        at("x", late_sums)
        + at("h", x_gate, y_gate, early_norms, early_stats, in_weight, first_in_weight, second_in_weight)
        + at("h", *small),
        [pltpu.VMEM((width, chans), f32), pltpu.VMEM((width, chans), f32)],
        limit=24, micros=5,
    )
    moments, updates, norms, stats = got[:10], got[10:15], got[15], got[16]
    norms_far = swap(norms)
    pairs = []
    for entry in [whole_in, whole_out, *shapes]:
        pairs += [entry, shape(entry.shape, bf16)]
    row = shape((half_width,), f32)
    done = call(
        apply_kernel,
        at(
            "h", *pairs, row, row, row, shape((half_width,), bf16), shape((2, 7), f32),
            shape((2, chans), f32),
        ),
        at("x", norms, norms_far)
        + at("h", stats, in_weight, out_weight, *weights, updates[0], u_gate, u_out, *updates[1:])
        + at("h", norm_gain) + at("x", moments_gain[0:1], moments_gain[1:2]) + smem,
        limit=24, micros=5,
    )
    flat = list(done[12:16])
    firsts_out = [moments[0], x_out, *moments[2::2]]
    seconds_out = [moments[1], y_out, *moments[3::2]]
    for place in range(6):
        entry = [firsts_out[place], seconds_out[place], done[2 * place], done[2 * place + 1]]
        if place == 2:
            entry = [flip(tensor) for tensor in entry]
        if place == 5:
            entry = [turn(tensor) for tensor in entry]
        flat += entry
    return (output.T, input_grad.T, *flat, done[16].T, done[17])


def solution(mesh):
    rows = P("dp", None)
    cells = P("dp", "chan")
    last = P(None, None, "chan")
    first = P("chan", None)
    middle = P(None, "chan", None)
    tensors = (last, first, middle, last, last, last)
    outs = [cells, cells] + [P("chan")] * 4
    for spec in tensors:
        outs += [spec] * 4
    return jax.shard_map(
        functools.partial(program, mesh.shape["dp"]),
        mesh=mesh,
        in_specs=(rows, cells, P("dp"), P(), *tensors, P("chan"), *tensors, P("chan"), *tensors),
        out_specs=(*outs, P(), P(None, "chan")),
        check_vma=False,
    )
```

```python
import functools

import jax
import jax.numpy as jnp
from jax import lax
from jax.experimental import pallas as pl
from jax.experimental.pallas import tpu as pltpu
from jax.sharding import PartitionSpec as P

STEP = 4
norm_eps = 1e-06
beta_one = 0.5
beta_two = 0.5
adam_eps = 1e-06
decay_rate = 0.01
learn_rate = 0.3
LOG2E = 1.4426950408889634
FAR = 1e30
FLOOR = -1e-26

f32 = jnp.float32
bf16 = jnp.bfloat16
HIGH = lax.Precision.HIGHEST
LANES = 128
ROWS = 16
MB = 1 << 20


def dot(left, right, dims, precision=None):
    return lax.dot_general(
        left, right, (dims, ((), ())), precision=precision, preferred_element_type=f32
    )


NN = ((1,), (0,))
TN = ((0,), (0,))
NT = ((1,), (1,))


def sigmoid(values):
    return lax.logistic(values)


def silu_slope(values, sigma):
    return sigma * (1.0 + values * (1.0 - sigma))


def softplus(values):
    return jnp.maximum(values, 0.0) + jnp.log1p(jnp.exp(-jnp.abs(values)))


def wide(tile, times):
    return jnp.concatenate([tile] * times, axis=1)


def fold(values):
    total = values[0:8]
    for start in range(8, values.shape[0], 8):
        total = total + values[start : start + 8]
    return total


def shape(dims, dtype):
    return jax.ShapeDtypeStruct(dims, dtype)


def each_rows(length, body, carry=None, rows=ROWS):
    def step(index, held):
        return body(pl.multiple_of(index * rows, rows), held)

    return lax.fori_loop(0, length // rows, step, carry)


def spread_segments(numbers, tokens):
    across = lax.broadcasted_iota(jnp.int32, (tokens, tokens), 0)
    along = lax.broadcasted_iota(jnp.int32, (tokens, tokens), 1)
    row = numbers.astype(f32).reshape(1, tokens)
    picked = jnp.where(across == along, row, 0.0).astype(bf16)
    return dot(picked, jnp.ones((tokens, LANES), bf16), NN)


def front_kernel(
    hid, gain, w_mix, w_gate, seg, taps, params, w_xp,
    mix_out, gate_out, conv_out, part_out, norm_out, low_out, same_out,
    padded, sgpad,
    *, need, save,
):
    tokens, width = hid.shape
    chans = mix_out.shape[1]
    tiles = chans // LANES

    need(hid, gain)
    gain_row = gain[...].reshape(1, width)

    def normalise(start, held):
        source = hid[pl.ds(start, ROWS), :].astype(f32)
        scale = lax.rsqrt(jnp.sum(source * source, axis=1, keepdims=True) / width + norm_eps)
        norm_out[pl.ds(start, ROWS), :] = (source * scale * gain_row).astype(bf16)
        return held

    each_rows(tokens, normalise, 0)
    need(w_mix, w_gate)
    low_out[0] = w_mix[...].astype(bf16)
    low_out[1] = w_gate[...].astype(bf16)
    save(low_out)
    normed = norm_out[...]
    mixing = dot(normed, low_out[0], NN)
    mix_out[...] = mixing
    padded[0:8, :] = jnp.zeros((8, chans), f32)
    padded[pl.ds(8, tokens), :] = mixing
    padded[pl.ds(8 + tokens, 8), :] = jnp.zeros((8, chans), f32)
    save(mix_out)
    gate_out[...] = dot(normed, low_out[1], NN)
    need(seg, taps, w_xp, params)
    numbers = spread_segments(seg[...], tokens)
    sgpad[0:8, :] = jnp.full((8, LANES), -1.0, f32)
    sgpad[pl.ds(8, tokens), :] = numbers
    sgpad[pl.ds(8 + tokens, 8), :] = jnp.full((8, LANES), -1.0, f32)
    width_taps = taps.shape[1]

    def convolve(start, held):
        window = padded[pl.ds(start, ROWS + 16), :]
        marks = sgpad[pl.ds(start, ROWS + 16), :]
        own = marks[8 : 8 + ROWS]
        base = window[8 : 8 + ROWS]
        for heading in range(2):
            total = params[0, heading : heading + 1, :] + taps[heading, 0:1, :] * base
            for offset in range(1, width_taps):
                begin = 8 - offset if heading == 0 else 8 + offset
                same = jnp.where(marks[begin : begin + ROWS] == own, 1.0, 0.0)
                if offset == 1:
                    same_out[heading, pl.ds(start, ROWS), :] = same
                moved = window[begin : begin + ROWS]
                total = total + taps[heading, offset : offset + 1, :] * moved * wide(same, tiles)
            conv_out[heading, pl.ds(start, ROWS), :] = total
        return held

    each_rows(tokens, convolve, 0)
    for heading in range(2):
        pre = conv_out[heading]
        act_low = (pre * sigmoid(pre)).astype(bf16)
        rows = w_xp.shape[1]
        part_out[heading * rows : (heading + 1) * rows, :] = dot(
            w_xp[heading].astype(bf16), act_low, NT
        )


SPAN = 64


class Sizes:
    def __init__(self, tokens, chans, count, rank):
        self.tokens, self.chans, self.count, self.rank = tokens, chans, count, rank
        self.tiles = chans // LANES
        self.blocks = tokens // LANES
        self.rows = rank + 2 * count
        self.block_rows = LANES * count
        self.pairs = [(heading, tile) for heading in range(2) for tile in range(self.tiles)]

    def base(self, heading, tile):
        return (heading * self.tiles + tile) * self.tokens

    def row(self, ref, heading, tile, at):
        return ref[pl.ds(self.base(heading, tile) + at, 1), :]

    def whole(self, ref, heading):
        starts = [self.base(heading, tile) for tile in range(self.tiles)]
        return jnp.concatenate([ref[start : start + self.tokens, :] for start in starts], axis=1)


def cols(tile):
    return slice(tile * LANES, (tile + 1) * LANES)


def split(values):
    high = values.astype(bf16)
    return high, (values - high.astype(f32)).astype(bf16)


def group_maps(target, tile, heading, count):
    groups = tile.shape[1] // count
    for group in range(groups):
        block, place = divmod(group * count, LANES)
        own = tile[:, cols(block)]
        if place:
            own = pltpu.roll(own, LANES - place, 1)
        target[heading, group] = own


def diagonal_maps(target, tile, heading, count):
    tokens = tile.shape[1]
    squared = count * count
    lane = lax.broadcasted_iota(jnp.int32, (count, squared), 1)
    row = lax.broadcasted_iota(jnp.int32, (count, squared), 0)
    repeat = jnp.where(lane % count == row, 1.0, 0.0).astype(bf16)
    token = lax.broadcasted_iota(jnp.int32, (tokens, squared), 0)
    place = lax.broadcasted_iota(jnp.int32, (tokens, squared), 1)
    mine = place // count == token % count
    for number, part in enumerate(split(tile)):
        spread = jnp.where(mine, dot(part, repeat, TN), 0.0).astype(bf16)
        target[heading, :, number] = spread.reshape(tokens // count, count, squared)


def weigh_states(left, maps):
    half = maps.shape[0] // 2
    got = dot(maps, left, NN)
    return got[:half] + got[half:]


def gather_states(left, right, count):
    products = dot(left, right, NT)
    lane = lax.broadcasted_iota(jnp.int32, (count, count), 1)
    total = products[0:count]
    for place in range(1, count):
        total = jnp.where(lane == place, products[place * count : (place + 1) * count], total)
    return total


def dot3(left, right, dims):
    (left_high, left_low), (right_high, right_low) = split(left), split(right)
    if dims == TN:
        lefts = jnp.concatenate([left_high, left_low, left_high], axis=0)
        return dot(lefts, jnp.concatenate([right_high, right_high, right_low], axis=0), dims)
    rows = left.shape[0]
    both = dot(jnp.concatenate([left_high, left_low], axis=0), right_high, dims)
    return both[:rows] + both[rows:] + dot(left_high, right_low, dims)


class Sweep:
    def __init__(self, z, turned):
        self.z, self.turned = z, turned
        self.groups = z.tokens // z.count
        self.stage_groups = self.groups // z.blocks

    def group(self, order, heading):
        return self.groups - 1 - order if heading == self.turned else order

    def block(self, stage, heading):
        return self.z.blocks - 1 - stage if heading == self.turned else stage

    def inner(self, ahead, heading):
        return self.z.count - 1 - ahead if heading == self.turned else ahead

    def rows(self, group):
        return pl.ds(pl.multiple_of(group * self.z.count, self.z.count), self.z.count)

    def run(self, z, carried, scan, post, between):
        def step(index, held):
            order = 2 * index
            post(jnp.maximum(order - 1, 0), 1)
            held = scan(order, held, 0)
            post(order, 0)
            return scan(order + 1, held, 1)

        per = self.stage_groups // 2
        for stage in range(z.blocks):
            between(stage, True)
            carried = lax.fori_loop(stage * per, (stage + 1) * per, step, carried)
            between(stage, False)
        post(self.groups - 1, 1)
        return carried


def store_gathered(target, target_row, gathered, heading, z):
    per = LANES // z.count
    for block in range(z.blocks):
        pieces = [gathered[heading, block * per + place] for place in range(per)]
        target[target_row : target_row + z.count, cols(block)] = jnp.concatenate(pieces, axis=1)


def fill_rates(rates, params, count):
    for heading in range(2):
        for n in range(count):
            value = -jnp.exp(params[3 + n, heading : heading + 1, :])
            rates[heading, n : n + 1, :] = jnp.minimum(value, FLOOR)


def forward_kernel(
    own_part, far_part, params, w_dt, cot_own, cot_far, w_out, conv_pre, gate, same, normed, core,
    states_out, proj, grad_maps, skips, far_step, grad_y, pre_step, inflow_low, gate_low, early, out_far, out_own,
    grad_branch, inflow, grad_y_low, result, branch_low, maps, diagonal, gathered, states, low_one, low_two,
    rates, sems,
    *, need, save,
):
    tokens, chans = gate.shape
    z = Sizes(tokens, chans, params.shape[0] - 3, w_dt.shape[1])
    count, rank, rows, tiles = z.count, z.rank, z.rows, z.tiles
    half_width = cot_own.shape[0]
    width = 2 * half_width
    me = core[0]
    sweep = Sweep(z, 1)
    lows = (low_one, low_two)

    proj[...] = own_part[...] + far_part[...]
    save(proj)
    for heading in range(2):
        first = heading * rows + rank
        group_maps(maps, proj[first : first + count, :], heading, count)
        diagonal_maps(diagonal, proj[first + count : first + 2 * count, :], heading, count)
    need(params, w_dt)
    fill_rates(rates, params, count)
    for heading in range(2):
        pre_step[heading] = (
            dot3(proj[heading * rows : heading * rows + rank, :], w_dt[heading], TN)
            + params[1, heading : heading + 1, :]
        )
    save(pre_step)
    need(w_out, cot_own)
    low_out = w_out[...].astype(bf16)
    low_cot = jnp.where(
        me == 0,
        jnp.concatenate([cot_own[...].astype(f32), cot_far[...].astype(f32)], 0),
        jnp.concatenate([cot_far[...].astype(f32), cot_own[...].astype(f32)], 0),
    ).astype(bf16)
    grad_branch[...] = dot(low_cot, low_out, ((0,), (1,)))

    for tile in range(tiles):

        def prepare(start, held, tile=tile):
            here = pl.ds(start, SPAN)
            for heading in range(2):
                pre = conv_pre[heading, here, cols(tile)]
                act = pre * sigmoid(pre)
                size = softplus(pre_step[heading, here, cols(tile)])
                there = pl.ds(z.base(heading, tile) + start, SPAN)
                entering = size * act
                inflow[there, :] = entering
                inflow_low[heading, here, cols(tile)] = entering.astype(bf16)
                far_step[there, :] = jnp.where(same[heading, here, :] > 0.5, size * LOG2E, FAR)
            gated = gate[here, cols(tile)]
            back = grad_branch[here, cols(tile)] * (gated * sigmoid(gated))
            grad_y[pl.ds(z.base(0, tile) + start, SPAN), :] = back
            grad_y_low[here, cols(tile)] = back.astype(bf16)
            return held

        each_rows(tokens, prepare, 0, SPAN)
    save(far_step, inflow_low, grad_y)

    blank = jnp.zeros((count, LANES), f32)
    states[0, 0:count, :] = jnp.zeros((count, chans), bf16)
    states[1, tokens * count : (tokens + 1) * count, :] = jnp.zeros((count, chans), bf16)
    low_two[...] = jnp.zeros(low_two.shape, bf16)
    speeds = [rates[heading, :, cols(tile)] for heading, tile in z.pairs]

    def scan(order, carried, slot):
        carried = list(carried)
        enters = [maps[heading, sweep.group(order, heading)] for heading in range(2)]
        for heading in range(2):
            for ahead in range(count):
                inner = sweep.inner(ahead, heading)
                at = sweep.group(order, heading) * count + inner
                kept = pl.multiple_of((at + (1 if heading == 0 else 0)) * count, count)
                enter = jnp.broadcast_to(enters[heading][:, inner : inner + 1], (count, LANES))
                for tile in range(tiles):
                    number = heading * tiles + tile
                    decay = jnp.exp2(z.row(far_step, heading, tile, at) * speeds[number])
                    state = decay * carried[number] + enter * z.row(inflow, heading, tile, at)
                    carried[number] = state
                    low = state.astype(bf16)
                    states[heading, pl.ds(kept, count), cols(tile)] = low
                    lows[slot][heading, inner * count : (inner + 1) * count, cols(tile)] = low
        return tuple(carried)

    def post(order, slot):
        for heading in range(2):
            group = sweep.group(order, heading)
            left = lows[slot][heading]
            gathered[heading, group] = gather_states(left, grad_y_low[sweep.rows(group), :], count)
            result[heading, sweep.rows(group), :] = weigh_states(
                left, diagonal[heading, group].reshape(2 * count, count * count)
            )

    keeps = []

    def between(stage, before):
        if before:
            return
        for heading in range(2):
            begin, extent = sweep.block(stage, heading) * z.block_rows, z.block_rows
            if stage == 0:
                extent += count
            elif heading == 0:
                begin += count
            piece = pl.ds(begin, extent)
            keep = pltpu.make_async_copy(
                states.at[heading, piece, :], states_out.at[heading, piece, :], sems.at[heading, stage]
            )
            keep.start()
            keeps.append(keep)

    sweep.run(z, (blank,) * len(z.pairs), scan, post, between)
    for heading in range(2):
        store_gathered(grad_maps, heading * count, gathered, heading, z)
    skips[...] = jnp.zeros(skips.shape, f32)
    for tile in range(tiles):

        def finish(start, held, tile=tile):
            here = pl.ds(start, SPAN)
            total = jnp.zeros((SPAN, LANES), f32)
            sums = []
            back = grad_y[pl.ds(z.base(0, tile) + start, SPAN), :]
            for heading in range(2):
                pre = conv_pre[heading, here, cols(tile)]
                act = pre * sigmoid(pre)
                total = total + result[heading, here, cols(tile)]
                total = total + params[2, heading : heading + 1, cols(tile)] * act
                sums.append(held[heading] + fold(back * act))
            gated = gate[here, cols(tile)]
            sigma = sigmoid(gated)
            branch_low[here, cols(tile)] = (total * (gated * sigma)).astype(bf16)
            gate_low[here, cols(tile)] = (
                grad_branch[here, cols(tile)] * total * silu_slope(gated, sigma)
            ).astype(bf16)
            return tuple(sums)

        sums = each_rows(tokens, finish, (jnp.zeros((8, LANES), f32),) * 2, SPAN)
        for heading in range(2):
            skips[heading : heading + 1, cols(tile)] = jnp.sum(sums[heading], axis=0, keepdims=True)
    save(gate_low, grad_maps, skips)
    branch = branch_low[...]
    sent = dot(low_out, branch, ((0,), (1,)))
    out_own[...] = jnp.where(me == 0, sent[:half_width], sent[half_width:])
    out_far[...] = jnp.where(me == 0, sent[half_width:], sent[:half_width])
    save(out_own)
    grad_w = dot(branch, low_cot, ((0,), (1,))).astype(bf16)
    for tile in range(width // LANES):
        early[tile * chans : (tile + 1) * chans, :] = grad_w[:, cols(tile)]
    base_row = chans * (width // LANES)
    grad_w = dot(normed[...], gate_low[...], TN).astype(bf16)
    for tile in range(tiles):
        early[base_row + tile * width : base_row + (tile + 1) * width, :] = grad_w[:, cols(tile)]
    base_row += tiles * width
    if early.shape[0] > base_row:
        early[base_row:, :] = jnp.zeros((early.shape[0] - base_row, LANES), bf16)
    for keep in keeps:
        keep.wait()


def backward_kernel(
    states_in, params, proj, far_step, grad_y, inflow_low, pre_step, conv_pre, grad_maps, skips, w_dt,
    grad_part, grad_act, grad_dt, grad_chan,
    result, decayed, maps, diagonal, gathered, states, low_one, low_two, products_one, products_two, rates, sems,
    *, need, save,
):
    _, tokens, chans = conv_pre.shape
    z = Sizes(tokens, chans, params.shape[0] - 3, w_dt.shape[1])
    count, rank, rows, tiles = z.count, z.rank, z.rows, z.tiles
    sweep = Sweep(z, 0)
    lows, products = (low_one, low_two), (products_one, products_two)
    loads = {}
    for stage in range(z.blocks):
        for heading in range(2):
            begin = sweep.block(stage, heading) * z.block_rows + (count if heading == 1 else 0)
            piece = pl.ds(begin, z.block_rows)
            load = pltpu.make_async_copy(
                states_in.at[heading, piece, :], states.at[heading, piece, :], sems.at[heading, stage]
            )
            load.start()
            loads[stage, heading] = load
    need(params, proj)
    fill_rates(rates, params, count)
    for heading in range(2):
        first = heading * rows + rank
        group_maps(maps, proj[first + count : first + 2 * count, :], heading, count)
        diagonal_maps(diagonal, proj[first : first + count, :], heading, count)
    for low in (low_two, products_two):
        low[...] = jnp.zeros(low.shape, bf16)
    blank = jnp.zeros((count, LANES), f32)
    speeds = [rates[heading, :, cols(tile)] for heading, tile in z.pairs]

    def scan(order, held, slot):
        waiting = list(held[: len(z.pairs)])
        totals = list(held[len(z.pairs) :])
        leaves = [maps[heading, sweep.group(order, heading)] for heading in range(2)]
        for heading in range(2):
            for ahead in range(count):
                inner = sweep.inner(ahead, heading)
                at = sweep.group(order, heading) * count + inner
                prior = pl.multiple_of((at + (0 if heading == 0 else 1)) * count, count)
                leave = jnp.broadcast_to(leaves[heading][:, inner : inner + 1], (count, LANES))
                here = slice(inner * count, (inner + 1) * count)
                for tile in range(tiles):
                    number = heading * tiles + tile
                    size = z.row(far_step, heading, tile, at)
                    decay = jnp.exp2(size * speeds[number])
                    grad = leave * z.row(grad_y, 0, tile, at) + waiting[number]
                    lead = decay * grad
                    waiting[number] = lead
                    slope = lead * states[heading, pl.ds(prior, count), cols(tile)].astype(f32)
                    totals[number] = totals[number] + slope * size
                    products[slot][heading, here, cols(tile)] = (slope * speeds[number]).astype(bf16)
                    lows[slot][heading, here, cols(tile)] = grad.astype(bf16)
        return tuple(waiting + totals)

    lane = lax.broadcasted_iota(jnp.int32, (count, count * count), 1)
    row = lax.broadcasted_iota(jnp.int32, (count, count * count), 0)
    ones = jnp.where(lane // count == row, 1.0, 0.0).astype(bf16)

    def post(order, slot):
        for heading in range(2):
            group = sweep.group(order, heading)
            left = lows[slot][heading]
            gathered[heading, group] = gather_states(left, inflow_low[heading, sweep.rows(group), :], count)
            result[heading, sweep.rows(group), :] = weigh_states(
                left, diagonal[heading, group].reshape(2 * count, count * count)
            )
            decayed[heading, sweep.rows(group), :] = dot(ones, products[slot][heading], NN)

    def between(stage, before):
        if before:
            if stage == 0:
                need(far_step, grad_y, inflow_low)
            for heading in range(2):
                loads[stage, heading].wait()

    held = sweep.run(z, (blank,) * (2 * len(z.pairs)), scan, post, between)
    for number, (heading, tile) in enumerate(z.pairs):
        slopes = held[len(z.pairs) + number] / LOG2E
        for n in range(count):
            grad_chan[3 + n, heading : heading + 1, cols(tile)] = slopes[n : n + 1] * -jnp.exp(
                params[3 + n, heading : heading + 1, cols(tile)]
            )
    need()
    for heading in range(2):
        first = heading * rows + rank
        store_gathered(grad_part, first, gathered, heading, z)
        grad_part[first + count : first + 2 * count, :] = grad_maps[
            heading * count : (heading + 1) * count, :
        ]

    for tile in range(tiles):

        def close(start, held, tile=tile):
            here = pl.ds(start, SPAN)
            sums = []
            back = grad_y[pl.ds(z.base(0, tile) + start, SPAN), :]
            for heading in range(2):
                pre = conv_pre[heading, here, cols(tile)]
                act = pre * sigmoid(pre)
                passed = result[heading, here, cols(tile)]
                reach = pre_step[heading, here, cols(tile)]
                grad_act[heading, here, cols(tile)] = (
                    passed * softplus(reach) + back * params[2, heading : heading + 1, cols(tile)]
                )
                grad_pre = (decayed[heading, here, cols(tile)] + passed * act) * sigmoid(reach)
                pre_step[heading, here, cols(tile)] = grad_pre
                sums.append(held[heading] + fold(grad_pre))
            return tuple(sums)

        biases = each_rows(tokens, close, (jnp.zeros((8, LANES), f32),) * 2, SPAN)
        for heading in range(2):
            grad_chan[1, heading : heading + 1, cols(tile)] = jnp.sum(
                biases[heading], axis=0, keepdims=True
            )
    save(grad_act)
    for heading in range(2):
        grad_chan[0, heading : heading + 1, :] = jnp.zeros((1, chans), f32)
        grad_chan[2, heading : heading + 1, :] = skips[heading : heading + 1, :]
        grad_pre = pre_step[heading]
        grad_part[heading * rows : heading * rows + rank, :] = dot3(w_dt[heading], grad_pre, NT)
        grad_dt[heading] = dot3(proj[heading * rows : heading * rows + rank, :], grad_pre, NN)


def forward_call(args, sizes, early_rows, half_width, kept, limit=30):
    z = sizes
    square = (z.tokens, z.chans)
    both = (2,) + square
    flat = (2 * z.tiles * z.tokens, LANES)
    groups = z.tokens // z.count
    squared = z.count * z.count
    states = (2, (z.tokens + 1) * z.count, z.chans)
    slot = pltpu.VMEM((2, squared, z.chans), bf16)
    return call(
        forward_kernel,
        at("m", shape(states, bf16))
        + at(
            "h", shape((2 * z.rows, z.tokens), f32), shape((2 * z.count, z.tokens), f32), shape((8, z.chans), f32),
            shape(flat, f32), shape((z.tiles * z.tokens, LANES), f32), shape(both, f32), shape(both, bf16),
            shape(square, bf16),
        )
        + at("x", shape((early_rows, LANES), bf16), shape((half_width, z.tokens), f32))
        + at("h", shape((half_width, z.tokens), f32)),
        args,
        [
            pltpu.VMEM(square, f32), pltpu.VMEM(flat, f32), pltpu.VMEM(square, bf16), pltpu.VMEM(both, f32),
            pltpu.VMEM(square, bf16), pltpu.VMEM((2, groups, z.count, LANES), f32),
            pltpu.VMEM((2, groups, 2, z.count, squared), bf16), pltpu.VMEM((2, groups, z.count, z.count), f32),
            pltpu.VMEM(states, bf16), slot, slot, pltpu.VMEM((2, z.count, z.chans), f32),
            pltpu.SemaphoreType.DMA((2, z.blocks)),
        ],
        limit=limit, micros=15, kept=kept,
    )


def backward_call(args, sizes, limit=30):
    z = sizes
    square = (z.tokens, z.chans)
    both = (2,) + square
    groups = z.tokens // z.count
    squared = z.count * z.count
    slot = pltpu.VMEM((2, squared, z.chans), bf16)
    return call(
        backward_kernel,
        at(
            "x", shape((2 * z.rows, z.tokens), f32), shape(both, f32), shape((2, z.rank, z.chans), f32),
            shape((3 + z.count, 2, z.chans), f32),
        ),
        args,
        [
            pltpu.VMEM(both, f32), pltpu.VMEM(both, f32), pltpu.VMEM((2, groups, z.count, LANES), f32),
            pltpu.VMEM((2, groups, 2, z.count, squared), bf16), pltpu.VMEM((2, groups, z.count, z.count), f32),
            pltpu.VMEM((2, (z.tokens + 1) * z.count, z.chans), bf16), slot, slot, slot, slot,
            pltpu.VMEM((2, z.count, z.chans), f32), pltpu.SemaphoreType.DMA((2, z.blocks)),
        ],
        limit=limit, micros=15,
    )


def back_kernel(
    own_part, far_part, seg, w_xp, taps, mixing, conv_pre, grad_act, grad_chan, normed, gate_low,
    low_in, hid, gain, grad_dt, core,
    sums_out, in_own, in_far,
    padded, gpad, sgpad, mixed_low, small, act_low,
    *, need, save,
):
    tokens, width = hid.shape
    chans = mixing.shape[1]
    tiles = chans // LANES
    rows = w_xp.shape[1]
    width_taps = taps.shape[1]
    me = core[0]
    half_width = in_own.shape[0] - 8
    edge = jnp.zeros((8, chans), f32)
    padded[0:8, :] = edge
    padded[pl.ds(8 + tokens, 8), :] = edge
    gpad[0, 0:8, :] = edge
    gpad[1, 0:8, :] = edge
    gpad[0, pl.ds(8 + tokens, 8), :] = edge
    gpad[1, pl.ds(8 + tokens, 8), :] = edge
    sgpad[0:8, :] = jnp.full((8, LANES), -1.0, f32)
    sgpad[pl.ds(8 + tokens, 8), :] = jnp.full((8, LANES), -1.0, f32)
    need(seg, w_xp, mixing)
    padded[pl.ds(8, tokens), :] = mixing[...]
    sgpad[pl.ds(8, tokens), :] = spread_segments(seg[...], tokens)

    parts = (own_part[...] + far_part[...]).astype(bf16)
    for heading in range(2):
        part = parts[heading * rows : (heading + 1) * rows, :]
        gpad[heading, pl.ds(8, tokens), :] = dot(part, w_xp[heading].astype(bf16), TN)

    blank = jnp.zeros((8, chans), f32)
    need(taps, conv_pre, grad_act, grad_chan)

    def through_conv(start, held):
        here = pl.ds(start, ROWS)
        window = padded[pl.ds(start, ROWS + 16), :]
        marks = sgpad[pl.ds(start, ROWS + 16), :]
        own = marks[8 : 8 + ROWS]
        base = window[8 : 8 + ROWS]
        sums = []
        for heading in range(2):
            pre = conv_pre[heading, here, :]
            sigma = sigmoid(pre)
            act_low[heading, here, :] = (pre * sigma).astype(bf16)
            inside = pl.ds(pl.multiple_of(start + 8, 8), ROWS)
            grad = (gpad[heading, inside, :] + grad_act[heading, here, :]) * silu_slope(pre, sigma)
            gpad[heading, inside, :] = grad
            sums.append(held[5 * heading] + fold(grad))
            sums.append(held[5 * heading + 1] + fold(grad * base))
            for offset in range(1, width_taps):
                begin = 8 - offset if heading == 0 else 8 + offset
                kept = jnp.where(marks[begin : begin + ROWS] == own, 1.0, 0.0)
                moved = window[begin : begin + ROWS]
                sums.append(held[5 * heading + 1 + offset] + fold(grad * moved * wide(kept, tiles)))
        return tuple(sums)

    sums = each_rows(tokens, through_conv, (blank,) * 10)
    small[...] = jnp.zeros(small.shape, f32)
    for heading in range(2):
        bias = jnp.sum(sums[5 * heading], axis=0, keepdims=True)
        for offset in range(width_taps):
            row = heading * width_taps + offset
            small[row : row + 1, :] = jnp.sum(sums[5 * heading + 1 + offset], axis=0, keepdims=True)
        for entry in range(grad_chan.shape[0]):
            row = 2 * width_taps + 2 * entry + heading
            small[row : row + 1, :] = (
                bias
                if entry == 0
                else grad_chan[entry, heading : heading + 1, :]
            )

    def mixed(start, held):
        here = pl.ds(start, ROWS)
        marks = sgpad[pl.ds(start, ROWS + 16), :]
        own = marks[8 : 8 + ROWS]
        total = jnp.zeros((ROWS, chans), f32)
        for heading in range(2):
            window = gpad[heading, pl.ds(start, ROWS + 16), :]
            total = total + window[8 : 8 + ROWS] * taps[heading, 0:1, :]
            for offset in range(1, width_taps):
                begin = 8 + offset if heading == 0 else 8 - offset
                kept = jnp.where(marks[begin : begin + ROWS] == own, 1.0, 0.0)
                total = total + window[begin : begin + ROWS] * wide(kept, tiles) * taps[
                    heading, offset : offset + 1, :
                ]
        mixed_low[here, :] = total.astype(bf16)
        return held

    each_rows(tokens, mixed, 0)

    base_row = 0

    def put(values):
        nonlocal base_row
        for tile in range(values.shape[1] // LANES):
            sums_out[base_row : base_row + values.shape[0], :] = values[
                :, tile * LANES : (tile + 1) * LANES
            ].astype(bf16)
            base_row += values.shape[0]

    need()
    partial = dot(mixed_low[...], low_in[0], NT) + dot(gate_low[...], low_in[1], NT)
    padded[pl.ds(8, tokens), :] = partial

    gain_row = gain[...].reshape(1, width)

    def gains(start, held):
        here = pl.ds(start, ROWS)
        source = hid[here, :].astype(f32)
        scale = lax.rsqrt(jnp.sum(source * source, axis=1, keepdims=True) / width + norm_eps)
        inside = pl.ds(pl.multiple_of(start + 8, 8), ROWS)
        grad = padded[inside, :]
        padded[inside, :] = grad * gain_row
        return held + fold(grad * source * scale)

    gain_sum = each_rows(tokens, gains, jnp.zeros((8, width), f32))
    small[46:47, :] = jnp.sum(gain_sum, axis=0, keepdims=True)
    weighted = padded[pl.ds(8, tokens), :]
    products = weighted * hid[...].astype(f32)
    turned = weighted.T
    row_dot = dot(jnp.ones((8, width), f32), products, NT, HIGH)
    in_own[0:half_width, :] = jnp.where(me == 0, turned[:half_width], turned[half_width:])
    in_far[0:half_width, :] = jnp.where(me == 0, turned[half_width:], turned[:half_width])
    in_own[pl.ds(half_width, 8), :] = row_dot
    in_far[pl.ds(half_width, 8), :] = row_dot
    save(in_own)
    put(dot(normed[...], mixed_low[...], TN))
    put(
        jnp.concatenate(
            [
                dot(parts[heading * rows : (heading + 1) * rows, :], act_low[heading], NN)
                for heading in range(2)
            ],
            axis=0,
        )
    )
    put(jnp.concatenate([grad_dt[0], grad_dt[1]], axis=0))

    put(small[...])
    sums_out[base_row:, :] = jnp.zeros((sums_out.shape[0] - base_row, LANES), bf16)


def outputs_kernel(hid, cot_own, out_own, out_far, in_own, in_far, core, output, input_grad, *, need, save):
    width = hid.shape[1]
    half_width = cot_own.shape[0]
    me = core[0]
    need()
    source = hid[...].astype(f32).T
    scale = lax.rsqrt(jnp.sum(source * source, axis=0, keepdims=True) / width + norm_eps)
    own = jnp.where(me == 0, source[:half_width], source[half_width:])
    output[...] = (own + (out_own[...] + out_far[...])).astype(bf16)
    weighted = in_own[0:half_width, :] + in_far[0:half_width, :]
    save(output)
    row_dot = in_own[half_width : half_width + 1, :] + in_far[half_width : half_width + 1, :]
    input_grad[...] = (
        cot_own[...].astype(f32)
        + scale * weighted
        - own * (scale * scale * scale) * (row_dot / width)
    )


def lamb_moments(weight, grad, first, second):
    first_new = beta_one * first + (1.0 - beta_one) * grad
    second_new = beta_two * second + (1.0 - beta_two) * grad * grad
    root = jnp.sqrt(second_new * (1.0 / (1.0 - beta_two**STEP)))
    update = first_new * (1.0 / (1.0 - beta_one**STEP)) / (root + adam_eps) + decay_rate * weight
    return (first_new, second_new, update)


def rows_sum(values):
    return jnp.sum(values, axis=0, keepdims=True)


def lanes_sum(values):
    total = rows_sum(values)
    lanes = total[:, 0:LANES]
    for tile in range(1, values.shape[1] // LANES):
        lanes = lanes + total[:, cols(tile)]
    return lanes


def fetch(sums, base, stride, start, count, number):
    return jnp.concatenate(
        [sums[pl.ds(base + tile * stride + start, count), :].astype(f32) for tile in range(number)], axis=1
    )


def spread_of(update, mean, length):
    def step(start, kept):
        away = update[pl.ds(start, ROWS), :] - mean
        return kept + fold(away * away)

    return rows_sum(each_rows(length, step, jnp.zeros((8, update.shape[1]), f32)))


def half_update(sums, base, stride, weights, a_ref, b_ref, x_ref, y_ref, u_ref):
    length, chans = weights.shape
    zero = jnp.zeros((8, chans), f32)

    def step(start, kept):
        here = pl.ds(start, ROWS)
        grad = fetch(sums, base, stride, start, ROWS, chans // LANES)
        weight = weights[here, :]
        first, second, update = lamb_moments(weight, grad, a_ref[here, :], b_ref[here, :])
        x_ref[here, :] = first
        y_ref[here, :] = second
        u_ref[here, :] = update
        return (
            kept[0] + fold(weight * weight), kept[1] + fold(update * update), kept[2] + fold(update)
        )

    return each_rows(length, step, (zero, zero, zero))


def early_kernel(
    sums, w_out, a_out, b_out, w_gate, a_gate, b_gate,
    x_out, y_out, x_gate, y_gate, u_gate, u_out, norms, stats,
    *, need, save,
):
    width, chans = w_gate.shape
    tiles = width // LANES
    norms[...] = jnp.zeros(norms.shape, f32)
    zero = jnp.zeros((8, width), f32)
    need(w_out, a_out, b_out)

    def one_out(start, kept):
        here = pl.ds(start, ROWS)
        grad = fetch(sums, 0, chans, start, ROWS, tiles)
        weight = w_out[here, :]
        first, second, update = lamb_moments(weight, grad, a_out[here, :], b_out[here, :])
        x_out[here, :] = first
        y_out[here, :] = second
        u_out[here, :] = update
        return (kept[0] + fold(weight * weight), kept[1] + fold(update * update))

    weight_sq, update_sq = each_rows(chans, one_out, (zero, zero))
    norms[1:2, :] = lanes_sum(weight_sq)
    norms[7:8, :] = lanes_sum(update_sq)
    save(x_out, y_out, u_out)
    need()
    weight_sq, update_sq, total = half_update(
        sums, chans * tiles, width, w_gate, a_gate, b_gate, x_gate, y_gate, u_gate
    )
    norms[0:1, :] = lanes_sum(weight_sq)
    norms[6:7, :] = lanes_sum(update_sq)
    save(x_gate, y_gate, u_gate)
    gate_mean = rows_sum(total) / width
    stats[0:1, :] = gate_mean
    stats[1:2, :] = spread_of(u_gate, gate_mean, width)
    ones = jnp.ones((8, width), f32)
    out_all = u_out[...]
    out_mean = jnp.sum(out_all, axis=1, keepdims=True) / width
    away = out_all - out_mean
    stats[2:3, :] = dot(ones, out_all, NT, HIGH)[0:1] / width
    stats[3:4, :] = dot(ones, away * away, NT, HIGH)[0:1]
    stats[4:8, :] = jnp.zeros((4, chans), f32)


def late_kernel(
    sums, early_norms, early_stats, *rest, need, save
):
    small_in, (a_mix, b_mix), rest = rest[:8], rest[8:10], rest[10:]
    x_mix, y_mix, x_xp, y_xp, x_dt, y_dt, x_cv, y_cv, x_cp, y_cp, *rest = rest
    u_mix, u_xp, u_dt, u_cv, u_cp, norms, stats, w_xp, w_dt, w_cv, w_cp, w_mix, *_ = rest
    a_xp, b_xp, a_dt, b_dt, a_cv, b_cv, a_cp, b_cp = small_in
    width, chans = w_mix.shape
    tiles = chans // LANES
    base = tiles * width
    need(early_norms, early_stats, *small_in, w_xp, w_dt, w_cv, w_cp)
    norms[...] = early_norms[...]
    stats[...] = early_stats[...]

    def small(place, items, weight, a_ref, b_ref, x_ref, y_ref, u_ref):
        weight_sq, update_sq = jnp.zeros((1, LANES), f32), jnp.zeros((1, LANES), f32)
        for index, grad in enumerate(items):
            held = weight[index]
            first, second, update = lamb_moments(held, grad, a_ref[index], b_ref[index])
            x_ref[index] = first
            y_ref[index] = second
            u_ref[index] = update
            weight_sq = weight_sq + lanes_sum(held * held)
            update_sq = update_sq + lanes_sum(update * update)
        norms[place : place + 1, :] = weight_sq
        norms[6 + place : 7 + place, :] = update_sq

    rows = w_xp.shape[1]
    grads = fetch(sums, base, 2 * rows, 0, 2 * rows, tiles)
    small(2, [grads[:rows], grads[rows:]], w_xp, a_xp, b_xp, x_xp, y_xp, u_xp)
    base += 2 * rows * tiles
    rank = w_dt.shape[1]
    grads = fetch(sums, base, 2 * rank, 0, 2 * rank, tiles)
    small(3, [grads[:rank], grads[rank:]], w_dt, a_dt, b_dt, x_dt, y_dt, u_dt)
    base += 2 * rank * tiles
    grads = fetch(sums, base, 48, 0, 48, tiles)
    taps = w_cv.shape[1]
    small(4, [grads[:taps], grads[taps : 2 * taps]], w_cv, a_cv, b_cv, x_cv, y_cv, u_cv)
    entries = w_cp.shape[0]
    items = [grads[2 * (taps + entry) : 2 * (taps + entry) + 2] for entry in range(entries)]
    small(5, items, w_cp, a_cp, b_cp, x_cp, y_cp, u_cp)
    for tile in range(tiles):
        norms[12 + tile : 13 + tile, :] = grads[46:47, cols(tile)]
    save()
    need(a_mix, b_mix, w_mix)
    weight_sq, update_sq, total = half_update(
        sums, 0, width, w_mix, a_mix, b_mix, x_mix, y_mix, u_mix
    )
    norms[0:1, :] += lanes_sum(weight_sq)
    norms[6:7, :] += lanes_sum(update_sq)
    mix_mean = rows_sum(total) / width
    stats[4:5, :] = mix_mean
    stats[5:6, :] = spread_of(u_mix, mix_mean, width)


def apply_kernel(
    norms_own, norms_far, stats,
    w_mix, w_gate, w_out, w_xp, w_dt, w_cv, w_cp,
    u_mix, u_gate, u_out, u_xp, u_dt, u_cv, u_cp,
    gain, gain_first, gain_second, x_mix, y_mix, core, x_given, y_given,
    n_in, c_in, n_out, c_out, n_xp, c_xp, n_dt, c_dt, n_cv, c_cv, n_cp, c_cp,
    g_first, g_second, g_new, g_copy, norms_out, stats_out, x_in, y_in,
    sems,
    *, need, save,
):
    width, chans = w_mix.shape
    moves = [
        pltpu.make_async_copy(held, target.at[:, 0, :], sems.at[number])
        for number, (held, target) in enumerate(((x_mix, x_in), (y_mix, y_in)))
    ]
    for move in moves:
        move.start()
    half_width = g_new.shape[0]
    me = core[0]
    totals = norms_own[...] + norms_far[...]
    sums = jnp.sum(totals, axis=1, keepdims=True)
    scales = [None]
    for place in range(6):
        weight_norm = jnp.sqrt(sums[place : place + 1])
        update_norm = jnp.sqrt(sums[6 + place : 7 + place])
        scales.append(learn_rate * weight_norm / (update_norm + adam_eps))
        norms_out[0:1, place + 1 : place + 2] = weight_norm
        norms_out[1:2, place + 1 : place + 2] = update_norm

    need(w_mix, w_gate)

    def one_in(start, held):
        here = pl.ds(start, ROWS)
        for half, weight, change in ((0, w_mix, u_mix), (1, w_gate, u_gate)):
            fresh = weight[here, :] - scales[1] * change[here, :]
            n_in[half, here, :] = fresh
            c_in[here, half, :] = fresh.astype(bf16)
        return held

    each_rows(width, one_in, 0)
    save(n_in, c_in)

    def one_out(start, held):
        here = pl.ds(start, ROWS)
        fresh = w_out[here, :] - scales[2] * u_out[here, :]
        n_out[here, :] = fresh
        c_out[here, :] = fresh.astype(bf16)
        return held

    each_rows(chans, one_out, 0)
    save(n_out, c_out)
    need()
    gain_grad = jnp.concatenate(
        [totals[12 + tile : 13 + tile, :] for tile in range(width // LANES)], axis=1
    )
    gain_row = gain[...].reshape(1, width)
    first, second, update = lamb_moments(gain_row, gain_grad, gain_first[...], gain_second[...])
    weight_norm = jnp.sqrt(jnp.sum(gain_row * gain_row, axis=1, keepdims=True))
    update_norm = jnp.sqrt(jnp.sum(update * update, axis=1, keepdims=True))
    norms_out[0:1, 0:1] = weight_norm
    norms_out[1:2, 0:1] = update_norm
    fresh = gain_row - learn_rate * weight_norm / (update_norm + adam_eps) * update

    def own(row):
        return jnp.where(me == 0, row[:, :half_width], row[:, half_width:]).reshape(half_width)

    g_first[...] = own(first)
    g_second[...] = own(second)
    g_new[...] = own(fresh)
    g_copy[...] = own(fresh).astype(bf16)
    for place, weight, change, fresh_ref, copy in (
        (3, w_xp, u_xp, n_xp, c_xp),
        (4, w_dt, u_dt, n_dt, c_dt),
        (5, w_cv, u_cv, n_cv, c_cv),
        (6, w_cp, u_cp, n_cp, c_cp),
    ):
        for index in range(weight.shape[0]):
            fresh = weight[index] - scales[place] * change[index]
            fresh_ref[index] = fresh
            copy[index] = fresh.astype(bf16)
    parts = [
        (scales[1], stats[4:5, :], stats[5:6, :]),
        (scales[1], stats[0:1, :], stats[1:2, :]),
        (scales[2], stats[2:3, :], stats[3:4, :]),
    ]
    means = [scale * part_mean for scale, part_mean, _ in parts]
    mean = (means[0] + means[1] + means[2]) / 3.0
    spread = jnp.zeros_like(mean)
    for (scale, _, squares), part_mean in zip(parts, means):
        gap = part_mean - mean
        spread = spread + scale * scale * squares + width * gap * gap
    stats_out[0:1, :] = mean
    stats_out[1:2, :] = spread / (3.0 * width)
    for move in moves:
        move.wait()


def join_kernel(pieces, copies, *, need, save):
    total = pieces[0].astype(f32)
    for place in range(1, pieces.shape[0]):
        total = total + pieces[place].astype(f32)
    low = total.astype(bf16)
    for place in range(pieces.shape[0]):
        copies[place] = low


def send_pieces(values, dp):
    chunk = values.shape[0] // dp
    return lax.all_to_all(values, "dp", 0, 0, tiled=True).reshape(dp, chunk, LANES)


def join_pieces(pieces):
    copies = call(join_kernel, at("x", shape(pieces.shape, bf16)), at("x", pieces), limit=8)[0]
    return copies.reshape(-1, LANES)


def call(kernel, outs, args, scratch=(), limit=32, micros=1, passed=(), kept=(), aliases=None):
    given = [array for array, _ in args] + [array for array, _ in passed]
    kinds = [kind for _, kind in args] + ["m"] * len(passed)
    n_own = len(outs)
    outs = list(outs)
    for array, kind in passed:
        dims = array.shape if kind == "h" else (array.shape[0], array.shape[-1])
        outs += at("x", shape(dims, array.dtype))
    outs += at("m", *[shape(given[place].shape, given[place].dtype) for place in kept])
    out_kinds = [kind for _, kind in outs]
    fetched = [place for place, kind in enumerate(kinds) if kind in "h01"]
    stored = [place for place, kind in enumerate(out_kinds) if kind in "h12"]

    def staged(array, kind):
        rows, columns = array.shape[0], array.shape[-1]
        dims = {"h": array.shape, "2": (2, rows, columns)}.get(kind, (rows, columns))
        return pltpu.VMEM(dims, array.dtype)

    staging = [staged(given[place], kinds[place]) for place in fetched]
    staging += [staged(outs[place][0], out_kinds[place]) for place in stored]
    moves = max(1, 2 * len(staging) + len(passed) + len(kept))

    def body(*refs):
        ins = list(refs[: len(given)])
        results = list(refs[len(given) : len(given) + len(outs)])
        rest = refs[len(given) + len(outs) :]
        stage, sems, own = rest[: len(staging)], rest[len(staging)], rest[len(staging) + 1 :]
        loads, saves = {}, {}
        for number, place in enumerate(fetched):
            source = ins[place] if kinds[place] == "h" else ins[place].at[:, int(kinds[place]), :]
            loads[id(stage[number])] = pltpu.make_async_copy(source, stage[number], sems.at[number])
            ins[place] = stage[number]
        for load in loads.values():
            load.start()
        for number, place in enumerate(stored, len(fetched)):
            held, target, kind = stage[number], results[place], out_kinds[place]
            parts = [(held, target)]
            if kind == "1":
                parts = [(held, target.at[:, 1, :])]
            if kind == "2":
                parts = [(held.at[half], target.at[:, half, :]) for half in range(2)]
            saves[id(held)] = [
                pltpu.make_async_copy(*pair, sems.at[moves - 1 - 2 * (number - len(fetched)) - half]) for half, pair in enumerate(parts)
            ]
            results[place] = held
        follow = []
        for number in range(len(passed)):
            held = results[n_own + number]
            source, kind = ins[len(args) + number], passed[number][1]
            source = source if kind == "h" else source.at[:, int(kind), :]
            loads[id(held)] = pltpu.make_async_copy(source, held, sems.at[len(staging) + number])
            follow.append(id(held))
        begun = []
        for number, place in enumerate(kept):
            begun.append(
                pltpu.make_async_copy(
                    ins[place], results[n_own + len(passed) + number],
                    sems.at[len(staging) + len(passed) + number],
                )
            )
            begun[-1].start()

        def need(*wanted):
            keys = [id(ref) for ref in wanted] or list(loads)
            for key in keys:
                if key in loads and key not in follow:
                    loads.pop(key).wait()
            while follow:
                loads[follow.pop(0)].start()
            for key in keys:
                if key in loads:
                    loads.pop(key).wait()

        def save(*ready):
            for key in [id(ref) for ref in ready] or list(saves):
                for move in saves.pop(key, ()):
                    move.start()
                    begun.append(move)

        kernel(*ins[: len(args)], *results[: n_own + len(passed)], *own, need=need, save=save)
        need()
        save()
        for move in begun:
            move.wait()

    spaces = {"x": pltpu.VMEM, "s": pltpu.SMEM}
    placed = [
        pltpu.with_memory_space_constraint(array, pltpu.HBM) if kind in "hm01" else array
        for array, kind in zip(given, kinds)
    ]
    return pl.pallas_call(
        body,
        out_shape=[out if kind == "x" else pltpu.HBM(out.shape, out.dtype) for out, kind in outs],
        in_specs=[pl.BlockSpec(memory_space=spaces.get(kind, pltpu.HBM)) for kind in kinds],
        out_specs=[pl.BlockSpec(memory_space=spaces.get(kind, pltpu.HBM)) for kind in out_kinds],
        input_output_aliases=aliases or {},
        scratch_shapes=[*staging, pltpu.SemaphoreType.DMA((moves,)), *scratch],
        compiler_params=pltpu.CompilerParams(vmem_limit_bytes=limit * MB),
        cost_estimate=pl.CostEstimate(flops=micros * 10**9, bytes_accessed=MB, transcendentals=0),
    )(*placed)


def at(kind, *things):
    return [(thing, kind) for thing in things]


def program(
    dp,
    hidden_in, out_cot, segment_ids,
    norm_gain, in_weight, out_weight, xproj_weight, dtproj_weight, conv_weight, chan_params,
    first_norm_gain, first_in_weight, first_out_weight, first_xproj_weight,
    first_dtproj_weight, first_conv_weight, first_chan_params,
    second_norm_gain, second_in_weight, second_out_weight, second_xproj_weight,
    second_dtproj_weight, second_conv_weight, second_chan_params,
):
    tokens, width = hidden_in.shape
    chans = in_weight.shape[2]
    half_width = first_norm_gain.shape[0]
    tiles = chans // LANES
    rank = dtproj_weight.shape[1]
    count = chan_params.shape[1] - 3
    rows = rank + 2 * count
    taps = conv_weight.shape[1]

    def swap(values):
        return lax.ppermute(values, "chan", [(0, 1), (1, 0)])

    me = lax.axis_index("chan")
    core = me.astype(jnp.int32).reshape(1)
    cot_own = out_cot.T
    cot_far = swap(cot_own)
    moments_own = jnp.stack([first_norm_gain, second_norm_gain])
    moments_far = swap(moments_own)
    moments_gain = jnp.where(
        me == 0,
        jnp.concatenate([moments_own, moments_far], 1),
        jnp.concatenate([moments_far, moments_own], 1),
    )

    def flip(values):
        return jnp.swapaxes(values, 1, 2)

    def turn(values):
        return jnp.swapaxes(values, 0, 1)

    w_xp = flip(xproj_weight)
    w_cp = turn(chan_params)
    square = (tokens, chans)
    z = Sizes(tokens, chans, count, rank)
    smem = at("s", core)

    def padded_rows(amount):
        return -(-amount // (dp * 16)) * 16 * dp

    mixing, gate, conv_pre, part, normed, low_in, same = call(
        front_kernel,
        at("h", shape(square, f32))
        + at(
            "x", shape(square, f32), shape((2,) + square, f32), shape((2 * rows, tokens), f32),
            shape((tokens, width), bf16),
        )
        + at("h", shape((2, width, chans), bf16))
        + at("x", shape((2, tokens, LANES), f32)),
        at("h", hidden_in, norm_gain) + at("0", in_weight) + at("1", in_weight)
        + at("h", segment_ids, conv_weight, w_cp, w_xp),
        [pltpu.VMEM((tokens + 16, chans), f32), pltpu.VMEM((tokens + 16, LANES), f32)],
        limit=14, micros=7,
    )
    part_far = swap(part)
    early_rows = padded_rows(tiles * width + (width // LANES) * chans)
    (
        states, proj, grad_maps, skips, far_step, grad_y, pre_step, inflow_low, gate_low, early, out_send, out_own,
        conv_kept, normed_kept,
    ) = forward_call(
        at("x", part, part_far) + at("h", w_cp, dtproj_weight, cot_own) + at("x", cot_far) + at("h", out_weight)
        + at("x", conv_pre, gate, same, normed) + smem,
        z, early_rows, half_width, (7, 10),
    )
    early_pieces = send_pieces(early, dp)
    grad_part, grad_act, grad_dt, grad_chan = backward_call(
        at("m", states) + at("h", w_cp, proj, far_step, grad_y, inflow_low, pre_step, conv_kept)
        + at("h", grad_maps, skips, dtproj_weight),
        z,
    )
    early_copies, grad_part = lax.optimization_barrier((join_pieces(early_pieces), grad_part))
    early_sums = lax.all_to_all(early_copies, "dp", 0, 0, tiled=True)
    grad_far = swap(grad_part)
    out_far = swap(out_send)
    late_rows = padded_rows(tiles * (width + 2 * rows + 2 * rank + 48))
    late, in_own, in_send = call(
        back_kernel,
        at("x", shape((late_rows, LANES), bf16))
        + at("h", shape((half_width + 8, tokens), f32))
        + at("x", shape((half_width + 8, tokens), f32)),
        at("x", grad_part, grad_far)
        + at("h", segment_ids, w_xp, conv_weight, mixing, conv_kept) + at("x", grad_act, grad_chan)
        + at("h", normed_kept, gate_low, low_in, hidden_in, norm_gain) + at("x", grad_dt)
        + smem,
        [
            pltpu.VMEM((tokens + 16, chans), f32), pltpu.VMEM((2, tokens + 16, chans), f32),
            pltpu.VMEM((tokens + 16, LANES), f32), pltpu.VMEM(square, bf16),
            pltpu.VMEM((48, chans), f32), pltpu.VMEM((2,) + square, bf16),
        ],
        limit=20, micros=2,
    )
    in_far = swap(in_send)
    late, early_sums = lax.optimization_barrier((late, early_sums))
    late_pieces = send_pieces(late, dp)
    output, input_grad = call(
        outputs_kernel,
        at("h", shape((half_width, tokens), bf16), shape((half_width, tokens), f32)),
        at("h", hidden_in, cot_own, out_own) + at("x", out_far) + at("h", in_own) + at("x", in_far) + smem,
        limit=16, micros=3,
    )
    firsts = [first_xproj_weight, first_dtproj_weight, first_conv_weight, first_chan_params]
    seconds = [second_xproj_weight, second_dtproj_weight, second_conv_weight, second_chan_params]
    for group in (firsts, seconds):
        group[0], group[3] = flip(group[0]), turn(group[3])
    weights = [w_xp, dtproj_weight, conv_weight, w_cp]
    half = shape((width, chans), f32)
    whole_in, whole_out = shape(in_weight.shape, f32), shape(out_weight.shape, f32)
    x_out, y_out, x_in, y_in, u_gate, u_out, early_norms, early_stats = call(
        early_kernel,
        at("h", whole_out, whole_out) + at("1", whole_in, whole_in)
        + at("h", half, whole_out, shape((16, LANES), f32), shape((8, chans), f32)),
        at("x", early_sums) + at("h", out_weight, first_out_weight, second_out_weight)
        + at("1", in_weight, first_in_weight, second_in_weight),
        limit=12, micros=5,
    )
    late_copies, output, input_grad = lax.optimization_barrier((join_pieces(late_pieces), output, input_grad))
    late_sums = lax.all_to_all(late_copies, "dp", 0, 0, tiled=True)
    shapes = [shape(tensor.shape, f32) for tensor in weights]
    late_outs = []
    for entry in shapes:
        late_outs += [entry, entry]
    moments_in = [tensor for pair in zip(firsts, seconds) for tensor in pair]
    got = call(
        late_kernel,
        at("x", half, half) + at("h", *late_outs)
        + at("x", half, *shapes, shape((16, LANES), f32), shape((8, chans), f32)),
        at("x", late_sums) + at("h", early_norms, early_stats, *moments_in)
        + at("0", first_in_weight, second_in_weight),
        limit=12, micros=5,
        passed=at("h", *weights) + at("0", in_weight) + at("1", in_weight) + at("h", out_weight, u_gate, u_out),
    )
    moments, updates, norms, stats, kept = got[:10], got[10:15], got[15], got[16], got[17:]
    kept_small, (kept_mix, kept_gate, kept_out, changed_gate, changed_out) = kept[0:4], kept[4:]
    norms_far = swap(norms)
    pairs = []
    for entry in [whole_in, whole_out, *shapes]:
        pairs += [entry, shape(entry.shape, bf16)]
    row = shape((half_width,), f32)
    whole_low = shape(whole_in.shape, bf16)
    done = call(
        apply_kernel,
        at("2", whole_in) + at("h", whole_low)
        + at(
            "h", *pairs[2:], row, row, row, shape((half_width,), bf16), shape((2, 7), f32),
            shape((2, chans), f32),
        )
        + at("m", whole_in, whole_in),
        at("x", norms, norms_far, stats, kept_mix, kept_gate, kept_out, *kept_small, updates[0], changed_gate, changed_out, *updates[1:])
        + at("h", norm_gain) + at("x", moments_gain[0:1], moments_gain[1:2], moments[0], moments[1])
        + smem + at("m", x_in, y_in),
        [pltpu.SemaphoreType.DMA((2,))],
        limit=14, micros=5, aliases={23: 18, 24: 19},
    )
    flat = list(done[12:16])
    firsts_out = [done[18], x_out, *moments[2::2]]
    seconds_out = [done[19], y_out, *moments[3::2]]
    for place in range(6):
        entry = [firsts_out[place], seconds_out[place], done[2 * place], done[2 * place + 1]]
        if place == 2:
            entry = [flip(tensor) for tensor in entry]
        if place == 5:
            entry = [turn(tensor) for tensor in entry]
        flat += entry
    return (output.T, input_grad.T, *flat, done[16].T, done[17])


def solution(mesh):
    rows = P("dp", None)
    cells = P("dp", "chan")
    last = P(None, None, "chan")
    first = P("chan", None)
    middle = P(None, "chan", None)
    tensors = (last, first, middle, last, last, last)
    outs = [cells, cells] + [P("chan")] * 4
    for spec in tensors:
        outs += [spec] * 4
    return jax.shard_map(
        functools.partial(program, mesh.shape["dp"]),
        mesh=mesh,
        in_specs=(rows, cells, P("dp"), P(), *tensors, P("chan"), *tensors, P("chan"), *tensors),
        out_specs=(*outs, P(), P(None, "chan")),
        check_vma=False,
    )
```

```python
import functools

import jax
import jax.numpy as jnp
from jax import lax
from jax.experimental import pallas as pl
from jax.experimental.pallas import tpu as pltpu
from jax.sharding import PartitionSpec as P

STEP = 4
norm_eps = 1e-06
beta_one = 0.5
beta_two = 0.5
adam_eps = 1e-06
decay_rate = 0.01
learn_rate = 0.3
LOG2E = 1.4426950408889634
FAR = 1e30
FLOOR = -1e-26

f32 = jnp.float32
bf16 = jnp.bfloat16
HIGH = lax.Precision.HIGHEST
LANES = 128
ROWS = 16
NORM_ROWS = 192
CONV_ROWS = 96
LAMB_ROWS = 32
MB = 1 << 20


def dot(left, right, dims, precision=None):
    return lax.dot_general(
        left, right, (dims, ((), ())), precision=precision, preferred_element_type=f32
    )


NN = ((1,), (0,))
TN = ((0,), (0,))
NT = ((1,), (1,))


def sigmoid(values):
    return lax.logistic(values)


def silu_slope(values, sigma):
    return sigma * (1.0 + values * (1.0 - sigma))


def softplus(values):
    return jnp.maximum(values, 0.0) + jnp.log1p(jnp.exp(-jnp.abs(values)))


def wide(tile, times):
    return jnp.concatenate([tile] * times, axis=1)


def fold(values):
    total = values[0:8]
    for start in range(8, values.shape[0], 8):
        total = total + values[start : start + 8]
    return total


def shape(dims, dtype):
    return jax.ShapeDtypeStruct(dims, dtype)


def each_rows(length, body, carry=None, rows=ROWS):
    def step(index, held):
        return body(pl.multiple_of(index * rows, rows), held)

    return lax.fori_loop(0, length // rows, step, carry)


def spread_segments(numbers, tokens):
    across = lax.broadcasted_iota(jnp.int32, (tokens, tokens), 0)
    along = lax.broadcasted_iota(jnp.int32, (tokens, tokens), 1)
    row = numbers.astype(f32).reshape(1, tokens)
    picked = jnp.where(across == along, row, 0.0).astype(bf16)
    return dot(picked, jnp.ones((tokens, LANES), bf16), NN)


def front_kernel(
    hid, gain, w_mix, w_gate, seg, taps, params, w_xp,
    mix_out, gate_out, conv_out, part_out, norm_out, low_out, same_out,
    padded, sgpad,
    *, need, save,
):
    tokens, width = hid.shape
    chans = mix_out.shape[1]
    tiles = chans // LANES

    need(hid, gain)
    gain_row = gain[...].reshape(1, width)

    def normalise(start, held):
        source = hid[pl.ds(start, NORM_ROWS), :].astype(f32)
        scale = lax.rsqrt(jnp.sum(source * source, axis=1, keepdims=True) / width + norm_eps)
        norm_out[pl.ds(start, NORM_ROWS), :] = (source * scale * gain_row).astype(bf16)
        return held

    each_rows(tokens, normalise, 0, NORM_ROWS)
    need(w_mix, w_gate)
    low_out[0] = w_mix[...].astype(bf16)
    low_out[1] = w_gate[...].astype(bf16)
    save(low_out)
    normed = norm_out[...]
    mixing = dot(normed, low_out[0], NN)
    mix_out[...] = mixing
    padded[0:8, :] = jnp.zeros((8, chans), f32)
    padded[pl.ds(8, tokens), :] = mixing
    padded[pl.ds(8 + tokens, 8), :] = jnp.zeros((8, chans), f32)
    save(mix_out)
    gate_out[...] = dot(normed, low_out[1], NN)
    need(seg, taps, w_xp, params)
    numbers = spread_segments(seg[...], tokens)
    sgpad[0:8, :] = jnp.full((8, LANES), -1.0, f32)
    sgpad[pl.ds(8, tokens), :] = numbers
    sgpad[pl.ds(8 + tokens, 8), :] = jnp.full((8, LANES), -1.0, f32)
    width_taps = taps.shape[1]

    def convolve(start, held):
        window = padded[pl.ds(start, CONV_ROWS + 16), :]
        marks = sgpad[pl.ds(start, CONV_ROWS + 16), :]
        own = marks[8 : 8 + CONV_ROWS]
        base = window[8 : 8 + CONV_ROWS]
        for heading in range(2):
            total = params[0, heading : heading + 1, :] + taps[heading, 0:1, :] * base
            for offset in range(1, width_taps):
                begin = 8 - offset if heading == 0 else 8 + offset
                same = jnp.where(marks[begin : begin + CONV_ROWS] == own, 1.0, 0.0)
                if offset == 1:
                    same_out[heading, pl.ds(start, CONV_ROWS), :] = same
                moved = window[begin : begin + CONV_ROWS]
                total = total + taps[heading, offset : offset + 1, :] * moved * wide(same, tiles)
            conv_out[heading, pl.ds(start, CONV_ROWS), :] = total
        return held

    each_rows(tokens, convolve, 0, CONV_ROWS)
    for heading in range(2):
        pre = conv_out[heading]
        act_low = (pre * sigmoid(pre)).astype(bf16)
        rows = w_xp.shape[1]
        part_out[heading * rows : (heading + 1) * rows, :] = dot(
            w_xp[heading].astype(bf16), act_low, NT
        )


SPAN = 64


class Sizes:
    def __init__(self, tokens, chans, count, rank):
        self.tokens, self.chans, self.count, self.rank = tokens, chans, count, rank
        self.tiles = chans // LANES
        self.blocks = tokens // LANES
        self.rows = rank + 2 * count
        self.block_rows = LANES * count
        self.pairs = [(heading, tile) for heading in range(2) for tile in range(self.tiles)]

    def base(self, heading, tile):
        return (heading * self.tiles + tile) * self.tokens

    def row(self, ref, heading, tile, at):
        return ref[pl.ds(self.base(heading, tile) + at, 1), :]

    def whole(self, ref, heading):
        starts = [self.base(heading, tile) for tile in range(self.tiles)]
        return jnp.concatenate([ref[start : start + self.tokens, :] for start in starts], axis=1)


def cols(tile):
    return slice(tile * LANES, (tile + 1) * LANES)


def split(values):
    high = values.astype(bf16)
    return high, (values - high.astype(f32)).astype(bf16)


def group_maps(target, tile, heading, count):
    groups = tile.shape[1] // count
    for group in range(groups):
        block, place = divmod(group * count, LANES)
        own = tile[:, cols(block)]
        if place:
            own = pltpu.roll(own, LANES - place, 1)
        target[heading, group] = own


def diagonal_maps(target, tile, heading, count):
    tokens = tile.shape[1]
    squared = count * count
    lane = lax.broadcasted_iota(jnp.int32, (count, squared), 1)
    row = lax.broadcasted_iota(jnp.int32, (count, squared), 0)
    repeat = jnp.where(lane % count == row, 1.0, 0.0).astype(bf16)
    token = lax.broadcasted_iota(jnp.int32, (tokens, squared), 0)
    place = lax.broadcasted_iota(jnp.int32, (tokens, squared), 1)
    mine = place // count == token % count
    for number, part in enumerate(split(tile)):
        spread = jnp.where(mine, dot(part, repeat, TN), 0.0).astype(bf16)
        target[heading, :, number] = spread.reshape(tokens // count, count, squared)


def weigh_states(left, maps):
    half = maps.shape[0] // 2
    got = dot(maps, left, NN)
    return got[:half] + got[half:]


def gather_states(left, right, count):
    products = dot(left, right, NT)
    lane = lax.broadcasted_iota(jnp.int32, (count, count), 1)
    total = products[0:count]
    for place in range(1, count):
        total = jnp.where(lane == place, products[place * count : (place + 1) * count], total)
    return total


def dot3(left, right, dims):
    (left_high, left_low), (right_high, right_low) = split(left), split(right)
    if dims == TN:
        lefts = jnp.concatenate([left_high, left_low, left_high], axis=0)
        return dot(lefts, jnp.concatenate([right_high, right_high, right_low], axis=0), dims)
    rows = left.shape[0]
    both = dot(jnp.concatenate([left_high, left_low], axis=0), right_high, dims)
    return both[:rows] + both[rows:] + dot(left_high, right_low, dims)


class Sweep:
    def __init__(self, z, turned):
        self.z, self.turned = z, turned
        self.groups = z.tokens // z.count
        self.stage_groups = self.groups // z.blocks

    def group(self, order, heading):
        return self.groups - 1 - order if heading == self.turned else order

    def block(self, stage, heading):
        return self.z.blocks - 1 - stage if heading == self.turned else stage

    def inner(self, ahead, heading):
        return self.z.count - 1 - ahead if heading == self.turned else ahead

    def rows(self, group):
        return pl.ds(pl.multiple_of(group * self.z.count, self.z.count), self.z.count)

    def run(self, z, carried, scan, post, between):
        def step(index, held):
            order = 2 * index
            post(jnp.maximum(order - 1, 0), 1)
            held = scan(order, held, 0)
            post(order, 0)
            return scan(order + 1, held, 1)

        per = self.stage_groups // 2
        for stage in range(z.blocks):
            between(stage, True)
            carried = lax.fori_loop(stage * per, (stage + 1) * per, step, carried)
            between(stage, False)
        post(self.groups - 1, 1)
        return carried


def store_gathered(target, target_row, gathered, heading, z):
    per = LANES // z.count
    for block in range(z.blocks):
        pieces = [gathered[heading, block * per + place] for place in range(per)]
        target[target_row : target_row + z.count, cols(block)] = jnp.concatenate(pieces, axis=1)


def fill_rates(rates, params, count):
    for heading in range(2):
        for n in range(count):
            value = -jnp.exp(params[3 + n, heading : heading + 1, :])
            rates[heading, n : n + 1, :] = jnp.minimum(value, FLOOR)


def forward_kernel(
    own_part, far_part, params, w_dt, cot_own, cot_far, w_out, conv_pre, gate, same, normed, core,
    states_out, proj, grad_maps, skips, far_step, grad_y, pre_step, inflow_low, gate_low, branch_low, early,
    grad_branch, inflow, grad_y_low, act, result, maps, diagonal, gathered, states, low_one, low_two,
    rates, sems,
    *, need, save,
):
    tokens, chans = gate.shape
    z = Sizes(tokens, chans, params.shape[0] - 3, w_dt.shape[1])
    count, rank, rows, tiles = z.count, z.rank, z.rows, z.tiles
    half_width = cot_own.shape[0]
    width = 2 * half_width
    me = core[0]
    sweep = Sweep(z, 1)
    lows = (low_one, low_two)

    proj[...] = own_part[...] + far_part[...]
    save(proj)
    for heading in range(2):
        first = heading * rows + rank
        group_maps(maps, proj[first : first + count, :], heading, count)
        diagonal_maps(diagonal, proj[first + count : first + 2 * count, :], heading, count)
    for tile in range(tiles):

        def activate(start, held, tile=tile):
            here = pl.ds(start, SPAN)
            for heading in range(2):
                pre = conv_pre[heading, here, cols(tile)]
                act[heading, here, cols(tile)] = pre * sigmoid(pre)
            return held

        each_rows(tokens, activate, 0, SPAN)
    need(params, w_dt)
    fill_rates(rates, params, count)
    for heading in range(2):
        pre_step[heading] = (
            dot3(proj[heading * rows : heading * rows + rank, :], w_dt[heading], TN)
            + params[1, heading : heading + 1, :]
        )
    save(pre_step)
    need(w_out, cot_own)
    low_out = w_out[...].astype(bf16)
    low_cot = jnp.where(
        me == 0,
        jnp.concatenate([cot_own[...].astype(f32), cot_far[...].astype(f32)], 0),
        jnp.concatenate([cot_far[...].astype(f32), cot_own[...].astype(f32)], 0),
    ).astype(bf16)
    grad_branch[...] = dot(low_cot, low_out, ((0,), (1,)))

    for tile in range(tiles):

        def prepare(start, held, tile=tile):
            here = pl.ds(start, SPAN)
            for heading in range(2):
                size = softplus(pre_step[heading, here, cols(tile)])
                there = pl.ds(z.base(heading, tile) + start, SPAN)
                entering = size * act[heading, here, cols(tile)]
                inflow[there, :] = entering
                inflow_low[heading, here, cols(tile)] = entering.astype(bf16)
                far_step[there, :] = jnp.where(same[heading, here, :] > 0.5, size * LOG2E, FAR)
            gated = gate[here, cols(tile)]
            back = grad_branch[here, cols(tile)] * (gated * sigmoid(gated))
            grad_y[pl.ds(z.base(0, tile) + start, SPAN), :] = back
            grad_y_low[here, cols(tile)] = back.astype(bf16)
            return held

        each_rows(tokens, prepare, 0, SPAN)
    save(far_step, inflow_low, grad_y)

    blank = jnp.zeros((count, LANES), f32)
    states[0, 0:count, :] = jnp.zeros((count, chans), bf16)
    states[1, tokens * count : (tokens + 1) * count, :] = jnp.zeros((count, chans), bf16)
    low_two[...] = jnp.zeros(low_two.shape, bf16)
    speeds = [rates[heading, :, cols(tile)] for heading, tile in z.pairs]

    def scan(order, carried, slot):
        carried = list(carried)
        enters = [maps[heading, sweep.group(order, heading)] for heading in range(2)]
        for heading in range(2):
            for ahead in range(count):
                inner = sweep.inner(ahead, heading)
                at = sweep.group(order, heading) * count + inner
                kept = pl.multiple_of((at + (1 if heading == 0 else 0)) * count, count)
                enter = jnp.broadcast_to(enters[heading][:, inner : inner + 1], (count, LANES))
                for tile in range(tiles):
                    number = heading * tiles + tile
                    decay = jnp.exp2(z.row(far_step, heading, tile, at) * speeds[number])
                    state = decay * carried[number] + enter * z.row(inflow, heading, tile, at)
                    carried[number] = state
                    low = state.astype(bf16)
                    states[heading, pl.ds(kept, count), cols(tile)] = low
                    lows[slot][heading, inner * count : (inner + 1) * count, cols(tile)] = low
        return tuple(carried)

    def post(order, slot):
        for heading in range(2):
            group = sweep.group(order, heading)
            left = lows[slot][heading]
            gathered[heading, group] = gather_states(left, grad_y_low[sweep.rows(group), :], count)
            result[heading, sweep.rows(group), :] = weigh_states(
                left, diagonal[heading, group].reshape(2 * count, count * count)
            )

    keeps = []

    def between(stage, before):
        if before:
            return
        for heading in range(2):
            begin, extent = sweep.block(stage, heading) * z.block_rows, z.block_rows
            if stage == 0:
                extent += count
            elif heading == 0:
                begin += count
            piece = pl.ds(begin, extent)
            keep = pltpu.make_async_copy(
                states.at[heading, piece, :], states_out.at[heading, piece, :], sems.at[heading, stage]
            )
            keep.start()
            keeps.append(keep)

    sweep.run(z, (blank,) * len(z.pairs), scan, post, between)
    for heading in range(2):
        store_gathered(grad_maps, heading * count, gathered, heading, z)
    skips[...] = jnp.zeros(skips.shape, f32)
    for tile in range(tiles):

        def finish(start, held, tile=tile):
            here = pl.ds(start, SPAN)
            total = jnp.zeros((SPAN, LANES), f32)
            sums = []
            back = grad_y[pl.ds(z.base(0, tile) + start, SPAN), :]
            for heading in range(2):
                active = act[heading, here, cols(tile)]
                total = total + result[heading, here, cols(tile)]
                total = total + params[2, heading : heading + 1, cols(tile)] * active
                sums.append(held[heading] + fold(back * active))
            gated = gate[here, cols(tile)]
            sigma = sigmoid(gated)
            branch_low[here, cols(tile)] = (total * (gated * sigma)).astype(bf16)
            gate_low[here, cols(tile)] = (
                grad_branch[here, cols(tile)] * total * silu_slope(gated, sigma)
            ).astype(bf16)
            return tuple(sums)

        sums = each_rows(tokens, finish, (jnp.zeros((8, LANES), f32),) * 2, SPAN)
        for heading in range(2):
            skips[heading : heading + 1, cols(tile)] = jnp.sum(sums[heading], axis=0, keepdims=True)
    save(gate_low, branch_low, grad_maps, skips)
    branch = branch_low[...]
    grad_w = dot(branch, low_cot, ((0,), (1,))).astype(bf16)
    for tile in range(width // LANES):
        early[tile * chans : (tile + 1) * chans, :] = grad_w[:, cols(tile)]
    base_row = chans * (width // LANES)
    grad_w = dot(normed[...], gate_low[...], TN).astype(bf16)
    for tile in range(tiles):
        early[base_row + tile * width : base_row + (tile + 1) * width, :] = grad_w[:, cols(tile)]
    base_row += tiles * width
    if early.shape[0] > base_row:
        early[base_row:, :] = jnp.zeros((early.shape[0] - base_row, LANES), bf16)
    for keep in keeps:
        keep.wait()


def backward_kernel(
    states_in, params, proj, far_step, grad_y, inflow_low, pre_step, conv_pre, grad_maps, skips, w_dt,
    grad_part, grad_act, grad_dt, grad_chan,
    result, decayed, maps, diagonal, gathered, states, low_one, low_two, products_one, products_two, rates, sems,
    *, need, save,
):
    _, tokens, chans = conv_pre.shape
    z = Sizes(tokens, chans, params.shape[0] - 3, w_dt.shape[1])
    count, rank, rows, tiles = z.count, z.rank, z.rows, z.tiles
    sweep = Sweep(z, 0)
    lows, products = (low_one, low_two), (products_one, products_two)
    loads = {}
    for stage in range(z.blocks):
        for heading in range(2):
            begin = sweep.block(stage, heading) * z.block_rows + (count if heading == 1 else 0)
            piece = pl.ds(begin, z.block_rows)
            load = pltpu.make_async_copy(
                states_in.at[heading, piece, :], states.at[heading, piece, :], sems.at[heading, stage]
            )
            load.start()
            loads[stage, heading] = load
    need(params, proj)
    fill_rates(rates, params, count)
    for heading in range(2):
        first = heading * rows + rank
        group_maps(maps, proj[first + count : first + 2 * count, :], heading, count)
        diagonal_maps(diagonal, proj[first : first + count, :], heading, count)
    for low in (low_two, products_two):
        low[...] = jnp.zeros(low.shape, bf16)
    blank = jnp.zeros((count, LANES), f32)
    speeds = [rates[heading, :, cols(tile)] for heading, tile in z.pairs]

    def scan(order, held, slot):
        waiting = list(held[: len(z.pairs)])
        totals = list(held[len(z.pairs) :])
        leaves = [maps[heading, sweep.group(order, heading)] for heading in range(2)]
        for heading in range(2):
            for ahead in range(count):
                inner = sweep.inner(ahead, heading)
                at = sweep.group(order, heading) * count + inner
                prior = pl.multiple_of((at + (0 if heading == 0 else 1)) * count, count)
                leave = jnp.broadcast_to(leaves[heading][:, inner : inner + 1], (count, LANES))
                here = slice(inner * count, (inner + 1) * count)
                for tile in range(tiles):
                    number = heading * tiles + tile
                    size = z.row(far_step, heading, tile, at)
                    decay = jnp.exp2(size * speeds[number])
                    grad = leave * z.row(grad_y, 0, tile, at) + waiting[number]
                    lead = decay * grad
                    waiting[number] = lead
                    slope = lead * states[heading, pl.ds(prior, count), cols(tile)].astype(f32)
                    totals[number] = totals[number] + slope * size
                    products[slot][heading, here, cols(tile)] = (slope * speeds[number]).astype(bf16)
                    lows[slot][heading, here, cols(tile)] = grad.astype(bf16)
        return tuple(waiting + totals)

    lane = lax.broadcasted_iota(jnp.int32, (count, count * count), 1)
    row = lax.broadcasted_iota(jnp.int32, (count, count * count), 0)
    ones = jnp.where(lane // count == row, 1.0, 0.0).astype(bf16)

    def post(order, slot):
        for heading in range(2):
            group = sweep.group(order, heading)
            left = lows[slot][heading]
            gathered[heading, group] = gather_states(left, inflow_low[heading, sweep.rows(group), :], count)
            result[heading, sweep.rows(group), :] = weigh_states(
                left, diagonal[heading, group].reshape(2 * count, count * count)
            )
            decayed[heading, sweep.rows(group), :] = dot(ones, products[slot][heading], NN)

    def between(stage, before):
        if before:
            if stage == 0:
                need(far_step, grad_y, inflow_low)
            for heading in range(2):
                loads[stage, heading].wait()

    held = sweep.run(z, (blank,) * (2 * len(z.pairs)), scan, post, between)
    for number, (heading, tile) in enumerate(z.pairs):
        slopes = held[len(z.pairs) + number] / LOG2E
        for n in range(count):
            grad_chan[3 + n, heading : heading + 1, cols(tile)] = slopes[n : n + 1] * -jnp.exp(
                params[3 + n, heading : heading + 1, cols(tile)]
            )
    need()
    for heading in range(2):
        first = heading * rows + rank
        store_gathered(grad_part, first, gathered, heading, z)
        grad_part[first + count : first + 2 * count, :] = grad_maps[
            heading * count : (heading + 1) * count, :
        ]

    for tile in range(tiles):

        def close(start, held, tile=tile):
            here = pl.ds(start, SPAN)
            sums = []
            back = grad_y[pl.ds(z.base(0, tile) + start, SPAN), :]
            for heading in range(2):
                pre = conv_pre[heading, here, cols(tile)]
                act = pre * sigmoid(pre)
                passed = result[heading, here, cols(tile)]
                reach = pre_step[heading, here, cols(tile)]
                grad_act[heading, here, cols(tile)] = (
                    passed * softplus(reach) + back * params[2, heading : heading + 1, cols(tile)]
                )
                grad_pre = (decayed[heading, here, cols(tile)] + passed * act) * sigmoid(reach)
                pre_step[heading, here, cols(tile)] = grad_pre
                sums.append(held[heading] + fold(grad_pre))
            return tuple(sums)

        biases = each_rows(tokens, close, (jnp.zeros((8, LANES), f32),) * 2, SPAN)
        for heading in range(2):
            grad_chan[1, heading : heading + 1, cols(tile)] = jnp.sum(
                biases[heading], axis=0, keepdims=True
            )
    save(grad_act)
    for heading in range(2):
        grad_chan[0, heading : heading + 1, :] = jnp.zeros((1, chans), f32)
        grad_chan[2, heading : heading + 1, :] = skips[heading : heading + 1, :]
        grad_pre = pre_step[heading]
        grad_part[heading * rows : heading * rows + rank, :] = dot3(w_dt[heading], grad_pre, NT)
        grad_dt[heading] = dot3(proj[heading * rows : heading * rows + rank, :], grad_pre, NN)


def forward_call(args, sizes, early_rows, half_width, kept, limit=30):
    z = sizes
    square = (z.tokens, z.chans)
    both = (2,) + square
    flat = (2 * z.tiles * z.tokens, LANES)
    groups = z.tokens // z.count
    squared = z.count * z.count
    states = (2, (z.tokens + 1) * z.count, z.chans)
    slot = pltpu.VMEM((2, squared, z.chans), bf16)
    return call(
        forward_kernel,
        at("m", shape(states, bf16))
        + at(
            "h", shape((2 * z.rows, z.tokens), f32), shape((2 * z.count, z.tokens), f32), shape((8, z.chans), f32),
            shape(flat, f32), shape((z.tiles * z.tokens, LANES), f32), shape(both, f32), shape(both, bf16),
            shape(square, bf16), shape(square, bf16),
        )
        + at("x", shape((early_rows, LANES), bf16)),
        args,
        [
            pltpu.VMEM(square, f32), pltpu.VMEM(flat, f32), pltpu.VMEM(square, bf16), pltpu.VMEM(both, f32),
            pltpu.VMEM(both, f32), pltpu.VMEM((2, groups, z.count, LANES), f32),
            pltpu.VMEM((2, groups, 2, z.count, squared), bf16), pltpu.VMEM((2, groups, z.count, z.count), f32),
            pltpu.VMEM(states, bf16), slot, slot, pltpu.VMEM((2, z.count, z.chans), f32),
            pltpu.SemaphoreType.DMA((2, z.blocks)),
        ],
        limit=limit, micros=15, kept=kept,
    )


def backward_call(args, sizes, limit=30):
    z = sizes
    square = (z.tokens, z.chans)
    both = (2,) + square
    groups = z.tokens // z.count
    squared = z.count * z.count
    slot = pltpu.VMEM((2, squared, z.chans), bf16)
    return call(
        backward_kernel,
        at(
            "x", shape((2 * z.rows, z.tokens), f32), shape(both, f32), shape((2, z.rank, z.chans), f32),
            shape((3 + z.count, 2, z.chans), f32),
        ),
        args,
        [
            pltpu.VMEM(both, f32), pltpu.VMEM(both, f32), pltpu.VMEM((2, groups, z.count, LANES), f32),
            pltpu.VMEM((2, groups, 2, z.count, squared), bf16), pltpu.VMEM((2, groups, z.count, z.count), f32),
            pltpu.VMEM((2, (z.tokens + 1) * z.count, z.chans), bf16), slot, slot, slot, slot,
            pltpu.VMEM((2, z.count, z.chans), f32), pltpu.SemaphoreType.DMA((2, z.blocks)),
        ],
        limit=limit, micros=15,
    )


def back_kernel(
    own_part, far_part, seg, w_xp, taps, mixing, conv_pre, grad_act, grad_chan, normed, gate_low,
    low_in, hid, gain, grad_dt, branch, w_out, core,
    sums_out, in_own, in_far, out_own, out_far,
    padded, gpad, sgpad, mixed_low, small, act_low,
    *, need, save,
):
    tokens, width = hid.shape
    chans = mixing.shape[1]
    tiles = chans // LANES
    rows = w_xp.shape[1]
    width_taps = taps.shape[1]
    me = core[0]
    half_width = in_own.shape[0] - 8
    edge = jnp.zeros((8, chans), f32)
    padded[0:8, :] = edge
    padded[pl.ds(8 + tokens, 8), :] = edge
    gpad[0, 0:8, :] = edge
    gpad[1, 0:8, :] = edge
    gpad[0, pl.ds(8 + tokens, 8), :] = edge
    gpad[1, pl.ds(8 + tokens, 8), :] = edge
    sgpad[0:8, :] = jnp.full((8, LANES), -1.0, f32)
    sgpad[pl.ds(8 + tokens, 8), :] = jnp.full((8, LANES), -1.0, f32)
    need(seg, w_xp, mixing)
    padded[pl.ds(8, tokens), :] = mixing[...]
    sgpad[pl.ds(8, tokens), :] = spread_segments(seg[...], tokens)

    parts = (own_part[...] + far_part[...]).astype(bf16)
    for heading in range(2):
        part = parts[heading * rows : (heading + 1) * rows, :]
        gpad[heading, pl.ds(8, tokens), :] = dot(part, w_xp[heading].astype(bf16), TN)

    blank = jnp.zeros((8, chans), f32)
    need(taps, conv_pre, grad_act, grad_chan)

    def through_conv(start, held):
        here = pl.ds(start, CONV_ROWS)
        window = padded[pl.ds(start, CONV_ROWS + 16), :]
        marks = sgpad[pl.ds(start, CONV_ROWS + 16), :]
        own = marks[8 : 8 + CONV_ROWS]
        base = window[8 : 8 + CONV_ROWS]
        sums = []
        for heading in range(2):
            pre = conv_pre[heading, here, :]
            sigma = sigmoid(pre)
            act_low[heading, here, :] = (pre * sigma).astype(bf16)
            inside = pl.ds(pl.multiple_of(start + 8, 8), CONV_ROWS)
            grad = (gpad[heading, inside, :] + grad_act[heading, here, :]) * silu_slope(pre, sigma)
            gpad[heading, inside, :] = grad
            sums.append(held[5 * heading] + fold(grad))
            sums.append(held[5 * heading + 1] + fold(grad * base))
            for offset in range(1, width_taps):
                begin = 8 - offset if heading == 0 else 8 + offset
                kept = jnp.where(marks[begin : begin + CONV_ROWS] == own, 1.0, 0.0)
                moved = window[begin : begin + CONV_ROWS]
                sums.append(held[5 * heading + 1 + offset] + fold(grad * moved * wide(kept, tiles)))
        return tuple(sums)

    sums = each_rows(tokens, through_conv, (blank,) * 10, CONV_ROWS)
    small[...] = jnp.zeros(small.shape, f32)
    for heading in range(2):
        bias = jnp.sum(sums[5 * heading], axis=0, keepdims=True)
        for offset in range(width_taps):
            row = heading * width_taps + offset
            small[row : row + 1, :] = jnp.sum(sums[5 * heading + 1 + offset], axis=0, keepdims=True)
        for entry in range(grad_chan.shape[0]):
            row = 2 * width_taps + 2 * entry + heading
            small[row : row + 1, :] = (
                bias
                if entry == 0
                else grad_chan[entry, heading : heading + 1, :]
            )

    def mixed(start, held):
        here = pl.ds(start, CONV_ROWS)
        marks = sgpad[pl.ds(start, CONV_ROWS + 16), :]
        own = marks[8 : 8 + CONV_ROWS]
        total = jnp.zeros((CONV_ROWS, chans), f32)
        for heading in range(2):
            window = gpad[heading, pl.ds(start, CONV_ROWS + 16), :]
            total = total + window[8 : 8 + CONV_ROWS] * taps[heading, 0:1, :]
            for offset in range(1, width_taps):
                begin = 8 + offset if heading == 0 else 8 - offset
                kept = jnp.where(marks[begin : begin + CONV_ROWS] == own, 1.0, 0.0)
                total = total + window[begin : begin + CONV_ROWS] * wide(kept, tiles) * taps[
                    heading, offset : offset + 1, :
                ]
        mixed_low[here, :] = total.astype(bf16)
        return held

    each_rows(tokens, mixed, 0, CONV_ROWS)

    base_row = 0

    def put(values):
        nonlocal base_row
        for tile in range(values.shape[1] // LANES):
            sums_out[base_row : base_row + values.shape[0], :] = values[
                :, tile * LANES : (tile + 1) * LANES
            ].astype(bf16)
            base_row += values.shape[0]

    need()
    partial = dot(mixed_low[...], low_in[0], NT) + dot(gate_low[...], low_in[1], NT)
    padded[pl.ds(8, tokens), :] = partial

    gain_row = gain[...].reshape(1, width)

    def gains(start, held):
        here = pl.ds(start, NORM_ROWS)
        source = hid[here, :].astype(f32)
        scale = lax.rsqrt(jnp.sum(source * source, axis=1, keepdims=True) / width + norm_eps)
        inside = pl.ds(pl.multiple_of(start + 8, 8), NORM_ROWS)
        grad = padded[inside, :]
        padded[inside, :] = grad * gain_row
        return held + fold(grad * source * scale)

    gain_sum = each_rows(tokens, gains, jnp.zeros((8, width), f32), NORM_ROWS)
    small[46:47, :] = jnp.sum(gain_sum, axis=0, keepdims=True)
    weighted = padded[pl.ds(8, tokens), :]
    products = weighted * hid[...].astype(f32)
    turned = weighted.T
    row_dot = dot(jnp.ones((8, width), f32), products, NT, HIGH)
    in_own[0:half_width, :] = jnp.where(me == 0, turned[:half_width], turned[half_width:])
    in_far[0:half_width, :] = jnp.where(me == 0, turned[half_width:], turned[:half_width])
    in_own[pl.ds(half_width, 8), :] = row_dot
    in_far[pl.ds(half_width, 8), :] = row_dot
    save(in_own)
    sent = dot(w_out[...].astype(bf16), branch[...], ((0,), (1,)))
    out_own[...] = jnp.where(me == 0, sent[:half_width], sent[half_width:])
    out_far[...] = jnp.where(me == 0, sent[half_width:], sent[:half_width])
    save(out_own)
    put(dot(normed[...], mixed_low[...], TN))
    put(
        jnp.concatenate(
            [
                dot(parts[heading * rows : (heading + 1) * rows, :], act_low[heading], NN)
                for heading in range(2)
            ],
            axis=0,
        )
    )
    put(jnp.concatenate([grad_dt[0], grad_dt[1]], axis=0))

    put(small[...])
    sums_out[base_row:, :] = jnp.zeros((sums_out.shape[0] - base_row, LANES), bf16)


def outputs_kernel(hid, cot_own, out_own, out_far, in_own, in_far, core, output, input_grad, *, need, save):
    width = hid.shape[1]
    half_width = cot_own.shape[0]
    me = core[0]
    need()
    source = hid[...].astype(f32).T
    scale = lax.rsqrt(jnp.sum(source * source, axis=0, keepdims=True) / width + norm_eps)
    own = jnp.where(me == 0, source[:half_width], source[half_width:])
    output[...] = (own + (out_own[...] + out_far[...])).astype(bf16)
    weighted = in_own[0:half_width, :] + in_far[0:half_width, :]
    save(output)
    row_dot = in_own[half_width : half_width + 1, :] + in_far[half_width : half_width + 1, :]
    input_grad[...] = (
        cot_own[...].astype(f32)
        + scale * weighted
        - own * (scale * scale * scale) * (row_dot / width)
    )


def lamb_moments(weight, grad, first, second):
    first_new = beta_one * first + (1.0 - beta_one) * grad
    second_new = beta_two * second + (1.0 - beta_two) * grad * grad
    root = jnp.sqrt(second_new * (1.0 / (1.0 - beta_two**STEP)))
    update = first_new * (1.0 / (1.0 - beta_one**STEP)) / (root + adam_eps) + decay_rate * weight
    return (first_new, second_new, update)


def rows_sum(values):
    return jnp.sum(values, axis=0, keepdims=True)


def lanes_sum(values):
    total = rows_sum(values)
    lanes = total[:, 0:LANES]
    for tile in range(1, values.shape[1] // LANES):
        lanes = lanes + total[:, cols(tile)]
    return lanes


def fetch(sums, base, stride, start, count, number):
    return jnp.concatenate(
        [sums[pl.ds(base + tile * stride + start, count), :].astype(f32) for tile in range(number)], axis=1
    )


def spread_of(update, mean, length):
    def step(start, kept):
        away = update[pl.ds(start, LAMB_ROWS), :] - mean
        return kept + fold(away * away)

    return rows_sum(each_rows(length, step, jnp.zeros((8, update.shape[1]), f32), LAMB_ROWS))


def half_update(sums, base, stride, weights, a_ref, b_ref, x_ref, y_ref, u_ref):
    length, chans = weights.shape
    zero = jnp.zeros((8, chans), f32)

    def step(start, kept):
        here = pl.ds(start, LAMB_ROWS)
        grad = fetch(sums, base, stride, start, LAMB_ROWS, chans // LANES)
        weight = weights[here, :]
        first, second, update = lamb_moments(weight, grad, a_ref[here, :], b_ref[here, :])
        x_ref[here, :] = first
        y_ref[here, :] = second
        u_ref[here, :] = update
        return (
            kept[0] + fold(weight * weight), kept[1] + fold(update * update), kept[2] + fold(update)
        )

    return each_rows(length, step, (zero, zero, zero), LAMB_ROWS)


def early_kernel(
    sums, w_out, a_out, b_out, w_gate, a_gate, b_gate,
    x_out, y_out, x_gate, y_gate, u_gate, u_out, norms, stats,
    *, need, save,
):
    width, chans = w_gate.shape
    tiles = width // LANES
    norms[...] = jnp.zeros(norms.shape, f32)
    zero = jnp.zeros((8, width), f32)
    need(w_out, a_out, b_out)

    def one_out(start, kept):
        here = pl.ds(start, LAMB_ROWS)
        grad = fetch(sums, 0, chans, start, LAMB_ROWS, tiles)
        weight = w_out[here, :]
        first, second, update = lamb_moments(weight, grad, a_out[here, :], b_out[here, :])
        x_out[here, :] = first
        y_out[here, :] = second
        u_out[here, :] = update
        return (kept[0] + fold(weight * weight), kept[1] + fold(update * update))

    weight_sq, update_sq = each_rows(chans, one_out, (zero, zero), LAMB_ROWS)
    norms[1:2, :] = lanes_sum(weight_sq)
    norms[7:8, :] = lanes_sum(update_sq)
    save(x_out, y_out, u_out)
    need()
    weight_sq, update_sq, total = half_update(
        sums, chans * tiles, width, w_gate, a_gate, b_gate, x_gate, y_gate, u_gate
    )
    norms[0:1, :] = lanes_sum(weight_sq)
    norms[6:7, :] = lanes_sum(update_sq)
    save(x_gate, y_gate, u_gate)
    gate_mean = rows_sum(total) / width
    stats[0:1, :] = gate_mean
    stats[1:2, :] = spread_of(u_gate, gate_mean, width)
    ones = jnp.ones((8, width), f32)
    out_all = u_out[...]
    out_mean = jnp.sum(out_all, axis=1, keepdims=True) / width
    away = out_all - out_mean
    stats[2:3, :] = dot(ones, out_all, NT, HIGH)[0:1] / width
    stats[3:4, :] = dot(ones, away * away, NT, HIGH)[0:1]
    stats[4:8, :] = jnp.zeros((4, chans), f32)


def late_kernel(
    sums, early_norms, early_stats, *rest, need, save
):
    small_in, (a_mix, b_mix), rest = rest[:8], rest[8:10], rest[10:]
    x_mix, y_mix, x_xp, y_xp, x_dt, y_dt, x_cv, y_cv, x_cp, y_cp, *rest = rest
    u_mix, u_xp, u_dt, u_cv, u_cp, norms, stats, w_xp, w_dt, w_cv, w_cp, w_mix, *_ = rest
    a_xp, b_xp, a_dt, b_dt, a_cv, b_cv, a_cp, b_cp = small_in
    width, chans = w_mix.shape
    tiles = chans // LANES
    base = tiles * width
    need(early_norms, early_stats, *small_in, w_xp, w_dt, w_cv, w_cp)
    norms[...] = early_norms[...]
    stats[...] = early_stats[...]

    def small(place, items, weight, a_ref, b_ref, x_ref, y_ref, u_ref):
        weight_sq, update_sq = jnp.zeros((1, LANES), f32), jnp.zeros((1, LANES), f32)
        for index, grad in enumerate(items):
            held = weight[index]
            first, second, update = lamb_moments(held, grad, a_ref[index], b_ref[index])
            x_ref[index] = first
            y_ref[index] = second
            u_ref[index] = update
            weight_sq = weight_sq + lanes_sum(held * held)
            update_sq = update_sq + lanes_sum(update * update)
        norms[place : place + 1, :] = weight_sq
        norms[6 + place : 7 + place, :] = update_sq

    rows = w_xp.shape[1]
    grads = fetch(sums, base, 2 * rows, 0, 2 * rows, tiles)
    small(2, [grads[:rows], grads[rows:]], w_xp, a_xp, b_xp, x_xp, y_xp, u_xp)
    base += 2 * rows * tiles
    rank = w_dt.shape[1]
    grads = fetch(sums, base, 2 * rank, 0, 2 * rank, tiles)
    small(3, [grads[:rank], grads[rank:]], w_dt, a_dt, b_dt, x_dt, y_dt, u_dt)
    base += 2 * rank * tiles
    grads = fetch(sums, base, 48, 0, 48, tiles)
    taps = w_cv.shape[1]
    small(4, [grads[:taps], grads[taps : 2 * taps]], w_cv, a_cv, b_cv, x_cv, y_cv, u_cv)
    entries = w_cp.shape[0]
    items = [grads[2 * (taps + entry) : 2 * (taps + entry) + 2] for entry in range(entries)]
    small(5, items, w_cp, a_cp, b_cp, x_cp, y_cp, u_cp)
    for tile in range(tiles):
        norms[12 + tile : 13 + tile, :] = grads[46:47, cols(tile)]
    save()
    need(a_mix, b_mix, w_mix)
    weight_sq, update_sq, total = half_update(
        sums, 0, width, w_mix, a_mix, b_mix, x_mix, y_mix, u_mix
    )
    norms[0:1, :] += lanes_sum(weight_sq)
    norms[6:7, :] += lanes_sum(update_sq)
    mix_mean = rows_sum(total) / width
    stats[4:5, :] = mix_mean


def spread_kernel(u_mix, stats, spread, *, need, save):
    spread[...] = jnp.broadcast_to(spread_of(u_mix, stats[4:5, :], u_mix.shape[0]), spread.shape)


def apply_kernel(
    norms_own, norms_far, stats, mix_spread,
    w_mix, w_gate, w_out, w_xp, w_dt, w_cv, w_cp,
    u_mix, u_gate, u_out, u_xp, u_dt, u_cv, u_cp,
    gain, gain_first, gain_second, x_mix, y_mix, core, x_given, y_given,
    n_in, c_in, n_out, c_out, n_xp, c_xp, n_dt, c_dt, n_cv, c_cv, n_cp, c_cp,
    g_first, g_second, g_new, g_copy, norms_out, stats_out, x_in, y_in,
    sems,
    *, need, save,
):
    width, chans = w_mix.shape
    moves = [
        pltpu.make_async_copy(held, target.at[:, 0, :], sems.at[number])
        for number, (held, target) in enumerate(((x_mix, x_in), (y_mix, y_in)))
    ]
    for move in moves:
        move.start()
    half_width = g_new.shape[0]
    me = core[0]
    totals = norms_own[...] + norms_far[...]
    sums = jnp.sum(totals, axis=1, keepdims=True)
    scales = [None]
    for place in range(6):
        weight_norm = jnp.sqrt(sums[place : place + 1])
        update_norm = jnp.sqrt(sums[6 + place : 7 + place])
        scales.append(learn_rate * weight_norm / (update_norm + adam_eps))
        norms_out[0:1, place + 1 : place + 2] = weight_norm
        norms_out[1:2, place + 1 : place + 2] = update_norm

    need(w_mix, w_gate)

    def one_in(start, held):
        here = pl.ds(start, LAMB_ROWS)
        for half, weight, change in ((0, w_mix, u_mix), (1, w_gate, u_gate)):
            fresh = weight[here, :] - scales[1] * change[here, :]
            n_in[half, here, :] = fresh
            c_in[here, half, :] = fresh.astype(bf16)
        return held

    each_rows(width, one_in, 0, LAMB_ROWS)
    save(n_in, c_in)

    def one_out(start, held):
        here = pl.ds(start, LAMB_ROWS)
        fresh = w_out[here, :] - scales[2] * u_out[here, :]
        n_out[here, :] = fresh
        c_out[here, :] = fresh.astype(bf16)
        return held

    each_rows(chans, one_out, 0, LAMB_ROWS)
    save(n_out, c_out)
    need()
    gain_grad = jnp.concatenate(
        [totals[12 + tile : 13 + tile, :] for tile in range(width // LANES)], axis=1
    )
    gain_row = gain[...].reshape(1, width)
    first, second, update = lamb_moments(gain_row, gain_grad, gain_first[...], gain_second[...])
    weight_norm = jnp.sqrt(jnp.sum(gain_row * gain_row, axis=1, keepdims=True))
    update_norm = jnp.sqrt(jnp.sum(update * update, axis=1, keepdims=True))
    norms_out[0:1, 0:1] = weight_norm
    norms_out[1:2, 0:1] = update_norm
    fresh = gain_row - learn_rate * weight_norm / (update_norm + adam_eps) * update

    def own(row):
        return jnp.where(me == 0, row[:, :half_width], row[:, half_width:]).reshape(half_width)

    g_first[...] = own(first)
    g_second[...] = own(second)
    g_new[...] = own(fresh)
    g_copy[...] = own(fresh).astype(bf16)
    for place, weight, change, fresh_ref, copy in (
        (3, w_xp, u_xp, n_xp, c_xp),
        (4, w_dt, u_dt, n_dt, c_dt),
        (5, w_cv, u_cv, n_cv, c_cv),
        (6, w_cp, u_cp, n_cp, c_cp),
    ):
        for index in range(weight.shape[0]):
            fresh = weight[index] - scales[place] * change[index]
            fresh_ref[index] = fresh
            copy[index] = fresh.astype(bf16)
    parts = [
        (scales[1], stats[4:5, :], mix_spread[0:1, :]),
        (scales[1], stats[0:1, :], stats[1:2, :]),
        (scales[2], stats[2:3, :], stats[3:4, :]),
    ]
    means = [scale * part_mean for scale, part_mean, _ in parts]
    mean = (means[0] + means[1] + means[2]) / 3.0
    spread = jnp.zeros_like(mean)
    for (scale, _, squares), part_mean in zip(parts, means):
        gap = part_mean - mean
        spread = spread + scale * scale * squares + width * gap * gap
    stats_out[0:1, :] = mean
    stats_out[1:2, :] = spread / (3.0 * width)
    for move in moves:
        move.wait()


def join_kernel(pieces, copies, *, need, save):
    total = pieces[0].astype(f32)
    for place in range(1, pieces.shape[0]):
        total = total + pieces[place].astype(f32)
    low = total.astype(bf16)
    for place in range(pieces.shape[0]):
        copies[place] = low


def send_pieces(values, dp):
    chunk = values.shape[0] // dp
    return lax.all_to_all(values, "dp", 0, 0, tiled=True).reshape(dp, chunk, LANES)


def join_pieces(pieces):
    copies = call(join_kernel, at("x", shape(pieces.shape, bf16)), at("x", pieces), limit=8)[0]
    return copies.reshape(-1, LANES)


def call(kernel, outs, args, scratch=(), limit=32, micros=1, passed=(), kept=(), aliases=None):
    given = [array for array, _ in args] + [array for array, _ in passed]
    kinds = [kind for _, kind in args] + ["m"] * len(passed)
    n_own = len(outs)
    outs = list(outs)
    for array, kind in passed:
        dims = array.shape if kind == "h" else (array.shape[0], array.shape[-1])
        outs += at("x", shape(dims, array.dtype))
    outs += at("m", *[shape(given[place].shape, given[place].dtype) for place in kept])
    out_kinds = [kind for _, kind in outs]
    fetched = [place for place, kind in enumerate(kinds) if kind in "h01"]
    stored = [place for place, kind in enumerate(out_kinds) if kind in "h12"]

    def staged(array, kind):
        rows, columns = array.shape[0], array.shape[-1]
        dims = {"h": array.shape, "2": (2, rows, columns)}.get(kind, (rows, columns))
        return pltpu.VMEM(dims, array.dtype)

    staging = [staged(given[place], kinds[place]) for place in fetched]
    staging += [staged(outs[place][0], out_kinds[place]) for place in stored]
    moves = max(1, 2 * len(staging) + len(passed) + len(kept))

    def body(*refs):
        ins = list(refs[: len(given)])
        results = list(refs[len(given) : len(given) + len(outs)])
        rest = refs[len(given) + len(outs) :]
        stage, sems, own = rest[: len(staging)], rest[len(staging)], rest[len(staging) + 1 :]
        loads, saves = {}, {}
        for number, place in enumerate(fetched):
            source = ins[place] if kinds[place] == "h" else ins[place].at[:, int(kinds[place]), :]
            loads[id(stage[number])] = pltpu.make_async_copy(source, stage[number], sems.at[number])
            ins[place] = stage[number]
        for load in loads.values():
            load.start()
        for number, place in enumerate(stored, len(fetched)):
            held, target, kind = stage[number], results[place], out_kinds[place]
            parts = [(held, target)]
            if kind == "1":
                parts = [(held, target.at[:, 1, :])]
            if kind == "2":
                parts = [(held.at[half], target.at[:, half, :]) for half in range(2)]
            saves[id(held)] = [
                pltpu.make_async_copy(*pair, sems.at[moves - 1 - 2 * (number - len(fetched)) - half]) for half, pair in enumerate(parts)
            ]
            results[place] = held
        follow = []
        for number in range(len(passed)):
            held = results[n_own + number]
            source, kind = ins[len(args) + number], passed[number][1]
            source = source if kind == "h" else source.at[:, int(kind), :]
            loads[id(held)] = pltpu.make_async_copy(source, held, sems.at[len(staging) + number])
            follow.append(id(held))
        begun = []
        for number, place in enumerate(kept):
            begun.append(
                pltpu.make_async_copy(
                    ins[place], results[n_own + len(passed) + number],
                    sems.at[len(staging) + len(passed) + number],
                )
            )
            begun[-1].start()

        def need(*wanted):
            keys = [id(ref) for ref in wanted] or list(loads)
            for key in keys:
                if key in loads and key not in follow:
                    loads.pop(key).wait()
            while follow:
                loads[follow.pop(0)].start()
            for key in keys:
                if key in loads:
                    loads.pop(key).wait()

        def save(*ready):
            for key in [id(ref) for ref in ready] or list(saves):
                for move in saves.pop(key, ()):
                    move.start()
                    begun.append(move)

        kernel(*ins[: len(args)], *results[: n_own + len(passed)], *own, need=need, save=save)
        need()
        save()
        for move in begun:
            move.wait()

    spaces = {"x": pltpu.VMEM, "s": pltpu.SMEM}
    placed = [
        pltpu.with_memory_space_constraint(array, pltpu.HBM) if kind in "hm01" else array
        for array, kind in zip(given, kinds)
    ]
    return pl.pallas_call(
        body,
        out_shape=[out if kind == "x" else pltpu.HBM(out.shape, out.dtype) for out, kind in outs],
        in_specs=[pl.BlockSpec(memory_space=spaces.get(kind, pltpu.HBM)) for kind in kinds],
        out_specs=[pl.BlockSpec(memory_space=spaces.get(kind, pltpu.HBM)) for kind in out_kinds],
        input_output_aliases=aliases or {},
        scratch_shapes=[*staging, pltpu.SemaphoreType.DMA((moves,)), *scratch],
        compiler_params=pltpu.CompilerParams(vmem_limit_bytes=limit * MB),
        cost_estimate=pl.CostEstimate(flops=micros * 10**9, bytes_accessed=MB, transcendentals=0),
    )(*placed)


def at(kind, *things):
    return [(thing, kind) for thing in things]


def program(
    dp,
    hidden_in, out_cot, segment_ids,
    norm_gain, in_weight, out_weight, xproj_weight, dtproj_weight, conv_weight, chan_params,
    first_norm_gain, first_in_weight, first_out_weight, first_xproj_weight,
    first_dtproj_weight, first_conv_weight, first_chan_params,
    second_norm_gain, second_in_weight, second_out_weight, second_xproj_weight,
    second_dtproj_weight, second_conv_weight, second_chan_params,
):
    tokens, width = hidden_in.shape
    chans = in_weight.shape[2]
    half_width = first_norm_gain.shape[0]
    tiles = chans // LANES
    rank = dtproj_weight.shape[1]
    count = chan_params.shape[1] - 3
    rows = rank + 2 * count
    taps = conv_weight.shape[1]

    def swap(values):
        return lax.ppermute(values, "chan", [(0, 1), (1, 0)])

    me = lax.axis_index("chan")
    core = me.astype(jnp.int32).reshape(1)
    cot_own = out_cot.T
    cot_far = swap(cot_own)
    moments_own = jnp.stack([first_norm_gain, second_norm_gain])
    moments_far = swap(moments_own)
    moments_gain = jnp.where(
        me == 0,
        jnp.concatenate([moments_own, moments_far], 1),
        jnp.concatenate([moments_far, moments_own], 1),
    )

    def flip(values):
        return jnp.swapaxes(values, 1, 2)

    def turn(values):
        return jnp.swapaxes(values, 0, 1)

    w_xp = flip(xproj_weight)
    w_cp = turn(chan_params)
    square = (tokens, chans)
    z = Sizes(tokens, chans, count, rank)
    smem = at("s", core)

    def padded_rows(amount):
        return -(-amount // (dp * 16)) * 16 * dp

    mixing, gate, conv_pre, part, normed, low_in, same = call(
        front_kernel,
        at("h", shape(square, f32))
        + at(
            "x", shape(square, f32), shape((2,) + square, f32), shape((2 * rows, tokens), f32),
            shape((tokens, width), bf16),
        )
        + at("h", shape((2, width, chans), bf16))
        + at("x", shape((2, tokens, LANES), f32)),
        at("h", hidden_in, norm_gain) + at("0", in_weight) + at("1", in_weight)
        + at("h", segment_ids, conv_weight, w_cp, w_xp),
        [pltpu.VMEM((tokens + 16, chans), f32), pltpu.VMEM((tokens + 16, LANES), f32)],
        limit=14, micros=7,
    )
    part_far = swap(part)
    early_rows = padded_rows(tiles * width + (width // LANES) * chans)
    (
        states, proj, grad_maps, skips, far_step, grad_y, pre_step, inflow_low, gate_low, branch_low, early,
        conv_kept, normed_kept,
    ) = forward_call(
        at("x", part, part_far) + at("h", w_cp, dtproj_weight, cot_own) + at("x", cot_far) + at("h", out_weight)
        + at("x", conv_pre, gate, same, normed) + smem,
        z, early_rows, half_width, (7, 10),
    )
    early_pieces = send_pieces(early, dp)
    grad_part, grad_act, grad_dt, grad_chan = backward_call(
        at("m", states) + at("h", w_cp, proj, far_step, grad_y, inflow_low, pre_step, conv_kept)
        + at("h", grad_maps, skips, dtproj_weight),
        z,
    )
    early_copies, grad_part = lax.optimization_barrier((join_pieces(early_pieces), grad_part))
    early_sums = lax.all_to_all(early_copies, "dp", 0, 0, tiled=True)
    grad_far = swap(grad_part)
    late_rows = padded_rows(tiles * (width + 2 * rows + 2 * rank + 48))
    late, in_own, in_send, out_own, out_send = call(
        back_kernel,
        at("x", shape((late_rows, LANES), bf16))
        + at("h", shape((half_width + 8, tokens), f32))
        + at("x", shape((half_width + 8, tokens), f32))
        + at("h", shape((half_width, tokens), f32))
        + at("x", shape((half_width, tokens), f32)),
        at("x", grad_part, grad_far)
        + at("h", segment_ids, w_xp, conv_weight, mixing, conv_kept) + at("x", grad_act, grad_chan)
        + at("h", normed_kept, gate_low, low_in, hidden_in, norm_gain) + at("x", grad_dt)
        + at("h", branch_low, out_weight)
        + smem,
        [
            pltpu.VMEM((tokens + 16, chans), f32), pltpu.VMEM((2, tokens + 16, chans), f32),
            pltpu.VMEM((tokens + 16, LANES), f32), pltpu.VMEM(square, bf16),
            pltpu.VMEM((48, chans), f32), pltpu.VMEM((2,) + square, bf16),
        ],
        limit=20, micros=2,
    )
    in_far = swap(in_send)
    out_far = swap(out_send)
    late, early_sums = lax.optimization_barrier((late, early_sums))
    late_pieces = send_pieces(late, dp)
    output, input_grad = call(
        outputs_kernel,
        at("h", shape((half_width, tokens), bf16), shape((half_width, tokens), f32)),
        at("h", hidden_in, cot_own, out_own) + at("x", out_far) + at("h", in_own) + at("x", in_far) + smem,
        limit=16, micros=3,
    )
    firsts = [first_xproj_weight, first_dtproj_weight, first_conv_weight, first_chan_params]
    seconds = [second_xproj_weight, second_dtproj_weight, second_conv_weight, second_chan_params]
    for group in (firsts, seconds):
        group[0], group[3] = flip(group[0]), turn(group[3])
    weights = [w_xp, dtproj_weight, conv_weight, w_cp]
    half = shape((width, chans), f32)
    whole_in, whole_out = shape(in_weight.shape, f32), shape(out_weight.shape, f32)
    x_out, y_out, x_in, y_in, u_gate, u_out, early_norms, early_stats = call(
        early_kernel,
        at("h", whole_out, whole_out) + at("1", whole_in, whole_in)
        + at("h", half, whole_out, shape((16, LANES), f32), shape((8, chans), f32)),
        at("x", early_sums) + at("h", out_weight, first_out_weight, second_out_weight)
        + at("1", in_weight, first_in_weight, second_in_weight),
        limit=12, micros=5,
    )
    late_copies, output, input_grad = lax.optimization_barrier((join_pieces(late_pieces), output, input_grad))
    late_sums = lax.all_to_all(late_copies, "dp", 0, 0, tiled=True)
    shapes = [shape(tensor.shape, f32) for tensor in weights]
    late_outs = []
    for entry in shapes:
        late_outs += [entry, entry]
    moments_in = [tensor for pair in zip(firsts, seconds) for tensor in pair]
    got = call(
        late_kernel,
        at("x", half, half) + at("h", *late_outs)
        + at("x", half, *shapes, shape((16, LANES), f32), shape((8, chans), f32)),
        at("x", late_sums) + at("h", early_norms, early_stats, *moments_in)
        + at("0", first_in_weight, second_in_weight),
        limit=12, micros=5,
        passed=at("h", *weights) + at("0", in_weight) + at("1", in_weight) + at("h", out_weight, u_gate, u_out),
    )
    moments, updates, norms, stats, kept = got[:10], got[10:15], got[15], got[16], got[17:]
    kept_small, (kept_mix, kept_gate, kept_out, changed_gate, changed_out) = kept[0:4], kept[4:]
    norms_far = swap(norms)
    mix_spread = call(
        spread_kernel, at("x", shape((8, chans), f32)), at("x", updates[0], stats), limit=8, micros=1
    )[0]
    pairs = []
    for entry in [whole_in, whole_out, *shapes]:
        pairs += [entry, shape(entry.shape, bf16)]
    row = shape((half_width,), f32)
    whole_low = shape(whole_in.shape, bf16)
    done = call(
        apply_kernel,
        at("2", whole_in) + at("h", whole_low)
        + at(
            "h", *pairs[2:], row, row, row, shape((half_width,), bf16), shape((2, 7), f32),
            shape((2, chans), f32),
        )
        + at("m", whole_in, whole_in),
        at("x", norms, norms_far, stats, mix_spread, kept_mix, kept_gate, kept_out, *kept_small, updates[0], changed_gate, changed_out, *updates[1:])
        + at("h", norm_gain) + at("x", moments_gain[0:1], moments_gain[1:2], moments[0], moments[1])
        + smem + at("m", x_in, y_in),
        [pltpu.SemaphoreType.DMA((2,))],
        limit=14, micros=5, aliases={24: 18, 25: 19},
    )
    flat = list(done[12:16])
    firsts_out = [done[18], x_out, *moments[2::2]]
    seconds_out = [done[19], y_out, *moments[3::2]]
    for place in range(6):
        entry = [firsts_out[place], seconds_out[place], done[2 * place], done[2 * place + 1]]
        if place == 2:
            entry = [flip(tensor) for tensor in entry]
        if place == 5:
            entry = [turn(tensor) for tensor in entry]
        flat += entry
    return (output.T, input_grad.T, *flat, done[16].T, done[17])


def solution(mesh):
    rows = P("dp", None)
    cells = P("dp", "chan")
    last = P(None, None, "chan")
    first = P("chan", None)
    middle = P(None, "chan", None)
    tensors = (last, first, middle, last, last, last)
    outs = [cells, cells] + [P("chan")] * 4
    for spec in tensors:
        outs += [spec] * 4
    return jax.shard_map(
        functools.partial(program, mesh.shape["dp"]),
        mesh=mesh,
        in_specs=(rows, cells, P("dp"), P(), *tensors, P("chan"), *tensors, P("chan"), *tensors),
        out_specs=(*outs, P(), P(None, "chan")),
        check_vma=False,
    )
```

```python
import functools

import jax
import jax.numpy as jnp
from jax import lax
from jax.experimental import pallas as pl
from jax.experimental.pallas import tpu as pltpu
from jax.sharding import PartitionSpec as P

STEP = 4
norm_eps = 1e-06
beta_one = 0.5
beta_two = 0.5
adam_eps = 1e-06
decay_rate = 0.01
learn_rate = 0.3
LOG2E = 1.4426950408889634
FAR = 1e30
FLOOR = -1e-26

f32 = jnp.float32
bf16 = jnp.bfloat16
HIGH = lax.Precision.HIGHEST
LANES = 128
ROWS = 16
NORM_ROWS = 192
CONV_ROWS = 96
LAMB_ROWS = 32
MB = 1 << 20


def dot(left, right, dims, precision=None):
    return lax.dot_general(
        left, right, (dims, ((), ())), precision=precision, preferred_element_type=f32
    )


NN = ((1,), (0,))
TN = ((0,), (0,))
NT = ((1,), (1,))


def sigmoid(values):
    return lax.logistic(values)


def silu_slope(values, sigma):
    return sigma * (1.0 + values * (1.0 - sigma))


def softplus(values):
    return jnp.maximum(values, 0.0) + jnp.log1p(jnp.exp(-jnp.abs(values)))


def wide(tile, times):
    return jnp.concatenate([tile] * times, axis=1)


def fold(values):
    total = values[0:8]
    for start in range(8, values.shape[0], 8):
        total = total + values[start : start + 8]
    return total


def shape(dims, dtype):
    return jax.ShapeDtypeStruct(dims, dtype)


def each_rows(length, body, carry=None, rows=ROWS):
    def step(index, held):
        return body(pl.multiple_of(index * rows, rows), held)

    return lax.fori_loop(0, length // rows, step, carry)


def spread_segments(numbers, tokens):
    across = lax.broadcasted_iota(jnp.int32, (tokens, tokens), 0)
    along = lax.broadcasted_iota(jnp.int32, (tokens, tokens), 1)
    row = numbers.astype(f32).reshape(1, tokens)
    picked = jnp.where(across == along, row, 0.0).astype(bf16)
    return dot(picked, jnp.ones((tokens, LANES), bf16), NN)


def front_kernel(
    hid, gain, w_mix, w_gate, seg, taps, w_xp,
    mix_out, gate_out, conv_out, part_out, norm_out, low_out, same_out, params, near_dt, near_cot,
    padded, sgpad,
    *, need, save,
):
    tokens, width = hid.shape
    chans = mix_out.shape[1]
    tiles = chans // LANES

    need(hid, gain)
    gain_row = gain[...].reshape(1, width)

    def normalise(start, held):
        source = hid[pl.ds(start, NORM_ROWS), :].astype(f32)
        scale = lax.rsqrt(jnp.sum(source * source, axis=1, keepdims=True) / width + norm_eps)
        norm_out[pl.ds(start, NORM_ROWS), :] = (source * scale * gain_row).astype(bf16)
        return held

    each_rows(tokens, normalise, 0, NORM_ROWS)
    save(norm_out)
    need(w_mix, w_gate)
    low_out[0] = w_mix[...].astype(bf16)
    low_out[1] = w_gate[...].astype(bf16)
    save(low_out)
    normed = norm_out[...]
    mixing = dot(normed, low_out[0], NN)
    mix_out[...] = mixing
    padded[0:8, :] = jnp.zeros((8, chans), f32)
    padded[pl.ds(8, tokens), :] = mixing
    padded[pl.ds(8 + tokens, 8), :] = jnp.zeros((8, chans), f32)
    save(mix_out)
    gate_out[...] = dot(normed, low_out[1], NN)
    need(seg, taps, w_xp, params)
    numbers = spread_segments(seg[...], tokens)
    sgpad[0:8, :] = jnp.full((8, LANES), -1.0, f32)
    sgpad[pl.ds(8, tokens), :] = numbers
    sgpad[pl.ds(8 + tokens, 8), :] = jnp.full((8, LANES), -1.0, f32)
    width_taps = taps.shape[1]

    def convolve(start, held):
        window = padded[pl.ds(start, CONV_ROWS + 16), :]
        marks = sgpad[pl.ds(start, CONV_ROWS + 16), :]
        own = marks[8 : 8 + CONV_ROWS]
        base = window[8 : 8 + CONV_ROWS]
        for heading in range(2):
            total = params[0, heading : heading + 1, :] + taps[heading, 0:1, :] * base
            for offset in range(1, width_taps):
                begin = 8 - offset if heading == 0 else 8 + offset
                same = jnp.where(marks[begin : begin + CONV_ROWS] == own, 1.0, 0.0)
                if offset == 1:
                    same_out[heading, pl.ds(start, CONV_ROWS), :] = same
                moved = window[begin : begin + CONV_ROWS]
                total = total + taps[heading, offset : offset + 1, :] * moved * wide(same, tiles)
            conv_out[heading, pl.ds(start, CONV_ROWS), :] = total
        return held

    each_rows(tokens, convolve, 0, CONV_ROWS)
    for heading in range(2):
        pre = conv_out[heading]
        act_low = (pre * sigmoid(pre)).astype(bf16)
        rows = w_xp.shape[1]
        part_out[heading * rows : (heading + 1) * rows, :] = dot(
            w_xp[heading].astype(bf16), act_low, NT
        )


SPAN = 128


class Sizes:
    def __init__(self, tokens, chans, count, rank):
        self.tokens, self.chans, self.count, self.rank = tokens, chans, count, rank
        self.tiles = chans // LANES
        self.blocks = tokens // LANES
        self.rows = rank + 2 * count
        self.block_rows = LANES * count
        self.pairs = [(heading, tile) for heading in range(2) for tile in range(self.tiles)]

    def base(self, heading, tile):
        return (heading * self.tiles + tile) * self.tokens

    def row(self, ref, heading, tile, at):
        return ref[pl.ds(self.base(heading, tile) + at, 1), :]

    def whole(self, ref, heading):
        starts = [self.base(heading, tile) for tile in range(self.tiles)]
        return jnp.concatenate([ref[start : start + self.tokens, :] for start in starts], axis=1)


def cols(tile):
    return slice(tile * LANES, (tile + 1) * LANES)


def split(values):
    high = values.astype(bf16)
    return high, (values - high.astype(f32)).astype(bf16)


def group_maps(target, tile, heading, count):
    groups = tile.shape[1] // count
    for group in range(groups):
        block, place = divmod(group * count, LANES)
        own = tile[:, cols(block)]
        if place:
            own = pltpu.roll(own, LANES - place, 1)
        target[heading, group] = own


def diagonal_maps(target, tile, heading, count):
    tokens = tile.shape[1]
    squared = count * count
    lane = lax.broadcasted_iota(jnp.int32, (count, squared), 1)
    row = lax.broadcasted_iota(jnp.int32, (count, squared), 0)
    repeat = jnp.where(lane % count == row, 1.0, 0.0).astype(bf16)
    token = lax.broadcasted_iota(jnp.int32, (tokens, squared), 0)
    place = lax.broadcasted_iota(jnp.int32, (tokens, squared), 1)
    mine = place // count == token % count
    for number, part in enumerate(split(tile)):
        spread = jnp.where(mine, dot(part, repeat, TN), 0.0).astype(bf16)
        target[heading, :, number] = spread.reshape(tokens // count, count, squared)


def weigh_states(left, maps):
    half = maps.shape[0] // 2
    got = dot(maps, left, NN)
    return got[:half] + got[half:]


def gather_states(left, right, count):
    products = dot(left, right, NT)
    lane = lax.broadcasted_iota(jnp.int32, (count, count), 1)
    total = products[0:count]
    for place in range(1, count):
        total = jnp.where(lane == place, products[place * count : (place + 1) * count], total)
    return total


def dot3(left, right, dims):
    (left_high, left_low), (right_high, right_low) = split(left), split(right)
    if dims == TN:
        lefts = jnp.concatenate([left_high, left_low, left_high], axis=0)
        return dot(lefts, jnp.concatenate([right_high, right_high, right_low], axis=0), dims)
    rows = left.shape[0]
    both = dot(jnp.concatenate([left_high, left_low], axis=0), right_high, dims)
    return both[:rows] + both[rows:] + dot(left_high, right_low, dims)


class Sweep:
    def __init__(self, z, turned):
        self.z, self.turned = z, turned
        self.groups = z.tokens // z.count
        self.stage_groups = self.groups // z.blocks

    def group(self, order, heading):
        return self.groups - 1 - order if heading == self.turned else order

    def block(self, stage, heading):
        return self.z.blocks - 1 - stage if heading == self.turned else stage

    def inner(self, ahead, heading):
        return self.z.count - 1 - ahead if heading == self.turned else ahead

    def rows(self, group):
        return pl.ds(pl.multiple_of(group * self.z.count, self.z.count), self.z.count)

    def run(self, z, carried, scan, post, between):
        def step(index, held):
            order = 2 * index
            post(jnp.maximum(order - 1, 0), 1)
            held = scan(order, held, 0)
            post(order, 0)
            return scan(order + 1, held, 1)

        per = self.stage_groups // 2
        for stage in range(z.blocks):
            between(stage, True)
            carried = lax.fori_loop(stage * per, (stage + 1) * per, step, carried)
            between(stage, False)
        post(self.groups - 1, 1)
        return carried


def store_gathered(target, target_row, gathered, heading, z):
    per = LANES // z.count
    for block in range(z.blocks):
        pieces = [gathered[heading, block * per + place] for place in range(per)]
        target[target_row : target_row + z.count, cols(block)] = jnp.concatenate(pieces, axis=1)


def fill_rates(rates, params, count):
    for heading in range(2):
        for n in range(count):
            value = -jnp.exp(params[3 + n, heading : heading + 1, :])
            rates[heading, n : n + 1, :] = jnp.minimum(value, FLOOR)


def forward_kernel(
    own_part, far_part, params, w_dt, cot_own, cot_far, w_out, conv_pre, gate, same, normed, core,
    states_out, proj, grad_maps, skips, far_step, grad_y, pre_step, inflow_low, gate_low, branch_low, early,
    grad_branch, inflow, grad_y_low, act, result, maps, diagonal, gathered, states, low_one, low_two,
    rates, sems,
    *, need, save,
):
    tokens, chans = gate.shape
    z = Sizes(tokens, chans, params.shape[0] - 3, w_dt.shape[1])
    count, rank, rows, tiles = z.count, z.rank, z.rows, z.tiles
    half_width = cot_own.shape[0]
    width = 2 * half_width
    me = core[0]
    sweep = Sweep(z, 1)
    lows = (low_one, low_two)

    proj[...] = own_part[...] + far_part[...]
    save(proj)
    for heading in range(2):
        first = heading * rows + rank
        group_maps(maps, proj[first : first + count, :], heading, count)
        diagonal_maps(diagonal, proj[first + count : first + 2 * count, :], heading, count)
    for tile in range(tiles):

        def activate(start, held, tile=tile):
            here = pl.ds(start, SPAN)
            for heading in range(2):
                pre = conv_pre[heading, here, cols(tile)]
                act[heading, here, cols(tile)] = pre * sigmoid(pre)
            return held

        each_rows(tokens, activate, 0, SPAN)
    need(params, w_dt)
    fill_rates(rates, params, count)
    for heading in range(2):
        pre_step[heading] = (
            dot3(proj[heading * rows : heading * rows + rank, :], w_dt[heading], TN)
            + params[1, heading : heading + 1, :]
        )
    save(pre_step)
    need(w_out, cot_own)
    low_out = w_out[...].astype(bf16)
    low_cot = jnp.where(
        me == 0,
        jnp.concatenate([cot_own[...].astype(f32), cot_far[...].astype(f32)], 0),
        jnp.concatenate([cot_far[...].astype(f32), cot_own[...].astype(f32)], 0),
    ).astype(bf16)
    grad_branch[...] = dot(low_cot, low_out, ((0,), (1,)))

    for tile in range(tiles):

        def prepare(start, held, tile=tile):
            here = pl.ds(start, SPAN)
            for heading in range(2):
                size = softplus(pre_step[heading, here, cols(tile)])
                there = pl.ds(z.base(heading, tile) + start, SPAN)
                entering = size * act[heading, here, cols(tile)]
                inflow[there, :] = entering
                inflow_low[heading, here, cols(tile)] = entering.astype(bf16)
                far_step[there, :] = jnp.where(same[heading, here, :] > 0.5, size * LOG2E, FAR)
            gated = gate[here, cols(tile)]
            back = grad_branch[here, cols(tile)] * (gated * sigmoid(gated))
            grad_y[pl.ds(z.base(0, tile) + start, SPAN), :] = back
            grad_y_low[here, cols(tile)] = back.astype(bf16)
            return held

        each_rows(tokens, prepare, 0, SPAN)
    save(far_step, inflow_low, grad_y)

    blank = jnp.zeros((count, LANES), f32)
    states[0, 0:count, :] = jnp.zeros((count, chans), bf16)
    states[1, tokens * count : (tokens + 1) * count, :] = jnp.zeros((count, chans), bf16)
    low_two[...] = jnp.zeros(low_two.shape, bf16)
    speeds = [rates[heading, :, cols(tile)] for heading, tile in z.pairs]

    def scan(order, carried, slot):
        carried = list(carried)
        enters = [maps[heading, sweep.group(order, heading)] for heading in range(2)]
        for heading in range(2):
            for ahead in range(count):
                inner = sweep.inner(ahead, heading)
                at = sweep.group(order, heading) * count + inner
                kept = pl.multiple_of((at + (1 if heading == 0 else 0)) * count, count)
                enter = jnp.broadcast_to(enters[heading][:, inner : inner + 1], (count, LANES))
                for tile in range(tiles):
                    number = heading * tiles + tile
                    decay = jnp.exp2(z.row(far_step, heading, tile, at) * speeds[number])
                    state = decay * carried[number] + enter * z.row(inflow, heading, tile, at)
                    carried[number] = state
                    low = state.astype(bf16)
                    states[heading, pl.ds(kept, count), cols(tile)] = low
                    lows[slot][heading, inner * count : (inner + 1) * count, cols(tile)] = low
        return tuple(carried)

    def post(order, slot):
        for heading in range(2):
            group = sweep.group(order, heading)
            left = lows[slot][heading]
            gathered[heading, group] = gather_states(left, grad_y_low[sweep.rows(group), :], count)
            result[heading, sweep.rows(group), :] = weigh_states(
                left, diagonal[heading, group].reshape(2 * count, count * count)
            )

    keeps = []

    def between(stage, before):
        if before:
            return
        for heading in range(2):
            begin, extent = sweep.block(stage, heading) * z.block_rows, z.block_rows
            if stage == 0:
                extent += count
            elif heading == 0:
                begin += count
            piece = pl.ds(begin, extent)
            keep = pltpu.make_async_copy(
                states.at[heading, piece, :], states_out.at[heading, piece, :], sems.at[heading, stage]
            )
            keep.start()
            keeps.append(keep)

    sweep.run(z, (blank,) * len(z.pairs), scan, post, between)
    for heading in range(2):
        store_gathered(grad_maps, heading * count, gathered, heading, z)
    skips[...] = jnp.zeros(skips.shape, f32)
    for tile in range(tiles):

        def finish(start, held, tile=tile):
            here = pl.ds(start, SPAN)
            total = jnp.zeros((SPAN, LANES), f32)
            sums = []
            back = grad_y[pl.ds(z.base(0, tile) + start, SPAN), :]
            for heading in range(2):
                active = act[heading, here, cols(tile)]
                total = total + result[heading, here, cols(tile)]
                total = total + params[2, heading : heading + 1, cols(tile)] * active
                sums.append(held[heading] + fold(back * active))
            gated = gate[here, cols(tile)]
            sigma = sigmoid(gated)
            branch_low[here, cols(tile)] = (total * (gated * sigma)).astype(bf16)
            gate_low[here, cols(tile)] = (
                grad_branch[here, cols(tile)] * total * silu_slope(gated, sigma)
            ).astype(bf16)
            return tuple(sums)

        sums = each_rows(tokens, finish, (jnp.zeros((8, LANES), f32),) * 2, SPAN)
        for heading in range(2):
            skips[heading : heading + 1, cols(tile)] = jnp.sum(sums[heading], axis=0, keepdims=True)
    save(gate_low, branch_low, grad_maps, skips)
    need()
    branch = branch_low[...]
    grad_w = dot(branch, low_cot, ((0,), (1,))).astype(bf16)
    for tile in range(width // LANES):
        early[tile * chans : (tile + 1) * chans, :] = grad_w[:, cols(tile)]
    base_row = chans * (width // LANES)
    grad_w = dot(normed[...], gate_low[...], TN).astype(bf16)
    for tile in range(tiles):
        early[base_row + tile * width : base_row + (tile + 1) * width, :] = grad_w[:, cols(tile)]
    base_row += tiles * width
    if early.shape[0] > base_row:
        early[base_row:, :] = jnp.zeros((early.shape[0] - base_row, LANES), bf16)
    for keep in keeps:
        keep.wait()


def backward_kernel(
    states_in, params, proj, far_step, grad_y, inflow_low, pre_step, conv_pre, grad_maps, skips, w_dt,
    grad_part, grad_act, grad_dt, grad_chan,
    result, decayed, maps, diagonal, gathered, states, low_one, low_two, products_one, products_two, rates, sems,
    *, need, save,
):
    _, tokens, chans = conv_pre.shape
    z = Sizes(tokens, chans, params.shape[0] - 3, w_dt.shape[1])
    count, rank, rows, tiles = z.count, z.rank, z.rows, z.tiles
    sweep = Sweep(z, 0)
    lows, products = (low_one, low_two), (products_one, products_two)
    loads = {}
    for stage in range(z.blocks):
        for heading in range(2):
            begin = sweep.block(stage, heading) * z.block_rows + (count if heading == 1 else 0)
            piece = pl.ds(begin, z.block_rows)
            load = pltpu.make_async_copy(
                states_in.at[heading, piece, :], states.at[heading, piece, :], sems.at[heading, stage]
            )
            load.start()
            loads[stage, heading] = load
    need(params, proj)
    fill_rates(rates, params, count)
    for heading in range(2):
        first = heading * rows + rank
        group_maps(maps, proj[first + count : first + 2 * count, :], heading, count)
        diagonal_maps(diagonal, proj[first : first + count, :], heading, count)
    for low in (low_two, products_two):
        low[...] = jnp.zeros(low.shape, bf16)
    blank = jnp.zeros((count, LANES), f32)
    speeds = [rates[heading, :, cols(tile)] for heading, tile in z.pairs]

    def scan(order, held, slot):
        waiting = list(held[: len(z.pairs)])
        totals = list(held[len(z.pairs) :])
        leaves = [maps[heading, sweep.group(order, heading)] for heading in range(2)]
        for heading in range(2):
            for ahead in range(count):
                inner = sweep.inner(ahead, heading)
                at = sweep.group(order, heading) * count + inner
                prior = pl.multiple_of((at + (0 if heading == 0 else 1)) * count, count)
                leave = jnp.broadcast_to(leaves[heading][:, inner : inner + 1], (count, LANES))
                here = slice(inner * count, (inner + 1) * count)
                for tile in range(tiles):
                    number = heading * tiles + tile
                    size = z.row(far_step, heading, tile, at)
                    decay = jnp.exp2(size * speeds[number])
                    grad = leave * z.row(grad_y, 0, tile, at) + waiting[number]
                    lead = decay * grad
                    waiting[number] = lead
                    slope = lead * states[heading, pl.ds(prior, count), cols(tile)].astype(f32)
                    totals[number] = totals[number] + slope * size
                    products[slot][heading, here, cols(tile)] = (slope * speeds[number]).astype(bf16)
                    lows[slot][heading, here, cols(tile)] = grad.astype(bf16)
        return tuple(waiting + totals)

    lane = lax.broadcasted_iota(jnp.int32, (count, count * count), 1)
    row = lax.broadcasted_iota(jnp.int32, (count, count * count), 0)
    ones = jnp.where(lane // count == row, 1.0, 0.0).astype(bf16)

    def post(order, slot):
        for heading in range(2):
            group = sweep.group(order, heading)
            left = lows[slot][heading]
            gathered[heading, group] = gather_states(left, inflow_low[heading, sweep.rows(group), :], count)
            result[heading, sweep.rows(group), :] = weigh_states(
                left, diagonal[heading, group].reshape(2 * count, count * count)
            )
            decayed[heading, sweep.rows(group), :] = dot(ones, products[slot][heading], NN)

    def between(stage, before):
        if before:
            if stage == 0:
                need(far_step, grad_y, inflow_low)
            for heading in range(2):
                loads[stage, heading].wait()

    held = sweep.run(z, (blank,) * (2 * len(z.pairs)), scan, post, between)
    for number, (heading, tile) in enumerate(z.pairs):
        slopes = held[len(z.pairs) + number] / LOG2E
        for n in range(count):
            grad_chan[3 + n, heading : heading + 1, cols(tile)] = slopes[n : n + 1] * -jnp.exp(
                params[3 + n, heading : heading + 1, cols(tile)]
            )
    need()
    for heading in range(2):
        first = heading * rows + rank
        store_gathered(grad_part, first, gathered, heading, z)
        grad_part[first + count : first + 2 * count, :] = grad_maps[
            heading * count : (heading + 1) * count, :
        ]

    for tile in range(tiles):

        def close(start, held, tile=tile):
            here = pl.ds(start, SPAN)
            sums = []
            back = grad_y[pl.ds(z.base(0, tile) + start, SPAN), :]
            for heading in range(2):
                pre = conv_pre[heading, here, cols(tile)]
                act = pre * sigmoid(pre)
                passed = result[heading, here, cols(tile)]
                reach = pre_step[heading, here, cols(tile)]
                grad_act[heading, here, cols(tile)] = (
                    passed * softplus(reach) + back * params[2, heading : heading + 1, cols(tile)]
                )
                grad_pre = (decayed[heading, here, cols(tile)] + passed * act) * sigmoid(reach)
                pre_step[heading, here, cols(tile)] = grad_pre
                sums.append(held[heading] + fold(grad_pre))
            return tuple(sums)

        biases = each_rows(tokens, close, (jnp.zeros((8, LANES), f32),) * 2, SPAN)
        for heading in range(2):
            grad_chan[1, heading : heading + 1, cols(tile)] = jnp.sum(
                biases[heading], axis=0, keepdims=True
            )
    save(grad_act)
    for heading in range(2):
        grad_chan[0, heading : heading + 1, :] = jnp.zeros((1, chans), f32)
        grad_chan[2, heading : heading + 1, :] = skips[heading : heading + 1, :]
        grad_pre = pre_step[heading]
        grad_part[heading * rows : heading * rows + rank, :] = dot3(w_dt[heading], grad_pre, NT)
        grad_dt[heading] = dot3(proj[heading * rows : heading * rows + rank, :], grad_pre, NN)


def forward_call(args, sizes, early_rows, half_width, kept, limit=30):
    z = sizes
    square = (z.tokens, z.chans)
    both = (2,) + square
    flat = (2 * z.tiles * z.tokens, LANES)
    groups = z.tokens // z.count
    squared = z.count * z.count
    states = (2, (z.tokens + 1) * z.count, z.chans)
    slot = pltpu.VMEM((2, squared, z.chans), bf16)
    return call(
        forward_kernel,
        at("m", shape(states, bf16))
        + at(
            "h", shape((2 * z.rows, z.tokens), f32), shape((2 * z.count, z.tokens), f32), shape((8, z.chans), f32),
            shape(flat, f32), shape((z.tiles * z.tokens, LANES), f32), shape(both, f32), shape(both, bf16),
            shape(square, bf16), shape(square, bf16),
        )
        + at("x", shape((early_rows, LANES), bf16)),
        args,
        [
            pltpu.VMEM(square, f32), pltpu.VMEM(flat, f32), pltpu.VMEM(square, bf16), pltpu.VMEM(both, f32),
            pltpu.VMEM(both, f32), pltpu.VMEM((2, groups, z.count, LANES), f32),
            pltpu.VMEM((2, groups, 2, z.count, squared), bf16), pltpu.VMEM((2, groups, z.count, z.count), f32),
            pltpu.VMEM(states, bf16), slot, slot, pltpu.VMEM((2, z.count, z.chans), f32),
            pltpu.SemaphoreType.DMA((2, z.blocks)),
        ],
        limit=limit, micros=15, kept=kept,
    )


def backward_call(args, sizes, limit=30):
    z = sizes
    square = (z.tokens, z.chans)
    both = (2,) + square
    groups = z.tokens // z.count
    squared = z.count * z.count
    slot = pltpu.VMEM((2, squared, z.chans), bf16)
    return call(
        backward_kernel,
        at(
            "x", shape((2 * z.rows, z.tokens), f32), shape(both, f32), shape((2, z.rank, z.chans), f32),
            shape((3 + z.count, 2, z.chans), f32),
        ),
        args,
        [
            pltpu.VMEM(both, f32), pltpu.VMEM(both, f32), pltpu.VMEM((2, groups, z.count, LANES), f32),
            pltpu.VMEM((2, groups, 2, z.count, squared), bf16), pltpu.VMEM((2, groups, z.count, z.count), f32),
            pltpu.VMEM((2, (z.tokens + 1) * z.count, z.chans), bf16), slot, slot, slot, slot,
            pltpu.VMEM((2, z.count, z.chans), f32), pltpu.SemaphoreType.DMA((2, z.blocks)),
        ],
        limit=limit, micros=15,
    )


def back_kernel(
    own_part, far_part, seg, w_xp, taps, mixing, conv_pre, grad_act, grad_chan, normed, gate_low,
    low_in, hid, gain, grad_dt, branch, w_out, core,
    sums_out, in_own, in_far, out_own, out_far,
    padded, gpad, sgpad, mixed_low, small, act_low,
    *, need, save,
):
    tokens, width = hid.shape
    chans = mixing.shape[1]
    tiles = chans // LANES
    rows = w_xp.shape[1]
    width_taps = taps.shape[1]
    me = core[0]
    half_width = in_own.shape[0] - 8
    edge = jnp.zeros((8, chans), f32)
    padded[0:8, :] = edge
    padded[pl.ds(8 + tokens, 8), :] = edge
    gpad[0, 0:8, :] = edge
    gpad[1, 0:8, :] = edge
    gpad[0, pl.ds(8 + tokens, 8), :] = edge
    gpad[1, pl.ds(8 + tokens, 8), :] = edge
    sgpad[0:8, :] = jnp.full((8, LANES), -1.0, f32)
    sgpad[pl.ds(8 + tokens, 8), :] = jnp.full((8, LANES), -1.0, f32)
    need(seg, w_xp, mixing)
    padded[pl.ds(8, tokens), :] = mixing[...]
    sgpad[pl.ds(8, tokens), :] = spread_segments(seg[...], tokens)

    parts = (own_part[...] + far_part[...]).astype(bf16)
    for heading in range(2):
        part = parts[heading * rows : (heading + 1) * rows, :]
        gpad[heading, pl.ds(8, tokens), :] = dot(part, w_xp[heading].astype(bf16), TN)

    blank = jnp.zeros((8, chans), f32)
    need(taps, conv_pre, grad_act, grad_chan)

    def through_conv(start, held):
        here = pl.ds(start, CONV_ROWS)
        window = padded[pl.ds(start, CONV_ROWS + 16), :]
        marks = sgpad[pl.ds(start, CONV_ROWS + 16), :]
        own = marks[8 : 8 + CONV_ROWS]
        base = window[8 : 8 + CONV_ROWS]
        sums = []
        for heading in range(2):
            pre = conv_pre[heading, here, :]
            sigma = sigmoid(pre)
            act_low[heading, here, :] = (pre * sigma).astype(bf16)
            inside = pl.ds(pl.multiple_of(start + 8, 8), CONV_ROWS)
            grad = (gpad[heading, inside, :] + grad_act[heading, here, :]) * silu_slope(pre, sigma)
            gpad[heading, inside, :] = grad
            sums.append(held[5 * heading] + fold(grad))
            sums.append(held[5 * heading + 1] + fold(grad * base))
            for offset in range(1, width_taps):
                begin = 8 - offset if heading == 0 else 8 + offset
                kept = jnp.where(marks[begin : begin + CONV_ROWS] == own, 1.0, 0.0)
                moved = window[begin : begin + CONV_ROWS]
                sums.append(held[5 * heading + 1 + offset] + fold(grad * moved * wide(kept, tiles)))
        return tuple(sums)

    sums = each_rows(tokens, through_conv, (blank,) * 10, CONV_ROWS)
    small[...] = jnp.zeros(small.shape, f32)
    for heading in range(2):
        bias = jnp.sum(sums[5 * heading], axis=0, keepdims=True)
        for offset in range(width_taps):
            row = heading * width_taps + offset
            small[row : row + 1, :] = jnp.sum(sums[5 * heading + 1 + offset], axis=0, keepdims=True)
        for entry in range(grad_chan.shape[0]):
            row = 2 * width_taps + 2 * entry + heading
            small[row : row + 1, :] = (
                bias
                if entry == 0
                else grad_chan[entry, heading : heading + 1, :]
            )

    def mixed(start, held):
        here = pl.ds(start, CONV_ROWS)
        marks = sgpad[pl.ds(start, CONV_ROWS + 16), :]
        own = marks[8 : 8 + CONV_ROWS]
        total = jnp.zeros((CONV_ROWS, chans), f32)
        for heading in range(2):
            window = gpad[heading, pl.ds(start, CONV_ROWS + 16), :]
            total = total + window[8 : 8 + CONV_ROWS] * taps[heading, 0:1, :]
            for offset in range(1, width_taps):
                begin = 8 + offset if heading == 0 else 8 - offset
                kept = jnp.where(marks[begin : begin + CONV_ROWS] == own, 1.0, 0.0)
                total = total + window[begin : begin + CONV_ROWS] * wide(kept, tiles) * taps[
                    heading, offset : offset + 1, :
                ]
        mixed_low[here, :] = total.astype(bf16)
        return held

    each_rows(tokens, mixed, 0, CONV_ROWS)

    base_row = 0

    def put(values):
        nonlocal base_row
        for tile in range(values.shape[1] // LANES):
            sums_out[base_row : base_row + values.shape[0], :] = values[
                :, tile * LANES : (tile + 1) * LANES
            ].astype(bf16)
            base_row += values.shape[0]

    need()
    partial = dot(mixed_low[...], low_in[0], NT) + dot(gate_low[...], low_in[1], NT)
    padded[pl.ds(8, tokens), :] = partial

    gain_row = gain[...].reshape(1, width)

    def gains(start, held):
        here = pl.ds(start, NORM_ROWS)
        source = hid[here, :].astype(f32)
        scale = lax.rsqrt(jnp.sum(source * source, axis=1, keepdims=True) / width + norm_eps)
        inside = pl.ds(pl.multiple_of(start + 8, 8), NORM_ROWS)
        grad = padded[inside, :]
        padded[inside, :] = grad * gain_row
        return held + fold(grad * source * scale)

    gain_sum = each_rows(tokens, gains, jnp.zeros((8, width), f32), NORM_ROWS)
    small[46:47, :] = jnp.sum(gain_sum, axis=0, keepdims=True)
    weighted = padded[pl.ds(8, tokens), :]
    products = weighted * hid[...].astype(f32)
    turned = weighted.T
    row_dot = dot(jnp.ones((8, width), f32), products, NT, HIGH)
    in_own[0:half_width, :] = jnp.where(me == 0, turned[:half_width], turned[half_width:])
    in_far[0:half_width, :] = jnp.where(me == 0, turned[half_width:], turned[:half_width])
    in_own[pl.ds(half_width, 8), :] = row_dot
    in_far[pl.ds(half_width, 8), :] = row_dot
    save(in_own)
    sent = dot(w_out[...].astype(bf16), branch[...], ((0,), (1,)))
    out_own[...] = jnp.where(me == 0, sent[:half_width], sent[half_width:])
    out_far[...] = jnp.where(me == 0, sent[half_width:], sent[:half_width])
    save(out_own)
    put(dot(normed[...], mixed_low[...], TN))
    put(
        jnp.concatenate(
            [
                dot(parts[heading * rows : (heading + 1) * rows, :], act_low[heading], NN)
                for heading in range(2)
            ],
            axis=0,
        )
    )
    put(jnp.concatenate([grad_dt[0], grad_dt[1]], axis=0))

    put(small[...])
    sums_out[base_row:, :] = jnp.zeros((sums_out.shape[0] - base_row, LANES), bf16)


def outputs_kernel(hid, cot_own, out_own, out_far, in_own, in_far, core, output, input_grad, *, need, save):
    width = hid.shape[1]
    half_width = cot_own.shape[0]
    me = core[0]
    need()
    source = hid[...].astype(f32).T
    scale = lax.rsqrt(jnp.sum(source * source, axis=0, keepdims=True) / width + norm_eps)
    own = jnp.where(me == 0, source[:half_width], source[half_width:])
    output[...] = (own + (out_own[...] + out_far[...])).astype(bf16)
    weighted = in_own[0:half_width, :] + in_far[0:half_width, :]
    save(output)
    row_dot = in_own[half_width : half_width + 1, :] + in_far[half_width : half_width + 1, :]
    input_grad[...] = (
        cot_own[...].astype(f32)
        + scale * weighted
        - own * (scale * scale * scale) * (row_dot / width)
    )


def lamb_moments(weight, grad, first, second):
    first_new = beta_one * first + (1.0 - beta_one) * grad
    second_new = beta_two * second + (1.0 - beta_two) * grad * grad
    root = jnp.sqrt(second_new * (1.0 / (1.0 - beta_two**STEP)))
    update = first_new * (1.0 / (1.0 - beta_one**STEP)) / (root + adam_eps) + decay_rate * weight
    return (first_new, second_new, update)


def rows_sum(values):
    return jnp.sum(values, axis=0, keepdims=True)


def lanes_sum(values):
    total = rows_sum(values)
    lanes = total[:, 0:LANES]
    for tile in range(1, values.shape[1] // LANES):
        lanes = lanes + total[:, cols(tile)]
    return lanes


def fetch(sums, base, stride, start, count, number):
    return jnp.concatenate(
        [sums[pl.ds(base + tile * stride + start, count), :].astype(f32) for tile in range(number)], axis=1
    )


def spread_of(update, mean, length):
    def step(start, kept):
        away = update[pl.ds(start, LAMB_ROWS), :] - mean
        return kept + fold(away * away)

    return rows_sum(each_rows(length, step, jnp.zeros((8, update.shape[1]), f32), LAMB_ROWS))


def half_update(sums, base, stride, weights, a_ref, b_ref, x_ref, y_ref, u_ref):
    length, chans = weights.shape
    zero = jnp.zeros((8, chans), f32)

    def step(start, kept):
        here = pl.ds(start, LAMB_ROWS)
        grad = fetch(sums, base, stride, start, LAMB_ROWS, chans // LANES)
        weight = weights[here, :]
        first, second, update = lamb_moments(weight, grad, a_ref[here, :], b_ref[here, :])
        x_ref[here, :] = first
        y_ref[here, :] = second
        u_ref[here, :] = update
        return (
            kept[0] + fold(weight * weight), kept[1] + fold(update * update), kept[2] + fold(update)
        )

    return each_rows(length, step, (zero, zero, zero), LAMB_ROWS)


def early_kernel(
    sums, w_out, a_out, b_out, w_gate, a_gate, b_gate,
    x_out, y_out, x_gate, y_gate, u_gate, u_out, norms, stats,
    *, need, save,
):
    width, chans = w_gate.shape
    tiles = width // LANES
    norms[...] = jnp.zeros(norms.shape, f32)
    zero = jnp.zeros((8, width), f32)
    need(w_out, a_out, b_out)

    def one_out(start, kept):
        here = pl.ds(start, LAMB_ROWS)
        grad = fetch(sums, 0, chans, start, LAMB_ROWS, tiles)
        weight = w_out[here, :]
        first, second, update = lamb_moments(weight, grad, a_out[here, :], b_out[here, :])
        x_out[here, :] = first
        y_out[here, :] = second
        u_out[here, :] = update
        return (kept[0] + fold(weight * weight), kept[1] + fold(update * update))

    weight_sq, update_sq = each_rows(chans, one_out, (zero, zero), LAMB_ROWS)
    norms[1:2, :] = lanes_sum(weight_sq)
    norms[7:8, :] = lanes_sum(update_sq)
    save(x_out, y_out, u_out)
    need()
    weight_sq, update_sq, total = half_update(
        sums, chans * tiles, width, w_gate, a_gate, b_gate, x_gate, y_gate, u_gate
    )
    norms[0:1, :] = lanes_sum(weight_sq)
    norms[6:7, :] = lanes_sum(update_sq)
    save(x_gate, y_gate, u_gate)
    gate_mean = rows_sum(total) / width
    stats[0:1, :] = gate_mean
    stats[1:2, :] = spread_of(u_gate, gate_mean, width)
    ones = jnp.ones((8, width), f32)
    out_all = u_out[...]
    out_mean = jnp.sum(out_all, axis=1, keepdims=True) / width
    away = out_all - out_mean
    stats[2:3, :] = dot(ones, out_all, NT, HIGH)[0:1] / width
    stats[3:4, :] = dot(ones, away * away, NT, HIGH)[0:1]
    stats[4:8, :] = jnp.zeros((4, chans), f32)


def late_kernel(
    sums, early_norms, early_stats, *rest, need, save
):
    small_in, (a_mix, b_mix), rest = rest[:8], rest[8:10], rest[10:]
    x_mix, y_mix, x_xp, y_xp, x_dt, y_dt, x_cv, y_cv, x_cp, y_cp, *rest = rest
    u_mix, u_xp, u_dt, u_cv, u_cp, norms, stats, w_xp, w_dt, w_cv, w_cp, w_mix, *_ = rest
    a_xp, b_xp, a_dt, b_dt, a_cv, b_cv, a_cp, b_cp = small_in
    width, chans = w_mix.shape
    tiles = chans // LANES
    base = tiles * width
    need(early_norms, early_stats, *small_in, w_xp, w_dt, w_cv, w_cp)
    norms[...] = early_norms[...]
    stats[...] = early_stats[...]

    def small(place, items, weight, a_ref, b_ref, x_ref, y_ref, u_ref):
        weight_sq, update_sq = jnp.zeros((1, LANES), f32), jnp.zeros((1, LANES), f32)
        for index, grad in enumerate(items):
            held = weight[index]
            first, second, update = lamb_moments(held, grad, a_ref[index], b_ref[index])
            x_ref[index] = first
            y_ref[index] = second
            u_ref[index] = update
            weight_sq = weight_sq + lanes_sum(held * held)
            update_sq = update_sq + lanes_sum(update * update)
        norms[place : place + 1, :] = weight_sq
        norms[6 + place : 7 + place, :] = update_sq

    rows = w_xp.shape[1]
    grads = fetch(sums, base, 2 * rows, 0, 2 * rows, tiles)
    small(2, [grads[:rows], grads[rows:]], w_xp, a_xp, b_xp, x_xp, y_xp, u_xp)
    base += 2 * rows * tiles
    rank = w_dt.shape[1]
    grads = fetch(sums, base, 2 * rank, 0, 2 * rank, tiles)
    small(3, [grads[:rank], grads[rank:]], w_dt, a_dt, b_dt, x_dt, y_dt, u_dt)
    base += 2 * rank * tiles
    grads = fetch(sums, base, 48, 0, 48, tiles)
    taps = w_cv.shape[1]
    small(4, [grads[:taps], grads[taps : 2 * taps]], w_cv, a_cv, b_cv, x_cv, y_cv, u_cv)
    entries = w_cp.shape[0]
    items = [grads[2 * (taps + entry) : 2 * (taps + entry) + 2] for entry in range(entries)]
    small(5, items, w_cp, a_cp, b_cp, x_cp, y_cp, u_cp)
    for tile in range(tiles):
        norms[12 + tile : 13 + tile, :] = grads[46:47, cols(tile)]
    save()
    need(a_mix, b_mix, w_mix)
    weight_sq, update_sq, total = half_update(
        sums, 0, width, w_mix, a_mix, b_mix, x_mix, y_mix, u_mix
    )
    norms[0:1, :] += lanes_sum(weight_sq)
    norms[6:7, :] += lanes_sum(update_sq)
    mix_mean = rows_sum(total) / width
    stats[4:5, :] = mix_mean


def spread_kernel(u_mix, stats, spread, *, need, save):
    spread[...] = jnp.broadcast_to(spread_of(u_mix, stats[4:5, :], u_mix.shape[0]), spread.shape)


def apply_kernel(
    norms_own, norms_far, stats, mix_spread,
    w_mix, w_gate, w_out, w_xp, w_dt, w_cv, w_cp,
    u_mix, u_gate, u_out, u_xp, u_dt, u_cv, u_cp,
    gain, gain_first, gain_second, x_mix, y_mix, core, x_given, y_given,
    n_in, c_in, n_out, c_out, n_xp, c_xp, n_dt, c_dt, n_cv, c_cv, n_cp, c_cp,
    g_first, g_second, g_new, g_copy, norms_out, stats_out, x_in, y_in,
    sems,
    *, need, save,
):
    width, chans = w_mix.shape
    moves = [
        pltpu.make_async_copy(held, target.at[:, 0, :], sems.at[number])
        for number, (held, target) in enumerate(((x_mix, x_in), (y_mix, y_in)))
    ]
    for move in moves:
        move.start()
    half_width = g_new.shape[0]
    me = core[0]
    totals = norms_own[...] + norms_far[...]
    sums = jnp.sum(totals, axis=1, keepdims=True)
    scales = [None]
    for place in range(6):
        weight_norm = jnp.sqrt(sums[place : place + 1])
        update_norm = jnp.sqrt(sums[6 + place : 7 + place])
        scales.append(learn_rate * weight_norm / (update_norm + adam_eps))
        norms_out[0:1, place + 1 : place + 2] = weight_norm
        norms_out[1:2, place + 1 : place + 2] = update_norm

    need(w_mix, w_gate)

    def one_in(start, held):
        here = pl.ds(start, LAMB_ROWS)
        for half, weight, change in ((0, w_mix, u_mix), (1, w_gate, u_gate)):
            fresh = weight[here, :] - scales[1] * change[here, :]
            n_in[half, here, :] = fresh
            c_in[here, half, :] = fresh.astype(bf16)
        return held

    each_rows(width, one_in, 0, LAMB_ROWS)
    save(n_in, c_in)

    def one_out(start, held):
        here = pl.ds(start, LAMB_ROWS)
        fresh = w_out[here, :] - scales[2] * u_out[here, :]
        n_out[here, :] = fresh
        c_out[here, :] = fresh.astype(bf16)
        return held

    each_rows(chans, one_out, 0, LAMB_ROWS)
    save(n_out, c_out)
    need()
    gain_grad = jnp.concatenate(
        [totals[12 + tile : 13 + tile, :] for tile in range(width // LANES)], axis=1
    )
    gain_row = gain[...].reshape(1, width)
    first, second, update = lamb_moments(gain_row, gain_grad, gain_first[...], gain_second[...])
    weight_norm = jnp.sqrt(jnp.sum(gain_row * gain_row, axis=1, keepdims=True))
    update_norm = jnp.sqrt(jnp.sum(update * update, axis=1, keepdims=True))
    norms_out[0:1, 0:1] = weight_norm
    norms_out[1:2, 0:1] = update_norm
    fresh = gain_row - learn_rate * weight_norm / (update_norm + adam_eps) * update

    def own(row):
        return jnp.where(me == 0, row[:, :half_width], row[:, half_width:]).reshape(half_width)

    g_first[...] = own(first)
    g_second[...] = own(second)
    g_new[...] = own(fresh)
    g_copy[...] = own(fresh).astype(bf16)
    for place, weight, change, fresh_ref, copy in (
        (3, w_xp, u_xp, n_xp, c_xp),
        (4, w_dt, u_dt, n_dt, c_dt),
        (5, w_cv, u_cv, n_cv, c_cv),
        (6, w_cp, u_cp, n_cp, c_cp),
    ):
        for index in range(weight.shape[0]):
            fresh = weight[index] - scales[place] * change[index]
            fresh_ref[index] = fresh
            copy[index] = fresh.astype(bf16)
    parts = [
        (scales[1], stats[4:5, :], mix_spread[0:1, :]),
        (scales[1], stats[0:1, :], stats[1:2, :]),
        (scales[2], stats[2:3, :], stats[3:4, :]),
    ]
    means = [scale * part_mean for scale, part_mean, _ in parts]
    mean = (means[0] + means[1] + means[2]) / 3.0
    spread = jnp.zeros_like(mean)
    for (scale, _, squares), part_mean in zip(parts, means):
        gap = part_mean - mean
        spread = spread + scale * scale * squares + width * gap * gap
    stats_out[0:1, :] = mean
    stats_out[1:2, :] = spread / (3.0 * width)
    for move in moves:
        move.wait()


def join_kernel(pieces, copies, *, need, save):
    total = pieces[0].astype(f32)
    for place in range(1, pieces.shape[0]):
        total = total + pieces[place].astype(f32)
    low = total.astype(bf16)
    for place in range(pieces.shape[0]):
        copies[place] = low


def send_pieces(values, dp):
    chunk = values.shape[0] // dp
    return lax.all_to_all(values, "dp", 0, 0, tiled=True).reshape(dp, chunk, LANES)


def join_pieces(pieces):
    copies = call(join_kernel, at("x", shape(pieces.shape, bf16)), at("x", pieces), limit=8)[0]
    return copies.reshape(-1, LANES)


def call(kernel, outs, args, scratch=(), limit=32, micros=1, passed=(), kept=(), aliases=None):
    given = [array for array, _ in args] + [array for array, _ in passed]
    kinds = [kind for _, kind in args] + ["m"] * len(passed)
    n_own = len(outs)
    outs = list(outs)
    for array, kind in passed:
        dims = array.shape if kind == "h" else (array.shape[0], array.shape[-1])
        outs += at("x", shape(dims, array.dtype))
    outs += at("m", *[shape(given[place].shape, given[place].dtype) for place in kept])
    out_kinds = [kind for _, kind in outs]
    fetched = [place for place, kind in enumerate(kinds) if kind in "h01"]
    stored = [place for place, kind in enumerate(out_kinds) if kind in "h12"]

    def staged(array, kind):
        rows, columns = array.shape[0], array.shape[-1]
        dims = {"h": array.shape, "2": (2, rows, columns)}.get(kind, (rows, columns))
        return pltpu.VMEM(dims, array.dtype)

    staging = [staged(given[place], kinds[place]) for place in fetched]
    staging += [staged(outs[place][0], out_kinds[place]) for place in stored]
    moves = max(1, 2 * len(staging) + len(passed) + len(kept))

    def body(*refs):
        ins = list(refs[: len(given)])
        results = list(refs[len(given) : len(given) + len(outs)])
        rest = refs[len(given) + len(outs) :]
        stage, sems, own = rest[: len(staging)], rest[len(staging)], rest[len(staging) + 1 :]
        loads, saves = {}, {}
        for number, place in enumerate(fetched):
            source = ins[place] if kinds[place] == "h" else ins[place].at[:, int(kinds[place]), :]
            loads[id(stage[number])] = pltpu.make_async_copy(source, stage[number], sems.at[number])
            ins[place] = stage[number]
        for load in loads.values():
            load.start()
        for number, place in enumerate(stored, len(fetched)):
            held, target, kind = stage[number], results[place], out_kinds[place]
            parts = [(held, target)]
            if kind == "1":
                parts = [(held, target.at[:, 1, :])]
            if kind == "2":
                parts = [(held.at[half], target.at[:, half, :]) for half in range(2)]
            saves[id(held)] = [
                pltpu.make_async_copy(*pair, sems.at[moves - 1 - 2 * (number - len(fetched)) - half]) for half, pair in enumerate(parts)
            ]
            results[place] = held
        follow = []
        for number in range(len(passed)):
            held = results[n_own + number]
            source, kind = ins[len(args) + number], passed[number][1]
            source = source if kind == "h" else source.at[:, int(kind), :]
            loads[id(held)] = pltpu.make_async_copy(source, held, sems.at[len(staging) + number])
            loads[id(held)].start()
        begun, resting = [], []
        for number, place in enumerate(kept):
            resting.append(
                pltpu.make_async_copy(
                    ins[place], results[n_own + len(passed) + number],
                    sems.at[len(staging) + len(passed) + number],
                )
            )

        def need(*wanted):
            keys = [id(ref) for ref in wanted] or list(loads)
            for key in keys:
                if key in loads and key not in follow:
                    loads.pop(key).wait()
            while follow:
                loads[follow.pop(0)].start()
            while resting:
                begun.append(resting.pop(0))
                begun[-1].start()
            for key in keys:
                if key in loads:
                    loads.pop(key).wait()

        def save(*ready):
            for key in [id(ref) for ref in ready] or list(saves):
                for move in saves.pop(key, ()):
                    move.start()
                    begun.append(move)

        kernel(*ins[: len(args)], *results[: n_own + len(passed)], *own, need=need, save=save)
        need()
        save()
        for move in begun:
            move.wait()

    spaces = {"x": pltpu.VMEM, "s": pltpu.SMEM}
    placed = [
        pltpu.with_memory_space_constraint(array, pltpu.HBM) if kind in "hm01" else array
        for array, kind in zip(given, kinds)
    ]
    return pl.pallas_call(
        body,
        out_shape=[out if kind == "x" else pltpu.HBM(out.shape, out.dtype) for out, kind in outs],
        in_specs=[pl.BlockSpec(memory_space=spaces.get(kind, pltpu.HBM)) for kind in kinds],
        out_specs=[pl.BlockSpec(memory_space=spaces.get(kind, pltpu.HBM)) for kind in out_kinds],
        input_output_aliases=aliases or {},
        scratch_shapes=[*staging, pltpu.SemaphoreType.DMA((moves,)), *scratch],
        compiler_params=pltpu.CompilerParams(vmem_limit_bytes=limit * MB),
        cost_estimate=pl.CostEstimate(flops=micros * 10**9, bytes_accessed=MB, transcendentals=0),
    )(*placed)


def at(kind, *things):
    return [(thing, kind) for thing in things]


def program(
    dp,
    hidden_in, out_cot, segment_ids,
    norm_gain, in_weight, out_weight, xproj_weight, dtproj_weight, conv_weight, chan_params,
    first_norm_gain, first_in_weight, first_out_weight, first_xproj_weight,
    first_dtproj_weight, first_conv_weight, first_chan_params,
    second_norm_gain, second_in_weight, second_out_weight, second_xproj_weight,
    second_dtproj_weight, second_conv_weight, second_chan_params,
):
    tokens, width = hidden_in.shape
    chans = in_weight.shape[2]
    half_width = first_norm_gain.shape[0]
    tiles = chans // LANES
    rank = dtproj_weight.shape[1]
    count = chan_params.shape[1] - 3
    rows = rank + 2 * count
    taps = conv_weight.shape[1]

    def swap(values):
        return lax.ppermute(values, "chan", [(0, 1), (1, 0)])

    me = lax.axis_index("chan")
    core = me.astype(jnp.int32).reshape(1)
    cot_own = out_cot.T
    cot_far = swap(cot_own)
    moments_own = jnp.stack([first_norm_gain, second_norm_gain])
    moments_far = swap(moments_own)
    moments_gain = jnp.where(
        me == 0,
        jnp.concatenate([moments_own, moments_far], 1),
        jnp.concatenate([moments_far, moments_own], 1),
    )

    def flip(values):
        return jnp.swapaxes(values, 1, 2)

    def turn(values):
        return jnp.swapaxes(values, 0, 1)

    w_xp = flip(xproj_weight)
    w_cp = turn(chan_params)
    square = (tokens, chans)
    z = Sizes(tokens, chans, count, rank)
    smem = at("s", core)

    def padded_rows(amount):
        return -(-amount // (dp * 16)) * 16 * dp

    mixing, gate, conv_pre, part, normed, low_in, same, near_cp, near_dt, near_cot = call(
        front_kernel,
        at("h", shape(square, f32))
        + at("x", shape(square, f32), shape((2,) + square, f32), shape((2 * rows, tokens), f32))
        + at("h", shape((tokens, width), bf16), shape((2, width, chans), bf16))
        + at("x", shape((2, tokens, LANES), f32)),
        at("h", hidden_in, norm_gain) + at("0", in_weight) + at("1", in_weight)
        + at("h", segment_ids, conv_weight, w_xp),
        [pltpu.VMEM((tokens + 16, chans), f32), pltpu.VMEM((tokens + 16, LANES), f32)],
        limit=14, micros=6, passed=at("h", w_cp, dtproj_weight, cot_own),
    )
    part_far = swap(part)
    early_rows = padded_rows(tiles * width + (width // LANES) * chans)
    (
        states, proj, grad_maps, skips, far_step, grad_y, pre_step, inflow_low, gate_low, branch_low, early,
        conv_kept,
    ) = forward_call(
        at("x", part, part_far, near_cp, near_dt, near_cot, cot_far) + at("h", out_weight)
        + at("x", conv_pre, gate, same) + at("h", normed) + smem,
        z, early_rows, half_width, (7,),
    )
    early_pieces = send_pieces(early, dp)
    grad_part, grad_act, grad_dt, grad_chan = backward_call(
        at("m", states) + at("h", w_cp, proj, far_step, grad_y, inflow_low, pre_step, conv_kept)
        + at("h", grad_maps, skips, dtproj_weight),
        z,
    )
    early_copies, grad_part = lax.optimization_barrier((join_pieces(early_pieces), grad_part))
    early_sums = lax.all_to_all(early_copies, "dp", 0, 0, tiled=True)
    grad_far = swap(grad_part)
    late_rows = padded_rows(tiles * (width + 2 * rows + 2 * rank + 48))
    late, in_own, in_send, out_own, out_send = call(
        back_kernel,
        at("x", shape((late_rows, LANES), bf16))
        + at("h", shape((half_width + 8, tokens), f32))
        + at("x", shape((half_width + 8, tokens), f32))
        + at("h", shape((half_width, tokens), f32))
        + at("x", shape((half_width, tokens), f32)),
        at("x", grad_part, grad_far)
        + at("h", segment_ids, w_xp, conv_weight, mixing, conv_kept) + at("x", grad_act, grad_chan)
        + at("h", normed, gate_low, low_in, hidden_in, norm_gain) + at("x", grad_dt)
        + at("h", branch_low, out_weight)
        + smem,
        [
            pltpu.VMEM((tokens + 16, chans), f32), pltpu.VMEM((2, tokens + 16, chans), f32),
            pltpu.VMEM((tokens + 16, LANES), f32), pltpu.VMEM(square, bf16),
            pltpu.VMEM((48, chans), f32), pltpu.VMEM((2,) + square, bf16),
        ],
        limit=20, micros=2,
    )
    in_far = swap(in_send)
    out_far = swap(out_send)
    late, early_sums = lax.optimization_barrier((late, early_sums))
    late_pieces = send_pieces(late, dp)
    output, input_grad = call(
        outputs_kernel,
        at("h", shape((half_width, tokens), bf16), shape((half_width, tokens), f32)),
        at("h", hidden_in, cot_own, out_own) + at("x", out_far) + at("h", in_own) + at("x", in_far) + smem,
        limit=16, micros=3,
    )
    firsts = [first_xproj_weight, first_dtproj_weight, first_conv_weight, first_chan_params]
    seconds = [second_xproj_weight, second_dtproj_weight, second_conv_weight, second_chan_params]
    for group in (firsts, seconds):
        group[0], group[3] = flip(group[0]), turn(group[3])
    weights = [w_xp, dtproj_weight, conv_weight, w_cp]
    half = shape((width, chans), f32)
    whole_in, whole_out = shape(in_weight.shape, f32), shape(out_weight.shape, f32)
    x_out, y_out, x_in, y_in, u_gate, u_out, early_norms, early_stats = call(
        early_kernel,
        at("h", whole_out, whole_out) + at("1", whole_in, whole_in)
        + at("h", half, whole_out, shape((16, LANES), f32), shape((8, chans), f32)),
        at("x", early_sums) + at("h", out_weight, first_out_weight, second_out_weight)
        + at("1", in_weight, first_in_weight, second_in_weight),
        limit=12, micros=5,
    )
    late_copies, output, input_grad = lax.optimization_barrier((join_pieces(late_pieces), output, input_grad))
    late_sums = lax.all_to_all(late_copies, "dp", 0, 0, tiled=True)
    shapes = [shape(tensor.shape, f32) for tensor in weights]
    late_outs = []
    for entry in shapes:
        late_outs += [entry, entry]
    moments_in = [tensor for pair in zip(firsts, seconds) for tensor in pair]
    got = call(
        late_kernel,
        at("x", half, half) + at("h", *late_outs)
        + at("x", half, *shapes, shape((16, LANES), f32), shape((8, chans), f32)),
        at("x", late_sums) + at("h", early_norms, early_stats, *moments_in)
        + at("0", first_in_weight, second_in_weight),
        limit=12, micros=5,
        passed=at("h", *weights) + at("0", in_weight) + at("1", in_weight) + at("h", out_weight, u_gate, u_out),
    )
    moments, updates, norms, stats, kept = got[:10], got[10:15], got[15], got[16], got[17:]
    kept_small, (kept_mix, kept_gate, kept_out, changed_gate, changed_out) = kept[0:4], kept[4:]
    norms_far = swap(norms)
    mix_spread = call(
        spread_kernel, at("x", shape((8, chans), f32)), at("x", updates[0], stats), limit=8, micros=1
    )[0]
    pairs = []
    for entry in [whole_in, whole_out, *shapes]:
        pairs += [entry, shape(entry.shape, bf16)]
    row = shape((half_width,), f32)
    whole_low = shape(whole_in.shape, bf16)
    done = call(
        apply_kernel,
        at("2", whole_in) + at("h", whole_low)
        + at(
            "h", *pairs[2:], row, row, row, shape((half_width,), bf16), shape((2, 7), f32),
            shape((2, chans), f32),
        )
        + at("m", whole_in, whole_in),
        at("x", norms, norms_far, stats, mix_spread, kept_mix, kept_gate, kept_out, *kept_small, updates[0], changed_gate, changed_out, *updates[1:])
        + at("h", norm_gain) + at("x", moments_gain[0:1], moments_gain[1:2], moments[0], moments[1])
        + smem + at("m", x_in, y_in),
        [pltpu.SemaphoreType.DMA((2,))],
        limit=14, micros=5, aliases={24: 18, 25: 19},
    )
    flat = list(done[12:16])
    firsts_out = [done[18], x_out, *moments[2::2]]
    seconds_out = [done[19], y_out, *moments[3::2]]
    for place in range(6):
        entry = [firsts_out[place], seconds_out[place], done[2 * place], done[2 * place + 1]]
        if place == 2:
            entry = [flip(tensor) for tensor in entry]
        if place == 5:
            entry = [turn(tensor) for tensor in entry]
        flat += entry
    return (output.T, input_grad.T, *flat, done[16].T, done[17])


def solution(mesh):
    rows = P("dp", None)
    cells = P("dp", "chan")
    last = P(None, None, "chan")
    first = P("chan", None)
    middle = P(None, "chan", None)
    tensors = (last, first, middle, last, last, last)
    outs = [cells, cells] + [P("chan")] * 4
    for spec in tensors:
        outs += [spec] * 4
    return jax.shard_map(
        functools.partial(program, mesh.shape["dp"]),
        mesh=mesh,
        in_specs=(rows, cells, P("dp"), P(), *tensors, P("chan"), *tensors, P("chan"), *tensors),
        out_specs=(*outs, P(), P(None, "chan")),
        check_vma=False,
    )
```

```python
import functools

import jax
import jax.numpy as jnp
from jax import lax
from jax.experimental import pallas as pl
from jax.experimental.pallas import tpu as pltpu
from jax.sharding import PartitionSpec as P

STEP = 4
norm_eps = 1e-06
beta_one = 0.5
beta_two = 0.5
adam_eps = 1e-06
decay_rate = 0.01
learn_rate = 0.3
LOG2E = 1.4426950408889634
FAR = 1e30
FLOOR = -1e-26

f32 = jnp.float32
bf16 = jnp.bfloat16
HIGH = lax.Precision.HIGHEST
LANES = 128
ROWS = 16
NORM_ROWS = 192
CONV_ROWS = 96
LAMB_ROWS = 32
MB = 1 << 20


def dot(left, right, dims, precision=None):
    return lax.dot_general(
        left, right, (dims, ((), ())), precision=precision, preferred_element_type=f32
    )


NN = ((1,), (0,))
TN = ((0,), (0,))
NT = ((1,), (1,))


def sigmoid(values):
    return lax.logistic(values)


def silu_slope(values, sigma):
    return sigma * (1.0 + values * (1.0 - sigma))


def softplus(values):
    return jnp.maximum(values, 0.0) + jnp.log1p(jnp.exp(-jnp.abs(values)))


def wide(tile, times):
    return jnp.concatenate([tile] * times, axis=1)


def fold(values):
    total = values[0:8]
    for start in range(8, values.shape[0], 8):
        total = total + values[start : start + 8]
    return total


def shape(dims, dtype):
    return jax.ShapeDtypeStruct(dims, dtype)


def each_rows(length, body, carry=None, rows=ROWS):
    def step(index, held):
        return body(pl.multiple_of(index * rows, rows), held)

    return lax.fori_loop(0, length // rows, step, carry)


def spread_segments(numbers, tokens):
    across = lax.broadcasted_iota(jnp.int32, (tokens, tokens), 0)
    along = lax.broadcasted_iota(jnp.int32, (tokens, tokens), 1)
    row = numbers.astype(f32).reshape(1, tokens)
    picked = jnp.where(across == along, row, 0.0).astype(bf16)
    return dot(picked, jnp.ones((tokens, LANES), bf16), NN)


def front_kernel(
    hid, gain, w_mix, w_gate, seg, taps, w_xp,
    mix_out, gate_out, conv_out, part_out, norm_out, low_out, same_out, params, near_dt, near_cot, near_out,
    padded, sgpad,
    *, need, save,
):
    tokens, width = hid.shape
    chans = mix_out.shape[1]
    tiles = chans // LANES

    need(hid, gain)
    gain_row = gain[...].reshape(1, width)

    def normalise(start, held):
        source = hid[pl.ds(start, NORM_ROWS), :].astype(f32)
        scale = lax.rsqrt(jnp.sum(source * source, axis=1, keepdims=True) / width + norm_eps)
        norm_out[pl.ds(start, NORM_ROWS), :] = (source * scale * gain_row).astype(bf16)
        return held

    each_rows(tokens, normalise, 0, NORM_ROWS)
    save(norm_out)
    need(w_mix, w_gate)
    low_out[0] = w_mix[...].astype(bf16)
    low_out[1] = w_gate[...].astype(bf16)
    save(low_out)
    normed = norm_out[...]
    mixing = dot(normed, low_out[0], NN)
    mix_out[...] = mixing
    padded[0:8, :] = jnp.zeros((8, chans), f32)
    padded[pl.ds(8, tokens), :] = mixing
    padded[pl.ds(8 + tokens, 8), :] = jnp.zeros((8, chans), f32)
    save(mix_out)
    gate_out[...] = dot(normed, low_out[1], NN)
    need(seg, taps, w_xp, params)
    numbers = spread_segments(seg[...], tokens)
    sgpad[0:8, :] = jnp.full((8, LANES), -1.0, f32)
    sgpad[pl.ds(8, tokens), :] = numbers
    sgpad[pl.ds(8 + tokens, 8), :] = jnp.full((8, LANES), -1.0, f32)
    width_taps = taps.shape[1]

    def convolve(start, held):
        window = padded[pl.ds(start, CONV_ROWS + 16), :]
        marks = sgpad[pl.ds(start, CONV_ROWS + 16), :]
        own = marks[8 : 8 + CONV_ROWS]
        base = window[8 : 8 + CONV_ROWS]
        for heading in range(2):
            total = params[0, heading : heading + 1, :] + taps[heading, 0:1, :] * base
            for offset in range(1, width_taps):
                begin = 8 - offset if heading == 0 else 8 + offset
                same = jnp.where(marks[begin : begin + CONV_ROWS] == own, 1.0, 0.0)
                if offset == 1:
                    same_out[heading, pl.ds(start, CONV_ROWS), :] = same
                moved = window[begin : begin + CONV_ROWS]
                total = total + taps[heading, offset : offset + 1, :] * moved * wide(same, tiles)
            conv_out[heading, pl.ds(start, CONV_ROWS), :] = total
        return held

    each_rows(tokens, convolve, 0, CONV_ROWS)
    for heading in range(2):
        pre = conv_out[heading]
        act_low = (pre * sigmoid(pre)).astype(bf16)
        rows = w_xp.shape[1]
        part_out[heading * rows : (heading + 1) * rows, :] = dot(
            w_xp[heading].astype(bf16), act_low, NT
        )


SPAN = 128


class Sizes:
    def __init__(self, tokens, chans, count, rank):
        self.tokens, self.chans, self.count, self.rank = tokens, chans, count, rank
        self.tiles = chans // LANES
        self.blocks = tokens // LANES
        self.rows = rank + 2 * count
        self.block_rows = LANES * count
        self.pairs = [(heading, tile) for heading in range(2) for tile in range(self.tiles)]

    def base(self, heading, tile):
        return (heading * self.tiles + tile) * self.tokens

    def row(self, ref, heading, tile, at):
        return ref[pl.ds(self.base(heading, tile) + at, 1), :]

    def whole(self, ref, heading):
        starts = [self.base(heading, tile) for tile in range(self.tiles)]
        return jnp.concatenate([ref[start : start + self.tokens, :] for start in starts], axis=1)


def cols(tile):
    return slice(tile * LANES, (tile + 1) * LANES)


def split(values):
    high = values.astype(bf16)
    return high, (values - high.astype(f32)).astype(bf16)


def group_maps(target, tile, heading, count):
    groups = tile.shape[1] // count
    for group in range(groups):
        block, place = divmod(group * count, LANES)
        own = tile[:, cols(block)]
        if place:
            own = pltpu.roll(own, LANES - place, 1)
        target[heading, group] = own


def diagonal_maps(target, tile, heading, count):
    tokens = tile.shape[1]
    squared = count * count
    lane = lax.broadcasted_iota(jnp.int32, (count, squared), 1)
    row = lax.broadcasted_iota(jnp.int32, (count, squared), 0)
    repeat = jnp.where(lane % count == row, 1.0, 0.0).astype(bf16)
    token = lax.broadcasted_iota(jnp.int32, (tokens, squared), 0)
    place = lax.broadcasted_iota(jnp.int32, (tokens, squared), 1)
    mine = place // count == token % count
    for number, part in enumerate(split(tile)):
        spread = jnp.where(mine, dot(part, repeat, TN), 0.0).astype(bf16)
        target[heading, :, number] = spread.reshape(tokens // count, count, squared)


def weigh_states(left, maps):
    half = maps.shape[0] // 2
    got = dot(maps, left, NN)
    return got[:half] + got[half:]


def gather_states(left, right, count):
    products = dot(left, right, NT)
    lane = lax.broadcasted_iota(jnp.int32, (count, count), 1)
    total = products[0:count]
    for place in range(1, count):
        total = jnp.where(lane == place, products[place * count : (place + 1) * count], total)
    return total


def dot3(left, right, dims):
    (left_high, left_low), (right_high, right_low) = split(left), split(right)
    if dims == TN:
        lefts = jnp.concatenate([left_high, left_low, left_high], axis=0)
        return dot(lefts, jnp.concatenate([right_high, right_high, right_low], axis=0), dims)
    rows = left.shape[0]
    both = dot(jnp.concatenate([left_high, left_low], axis=0), right_high, dims)
    return both[:rows] + both[rows:] + dot(left_high, right_low, dims)


class Sweep:
    def __init__(self, z, turned):
        self.z, self.turned = z, turned
        self.groups = z.tokens // z.count
        self.stage_groups = self.groups // z.blocks

    def group(self, order, heading):
        return self.groups - 1 - order if heading == self.turned else order

    def block(self, stage, heading):
        return self.z.blocks - 1 - stage if heading == self.turned else stage

    def inner(self, ahead, heading):
        return self.z.count - 1 - ahead if heading == self.turned else ahead

    def rows(self, group):
        return pl.ds(pl.multiple_of(group * self.z.count, self.z.count), self.z.count)

    def run(self, z, carried, scan, post, between):
        def step(index, held):
            order = 2 * index
            post(jnp.maximum(order - 1, 0), 1)
            held = scan(order, held, 0)
            post(order, 0)
            return scan(order + 1, held, 1)

        per = self.stage_groups // 2
        for stage in range(z.blocks):
            between(stage, True)
            carried = lax.fori_loop(stage * per, (stage + 1) * per, step, carried)
            between(stage, False)
        post(self.groups - 1, 1)
        return carried


def store_gathered(target, target_row, gathered, heading, z):
    per = LANES // z.count
    for block in range(z.blocks):
        pieces = [gathered[heading, block * per + place] for place in range(per)]
        target[target_row : target_row + z.count, cols(block)] = jnp.concatenate(pieces, axis=1)


def fill_rates(rates, params, count):
    for heading in range(2):
        for n in range(count):
            value = -jnp.exp(params[3 + n, heading : heading + 1, :])
            rates[heading, n : n + 1, :] = jnp.minimum(value, FLOOR)


def activate_kernel(conv_pre, act, *, need, save):
    for heading in range(2):
        for tile in range(conv_pre.shape[2] // LANES):

            def activate(start, held, heading=heading, tile=tile):
                here = pl.ds(start, SPAN)
                pre = conv_pre[heading, here, cols(tile)]
                act[heading, here, cols(tile)] = pre * sigmoid(pre)
                return held

            each_rows(conv_pre.shape[1], activate, 0, SPAN)


def forward_kernel(
    own_part, far_part, params, w_dt, cot_own, cot_far, w_out, conv_pre, act, gate, same, normed, core,
    states_out, proj, grad_maps, skips, far_step, grad_y, pre_step, inflow_low, gate_low, branch_low, early,
    grad_branch, inflow, grad_y_low, result, maps, diagonal, gathered, states, low_one, low_two,
    rates, sems,
    *, need, save,
):
    tokens, chans = gate.shape
    z = Sizes(tokens, chans, params.shape[0] - 3, w_dt.shape[1])
    count, rank, rows, tiles = z.count, z.rank, z.rows, z.tiles
    half_width = cot_own.shape[0]
    width = 2 * half_width
    me = core[0]
    sweep = Sweep(z, 1)
    lows = (low_one, low_two)

    proj[...] = own_part[...] + far_part[...]
    save(proj)
    for heading in range(2):
        first = heading * rows + rank
        group_maps(maps, proj[first : first + count, :], heading, count)
        diagonal_maps(diagonal, proj[first + count : first + 2 * count, :], heading, count)
    need(params, w_dt)
    fill_rates(rates, params, count)
    for heading in range(2):
        pre_step[heading] = (
            dot3(proj[heading * rows : heading * rows + rank, :], w_dt[heading], TN)
            + params[1, heading : heading + 1, :]
        )
    save(pre_step)
    need(w_out, cot_own)
    low_out = w_out[...].astype(bf16)
    low_cot = jnp.where(
        me == 0,
        jnp.concatenate([cot_own[...].astype(f32), cot_far[...].astype(f32)], 0),
        jnp.concatenate([cot_far[...].astype(f32), cot_own[...].astype(f32)], 0),
    ).astype(bf16)
    grad_branch[...] = dot(low_cot, low_out, ((0,), (1,)))

    for tile in range(tiles):

        def prepare(start, held, tile=tile):
            here = pl.ds(start, SPAN)
            for heading in range(2):
                size = softplus(pre_step[heading, here, cols(tile)])
                there = pl.ds(z.base(heading, tile) + start, SPAN)
                entering = size * act[heading, here, cols(tile)]
                inflow[there, :] = entering
                inflow_low[heading, here, cols(tile)] = entering.astype(bf16)
                far_step[there, :] = jnp.where(same[heading, here, :] > 0.5, size * LOG2E, FAR)
            gated = gate[here, cols(tile)]
            back = grad_branch[here, cols(tile)] * (gated * sigmoid(gated))
            grad_y[pl.ds(z.base(0, tile) + start, SPAN), :] = back
            grad_y_low[here, cols(tile)] = back.astype(bf16)
            return held

        each_rows(tokens, prepare, 0, SPAN)
    save(far_step, inflow_low, grad_y)

    blank = jnp.zeros((count, LANES), f32)
    states[0, 0:count, :] = jnp.zeros((count, chans), bf16)
    states[1, tokens * count : (tokens + 1) * count, :] = jnp.zeros((count, chans), bf16)
    low_two[...] = jnp.zeros(low_two.shape, bf16)
    speeds = [rates[heading, :, cols(tile)] for heading, tile in z.pairs]

    def scan(order, carried, slot):
        carried = list(carried)
        enters = [maps[heading, sweep.group(order, heading)] for heading in range(2)]
        for heading in range(2):
            for ahead in range(count):
                inner = sweep.inner(ahead, heading)
                at = sweep.group(order, heading) * count + inner
                kept = pl.multiple_of((at + (1 if heading == 0 else 0)) * count, count)
                enter = jnp.broadcast_to(enters[heading][:, inner : inner + 1], (count, LANES))
                for tile in range(tiles):
                    number = heading * tiles + tile
                    decay = jnp.exp2(z.row(far_step, heading, tile, at) * speeds[number])
                    state = decay * carried[number] + enter * z.row(inflow, heading, tile, at)
                    carried[number] = state
                    low = state.astype(bf16)
                    states[heading, pl.ds(kept, count), cols(tile)] = low
                    lows[slot][heading, inner * count : (inner + 1) * count, cols(tile)] = low
        return tuple(carried)

    def post(order, slot):
        for heading in range(2):
            group = sweep.group(order, heading)
            left = lows[slot][heading]
            gathered[heading, group] = gather_states(left, grad_y_low[sweep.rows(group), :], count)
            result[heading, sweep.rows(group), :] = weigh_states(
                left, diagonal[heading, group].reshape(2 * count, count * count)
            )

    keeps = []

    def between(stage, before):
        if before:
            return
        for heading in range(2):
            begin, extent = sweep.block(stage, heading) * z.block_rows, z.block_rows
            if stage == 0:
                extent += count
            elif heading == 0:
                begin += count
            piece = pl.ds(begin, extent)
            keep = pltpu.make_async_copy(
                states.at[heading, piece, :], states_out.at[heading, piece, :], sems.at[heading, stage]
            )
            keep.start()
            keeps.append(keep)

    sweep.run(z, (blank,) * len(z.pairs), scan, post, between)
    for heading in range(2):
        store_gathered(grad_maps, heading * count, gathered, heading, z)
    skips[...] = jnp.zeros(skips.shape, f32)
    for tile in range(tiles):

        def finish(start, held, tile=tile):
            here = pl.ds(start, SPAN)
            total = jnp.zeros((SPAN, LANES), f32)
            sums = []
            back = grad_y[pl.ds(z.base(0, tile) + start, SPAN), :]
            for heading in range(2):
                active = act[heading, here, cols(tile)]
                total = total + result[heading, here, cols(tile)]
                total = total + params[2, heading : heading + 1, cols(tile)] * active
                sums.append(held[heading] + fold(back * active))
            gated = gate[here, cols(tile)]
            sigma = sigmoid(gated)
            branch_low[here, cols(tile)] = (total * (gated * sigma)).astype(bf16)
            gate_low[here, cols(tile)] = (
                grad_branch[here, cols(tile)] * total * silu_slope(gated, sigma)
            ).astype(bf16)
            return tuple(sums)

        sums = each_rows(tokens, finish, (jnp.zeros((8, LANES), f32),) * 2, SPAN)
        for heading in range(2):
            skips[heading : heading + 1, cols(tile)] = jnp.sum(sums[heading], axis=0, keepdims=True)
    save(gate_low, branch_low, grad_maps, skips)
    need()
    branch = branch_low[...]
    grad_w = dot(branch, low_cot, ((0,), (1,))).astype(bf16)
    for tile in range(width // LANES):
        early[tile * chans : (tile + 1) * chans, :] = grad_w[:, cols(tile)]
    base_row = chans * (width // LANES)
    grad_w = dot(normed[...], gate_low[...], TN).astype(bf16)
    for tile in range(tiles):
        early[base_row + tile * width : base_row + (tile + 1) * width, :] = grad_w[:, cols(tile)]
    base_row += tiles * width
    if early.shape[0] > base_row:
        early[base_row:, :] = jnp.zeros((early.shape[0] - base_row, LANES), bf16)
    for keep in keeps:
        keep.wait()


def backward_kernel(
    states_in, params, proj, far_step, grad_y, inflow_low, pre_step, conv_pre, grad_maps, skips, w_dt,
    grad_part, grad_act, grad_dt, grad_chan,
    result, decayed, maps, diagonal, gathered, states, low_one, low_two, products_one, products_two, rates, sems,
    *, need, save,
):
    _, tokens, chans = conv_pre.shape
    z = Sizes(tokens, chans, params.shape[0] - 3, w_dt.shape[1])
    count, rank, rows, tiles = z.count, z.rank, z.rows, z.tiles
    sweep = Sweep(z, 0)
    lows, products = (low_one, low_two), (products_one, products_two)
    loads = {}
    for stage in range(z.blocks):
        for heading in range(2):
            begin = sweep.block(stage, heading) * z.block_rows + (count if heading == 1 else 0)
            piece = pl.ds(begin, z.block_rows)
            load = pltpu.make_async_copy(
                states_in.at[heading, piece, :], states.at[heading, piece, :], sems.at[heading, stage]
            )
            load.start()
            loads[stage, heading] = load
    need(params, proj)
    fill_rates(rates, params, count)
    for heading in range(2):
        first = heading * rows + rank
        group_maps(maps, proj[first + count : first + 2 * count, :], heading, count)
        diagonal_maps(diagonal, proj[first : first + count, :], heading, count)
    for low in (low_two, products_two):
        low[...] = jnp.zeros(low.shape, bf16)
    blank = jnp.zeros((count, LANES), f32)
    speeds = [rates[heading, :, cols(tile)] for heading, tile in z.pairs]

    def scan(order, held, slot):
        waiting = list(held[: len(z.pairs)])
        totals = list(held[len(z.pairs) :])
        leaves = [maps[heading, sweep.group(order, heading)] for heading in range(2)]
        for heading in range(2):
            for ahead in range(count):
                inner = sweep.inner(ahead, heading)
                at = sweep.group(order, heading) * count + inner
                prior = pl.multiple_of((at + (0 if heading == 0 else 1)) * count, count)
                leave = jnp.broadcast_to(leaves[heading][:, inner : inner + 1], (count, LANES))
                here = slice(inner * count, (inner + 1) * count)
                for tile in range(tiles):
                    number = heading * tiles + tile
                    size = z.row(far_step, heading, tile, at)
                    decay = jnp.exp2(size * speeds[number])
                    grad = leave * z.row(grad_y, 0, tile, at) + waiting[number]
                    lead = decay * grad
                    waiting[number] = lead
                    slope = lead * states[heading, pl.ds(prior, count), cols(tile)].astype(f32)
                    totals[number] = totals[number] + slope * size
                    products[slot][heading, here, cols(tile)] = (slope * speeds[number]).astype(bf16)
                    lows[slot][heading, here, cols(tile)] = grad.astype(bf16)
        return tuple(waiting + totals)

    lane = lax.broadcasted_iota(jnp.int32, (count, count * count), 1)
    row = lax.broadcasted_iota(jnp.int32, (count, count * count), 0)
    ones = jnp.where(lane // count == row, 1.0, 0.0).astype(bf16)

    def post(order, slot):
        for heading in range(2):
            group = sweep.group(order, heading)
            left = lows[slot][heading]
            gathered[heading, group] = gather_states(left, inflow_low[heading, sweep.rows(group), :], count)
            result[heading, sweep.rows(group), :] = weigh_states(
                left, diagonal[heading, group].reshape(2 * count, count * count)
            )
            decayed[heading, sweep.rows(group), :] = dot(ones, products[slot][heading], NN)

    def between(stage, before):
        if before:
            if stage == 0:
                need(far_step, grad_y, inflow_low)
            for heading in range(2):
                loads[stage, heading].wait()

    held = sweep.run(z, (blank,) * (2 * len(z.pairs)), scan, post, between)
    for number, (heading, tile) in enumerate(z.pairs):
        slopes = held[len(z.pairs) + number] / LOG2E
        for n in range(count):
            grad_chan[3 + n, heading : heading + 1, cols(tile)] = slopes[n : n + 1] * -jnp.exp(
                params[3 + n, heading : heading + 1, cols(tile)]
            )
    need()
    for heading in range(2):
        first = heading * rows + rank
        store_gathered(grad_part, first, gathered, heading, z)
        grad_part[first + count : first + 2 * count, :] = grad_maps[
            heading * count : (heading + 1) * count, :
        ]

    for tile in range(tiles):

        def close(start, held, tile=tile):
            here = pl.ds(start, SPAN)
            sums = []
            back = grad_y[pl.ds(z.base(0, tile) + start, SPAN), :]
            for heading in range(2):
                pre = conv_pre[heading, here, cols(tile)]
                act = pre * sigmoid(pre)
                passed = result[heading, here, cols(tile)]
                reach = pre_step[heading, here, cols(tile)]
                grad_act[heading, here, cols(tile)] = (
                    passed * softplus(reach) + back * params[2, heading : heading + 1, cols(tile)]
                )
                grad_pre = (decayed[heading, here, cols(tile)] + passed * act) * sigmoid(reach)
                pre_step[heading, here, cols(tile)] = grad_pre
                sums.append(held[heading] + fold(grad_pre))
            return tuple(sums)

        biases = each_rows(tokens, close, (jnp.zeros((8, LANES), f32),) * 2, SPAN)
        for heading in range(2):
            grad_chan[1, heading : heading + 1, cols(tile)] = jnp.sum(
                biases[heading], axis=0, keepdims=True
            )
    save(grad_act)
    for heading in range(2):
        grad_chan[0, heading : heading + 1, :] = jnp.zeros((1, chans), f32)
        grad_chan[2, heading : heading + 1, :] = skips[heading : heading + 1, :]
        grad_pre = pre_step[heading]
        grad_part[heading * rows : heading * rows + rank, :] = dot3(w_dt[heading], grad_pre, NT)
        grad_dt[heading] = dot3(proj[heading * rows : heading * rows + rank, :], grad_pre, NN)


def forward_call(args, sizes, early_rows, half_width, kept, limit=30):
    z = sizes
    square = (z.tokens, z.chans)
    both = (2,) + square
    flat = (2 * z.tiles * z.tokens, LANES)
    groups = z.tokens // z.count
    squared = z.count * z.count
    states = (2, (z.tokens + 1) * z.count, z.chans)
    slot = pltpu.VMEM((2, squared, z.chans), bf16)
    return call(
        forward_kernel,
        at("m", shape(states, bf16))
        + at(
            "h", shape((2 * z.rows, z.tokens), f32), shape((2 * z.count, z.tokens), f32), shape((8, z.chans), f32),
            shape(flat, f32), shape((z.tiles * z.tokens, LANES), f32), shape(both, f32), shape(both, bf16),
            shape(square, bf16), shape(square, bf16),
        )
        + at("x", shape((early_rows, LANES), bf16)),
        args,
        [
            pltpu.VMEM(square, f32), pltpu.VMEM(flat, f32), pltpu.VMEM(square, bf16), pltpu.VMEM(both, f32),
            pltpu.VMEM((2, groups, z.count, LANES), f32),
            pltpu.VMEM((2, groups, 2, z.count, squared), bf16), pltpu.VMEM((2, groups, z.count, z.count), f32),
            pltpu.VMEM(states, bf16), slot, slot, pltpu.VMEM((2, z.count, z.chans), f32),
            pltpu.SemaphoreType.DMA((2, z.blocks)),
        ],
        limit=limit, micros=15, kept=kept,
    )


def backward_call(args, sizes, limit=30):
    z = sizes
    square = (z.tokens, z.chans)
    both = (2,) + square
    groups = z.tokens // z.count
    squared = z.count * z.count
    slot = pltpu.VMEM((2, squared, z.chans), bf16)
    return call(
        backward_kernel,
        at(
            "x", shape((2 * z.rows, z.tokens), f32), shape(both, f32), shape((2, z.rank, z.chans), f32),
            shape((3 + z.count, 2, z.chans), f32),
        ),
        args,
        [
            pltpu.VMEM(both, f32), pltpu.VMEM(both, f32), pltpu.VMEM((2, groups, z.count, LANES), f32),
            pltpu.VMEM((2, groups, 2, z.count, squared), bf16), pltpu.VMEM((2, groups, z.count, z.count), f32),
            pltpu.VMEM((2, (z.tokens + 1) * z.count, z.chans), bf16), slot, slot, slot, slot,
            pltpu.VMEM((2, z.count, z.chans), f32), pltpu.SemaphoreType.DMA((2, z.blocks)),
        ],
        limit=limit, micros=15,
    )


def back_kernel(
    own_part, far_part, seg, w_xp, taps, mixing, conv_pre, grad_act, grad_chan, normed, gate_low,
    low_in, hid, gain, grad_dt, branch, w_out, core,
    sums_out, in_own, in_far, out_own, out_far,
    padded, gpad, sgpad, mixed_low, small, act_low,
    *, need, save,
):
    tokens, width = hid.shape
    chans = mixing.shape[1]
    tiles = chans // LANES
    rows = w_xp.shape[1]
    width_taps = taps.shape[1]
    me = core[0]
    half_width = in_own.shape[0] - 8
    edge = jnp.zeros((8, chans), f32)
    padded[0:8, :] = edge
    padded[pl.ds(8 + tokens, 8), :] = edge
    gpad[0, 0:8, :] = edge
    gpad[1, 0:8, :] = edge
    gpad[0, pl.ds(8 + tokens, 8), :] = edge
    gpad[1, pl.ds(8 + tokens, 8), :] = edge
    sgpad[0:8, :] = jnp.full((8, LANES), -1.0, f32)
    sgpad[pl.ds(8 + tokens, 8), :] = jnp.full((8, LANES), -1.0, f32)
    need(seg, w_xp, mixing)
    padded[pl.ds(8, tokens), :] = mixing[...]
    sgpad[pl.ds(8, tokens), :] = spread_segments(seg[...], tokens)

    parts = (own_part[...] + far_part[...]).astype(bf16)
    for heading in range(2):
        part = parts[heading * rows : (heading + 1) * rows, :]
        gpad[heading, pl.ds(8, tokens), :] = dot(part, w_xp[heading].astype(bf16), TN)

    blank = jnp.zeros((8, chans), f32)
    need(taps, conv_pre, grad_act, grad_chan)

    def through_conv(start, held):
        here = pl.ds(start, CONV_ROWS)
        window = padded[pl.ds(start, CONV_ROWS + 16), :]
        marks = sgpad[pl.ds(start, CONV_ROWS + 16), :]
        own = marks[8 : 8 + CONV_ROWS]
        base = window[8 : 8 + CONV_ROWS]
        sums = []
        for heading in range(2):
            pre = conv_pre[heading, here, :]
            sigma = sigmoid(pre)
            act_low[heading, here, :] = (pre * sigma).astype(bf16)
            inside = pl.ds(pl.multiple_of(start + 8, 8), CONV_ROWS)
            grad = (gpad[heading, inside, :] + grad_act[heading, here, :]) * silu_slope(pre, sigma)
            gpad[heading, inside, :] = grad
            sums.append(held[5 * heading] + fold(grad))
            sums.append(held[5 * heading + 1] + fold(grad * base))
            for offset in range(1, width_taps):
                begin = 8 - offset if heading == 0 else 8 + offset
                kept = jnp.where(marks[begin : begin + CONV_ROWS] == own, 1.0, 0.0)
                moved = window[begin : begin + CONV_ROWS]
                sums.append(held[5 * heading + 1 + offset] + fold(grad * moved * wide(kept, tiles)))
        return tuple(sums)

    sums = each_rows(tokens, through_conv, (blank,) * 10, CONV_ROWS)
    small[...] = jnp.zeros(small.shape, f32)
    for heading in range(2):
        bias = jnp.sum(sums[5 * heading], axis=0, keepdims=True)
        for offset in range(width_taps):
            row = heading * width_taps + offset
            small[row : row + 1, :] = jnp.sum(sums[5 * heading + 1 + offset], axis=0, keepdims=True)
        for entry in range(grad_chan.shape[0]):
            row = 2 * width_taps + 2 * entry + heading
            small[row : row + 1, :] = (
                bias
                if entry == 0
                else grad_chan[entry, heading : heading + 1, :]
            )

    def mixed(start, held):
        here = pl.ds(start, CONV_ROWS)
        marks = sgpad[pl.ds(start, CONV_ROWS + 16), :]
        own = marks[8 : 8 + CONV_ROWS]
        total = jnp.zeros((CONV_ROWS, chans), f32)
        for heading in range(2):
            window = gpad[heading, pl.ds(start, CONV_ROWS + 16), :]
            total = total + window[8 : 8 + CONV_ROWS] * taps[heading, 0:1, :]
            for offset in range(1, width_taps):
                begin = 8 + offset if heading == 0 else 8 - offset
                kept = jnp.where(marks[begin : begin + CONV_ROWS] == own, 1.0, 0.0)
                total = total + window[begin : begin + CONV_ROWS] * wide(kept, tiles) * taps[
                    heading, offset : offset + 1, :
                ]
        mixed_low[here, :] = total.astype(bf16)
        return held

    each_rows(tokens, mixed, 0, CONV_ROWS)

    base_row = 0

    def put(values):
        nonlocal base_row
        for tile in range(values.shape[1] // LANES):
            sums_out[base_row : base_row + values.shape[0], :] = values[
                :, tile * LANES : (tile + 1) * LANES
            ].astype(bf16)
            base_row += values.shape[0]

    need()
    partial = dot(mixed_low[...], low_in[0], NT) + dot(gate_low[...], low_in[1], NT)
    padded[pl.ds(8, tokens), :] = partial

    gain_row = gain[...].reshape(1, width)

    def gains(start, held):
        here = pl.ds(start, NORM_ROWS)
        source = hid[here, :].astype(f32)
        scale = lax.rsqrt(jnp.sum(source * source, axis=1, keepdims=True) / width + norm_eps)
        inside = pl.ds(pl.multiple_of(start + 8, 8), NORM_ROWS)
        grad = padded[inside, :]
        padded[inside, :] = grad * gain_row
        return held + fold(grad * source * scale)

    gain_sum = each_rows(tokens, gains, jnp.zeros((8, width), f32), NORM_ROWS)
    small[46:47, :] = jnp.sum(gain_sum, axis=0, keepdims=True)
    weighted = padded[pl.ds(8, tokens), :]
    products = weighted * hid[...].astype(f32)
    turned = weighted.T
    row_dot = dot(jnp.ones((8, width), f32), products, NT, HIGH)
    in_own[0:half_width, :] = jnp.where(me == 0, turned[:half_width], turned[half_width:])
    in_far[0:half_width, :] = jnp.where(me == 0, turned[half_width:], turned[:half_width])
    in_own[pl.ds(half_width, 8), :] = row_dot
    in_far[pl.ds(half_width, 8), :] = row_dot
    save(in_own)
    sent = dot(w_out[...].astype(bf16), branch[...], ((0,), (1,)))
    out_own[...] = jnp.where(me == 0, sent[:half_width], sent[half_width:])
    out_far[...] = jnp.where(me == 0, sent[half_width:], sent[:half_width])
    save(out_own)
    put(dot(normed[...], mixed_low[...], TN))
    put(
        jnp.concatenate(
            [
                dot(parts[heading * rows : (heading + 1) * rows, :], act_low[heading], NN)
                for heading in range(2)
            ],
            axis=0,
        )
    )
    put(jnp.concatenate([grad_dt[0], grad_dt[1]], axis=0))

    put(small[...])
    sums_out[base_row:, :] = jnp.zeros((sums_out.shape[0] - base_row, LANES), bf16)


def outputs_kernel(hid, cot_own, out_own, out_far, in_own, in_far, core, output, input_grad, *, need, save):
    width = hid.shape[1]
    half_width = cot_own.shape[0]
    me = core[0]
    need()
    source = hid[...].astype(f32).T
    scale = lax.rsqrt(jnp.sum(source * source, axis=0, keepdims=True) / width + norm_eps)
    own = jnp.where(me == 0, source[:half_width], source[half_width:])
    output[...] = (own + (out_own[...] + out_far[...])).astype(bf16)
    weighted = in_own[0:half_width, :] + in_far[0:half_width, :]
    save(output)
    row_dot = in_own[half_width : half_width + 1, :] + in_far[half_width : half_width + 1, :]
    input_grad[...] = (
        cot_own[...].astype(f32)
        + scale * weighted
        - own * (scale * scale * scale) * (row_dot / width)
    )


def lamb_moments(weight, grad, first, second):
    first_new = beta_one * first + (1.0 - beta_one) * grad
    second_new = beta_two * second + (1.0 - beta_two) * grad * grad
    root = jnp.sqrt(second_new * (1.0 / (1.0 - beta_two**STEP)))
    update = first_new * (1.0 / (1.0 - beta_one**STEP)) / (root + adam_eps) + decay_rate * weight
    return (first_new, second_new, update)


def rows_sum(values):
    return jnp.sum(values, axis=0, keepdims=True)


def lanes_sum(values):
    total = rows_sum(values)
    lanes = total[:, 0:LANES]
    for tile in range(1, values.shape[1] // LANES):
        lanes = lanes + total[:, cols(tile)]
    return lanes


def fetch(sums, base, stride, start, count, number):
    return jnp.concatenate(
        [sums[pl.ds(base + tile * stride + start, count), :].astype(f32) for tile in range(number)], axis=1
    )


def spread_of(update, mean, length):
    def step(start, kept):
        away = update[pl.ds(start, LAMB_ROWS), :] - mean
        return kept + fold(away * away)

    return rows_sum(each_rows(length, step, jnp.zeros((8, update.shape[1]), f32), LAMB_ROWS))


def half_update(sums, base, stride, weights, a_ref, b_ref, x_ref, y_ref, u_ref):
    length, chans = weights.shape
    zero = jnp.zeros((8, chans), f32)

    def step(start, kept):
        here = pl.ds(start, LAMB_ROWS)
        grad = fetch(sums, base, stride, start, LAMB_ROWS, chans // LANES)
        weight = weights[here, :]
        first, second, update = lamb_moments(weight, grad, a_ref[here, :], b_ref[here, :])
        x_ref[here, :] = first
        y_ref[here, :] = second
        u_ref[here, :] = update
        return (
            kept[0] + fold(weight * weight), kept[1] + fold(update * update), kept[2] + fold(update)
        )

    return each_rows(length, step, (zero, zero, zero), LAMB_ROWS)


def early_kernel(
    sums, w_out, a_out, b_out, w_gate, a_gate, b_gate,
    x_out, y_out, x_gate, y_gate, u_gate, u_out, norms, stats,
    *, need, save,
):
    width, chans = w_gate.shape
    tiles = width // LANES
    norms[...] = jnp.zeros(norms.shape, f32)
    zero = jnp.zeros((8, width), f32)
    need(w_out, a_out, b_out)

    def one_out(start, kept):
        here = pl.ds(start, LAMB_ROWS)
        grad = fetch(sums, 0, chans, start, LAMB_ROWS, tiles)
        weight = w_out[here, :]
        first, second, update = lamb_moments(weight, grad, a_out[here, :], b_out[here, :])
        x_out[here, :] = first
        y_out[here, :] = second
        u_out[here, :] = update
        return (kept[0] + fold(weight * weight), kept[1] + fold(update * update))

    weight_sq, update_sq = each_rows(chans, one_out, (zero, zero), LAMB_ROWS)
    norms[1:2, :] = lanes_sum(weight_sq)
    norms[7:8, :] = lanes_sum(update_sq)
    save(x_out, y_out, u_out)
    need()
    weight_sq, update_sq, total = half_update(
        sums, chans * tiles, width, w_gate, a_gate, b_gate, x_gate, y_gate, u_gate
    )
    norms[0:1, :] = lanes_sum(weight_sq)
    norms[6:7, :] = lanes_sum(update_sq)
    save(x_gate, y_gate, u_gate)
    gate_mean = rows_sum(total) / width
    stats[0:1, :] = gate_mean
    stats[1:2, :] = spread_of(u_gate, gate_mean, width)
    ones = jnp.ones((8, width), f32)
    out_all = u_out[...]
    out_mean = jnp.sum(out_all, axis=1, keepdims=True) / width
    away = out_all - out_mean
    stats[2:3, :] = dot(ones, out_all, NT, HIGH)[0:1] / width
    stats[3:4, :] = dot(ones, away * away, NT, HIGH)[0:1]
    stats[4:8, :] = jnp.zeros((4, chans), f32)


def late_kernel(
    sums, early_norms, early_stats, *rest, need, save
):
    small_in, (a_mix, b_mix), rest = rest[:8], rest[8:10], rest[10:]
    x_mix, y_mix, x_xp, y_xp, x_dt, y_dt, x_cv, y_cv, x_cp, y_cp, *rest = rest
    u_mix, u_xp, u_dt, u_cv, u_cp, norms, stats, w_xp, w_dt, w_cv, w_cp, w_mix, *_ = rest
    a_xp, b_xp, a_dt, b_dt, a_cv, b_cv, a_cp, b_cp = small_in
    width, chans = w_mix.shape
    tiles = chans // LANES
    base = tiles * width
    need(early_norms, early_stats, *small_in, w_xp, w_dt, w_cv, w_cp)
    norms[...] = early_norms[...]
    stats[...] = early_stats[...]

    def small(place, items, weight, a_ref, b_ref, x_ref, y_ref, u_ref):
        weight_sq, update_sq = jnp.zeros((1, LANES), f32), jnp.zeros((1, LANES), f32)
        for index, grad in enumerate(items):
            held = weight[index]
            first, second, update = lamb_moments(held, grad, a_ref[index], b_ref[index])
            x_ref[index] = first
            y_ref[index] = second
            u_ref[index] = update
            weight_sq = weight_sq + lanes_sum(held * held)
            update_sq = update_sq + lanes_sum(update * update)
        norms[place : place + 1, :] = weight_sq
        norms[6 + place : 7 + place, :] = update_sq

    rows = w_xp.shape[1]
    grads = fetch(sums, base, 2 * rows, 0, 2 * rows, tiles)
    small(2, [grads[:rows], grads[rows:]], w_xp, a_xp, b_xp, x_xp, y_xp, u_xp)
    base += 2 * rows * tiles
    rank = w_dt.shape[1]
    grads = fetch(sums, base, 2 * rank, 0, 2 * rank, tiles)
    small(3, [grads[:rank], grads[rank:]], w_dt, a_dt, b_dt, x_dt, y_dt, u_dt)
    base += 2 * rank * tiles
    grads = fetch(sums, base, 48, 0, 48, tiles)
    taps = w_cv.shape[1]
    small(4, [grads[:taps], grads[taps : 2 * taps]], w_cv, a_cv, b_cv, x_cv, y_cv, u_cv)
    entries = w_cp.shape[0]
    items = [grads[2 * (taps + entry) : 2 * (taps + entry) + 2] for entry in range(entries)]
    small(5, items, w_cp, a_cp, b_cp, x_cp, y_cp, u_cp)
    for tile in range(tiles):
        norms[12 + tile : 13 + tile, :] = grads[46:47, cols(tile)]
    save()
    need(a_mix, b_mix, w_mix)
    weight_sq, update_sq, total = half_update(
        sums, 0, width, w_mix, a_mix, b_mix, x_mix, y_mix, u_mix
    )
    norms[0:1, :] += lanes_sum(weight_sq)
    norms[6:7, :] += lanes_sum(update_sq)
    mix_mean = rows_sum(total) / width
    stats[4:5, :] = mix_mean


def spread_kernel(u_mix, stats, spread, *, need, save):
    spread[...] = jnp.broadcast_to(spread_of(u_mix, stats[4:5, :], u_mix.shape[0]), spread.shape)


def apply_out_kernel(norms_own, norms_far, w_out, u_out, n_out, c_out, *, need, save):
    chans = w_out.shape[0]
    need(norms_own)
    sums = jnp.sum(norms_own[...] + norms_far[...], axis=1, keepdims=True)
    scale = learn_rate * jnp.sqrt(sums[1:2]) / (jnp.sqrt(sums[7:8]) + adam_eps)
    need()

    def one_out(start, held):
        here = pl.ds(start, LAMB_ROWS)
        fresh = w_out[here, :] - scale * u_out[here, :]
        n_out[here, :] = fresh
        c_out[here, :] = fresh.astype(bf16)
        return held

    each_rows(chans, one_out, 0, LAMB_ROWS)


def apply_kernel(
    norms_own, norms_far, stats, mix_spread,
    w_mix, w_gate, w_xp, w_dt, w_cv, w_cp,
    u_mix, u_gate, u_xp, u_dt, u_cv, u_cp,
    gain, gain_first, gain_second, x_mix, y_mix, core, x_given, y_given,
    n_in, c_in, n_xp, c_xp, n_dt, c_dt, n_cv, c_cv, n_cp, c_cp,
    g_first, g_second, g_new, g_copy, norms_out, stats_out, x_in, y_in,
    sems,
    *, need, save,
):
    width, chans = w_mix.shape
    moves = [
        pltpu.make_async_copy(held, target.at[:, 0, :], sems.at[number])
        for number, (held, target) in enumerate(((x_mix, x_in), (y_mix, y_in)))
    ]
    for move in moves:
        move.start()
    half_width = g_new.shape[0]
    me = core[0]
    totals = norms_own[...] + norms_far[...]
    sums = jnp.sum(totals, axis=1, keepdims=True)
    scales = [None]
    for place in range(6):
        weight_norm = jnp.sqrt(sums[place : place + 1])
        update_norm = jnp.sqrt(sums[6 + place : 7 + place])
        scales.append(learn_rate * weight_norm / (update_norm + adam_eps))
        norms_out[0:1, place + 1 : place + 2] = weight_norm
        norms_out[1:2, place + 1 : place + 2] = update_norm

    need(w_mix, w_gate)

    def one_in(start, held):
        here = pl.ds(start, LAMB_ROWS)
        for half, weight, change in ((0, w_mix, u_mix), (1, w_gate, u_gate)):
            fresh = weight[here, :] - scales[1] * change[here, :]
            n_in[half, here, :] = fresh
            c_in[here, half, :] = fresh.astype(bf16)
        return held

    each_rows(width, one_in, 0, LAMB_ROWS)
    save(n_in, c_in)

    need()
    gain_grad = jnp.concatenate(
        [totals[12 + tile : 13 + tile, :] for tile in range(width // LANES)], axis=1
    )
    gain_row = gain[...].reshape(1, width)
    first, second, update = lamb_moments(gain_row, gain_grad, gain_first[...], gain_second[...])
    weight_norm = jnp.sqrt(jnp.sum(gain_row * gain_row, axis=1, keepdims=True))
    update_norm = jnp.sqrt(jnp.sum(update * update, axis=1, keepdims=True))
    norms_out[0:1, 0:1] = weight_norm
    norms_out[1:2, 0:1] = update_norm
    fresh = gain_row - learn_rate * weight_norm / (update_norm + adam_eps) * update

    def own(row):
        return jnp.where(me == 0, row[:, :half_width], row[:, half_width:]).reshape(half_width)

    g_first[...] = own(first)
    g_second[...] = own(second)
    g_new[...] = own(fresh)
    g_copy[...] = own(fresh).astype(bf16)
    for place, weight, change, fresh_ref, copy in (
        (3, w_xp, u_xp, n_xp, c_xp),
        (4, w_dt, u_dt, n_dt, c_dt),
        (5, w_cv, u_cv, n_cv, c_cv),
        (6, w_cp, u_cp, n_cp, c_cp),
    ):
        for index in range(weight.shape[0]):
            fresh = weight[index] - scales[place] * change[index]
            fresh_ref[index] = fresh
            copy[index] = fresh.astype(bf16)
    parts = [
        (scales[1], stats[4:5, :], mix_spread[0:1, :]),
        (scales[1], stats[0:1, :], stats[1:2, :]),
        (scales[2], stats[2:3, :], stats[3:4, :]),
    ]
    means = [scale * part_mean for scale, part_mean, _ in parts]
    mean = (means[0] + means[1] + means[2]) / 3.0
    spread = jnp.zeros_like(mean)
    for (scale, _, squares), part_mean in zip(parts, means):
        gap = part_mean - mean
        spread = spread + scale * scale * squares + width * gap * gap
    stats_out[0:1, :] = mean
    stats_out[1:2, :] = spread / (3.0 * width)
    for move in moves:
        move.wait()


def join_kernel(pieces, copies, *, need, save):
    total = pieces[0].astype(f32)
    for place in range(1, pieces.shape[0]):
        total = total + pieces[place].astype(f32)
    low = total.astype(bf16)
    for place in range(pieces.shape[0]):
        copies[place] = low


def send_pieces(values, dp):
    chunk = values.shape[0] // dp
    return lax.all_to_all(values, "dp", 0, 0, tiled=True).reshape(dp, chunk, LANES)


def join_pieces(pieces):
    copies = call(join_kernel, at("x", shape(pieces.shape, bf16)), at("x", pieces), limit=8)[0]
    return copies.reshape(-1, LANES)


def call(kernel, outs, args, scratch=(), limit=32, micros=1, passed=(), kept=(), aliases=None):
    given = [array for array, _ in args] + [array for array, _ in passed]
    kinds = [kind for _, kind in args] + ["m"] * len(passed)
    n_own = len(outs)
    outs = list(outs)
    for array, kind in passed:
        dims = array.shape if kind == "h" else (array.shape[0], array.shape[-1])
        outs += at("x", shape(dims, array.dtype))
    outs += at("m", *[shape(given[place].shape, given[place].dtype) for place in kept])
    out_kinds = [kind for _, kind in outs]
    fetched = [place for place, kind in enumerate(kinds) if kind in "h01"]
    stored = [place for place, kind in enumerate(out_kinds) if kind in "h12"]

    def staged(array, kind):
        rows, columns = array.shape[0], array.shape[-1]
        dims = {"h": array.shape, "2": (2, rows, columns)}.get(kind, (rows, columns))
        return pltpu.VMEM(dims, array.dtype)

    staging = [staged(given[place], kinds[place]) for place in fetched]
    staging += [staged(outs[place][0], out_kinds[place]) for place in stored]
    moves = max(1, 2 * len(staging) + len(passed) + len(kept))

    def body(*refs):
        ins = list(refs[: len(given)])
        results = list(refs[len(given) : len(given) + len(outs)])
        rest = refs[len(given) + len(outs) :]
        stage, sems, own = rest[: len(staging)], rest[len(staging)], rest[len(staging) + 1 :]
        loads, saves = {}, {}
        for number, place in enumerate(fetched):
            source = ins[place] if kinds[place] == "h" else ins[place].at[:, int(kinds[place]), :]
            loads[id(stage[number])] = pltpu.make_async_copy(source, stage[number], sems.at[number])
            ins[place] = stage[number]
        for load in loads.values():
            load.start()
        for number, place in enumerate(stored, len(fetched)):
            held, target, kind = stage[number], results[place], out_kinds[place]
            parts = [(held, target)]
            if kind == "1":
                parts = [(held, target.at[:, 1, :])]
            if kind == "2":
                parts = [(held.at[half], target.at[:, half, :]) for half in range(2)]
            saves[id(held)] = [
                pltpu.make_async_copy(*pair, sems.at[moves - 1 - 2 * (number - len(fetched)) - half]) for half, pair in enumerate(parts)
            ]
            results[place] = held
        follow = []
        for number in range(len(passed)):
            held = results[n_own + number]
            source, kind = ins[len(args) + number], passed[number][1]
            source = source if kind == "h" else source.at[:, int(kind), :]
            loads[id(held)] = pltpu.make_async_copy(source, held, sems.at[len(staging) + number])
            loads[id(held)].start()
        begun, resting = [], []
        for number, place in enumerate(kept):
            resting.append(
                pltpu.make_async_copy(
                    ins[place], results[n_own + len(passed) + number],
                    sems.at[len(staging) + len(passed) + number],
                )
            )

        def need(*wanted):
            keys = [id(ref) for ref in wanted] or list(loads)
            for key in keys:
                if key in loads and key not in follow:
                    loads.pop(key).wait()
            while follow:
                loads[follow.pop(0)].start()
            while resting:
                begun.append(resting.pop(0))
                begun[-1].start()
            for key in keys:
                if key in loads:
                    loads.pop(key).wait()

        def save(*ready):
            for key in [id(ref) for ref in ready] or list(saves):
                for move in saves.pop(key, ()):
                    move.start()
                    begun.append(move)

        kernel(*ins[: len(args)], *results[: n_own + len(passed)], *own, need=need, save=save)
        need()
        save()
        for move in begun:
            move.wait()

    spaces = {"x": pltpu.VMEM, "s": pltpu.SMEM}
    placed = [
        pltpu.with_memory_space_constraint(array, pltpu.HBM) if kind in "hm01" else array
        for array, kind in zip(given, kinds)
    ]
    return pl.pallas_call(
        body,
        out_shape=[out if kind == "x" else pltpu.HBM(out.shape, out.dtype) for out, kind in outs],
        in_specs=[pl.BlockSpec(memory_space=spaces.get(kind, pltpu.HBM)) for kind in kinds],
        out_specs=[pl.BlockSpec(memory_space=spaces.get(kind, pltpu.HBM)) for kind in out_kinds],
        input_output_aliases=aliases or {},
        scratch_shapes=[*staging, pltpu.SemaphoreType.DMA((moves,)), *scratch],
        compiler_params=pltpu.CompilerParams(vmem_limit_bytes=limit * MB),
        cost_estimate=pl.CostEstimate(flops=micros * 10**9, bytes_accessed=MB, transcendentals=0),
    )(*placed)


def at(kind, *things):
    return [(thing, kind) for thing in things]


def program(
    dp,
    hidden_in, out_cot, segment_ids,
    norm_gain, in_weight, out_weight, xproj_weight, dtproj_weight, conv_weight, chan_params,
    first_norm_gain, first_in_weight, first_out_weight, first_xproj_weight,
    first_dtproj_weight, first_conv_weight, first_chan_params,
    second_norm_gain, second_in_weight, second_out_weight, second_xproj_weight,
    second_dtproj_weight, second_conv_weight, second_chan_params,
):
    tokens, width = hidden_in.shape
    chans = in_weight.shape[2]
    half_width = first_norm_gain.shape[0]
    tiles = chans // LANES
    rank = dtproj_weight.shape[1]
    count = chan_params.shape[1] - 3
    rows = rank + 2 * count
    taps = conv_weight.shape[1]

    def swap(values):
        return lax.ppermute(values, "chan", [(0, 1), (1, 0)])

    me = lax.axis_index("chan")
    core = me.astype(jnp.int32).reshape(1)
    cot_own = out_cot.T
    cot_far = swap(cot_own)
    moments_own = jnp.stack([first_norm_gain, second_norm_gain])
    moments_far = swap(moments_own)
    moments_gain = jnp.where(
        me == 0,
        jnp.concatenate([moments_own, moments_far], 1),
        jnp.concatenate([moments_far, moments_own], 1),
    )

    def flip(values):
        return jnp.swapaxes(values, 1, 2)

    def turn(values):
        return jnp.swapaxes(values, 0, 1)

    w_xp = flip(xproj_weight)
    w_cp = turn(chan_params)
    square = (tokens, chans)
    z = Sizes(tokens, chans, count, rank)
    smem = at("s", core)

    def padded_rows(amount):
        return -(-amount // (dp * 16)) * 16 * dp

    mixing, gate, conv_pre, part, normed, low_in, same, near_cp, near_dt, near_cot, near_out = call(
        front_kernel,
        at("h", shape(square, f32))
        + at("x", shape(square, f32), shape((2,) + square, f32), shape((2 * rows, tokens), f32))
        + at("h", shape((tokens, width), bf16), shape((2, width, chans), bf16))
        + at("x", shape((2, tokens, LANES), f32)),
        at("h", hidden_in, norm_gain) + at("0", in_weight) + at("1", in_weight)
        + at("h", segment_ids, conv_weight, w_xp),
        [pltpu.VMEM((tokens + 16, chans), f32), pltpu.VMEM((tokens + 16, LANES), f32)],
        limit=14, micros=6, passed=at("h", w_cp, dtproj_weight, cot_own, out_weight),
    )
    part_far = swap(part)
    act = call(
        activate_kernel, at("x", shape((2,) + square, f32)), at("x", conv_pre), limit=4, micros=1
    )[0]
    early_rows = padded_rows(tiles * width + (width // LANES) * chans)
    (
        states, proj, grad_maps, skips, far_step, grad_y, pre_step, inflow_low, gate_low, branch_low, early,
        conv_kept,
    ) = forward_call(
        at("x", part, part_far, near_cp, near_dt, near_cot, cot_far, near_out)
        + at("x", conv_pre, act, gate, same) + at("h", normed) + smem,
        z, early_rows, half_width, (7,),
    )
    early_pieces = send_pieces(early, dp)
    grad_part, grad_act, grad_dt, grad_chan = backward_call(
        at("m", states) + at("h", w_cp, proj, far_step, grad_y, inflow_low, pre_step, conv_kept)
        + at("h", grad_maps, skips, dtproj_weight),
        z,
    )
    early_copies, grad_part = lax.optimization_barrier((join_pieces(early_pieces), grad_part))
    early_sums = lax.all_to_all(early_copies, "dp", 0, 0, tiled=True)
    grad_far = swap(grad_part)
    late_rows = padded_rows(tiles * (width + 2 * rows + 2 * rank + 48))
    late, in_own, in_send, out_own, out_send = call(
        back_kernel,
        at("x", shape((late_rows, LANES), bf16))
        + at("h", shape((half_width + 8, tokens), f32))
        + at("x", shape((half_width + 8, tokens), f32))
        + at("h", shape((half_width, tokens), f32))
        + at("x", shape((half_width, tokens), f32)),
        at("x", grad_part, grad_far)
        + at("h", segment_ids, w_xp, conv_weight, mixing, conv_kept) + at("x", grad_act, grad_chan)
        + at("h", normed, gate_low, low_in, hidden_in, norm_gain) + at("x", grad_dt)
        + at("h", branch_low, out_weight)
        + smem,
        [
            pltpu.VMEM((tokens + 16, chans), f32), pltpu.VMEM((2, tokens + 16, chans), f32),
            pltpu.VMEM((tokens + 16, LANES), f32), pltpu.VMEM(square, bf16),
            pltpu.VMEM((48, chans), f32), pltpu.VMEM((2,) + square, bf16),
        ],
        limit=20, micros=2,
    )
    in_far = swap(in_send)
    out_far = swap(out_send)
    late, early_sums = lax.optimization_barrier((late, early_sums))
    late_pieces = send_pieces(late, dp)
    output, input_grad = call(
        outputs_kernel,
        at("h", shape((half_width, tokens), bf16), shape((half_width, tokens), f32)),
        at("h", hidden_in, cot_own, out_own) + at("x", out_far) + at("h", in_own) + at("x", in_far) + smem,
        limit=16, micros=3,
    )
    firsts = [first_xproj_weight, first_dtproj_weight, first_conv_weight, first_chan_params]
    seconds = [second_xproj_weight, second_dtproj_weight, second_conv_weight, second_chan_params]
    for group in (firsts, seconds):
        group[0], group[3] = flip(group[0]), turn(group[3])
    weights = [w_xp, dtproj_weight, conv_weight, w_cp]
    half = shape((width, chans), f32)
    whole_in, whole_out = shape(in_weight.shape, f32), shape(out_weight.shape, f32)
    x_out, y_out, x_in, y_in, u_gate, u_out, early_norms, early_stats = call(
        early_kernel,
        at("h", whole_out, whole_out) + at("1", whole_in, whole_in)
        + at("h", half, whole_out, shape((16, LANES), f32), shape((8, chans), f32)),
        at("x", early_sums) + at("h", out_weight, first_out_weight, second_out_weight)
        + at("1", in_weight, first_in_weight, second_in_weight),
        limit=12, micros=5,
    )
    late_copies, output, input_grad = lax.optimization_barrier((join_pieces(late_pieces), output, input_grad))
    late_sums = lax.all_to_all(late_copies, "dp", 0, 0, tiled=True)
    n_out, c_out = call(
        apply_out_kernel, at("h", whole_out, shape(whole_out.shape, bf16)),
        at("h", early_norms) + at("x", swap(early_norms)) + at("h", out_weight, u_out),
        limit=8, micros=2,
    )
    late_sums, n_out, c_out = lax.optimization_barrier((late_sums, n_out, c_out))
    shapes = [shape(tensor.shape, f32) for tensor in weights]
    late_outs = []
    for entry in shapes:
        late_outs += [entry, entry]
    moments_in = [tensor for pair in zip(firsts, seconds) for tensor in pair]
    got = call(
        late_kernel,
        at("x", half, half) + at("h", *late_outs)
        + at("x", half, *shapes, shape((16, LANES), f32), shape((8, chans), f32)),
        at("x", late_sums) + at("h", early_norms, early_stats, *moments_in)
        + at("0", first_in_weight, second_in_weight),
        limit=12, micros=5,
        passed=at("h", *weights) + at("0", in_weight) + at("1", in_weight) + at("h", u_gate),
    )
    moments, updates, norms, stats, kept = got[:10], got[10:15], got[15], got[16], got[17:]
    kept_small, (kept_mix, kept_gate, changed_gate) = kept[0:4], kept[4:]
    norms_far = swap(norms)
    mix_spread = call(
        spread_kernel, at("x", shape((8, chans), f32)), at("x", updates[0], stats), limit=8, micros=1
    )[0]
    pairs = []
    for entry in [whole_in, *shapes]:
        pairs += [entry, shape(entry.shape, bf16)]
    row = shape((half_width,), f32)
    whole_low = shape(whole_in.shape, bf16)
    done = call(
        apply_kernel,
        at("2", whole_in) + at("h", whole_low)
        + at(
            "h", *pairs[2:], row, row, row, shape((half_width,), bf16), shape((2, 7), f32),
            shape((2, chans), f32),
        )
        + at("m", whole_in, whole_in),
        at("x", norms, norms_far, stats, mix_spread, kept_mix, kept_gate, *kept_small, updates[0], changed_gate, *updates[1:])
        + at("h", norm_gain) + at("x", moments_gain[0:1], moments_gain[1:2], moments[0], moments[1])
        + smem + at("m", x_in, y_in),
        [pltpu.SemaphoreType.DMA((2,))],
        limit=14, micros=5, aliases={22: 16, 23: 17},
    )
    flat = list(done[10:14])
    firsts_out = [done[16], x_out, *moments[2::2]]
    seconds_out = [done[17], y_out, *moments[3::2]]
    fresh = [done[0], n_out, *done[2:10:2]]
    copied = [done[1], c_out, *done[3:10:2]]
    for place in range(6):
        entry = [firsts_out[place], seconds_out[place], fresh[place], copied[place]]
        if place == 2:
            entry = [flip(tensor) for tensor in entry]
        if place == 5:
            entry = [turn(tensor) for tensor in entry]
        flat += entry
    return (output.T, input_grad.T, *flat, done[14].T, done[15])


def solution(mesh):
    rows = P("dp", None)
    cells = P("dp", "chan")
    last = P(None, None, "chan")
    first = P("chan", None)
    middle = P(None, "chan", None)
    tensors = (last, first, middle, last, last, last)
    outs = [cells, cells] + [P("chan")] * 4
    for spec in tensors:
        outs += [spec] * 4
    return jax.shard_map(
        functools.partial(program, mesh.shape["dp"]),
        mesh=mesh,
        in_specs=(rows, cells, P("dp"), P(), *tensors, P("chan"), *tensors, P("chan"), *tensors),
        out_specs=(*outs, P(), P(None, "chan")),
        check_vma=False,
    )
```

```python
import functools

import jax
import jax.numpy as jnp
from jax import lax
from jax.experimental import pallas as pl
from jax.experimental.pallas import tpu as pltpu
from jax.sharding import PartitionSpec as P

STEP = 4
norm_eps = 1e-06
beta_one = 0.5
beta_two = 0.5
adam_eps = 1e-06
decay_rate = 0.01
learn_rate = 0.3
LOG2E = 1.4426950408889634
FAR = 1e30
FLOOR = -1e-26

f32 = jnp.float32
bf16 = jnp.bfloat16
HIGH = lax.Precision.HIGHEST
LANES = 128
ROWS = 16
NORM_ROWS = 192
CONV_ROWS = 96
LAMB_ROWS = 32
MB = 1 << 20


def dot(left, right, dims, precision=None):
    return lax.dot_general(
        left, right, (dims, ((), ())), precision=precision, preferred_element_type=f32
    )


NN = ((1,), (0,))
TN = ((0,), (0,))
NT = ((1,), (1,))


def sigmoid(values):
    return lax.logistic(values)


def silu_slope(values, sigma):
    return sigma * (1.0 + values * (1.0 - sigma))


def softplus(values):
    return jnp.maximum(values, 0.0) + jnp.log1p(jnp.exp(-jnp.abs(values)))


def wide(tile, times):
    return jnp.concatenate([tile] * times, axis=1)


def fold(values):
    total = values[0:8]
    for start in range(8, values.shape[0], 8):
        total = total + values[start : start + 8]
    return total


def shape(dims, dtype):
    return jax.ShapeDtypeStruct(dims, dtype)


def each_rows(length, body, carry=None, rows=ROWS):
    def step(index, held):
        return body(pl.multiple_of(index * rows, rows), held)

    return lax.fori_loop(0, length // rows, step, carry)


def spread_segments(numbers, tokens):
    across = lax.broadcasted_iota(jnp.int32, (tokens, tokens), 0)
    along = lax.broadcasted_iota(jnp.int32, (tokens, tokens), 1)
    row = numbers.astype(f32).reshape(1, tokens)
    picked = jnp.where(across == along, row, 0.0).astype(bf16)
    return dot(picked, jnp.ones((tokens, LANES), bf16), NN)


def front_kernel(
    hid, gain, w_mix, w_gate, seg, taps, w_xp,
    mix_out, gate_out, conv_out, part_out, norm_out, low_out, same_out, params, near_dt, near_cot, near_out,
    padded, sgpad,
    *, need, save,
):
    tokens, width = hid.shape
    chans = mix_out.shape[1]
    tiles = chans // LANES

    need(hid, gain)
    gain_row = gain[...].reshape(1, width)

    def normalise(start, held):
        source = hid[pl.ds(start, NORM_ROWS), :].astype(f32)
        scale = lax.rsqrt(jnp.sum(source * source, axis=1, keepdims=True) / width + norm_eps)
        norm_out[pl.ds(start, NORM_ROWS), :] = (source * scale * gain_row).astype(bf16)
        return held

    each_rows(tokens, normalise, 0, NORM_ROWS)
    save(norm_out)
    need(w_mix, w_gate)
    low_out[0] = w_mix[...].astype(bf16)
    low_out[1] = w_gate[...].astype(bf16)
    save(low_out)
    normed = norm_out[...]
    mixing = dot(normed, low_out[0], NN)
    mix_out[...] = mixing
    padded[0:8, :] = jnp.zeros((8, chans), f32)
    padded[pl.ds(8, tokens), :] = mixing
    padded[pl.ds(8 + tokens, 8), :] = jnp.zeros((8, chans), f32)
    save(mix_out)
    gate_out[...] = dot(normed, low_out[1], NN)
    need(seg, taps, w_xp, params)
    numbers = spread_segments(seg[...], tokens)
    sgpad[0:8, :] = jnp.full((8, LANES), -1.0, f32)
    sgpad[pl.ds(8, tokens), :] = numbers
    sgpad[pl.ds(8 + tokens, 8), :] = jnp.full((8, LANES), -1.0, f32)
    width_taps = taps.shape[1]

    def convolve(start, held):
        window = padded[pl.ds(start, CONV_ROWS + 16), :]
        marks = sgpad[pl.ds(start, CONV_ROWS + 16), :]
        own = marks[8 : 8 + CONV_ROWS]
        base = window[8 : 8 + CONV_ROWS]
        for heading in range(2):
            total = params[0, heading : heading + 1, :] + taps[heading, 0:1, :] * base
            for offset in range(1, width_taps):
                begin = 8 - offset if heading == 0 else 8 + offset
                same = jnp.where(marks[begin : begin + CONV_ROWS] == own, 1.0, 0.0)
                if offset == 1:
                    same_out[heading, pl.ds(start, CONV_ROWS), :] = same
                moved = window[begin : begin + CONV_ROWS]
                total = total + taps[heading, offset : offset + 1, :] * moved * wide(same, tiles)
            conv_out[heading, pl.ds(start, CONV_ROWS), :] = total
        return held

    each_rows(tokens, convolve, 0, CONV_ROWS)
    for heading in range(2):
        pre = conv_out[heading]
        act_low = (pre * sigmoid(pre)).astype(bf16)
        rows = w_xp.shape[1]
        part_out[heading * rows : (heading + 1) * rows, :] = dot(
            w_xp[heading].astype(bf16), act_low, NT
        )


SPAN = 128


class Sizes:
    def __init__(self, tokens, chans, count, rank):
        self.tokens, self.chans, self.count, self.rank = tokens, chans, count, rank
        self.tiles = chans // LANES
        self.blocks = tokens // LANES
        self.rows = rank + 2 * count
        self.block_rows = LANES * count
        self.pairs = [(heading, tile) for heading in range(2) for tile in range(self.tiles)]

    def base(self, heading, tile):
        return (heading * self.tiles + tile) * self.tokens

    def row(self, ref, heading, tile, at):
        return ref[pl.ds(self.base(heading, tile) + at, 1), :]

    def whole(self, ref, heading):
        starts = [self.base(heading, tile) for tile in range(self.tiles)]
        return jnp.concatenate([ref[start : start + self.tokens, :] for start in starts], axis=1)


def cols(tile):
    return slice(tile * LANES, (tile + 1) * LANES)


def split(values):
    high = values.astype(bf16)
    return high, (values - high.astype(f32)).astype(bf16)


def group_maps(target, tile, heading, count):
    groups = tile.shape[1] // count
    for group in range(groups):
        block, place = divmod(group * count, LANES)
        own = tile[:, cols(block)]
        if place:
            own = pltpu.roll(own, LANES - place, 1)
        target[heading, group] = own


def diagonal_maps(target, tile, heading, count):
    tokens = tile.shape[1]
    squared = count * count
    lane = lax.broadcasted_iota(jnp.int32, (count, squared), 1)
    row = lax.broadcasted_iota(jnp.int32, (count, squared), 0)
    repeat = jnp.where(lane % count == row, 1.0, 0.0).astype(bf16)
    token = lax.broadcasted_iota(jnp.int32, (tokens, squared), 0)
    place = lax.broadcasted_iota(jnp.int32, (tokens, squared), 1)
    mine = place // count == token % count
    for number, part in enumerate(split(tile)):
        spread = jnp.where(mine, dot(part, repeat, TN), 0.0).astype(bf16)
        target[heading, :, number] = spread.reshape(tokens // count, count, squared)


def weigh_states(left, maps):
    half = maps.shape[0] // 2
    got = dot(maps, left, NN)
    return got[:half] + got[half:]


def gather_states(left, right, count):
    products = dot(left, right, NT)
    lane = lax.broadcasted_iota(jnp.int32, (count, count), 1)
    total = products[0:count]
    for place in range(1, count):
        total = jnp.where(lane == place, products[place * count : (place + 1) * count], total)
    return total


def dot3(left, right, dims):
    (left_high, left_low), (right_high, right_low) = split(left), split(right)
    if dims == TN:
        lefts = jnp.concatenate([left_high, left_low, left_high], axis=0)
        return dot(lefts, jnp.concatenate([right_high, right_high, right_low], axis=0), dims)
    rows = left.shape[0]
    both = dot(jnp.concatenate([left_high, left_low], axis=0), right_high, dims)
    return both[:rows] + both[rows:] + dot(left_high, right_low, dims)


class Sweep:
    def __init__(self, z, turned, stages):
        self.z, self.turned, self.stages = z, turned, stages
        self.stage_rows = z.tokens * z.count // stages
        self.groups = z.tokens // z.count
        self.stage_groups = self.groups // stages

    def group(self, order, heading):
        return self.groups - 1 - order if heading == self.turned else order

    def block(self, stage, heading):
        return self.stages - 1 - stage if heading == self.turned else stage

    def inner(self, ahead, heading):
        return self.z.count - 1 - ahead if heading == self.turned else ahead

    def rows(self, group):
        return pl.ds(pl.multiple_of(group * self.z.count, self.z.count), self.z.count)

    def run(self, z, carried, scan, post, between):
        def step(index, held):
            order = 2 * index
            post(jnp.maximum(order - 1, 0), 1)
            held = scan(order, held, 0)
            post(order, 0)
            return scan(order + 1, held, 1)

        per = self.stage_groups // 2
        for stage in range(self.stages):
            between(stage, True)
            carried = lax.fori_loop(stage * per, (stage + 1) * per, step, carried)
            between(stage, False)
        post(self.groups - 1, 1)
        return carried


def store_gathered(target, target_row, gathered, heading, z):
    per = LANES // z.count
    for block in range(z.blocks):
        pieces = [gathered[heading, block * per + place] for place in range(per)]
        target[target_row : target_row + z.count, cols(block)] = jnp.concatenate(pieces, axis=1)


def fill_rates(rates, params, count):
    for heading in range(2):
        for n in range(count):
            value = -jnp.exp(params[3 + n, heading : heading + 1, :])
            rates[heading, n : n + 1, :] = jnp.minimum(value, FLOOR)


def activate_kernel(conv_pre, act, *, need, save):
    for heading in range(2):
        for tile in range(conv_pre.shape[2] // LANES):

            def activate(start, held, heading=heading, tile=tile):
                here = pl.ds(start, SPAN)
                pre = conv_pre[heading, here, cols(tile)]
                act[heading, here, cols(tile)] = pre * sigmoid(pre)
                return held

            each_rows(conv_pre.shape[1], activate, 0, SPAN)


def forward_kernel(
    own_part, far_part, params, w_dt, cot_own, cot_far, w_out, conv_pre, act, gate, same, normed, core,
    states_out, proj, grad_maps, skips, far_step, grad_y, pre_step, inflow_low, gate_low, branch_low, early,
    grad_branch, inflow, grad_y_low, result, maps, diagonal, gathered, states, low_one, low_two,
    rates, sems,
    *, need, save,
):
    tokens, chans = gate.shape
    z = Sizes(tokens, chans, params.shape[0] - 3, w_dt.shape[1])
    count, rank, rows, tiles = z.count, z.rank, z.rows, z.tiles
    half_width = cot_own.shape[0]
    width = 2 * half_width
    me = core[0]
    sweep = Sweep(z, 1, sems.shape[1])
    lows = (low_one, low_two)

    proj[...] = own_part[...] + far_part[...]
    save(proj)
    for heading in range(2):
        first = heading * rows + rank
        group_maps(maps, proj[first : first + count, :], heading, count)
        diagonal_maps(diagonal, proj[first + count : first + 2 * count, :], heading, count)
    need(params, w_dt)
    fill_rates(rates, params, count)
    for heading in range(2):
        pre_step[heading] = (
            dot3(proj[heading * rows : heading * rows + rank, :], w_dt[heading], TN)
            + params[1, heading : heading + 1, :]
        )
    save(pre_step)
    need(w_out, cot_own)
    low_out = w_out[...].astype(bf16)
    low_cot = jnp.where(
        me == 0,
        jnp.concatenate([cot_own[...].astype(f32), cot_far[...].astype(f32)], 0),
        jnp.concatenate([cot_far[...].astype(f32), cot_own[...].astype(f32)], 0),
    ).astype(bf16)
    grad_branch[...] = dot(low_cot, low_out, ((0,), (1,)))

    for tile in range(tiles):

        def prepare(start, held, tile=tile):
            here = pl.ds(start, SPAN)
            for heading in range(2):
                size = softplus(pre_step[heading, here, cols(tile)])
                there = pl.ds(z.base(heading, tile) + start, SPAN)
                entering = size * act[heading, here, cols(tile)]
                inflow[there, :] = entering
                inflow_low[heading, here, cols(tile)] = entering.astype(bf16)
                far_step[there, :] = jnp.where(same[heading, here, :] > 0.5, size * LOG2E, FAR)
            gated = gate[here, cols(tile)]
            back = grad_branch[here, cols(tile)] * (gated * sigmoid(gated))
            grad_y[pl.ds(z.base(0, tile) + start, SPAN), :] = back
            grad_y_low[here, cols(tile)] = back.astype(bf16)
            return held

        each_rows(tokens, prepare, 0, SPAN)
    save(far_step, inflow_low, grad_y)

    blank = jnp.zeros((count, LANES), f32)
    states[0, 0:count, :] = jnp.zeros((count, chans), bf16)
    states[1, tokens * count : (tokens + 1) * count, :] = jnp.zeros((count, chans), bf16)
    low_two[...] = jnp.zeros(low_two.shape, bf16)
    speeds = [rates[heading, :, cols(tile)] for heading, tile in z.pairs]

    def scan(order, carried, slot):
        carried = list(carried)
        enters = [maps[heading, sweep.group(order, heading)] for heading in range(2)]
        for heading in range(2):
            for ahead in range(count):
                inner = sweep.inner(ahead, heading)
                at = sweep.group(order, heading) * count + inner
                kept = pl.multiple_of((at + (1 if heading == 0 else 0)) * count, count)
                enter = jnp.broadcast_to(enters[heading][:, inner : inner + 1], (count, LANES))
                for tile in range(tiles):
                    number = heading * tiles + tile
                    decay = jnp.exp2(z.row(far_step, heading, tile, at) * speeds[number])
                    state = decay * carried[number] + enter * z.row(inflow, heading, tile, at)
                    carried[number] = state
                    low = state.astype(bf16)
                    states[heading, pl.ds(kept, count), cols(tile)] = low
                    lows[slot][heading, inner * count : (inner + 1) * count, cols(tile)] = low
        return tuple(carried)

    def post(order, slot):
        for heading in range(2):
            group = sweep.group(order, heading)
            left = lows[slot][heading]
            gathered[heading, group] = gather_states(left, grad_y_low[sweep.rows(group), :], count)
            result[heading, sweep.rows(group), :] = weigh_states(
                left, diagonal[heading, group].reshape(2 * count, count * count)
            )

    keeps = []

    def between(stage, before):
        if before:
            return
        for heading in range(2):
            begin, extent = sweep.block(stage, heading) * sweep.stage_rows, sweep.stage_rows
            if stage == 0:
                extent += count
            elif heading == 0:
                begin += count
            piece = pl.ds(begin, extent)
            keep = pltpu.make_async_copy(
                states.at[heading, piece, :], states_out.at[heading, piece, :], sems.at[heading, stage]
            )
            keep.start()
            keeps.append(keep)

    sweep.run(z, (blank,) * len(z.pairs), scan, post, between)
    for heading in range(2):
        store_gathered(grad_maps, heading * count, gathered, heading, z)
    skips[...] = jnp.zeros(skips.shape, f32)
    for tile in range(tiles):

        def finish(start, held, tile=tile):
            here = pl.ds(start, SPAN)
            total = jnp.zeros((SPAN, LANES), f32)
            sums = []
            back = grad_y[pl.ds(z.base(0, tile) + start, SPAN), :]
            for heading in range(2):
                active = act[heading, here, cols(tile)]
                total = total + result[heading, here, cols(tile)]
                total = total + params[2, heading : heading + 1, cols(tile)] * active
                sums.append(held[heading] + fold(back * active))
            gated = gate[here, cols(tile)]
            sigma = sigmoid(gated)
            branch_low[here, cols(tile)] = (total * (gated * sigma)).astype(bf16)
            gate_low[here, cols(tile)] = (
                grad_branch[here, cols(tile)] * total * silu_slope(gated, sigma)
            ).astype(bf16)
            return tuple(sums)

        sums = each_rows(tokens, finish, (jnp.zeros((8, LANES), f32),) * 2, SPAN)
        for heading in range(2):
            skips[heading : heading + 1, cols(tile)] = jnp.sum(sums[heading], axis=0, keepdims=True)
    save(gate_low, branch_low, grad_maps, skips)
    need()
    branch = branch_low[...]
    grad_w = dot(branch, low_cot, ((0,), (1,))).astype(bf16)
    for tile in range(width // LANES):
        early[tile * chans : (tile + 1) * chans, :] = grad_w[:, cols(tile)]
    base_row = chans * (width // LANES)
    grad_w = dot(normed[...], gate_low[...], TN).astype(bf16)
    for tile in range(tiles):
        early[base_row + tile * width : base_row + (tile + 1) * width, :] = grad_w[:, cols(tile)]
    base_row += tiles * width
    if early.shape[0] > base_row:
        early[base_row:, :] = jnp.zeros((early.shape[0] - base_row, LANES), bf16)
    for keep in keeps:
        keep.wait()


def backward_kernel(
    states_in, params, proj, far_step, grad_y, inflow_low, pre_step, conv_pre, grad_maps, skips, w_dt,
    grad_part, grad_act, grad_dt, grad_chan,
    result, decayed, maps, diagonal, gathered, states, low_one, low_two, products_one, products_two, rates, sems,
    *, need, save,
):
    _, tokens, chans = conv_pre.shape
    z = Sizes(tokens, chans, params.shape[0] - 3, w_dt.shape[1])
    count, rank, rows, tiles = z.count, z.rank, z.rows, z.tiles
    sweep = Sweep(z, 0, sems.shape[1])
    lows, products = (low_one, low_two), (products_one, products_two)
    loads = {}
    for stage in range(sweep.stages):
        for heading in range(2):
            begin = sweep.block(stage, heading) * sweep.stage_rows + (count if heading == 1 else 0)
            piece = pl.ds(begin, sweep.stage_rows)
            load = pltpu.make_async_copy(
                states_in.at[heading, piece, :], states.at[heading, piece, :], sems.at[heading, stage]
            )
            load.start()
            loads[stage, heading] = load
    need(params, proj)
    fill_rates(rates, params, count)
    for heading in range(2):
        first = heading * rows + rank
        group_maps(maps, proj[first + count : first + 2 * count, :], heading, count)
        diagonal_maps(diagonal, proj[first : first + count, :], heading, count)
    for low in (low_two, products_two):
        low[...] = jnp.zeros(low.shape, bf16)
    blank = jnp.zeros((count, LANES), f32)
    speeds = [rates[heading, :, cols(tile)] for heading, tile in z.pairs]

    def scan(order, held, slot):
        waiting = list(held[: len(z.pairs)])
        totals = list(held[len(z.pairs) :])
        leaves = [maps[heading, sweep.group(order, heading)] for heading in range(2)]
        for heading in range(2):
            for ahead in range(count):
                inner = sweep.inner(ahead, heading)
                at = sweep.group(order, heading) * count + inner
                prior = pl.multiple_of((at + (0 if heading == 0 else 1)) * count, count)
                leave = jnp.broadcast_to(leaves[heading][:, inner : inner + 1], (count, LANES))
                here = slice(inner * count, (inner + 1) * count)
                for tile in range(tiles):
                    number = heading * tiles + tile
                    size = z.row(far_step, heading, tile, at)
                    decay = jnp.exp2(size * speeds[number])
                    grad = leave * z.row(grad_y, 0, tile, at) + waiting[number]
                    lead = decay * grad
                    waiting[number] = lead
                    slope = lead * states[heading, pl.ds(prior, count), cols(tile)].astype(f32)
                    totals[number] = totals[number] + slope * size
                    products[slot][heading, here, cols(tile)] = (slope * speeds[number]).astype(bf16)
                    lows[slot][heading, here, cols(tile)] = grad.astype(bf16)
        return tuple(waiting + totals)

    lane = lax.broadcasted_iota(jnp.int32, (count, count * count), 1)
    row = lax.broadcasted_iota(jnp.int32, (count, count * count), 0)
    ones = jnp.where(lane // count == row, 1.0, 0.0).astype(bf16)

    def post(order, slot):
        for heading in range(2):
            group = sweep.group(order, heading)
            left = lows[slot][heading]
            gathered[heading, group] = gather_states(left, inflow_low[heading, sweep.rows(group), :], count)
            result[heading, sweep.rows(group), :] = weigh_states(
                left, diagonal[heading, group].reshape(2 * count, count * count)
            )
            decayed[heading, sweep.rows(group), :] = dot(ones, products[slot][heading], NN)

    def between(stage, before):
        if before:
            if stage == 0:
                need(far_step, grad_y, inflow_low)
            for heading in range(2):
                loads[stage, heading].wait()

    held = sweep.run(z, (blank,) * (2 * len(z.pairs)), scan, post, between)
    for number, (heading, tile) in enumerate(z.pairs):
        slopes = held[len(z.pairs) + number] / LOG2E
        for n in range(count):
            grad_chan[3 + n, heading : heading + 1, cols(tile)] = slopes[n : n + 1] * -jnp.exp(
                params[3 + n, heading : heading + 1, cols(tile)]
            )
    need()
    for heading in range(2):
        first = heading * rows + rank
        store_gathered(grad_part, first, gathered, heading, z)
        grad_part[first + count : first + 2 * count, :] = grad_maps[
            heading * count : (heading + 1) * count, :
        ]

    for tile in range(tiles):

        def close(start, held, tile=tile):
            here = pl.ds(start, SPAN)
            sums = []
            back = grad_y[pl.ds(z.base(0, tile) + start, SPAN), :]
            for heading in range(2):
                pre = conv_pre[heading, here, cols(tile)]
                act = pre * sigmoid(pre)
                passed = result[heading, here, cols(tile)]
                reach = pre_step[heading, here, cols(tile)]
                grad_act[heading, here, cols(tile)] = (
                    passed * softplus(reach) + back * params[2, heading : heading + 1, cols(tile)]
                )
                grad_pre = (decayed[heading, here, cols(tile)] + passed * act) * sigmoid(reach)
                pre_step[heading, here, cols(tile)] = grad_pre
                sums.append(held[heading] + fold(grad_pre))
            return tuple(sums)

        biases = each_rows(tokens, close, (jnp.zeros((8, LANES), f32),) * 2, SPAN)
        for heading in range(2):
            grad_chan[1, heading : heading + 1, cols(tile)] = jnp.sum(
                biases[heading], axis=0, keepdims=True
            )
    save(grad_act)
    for heading in range(2):
        grad_chan[0, heading : heading + 1, :] = jnp.zeros((1, chans), f32)
        grad_chan[2, heading : heading + 1, :] = skips[heading : heading + 1, :]
        grad_pre = pre_step[heading]
        grad_part[heading * rows : heading * rows + rank, :] = dot3(w_dt[heading], grad_pre, NT)
        grad_dt[heading] = dot3(proj[heading * rows : heading * rows + rank, :], grad_pre, NN)


def forward_call(args, sizes, early_rows, half_width, kept, limit=30):
    z = sizes
    square = (z.tokens, z.chans)
    both = (2,) + square
    flat = (2 * z.tiles * z.tokens, LANES)
    groups = z.tokens // z.count
    squared = z.count * z.count
    states = (2, (z.tokens + 1) * z.count, z.chans)
    slot = pltpu.VMEM((2, squared, z.chans), bf16)
    return call(
        forward_kernel,
        at("m", shape(states, bf16))
        + at(
            "h", shape((2 * z.rows, z.tokens), f32), shape((2 * z.count, z.tokens), f32), shape((8, z.chans), f32),
            shape(flat, f32), shape((z.tiles * z.tokens, LANES), f32), shape(both, f32), shape(both, bf16),
            shape(square, bf16), shape(square, bf16),
        )
        + at("x", shape((early_rows, LANES), bf16)),
        args,
        [
            pltpu.VMEM(square, f32), pltpu.VMEM(flat, f32), pltpu.VMEM(square, bf16), pltpu.VMEM(both, f32),
            pltpu.VMEM((2, groups, z.count, LANES), f32),
            pltpu.VMEM((2, groups, 2, z.count, squared), bf16), pltpu.VMEM((2, groups, z.count, z.count), f32),
            pltpu.VMEM(states, bf16), slot, slot, pltpu.VMEM((2, z.count, z.chans), f32),
            pltpu.SemaphoreType.DMA((2, 2 * z.blocks)),
        ],
        limit=limit, micros=15, kept=kept,
    )


def backward_call(args, sizes, limit=30):
    z = sizes
    square = (z.tokens, z.chans)
    both = (2,) + square
    groups = z.tokens // z.count
    squared = z.count * z.count
    slot = pltpu.VMEM((2, squared, z.chans), bf16)
    return call(
        backward_kernel,
        at(
            "x", shape((2 * z.rows, z.tokens), f32), shape(both, f32), shape((2, z.rank, z.chans), f32),
            shape((3 + z.count, 2, z.chans), f32),
        ),
        args,
        [
            pltpu.VMEM(both, f32), pltpu.VMEM(both, f32), pltpu.VMEM((2, groups, z.count, LANES), f32),
            pltpu.VMEM((2, groups, 2, z.count, squared), bf16), pltpu.VMEM((2, groups, z.count, z.count), f32),
            pltpu.VMEM((2, (z.tokens + 1) * z.count, z.chans), bf16), slot, slot, slot, slot,
            pltpu.VMEM((2, z.count, z.chans), f32), pltpu.SemaphoreType.DMA((2, 2 * z.blocks)),
        ],
        limit=limit, micros=15,
    )


def back_kernel(
    own_part, far_part, seg, w_xp, taps, mixing, conv_pre, grad_act, grad_chan, normed, gate_low,
    low_in, hid, gain, grad_dt, branch, w_out, core,
    sums_out, in_own, in_far, out_own, out_far,
    padded, gpad, sgpad, mixed_low, small, act_low,
    *, need, save,
):
    tokens, width = hid.shape
    chans = mixing.shape[1]
    tiles = chans // LANES
    rows = w_xp.shape[1]
    width_taps = taps.shape[1]
    me = core[0]
    half_width = in_own.shape[0] - 8
    edge = jnp.zeros((8, chans), f32)
    padded[0:8, :] = edge
    padded[pl.ds(8 + tokens, 8), :] = edge
    gpad[0, 0:8, :] = edge
    gpad[1, 0:8, :] = edge
    gpad[0, pl.ds(8 + tokens, 8), :] = edge
    gpad[1, pl.ds(8 + tokens, 8), :] = edge
    sgpad[0:8, :] = jnp.full((8, LANES), -1.0, f32)
    sgpad[pl.ds(8 + tokens, 8), :] = jnp.full((8, LANES), -1.0, f32)
    need(seg, w_xp, mixing)
    padded[pl.ds(8, tokens), :] = mixing[...]
    sgpad[pl.ds(8, tokens), :] = spread_segments(seg[...], tokens)

    parts = (own_part[...] + far_part[...]).astype(bf16)
    for heading in range(2):
        part = parts[heading * rows : (heading + 1) * rows, :]
        gpad[heading, pl.ds(8, tokens), :] = dot(part, w_xp[heading].astype(bf16), TN)

    blank = jnp.zeros((8, chans), f32)
    need(taps, conv_pre, grad_act, grad_chan)

    def through_conv(start, held):
        here = pl.ds(start, CONV_ROWS)
        window = padded[pl.ds(start, CONV_ROWS + 16), :]
        marks = sgpad[pl.ds(start, CONV_ROWS + 16), :]
        own = marks[8 : 8 + CONV_ROWS]
        base = window[8 : 8 + CONV_ROWS]
        sums = []
        for heading in range(2):
            pre = conv_pre[heading, here, :]
            sigma = sigmoid(pre)
            act_low[heading, here, :] = (pre * sigma).astype(bf16)
            inside = pl.ds(pl.multiple_of(start + 8, 8), CONV_ROWS)
            grad = (gpad[heading, inside, :] + grad_act[heading, here, :]) * silu_slope(pre, sigma)
            gpad[heading, inside, :] = grad
            sums.append(held[5 * heading] + fold(grad))
            sums.append(held[5 * heading + 1] + fold(grad * base))
            for offset in range(1, width_taps):
                begin = 8 - offset if heading == 0 else 8 + offset
                kept = jnp.where(marks[begin : begin + CONV_ROWS] == own, 1.0, 0.0)
                moved = window[begin : begin + CONV_ROWS]
                sums.append(held[5 * heading + 1 + offset] + fold(grad * moved * wide(kept, tiles)))
        return tuple(sums)

    sums = each_rows(tokens, through_conv, (blank,) * 10, CONV_ROWS)
    small[...] = jnp.zeros(small.shape, f32)
    for heading in range(2):
        bias = jnp.sum(sums[5 * heading], axis=0, keepdims=True)
        for offset in range(width_taps):
            row = heading * width_taps + offset
            small[row : row + 1, :] = jnp.sum(sums[5 * heading + 1 + offset], axis=0, keepdims=True)
        for entry in range(grad_chan.shape[0]):
            row = 2 * width_taps + 2 * entry + heading
            small[row : row + 1, :] = (
                bias
                if entry == 0
                else grad_chan[entry, heading : heading + 1, :]
            )

    def mixed(start, held):
        here = pl.ds(start, CONV_ROWS)
        marks = sgpad[pl.ds(start, CONV_ROWS + 16), :]
        own = marks[8 : 8 + CONV_ROWS]
        total = jnp.zeros((CONV_ROWS, chans), f32)
        for heading in range(2):
            window = gpad[heading, pl.ds(start, CONV_ROWS + 16), :]
            total = total + window[8 : 8 + CONV_ROWS] * taps[heading, 0:1, :]
            for offset in range(1, width_taps):
                begin = 8 + offset if heading == 0 else 8 - offset
                kept = jnp.where(marks[begin : begin + CONV_ROWS] == own, 1.0, 0.0)
                total = total + window[begin : begin + CONV_ROWS] * wide(kept, tiles) * taps[
                    heading, offset : offset + 1, :
                ]
        mixed_low[here, :] = total.astype(bf16)
        return held

    each_rows(tokens, mixed, 0, CONV_ROWS)

    base_row = 0

    def put(values):
        nonlocal base_row
        for tile in range(values.shape[1] // LANES):
            sums_out[base_row : base_row + values.shape[0], :] = values[
                :, tile * LANES : (tile + 1) * LANES
            ].astype(bf16)
            base_row += values.shape[0]

    need()
    partial = dot(mixed_low[...], low_in[0], NT) + dot(gate_low[...], low_in[1], NT)
    padded[pl.ds(8, tokens), :] = partial

    gain_row = gain[...].reshape(1, width)

    def gains(start, held):
        here = pl.ds(start, NORM_ROWS)
        source = hid[here, :].astype(f32)
        scale = lax.rsqrt(jnp.sum(source * source, axis=1, keepdims=True) / width + norm_eps)
        inside = pl.ds(pl.multiple_of(start + 8, 8), NORM_ROWS)
        grad = padded[inside, :]
        padded[inside, :] = grad * gain_row
        return held + fold(grad * source * scale)

    gain_sum = each_rows(tokens, gains, jnp.zeros((8, width), f32), NORM_ROWS)
    small[46:47, :] = jnp.sum(gain_sum, axis=0, keepdims=True)
    weighted = padded[pl.ds(8, tokens), :]
    products = weighted * hid[...].astype(f32)
    turned = weighted.T
    row_dot = dot(jnp.ones((8, width), f32), products, NT, HIGH)
    in_own[0:half_width, :] = jnp.where(me == 0, turned[:half_width], turned[half_width:])
    in_far[0:half_width, :] = jnp.where(me == 0, turned[half_width:], turned[:half_width])
    in_own[pl.ds(half_width, 8), :] = row_dot
    in_far[pl.ds(half_width, 8), :] = row_dot
    save(in_own)
    sent = dot(w_out[...].astype(bf16), branch[...], ((0,), (1,)))
    out_own[...] = jnp.where(me == 0, sent[:half_width], sent[half_width:])
    out_far[...] = jnp.where(me == 0, sent[half_width:], sent[:half_width])
    save(out_own)
    put(dot(normed[...], mixed_low[...], TN))
    put(
        jnp.concatenate(
            [
                dot(parts[heading * rows : (heading + 1) * rows, :], act_low[heading], NN)
                for heading in range(2)
            ],
            axis=0,
        )
    )
    put(jnp.concatenate([grad_dt[0], grad_dt[1]], axis=0))

    put(small[...])
    sums_out[base_row:, :] = jnp.zeros((sums_out.shape[0] - base_row, LANES), bf16)


def outputs_kernel(hid, cot_own, out_own, out_far, in_own, in_far, core, output, input_grad, *, need, save):
    width = hid.shape[1]
    half_width = cot_own.shape[0]
    me = core[0]
    need()
    source = hid[...].astype(f32).T
    scale = lax.rsqrt(jnp.sum(source * source, axis=0, keepdims=True) / width + norm_eps)
    own = jnp.where(me == 0, source[:half_width], source[half_width:])
    output[...] = (own + (out_own[...] + out_far[...])).astype(bf16)
    weighted = in_own[0:half_width, :] + in_far[0:half_width, :]
    save(output)
    row_dot = in_own[half_width : half_width + 1, :] + in_far[half_width : half_width + 1, :]
    input_grad[...] = (
        cot_own[...].astype(f32)
        + scale * weighted
        - own * (scale * scale * scale) * (row_dot / width)
    )


def lamb_moments(weight, grad, first, second):
    first_new = beta_one * first + (1.0 - beta_one) * grad
    second_new = beta_two * second + (1.0 - beta_two) * grad * grad
    root = jnp.sqrt(second_new * (1.0 / (1.0 - beta_two**STEP)))
    update = first_new * (1.0 / (1.0 - beta_one**STEP)) / (root + adam_eps) + decay_rate * weight
    return (first_new, second_new, update)


def rows_sum(values):
    return jnp.sum(values, axis=0, keepdims=True)


def lanes_sum(values):
    total = rows_sum(values)
    lanes = total[:, 0:LANES]
    for tile in range(1, values.shape[1] // LANES):
        lanes = lanes + total[:, cols(tile)]
    return lanes


def fetch(sums, base, stride, start, count, number):
    return jnp.concatenate(
        [sums[pl.ds(base + tile * stride + start, count), :].astype(f32) for tile in range(number)], axis=1
    )


def spread_of(update, mean, length):
    def step(start, kept):
        away = update[pl.ds(start, LAMB_ROWS), :] - mean
        return kept + fold(away * away)

    return rows_sum(each_rows(length, step, jnp.zeros((8, update.shape[1]), f32), LAMB_ROWS))


def half_update(sums, base, stride, weights, a_ref, b_ref, x_ref, y_ref, u_ref):
    length, chans = weights.shape
    zero = jnp.zeros((8, chans), f32)

    def step(start, kept):
        here = pl.ds(start, LAMB_ROWS)
        grad = fetch(sums, base, stride, start, LAMB_ROWS, chans // LANES)
        weight = weights[here, :]
        first, second, update = lamb_moments(weight, grad, a_ref[here, :], b_ref[here, :])
        x_ref[here, :] = first
        y_ref[here, :] = second
        u_ref[here, :] = update
        return (
            kept[0] + fold(weight * weight), kept[1] + fold(update * update), kept[2] + fold(update)
        )

    return each_rows(length, step, (zero, zero, zero), LAMB_ROWS)


def early_kernel(
    sums, w_out, a_out, b_out, w_gate, a_gate, b_gate,
    x_out, y_out, x_gate, y_gate, u_gate, u_out, norms, stats,
    *, need, save,
):
    width, chans = w_gate.shape
    tiles = width // LANES
    norms[...] = jnp.zeros(norms.shape, f32)
    zero = jnp.zeros((8, width), f32)
    need(w_out, a_out, b_out)

    def one_out(start, kept):
        here = pl.ds(start, LAMB_ROWS)
        grad = fetch(sums, 0, chans, start, LAMB_ROWS, tiles)
        weight = w_out[here, :]
        first, second, update = lamb_moments(weight, grad, a_out[here, :], b_out[here, :])
        x_out[here, :] = first
        y_out[here, :] = second
        u_out[here, :] = update
        return (kept[0] + fold(weight * weight), kept[1] + fold(update * update))

    weight_sq, update_sq = each_rows(chans, one_out, (zero, zero), LAMB_ROWS)
    norms[1:2, :] = lanes_sum(weight_sq)
    norms[7:8, :] = lanes_sum(update_sq)
    save(x_out, y_out, u_out)
    need()
    weight_sq, update_sq, total = half_update(
        sums, chans * tiles, width, w_gate, a_gate, b_gate, x_gate, y_gate, u_gate
    )
    norms[0:1, :] = lanes_sum(weight_sq)
    norms[6:7, :] = lanes_sum(update_sq)
    save(x_gate, y_gate, u_gate)
    gate_mean = rows_sum(total) / width
    stats[0:1, :] = gate_mean
    stats[1:2, :] = spread_of(u_gate, gate_mean, width)
    ones = jnp.ones((8, width), f32)
    out_all = u_out[...]
    out_mean = jnp.sum(out_all, axis=1, keepdims=True) / width
    away = out_all - out_mean
    stats[2:3, :] = dot(ones, out_all, NT, HIGH)[0:1] / width
    stats[3:4, :] = dot(ones, away * away, NT, HIGH)[0:1]
    stats[4:8, :] = jnp.zeros((4, chans), f32)


def late_kernel(
    sums, early_norms, early_stats, *rest, need, save
):
    small_in, (a_mix, b_mix), rest = rest[:8], rest[8:10], rest[10:]
    x_mix, y_mix, x_xp, y_xp, x_dt, y_dt, x_cv, y_cv, x_cp, y_cp, *rest = rest
    u_mix, u_xp, u_dt, u_cv, u_cp, norms, stats, w_xp, w_dt, w_cv, w_cp, w_mix, *_ = rest
    a_xp, b_xp, a_dt, b_dt, a_cv, b_cv, a_cp, b_cp = small_in
    width, chans = w_mix.shape
    tiles = chans // LANES
    base = tiles * width
    need(early_norms, early_stats, *small_in, w_xp, w_dt, w_cv, w_cp)
    norms[...] = early_norms[...]
    stats[...] = early_stats[...]

    def small(place, items, weight, a_ref, b_ref, x_ref, y_ref, u_ref):
        weight_sq, update_sq = jnp.zeros((1, LANES), f32), jnp.zeros((1, LANES), f32)
        for index, grad in enumerate(items):
            held = weight[index]
            first, second, update = lamb_moments(held, grad, a_ref[index], b_ref[index])
            x_ref[index] = first
            y_ref[index] = second
            u_ref[index] = update
            weight_sq = weight_sq + lanes_sum(held * held)
            update_sq = update_sq + lanes_sum(update * update)
        norms[place : place + 1, :] = weight_sq
        norms[6 + place : 7 + place, :] = update_sq

    rows = w_xp.shape[1]
    grads = fetch(sums, base, 2 * rows, 0, 2 * rows, tiles)
    small(2, [grads[:rows], grads[rows:]], w_xp, a_xp, b_xp, x_xp, y_xp, u_xp)
    base += 2 * rows * tiles
    rank = w_dt.shape[1]
    grads = fetch(sums, base, 2 * rank, 0, 2 * rank, tiles)
    small(3, [grads[:rank], grads[rank:]], w_dt, a_dt, b_dt, x_dt, y_dt, u_dt)
    base += 2 * rank * tiles
    grads = fetch(sums, base, 48, 0, 48, tiles)
    taps = w_cv.shape[1]
    small(4, [grads[:taps], grads[taps : 2 * taps]], w_cv, a_cv, b_cv, x_cv, y_cv, u_cv)
    entries = w_cp.shape[0]
    items = [grads[2 * (taps + entry) : 2 * (taps + entry) + 2] for entry in range(entries)]
    small(5, items, w_cp, a_cp, b_cp, x_cp, y_cp, u_cp)
    for tile in range(tiles):
        norms[12 + tile : 13 + tile, :] = grads[46:47, cols(tile)]
    save()
    need(a_mix, b_mix, w_mix)
    weight_sq, update_sq, total = half_update(
        sums, 0, width, w_mix, a_mix, b_mix, x_mix, y_mix, u_mix
    )
    norms[0:1, :] += lanes_sum(weight_sq)
    norms[6:7, :] += lanes_sum(update_sq)
    mix_mean = rows_sum(total) / width
    stats[4:5, :] = mix_mean


def spread_kernel(u_mix, stats, spread, *, need, save):
    spread[...] = jnp.broadcast_to(spread_of(u_mix, stats[4:5, :], u_mix.shape[0]), spread.shape)


def apply_out_kernel(norms_own, norms_far, w_out, u_out, n_out, c_out, *, need, save):
    chans = w_out.shape[0]
    need(norms_own)
    sums = jnp.sum(norms_own[...] + norms_far[...], axis=1, keepdims=True)
    scale = learn_rate * jnp.sqrt(sums[1:2]) / (jnp.sqrt(sums[7:8]) + adam_eps)
    need()

    def one_out(start, held):
        here = pl.ds(start, LAMB_ROWS)
        fresh = w_out[here, :] - scale * u_out[here, :]
        n_out[here, :] = fresh
        c_out[here, :] = fresh.astype(bf16)
        return held

    each_rows(chans, one_out, 0, LAMB_ROWS)


def apply_kernel(
    norms_own, norms_far, stats, mix_spread,
    w_mix, w_gate, w_xp, w_dt, w_cv, w_cp,
    u_mix, u_gate, u_xp, u_dt, u_cv, u_cp,
    gain, gain_first, gain_second, x_mix, y_mix, core, x_given, y_given,
    n_in, c_in, n_xp, c_xp, n_dt, c_dt, n_cv, c_cv, n_cp, c_cp,
    g_first, g_second, g_new, g_copy, norms_out, stats_out, x_in, y_in,
    sems,
    *, need, save,
):
    width, chans = w_mix.shape
    moves = [
        pltpu.make_async_copy(held, target.at[:, 0, :], sems.at[number])
        for number, (held, target) in enumerate(((x_mix, x_in), (y_mix, y_in)))
    ]
    for move in moves:
        move.start()
    half_width = g_new.shape[0]
    me = core[0]
    totals = norms_own[...] + norms_far[...]
    sums = jnp.sum(totals, axis=1, keepdims=True)
    scales = [None]
    for place in range(6):
        weight_norm = jnp.sqrt(sums[place : place + 1])
        update_norm = jnp.sqrt(sums[6 + place : 7 + place])
        scales.append(learn_rate * weight_norm / (update_norm + adam_eps))
        norms_out[0:1, place + 1 : place + 2] = weight_norm
        norms_out[1:2, place + 1 : place + 2] = update_norm

    need(w_mix, w_gate)

    def one_in(start, held):
        here = pl.ds(start, LAMB_ROWS)
        for half, weight, change in ((0, w_mix, u_mix), (1, w_gate, u_gate)):
            fresh = weight[here, :] - scales[1] * change[here, :]
            n_in[half, here, :] = fresh
            c_in[here, half, :] = fresh.astype(bf16)
        return held

    each_rows(width, one_in, 0, LAMB_ROWS)
    save(n_in, c_in)

    need()
    gain_grad = jnp.concatenate(
        [totals[12 + tile : 13 + tile, :] for tile in range(width // LANES)], axis=1
    )
    gain_row = gain[...].reshape(1, width)
    first, second, update = lamb_moments(gain_row, gain_grad, gain_first[...], gain_second[...])
    weight_norm = jnp.sqrt(jnp.sum(gain_row * gain_row, axis=1, keepdims=True))
    update_norm = jnp.sqrt(jnp.sum(update * update, axis=1, keepdims=True))
    norms_out[0:1, 0:1] = weight_norm
    norms_out[1:2, 0:1] = update_norm
    fresh = gain_row - learn_rate * weight_norm / (update_norm + adam_eps) * update

    def own(row):
        return jnp.where(me == 0, row[:, :half_width], row[:, half_width:]).reshape(half_width)

    g_first[...] = own(first)
    g_second[...] = own(second)
    g_new[...] = own(fresh)
    g_copy[...] = own(fresh).astype(bf16)
    for place, weight, change, fresh_ref, copy in (
        (3, w_xp, u_xp, n_xp, c_xp),
        (4, w_dt, u_dt, n_dt, c_dt),
        (5, w_cv, u_cv, n_cv, c_cv),
        (6, w_cp, u_cp, n_cp, c_cp),
    ):
        for index in range(weight.shape[0]):
            fresh = weight[index] - scales[place] * change[index]
            fresh_ref[index] = fresh
            copy[index] = fresh.astype(bf16)
    parts = [
        (scales[1], stats[4:5, :], mix_spread[0:1, :]),
        (scales[1], stats[0:1, :], stats[1:2, :]),
        (scales[2], stats[2:3, :], stats[3:4, :]),
    ]
    means = [scale * part_mean for scale, part_mean, _ in parts]
    mean = (means[0] + means[1] + means[2]) / 3.0
    spread = jnp.zeros_like(mean)
    for (scale, _, squares), part_mean in zip(parts, means):
        gap = part_mean - mean
        spread = spread + scale * scale * squares + width * gap * gap
    stats_out[0:1, :] = mean
    stats_out[1:2, :] = spread / (3.0 * width)
    for move in moves:
        move.wait()


def join_kernel(pieces, copies, *, need, save):
    total = pieces[0].astype(f32)
    for place in range(1, pieces.shape[0]):
        total = total + pieces[place].astype(f32)
    low = total.astype(bf16)
    for place in range(pieces.shape[0]):
        copies[place] = low


def send_pieces(values, dp):
    chunk = values.shape[0] // dp
    return lax.all_to_all(values, "dp", 0, 0, tiled=True).reshape(dp, chunk, LANES)


def join_pieces(pieces):
    copies = call(join_kernel, at("x", shape(pieces.shape, bf16)), at("x", pieces), limit=8)[0]
    return copies.reshape(-1, LANES)


def call(kernel, outs, args, scratch=(), limit=32, micros=1, passed=(), kept=(), aliases=None):
    given = [array for array, _ in args] + [array for array, _ in passed]
    kinds = [kind for _, kind in args] + ["m"] * len(passed)
    n_own = len(outs)
    outs = list(outs)
    for array, kind in passed:
        dims = array.shape if kind == "h" else (array.shape[0], array.shape[-1])
        outs += at("x", shape(dims, array.dtype))
    outs += at("m", *[shape(given[place].shape, given[place].dtype) for place in kept])
    out_kinds = [kind for _, kind in outs]
    fetched = [place for place, kind in enumerate(kinds) if kind in "h01"]
    stored = [place for place, kind in enumerate(out_kinds) if kind in "h12"]

    def staged(array, kind):
        rows, columns = array.shape[0], array.shape[-1]
        dims = {"h": array.shape, "2": (2, rows, columns)}.get(kind, (rows, columns))
        return pltpu.VMEM(dims, array.dtype)

    staging = [staged(given[place], kinds[place]) for place in fetched]
    staging += [staged(outs[place][0], out_kinds[place]) for place in stored]
    moves = max(1, 2 * len(staging) + len(passed) + len(kept))

    def body(*refs):
        ins = list(refs[: len(given)])
        results = list(refs[len(given) : len(given) + len(outs)])
        rest = refs[len(given) + len(outs) :]
        stage, sems, own = rest[: len(staging)], rest[len(staging)], rest[len(staging) + 1 :]
        loads, saves = {}, {}
        for number, place in enumerate(fetched):
            source = ins[place] if kinds[place] == "h" else ins[place].at[:, int(kinds[place]), :]
            loads[id(stage[number])] = pltpu.make_async_copy(source, stage[number], sems.at[number])
            ins[place] = stage[number]
        for load in loads.values():
            load.start()
        for number, place in enumerate(stored, len(fetched)):
            held, target, kind = stage[number], results[place], out_kinds[place]
            parts = [(held, target)]
            if kind == "1":
                parts = [(held, target.at[:, 1, :])]
            if kind == "2":
                parts = [(held.at[half], target.at[:, half, :]) for half in range(2)]
            saves[id(held)] = [
                pltpu.make_async_copy(*pair, sems.at[moves - 1 - 2 * (number - len(fetched)) - half]) for half, pair in enumerate(parts)
            ]
            results[place] = held
        follow = []
        for number in range(len(passed)):
            held = results[n_own + number]
            source, kind = ins[len(args) + number], passed[number][1]
            source = source if kind == "h" else source.at[:, int(kind), :]
            loads[id(held)] = pltpu.make_async_copy(source, held, sems.at[len(staging) + number])
            loads[id(held)].start()
        begun, resting = [], []
        for number, place in enumerate(kept):
            resting.append(
                pltpu.make_async_copy(
                    ins[place], results[n_own + len(passed) + number],
                    sems.at[len(staging) + len(passed) + number],
                )
            )

        def need(*wanted):
            keys = [id(ref) for ref in wanted] or list(loads)
            for key in keys:
                if key in loads and key not in follow:
                    loads.pop(key).wait()
            while follow:
                loads[follow.pop(0)].start()
            while resting:
                begun.append(resting.pop(0))
                begun[-1].start()
            for key in keys:
                if key in loads:
                    loads.pop(key).wait()

        def save(*ready):
            for key in [id(ref) for ref in ready] or list(saves):
                for move in saves.pop(key, ()):
                    move.start()
                    begun.append(move)

        kernel(*ins[: len(args)], *results[: n_own + len(passed)], *own, need=need, save=save)
        need()
        save()
        for move in begun:
            move.wait()

    spaces = {"x": pltpu.VMEM, "s": pltpu.SMEM}
    placed = [
        pltpu.with_memory_space_constraint(array, pltpu.HBM) if kind in "hm01" else array
        for array, kind in zip(given, kinds)
    ]
    return pl.pallas_call(
        body,
        out_shape=[out if kind == "x" else pltpu.HBM(out.shape, out.dtype) for out, kind in outs],
        in_specs=[pl.BlockSpec(memory_space=spaces.get(kind, pltpu.HBM)) for kind in kinds],
        out_specs=[pl.BlockSpec(memory_space=spaces.get(kind, pltpu.HBM)) for kind in out_kinds],
        input_output_aliases=aliases or {},
        scratch_shapes=[*staging, pltpu.SemaphoreType.DMA((moves,)), *scratch],
        compiler_params=pltpu.CompilerParams(vmem_limit_bytes=limit * MB),
        cost_estimate=pl.CostEstimate(flops=micros * 10**9, bytes_accessed=MB, transcendentals=0),
    )(*placed)


def at(kind, *things):
    return [(thing, kind) for thing in things]


def program(
    dp,
    hidden_in, out_cot, segment_ids,
    norm_gain, in_weight, out_weight, xproj_weight, dtproj_weight, conv_weight, chan_params,
    first_norm_gain, first_in_weight, first_out_weight, first_xproj_weight,
    first_dtproj_weight, first_conv_weight, first_chan_params,
    second_norm_gain, second_in_weight, second_out_weight, second_xproj_weight,
    second_dtproj_weight, second_conv_weight, second_chan_params,
):
    tokens, width = hidden_in.shape
    chans = in_weight.shape[2]
    half_width = first_norm_gain.shape[0]
    tiles = chans // LANES
    rank = dtproj_weight.shape[1]
    count = chan_params.shape[1] - 3
    rows = rank + 2 * count
    taps = conv_weight.shape[1]

    def swap(values):
        return lax.ppermute(values, "chan", [(0, 1), (1, 0)])

    me = lax.axis_index("chan")
    core = me.astype(jnp.int32).reshape(1)
    cot_own = out_cot.T
    cot_far = swap(cot_own)
    moments_own = jnp.stack([first_norm_gain, second_norm_gain])
    moments_far = swap(moments_own)
    moments_gain = jnp.where(
        me == 0,
        jnp.concatenate([moments_own, moments_far], 1),
        jnp.concatenate([moments_far, moments_own], 1),
    )

    def flip(values):
        return jnp.swapaxes(values, 1, 2)

    def turn(values):
        return jnp.swapaxes(values, 0, 1)

    w_xp = flip(xproj_weight)
    w_cp = turn(chan_params)
    square = (tokens, chans)
    z = Sizes(tokens, chans, count, rank)
    smem = at("s", core)

    def padded_rows(amount):
        return -(-amount // (dp * 16)) * 16 * dp

    mixing, gate, conv_pre, part, normed, low_in, same, near_cp, near_dt, near_cot, near_out = call(
        front_kernel,
        at("h", shape(square, f32))
        + at("x", shape(square, f32), shape((2,) + square, f32), shape((2 * rows, tokens), f32))
        + at("h", shape((tokens, width), bf16), shape((2, width, chans), bf16))
        + at("x", shape((2, tokens, LANES), f32)),
        at("h", hidden_in, norm_gain) + at("0", in_weight) + at("1", in_weight)
        + at("h", segment_ids, conv_weight, w_xp),
        [pltpu.VMEM((tokens + 16, chans), f32), pltpu.VMEM((tokens + 16, LANES), f32)],
        limit=14, micros=6, passed=at("h", w_cp, dtproj_weight, cot_own, out_weight),
    )
    part_far = swap(part)
    act = call(
        activate_kernel, at("x", shape((2,) + square, f32)), at("x", conv_pre), limit=4, micros=1
    )[0]
    early_rows = padded_rows(tiles * width + (width // LANES) * chans)
    (
        states, proj, grad_maps, skips, far_step, grad_y, pre_step, inflow_low, gate_low, branch_low, early,
        conv_kept,
    ) = forward_call(
        at("x", part, part_far, near_cp, near_dt, near_cot, cot_far, near_out)
        + at("x", conv_pre, act, gate, same) + at("h", normed) + smem,
        z, early_rows, half_width, (7,),
    )
    early_pieces = send_pieces(early, dp)
    grad_part, grad_act, grad_dt, grad_chan = backward_call(
        at("m", states) + at("h", w_cp, proj, far_step, grad_y, inflow_low, pre_step, conv_kept)
        + at("h", grad_maps, skips, dtproj_weight),
        z,
    )
    early_copies, grad_part = lax.optimization_barrier((join_pieces(early_pieces), grad_part))
    early_sums = lax.all_to_all(early_copies, "dp", 0, 0, tiled=True)
    grad_far = swap(grad_part)
    late_rows = padded_rows(tiles * (width + 2 * rows + 2 * rank + 48))
    late, in_own, in_send, out_own, out_send = call(
        back_kernel,
        at("x", shape((late_rows, LANES), bf16))
        + at("h", shape((half_width + 8, tokens), f32))
        + at("x", shape((half_width + 8, tokens), f32))
        + at("h", shape((half_width, tokens), f32))
        + at("x", shape((half_width, tokens), f32)),
        at("x", grad_part, grad_far)
        + at("h", segment_ids, w_xp, conv_weight, mixing, conv_kept) + at("x", grad_act, grad_chan)
        + at("h", normed, gate_low, low_in, hidden_in, norm_gain) + at("x", grad_dt)
        + at("h", branch_low, out_weight)
        + smem,
        [
            pltpu.VMEM((tokens + 16, chans), f32), pltpu.VMEM((2, tokens + 16, chans), f32),
            pltpu.VMEM((tokens + 16, LANES), f32), pltpu.VMEM(square, bf16),
            pltpu.VMEM((48, chans), f32), pltpu.VMEM((2,) + square, bf16),
        ],
        limit=20, micros=2,
    )
    in_far = swap(in_send)
    out_far = swap(out_send)
    late, early_sums = lax.optimization_barrier((late, early_sums))
    late_pieces = send_pieces(late, dp)
    output, input_grad = call(
        outputs_kernel,
        at("h", shape((half_width, tokens), bf16), shape((half_width, tokens), f32)),
        at("h", hidden_in, cot_own, out_own) + at("x", out_far) + at("h", in_own) + at("x", in_far) + smem,
        limit=16, micros=3,
    )
    firsts = [first_xproj_weight, first_dtproj_weight, first_conv_weight, first_chan_params]
    seconds = [second_xproj_weight, second_dtproj_weight, second_conv_weight, second_chan_params]
    for group in (firsts, seconds):
        group[0], group[3] = flip(group[0]), turn(group[3])
    weights = [w_xp, dtproj_weight, conv_weight, w_cp]
    half = shape((width, chans), f32)
    whole_in, whole_out = shape(in_weight.shape, f32), shape(out_weight.shape, f32)
    x_out, y_out, x_in, y_in, u_gate, u_out, early_norms, early_stats = call(
        early_kernel,
        at("h", whole_out, whole_out) + at("1", whole_in, whole_in)
        + at("h", half, whole_out, shape((16, LANES), f32), shape((8, chans), f32)),
        at("x", early_sums) + at("h", out_weight, first_out_weight, second_out_weight)
        + at("1", in_weight, first_in_weight, second_in_weight),
        limit=12, micros=5,
    )
    late_copies, output, input_grad = lax.optimization_barrier((join_pieces(late_pieces), output, input_grad))
    late_sums = lax.all_to_all(late_copies, "dp", 0, 0, tiled=True)
    n_out, c_out = call(
        apply_out_kernel, at("h", whole_out, shape(whole_out.shape, bf16)),
        at("h", early_norms) + at("x", swap(early_norms)) + at("h", out_weight, u_out),
        limit=8, micros=2,
    )
    late_sums, n_out, c_out = lax.optimization_barrier((late_sums, n_out, c_out))
    shapes = [shape(tensor.shape, f32) for tensor in weights]
    late_outs = []
    for entry in shapes:
        late_outs += [entry, entry]
    moments_in = [tensor for pair in zip(firsts, seconds) for tensor in pair]
    got = call(
        late_kernel,
        at("x", half, half) + at("h", *late_outs)
        + at("x", half, *shapes, shape((16, LANES), f32), shape((8, chans), f32)),
        at("x", late_sums) + at("h", early_norms, early_stats, *moments_in)
        + at("0", first_in_weight, second_in_weight),
        limit=12, micros=5,
        passed=at("h", *weights) + at("0", in_weight) + at("1", in_weight) + at("h", u_gate),
    )
    moments, updates, norms, stats, kept = got[:10], got[10:15], got[15], got[16], got[17:]
    kept_small, (kept_mix, kept_gate, changed_gate) = kept[0:4], kept[4:]
    norms_far = swap(norms)
    mix_spread = call(
        spread_kernel, at("x", shape((8, chans), f32)), at("x", updates[0], stats), limit=8, micros=1
    )[0]
    pairs = []
    for entry in [whole_in, *shapes]:
        pairs += [entry, shape(entry.shape, bf16)]
    row = shape((half_width,), f32)
    whole_low = shape(whole_in.shape, bf16)
    done = call(
        apply_kernel,
        at("2", whole_in) + at("h", whole_low)
        + at(
            "h", *pairs[2:], row, row, row, shape((half_width,), bf16), shape((2, 7), f32),
            shape((2, chans), f32),
        )
        + at("m", whole_in, whole_in),
        at("x", norms, norms_far, stats, mix_spread, kept_mix, kept_gate, *kept_small, updates[0], changed_gate, *updates[1:])
        + at("h", norm_gain) + at("x", moments_gain[0:1], moments_gain[1:2], moments[0], moments[1])
        + smem + at("m", x_in, y_in),
        [pltpu.SemaphoreType.DMA((2,))],
        limit=14, micros=5, aliases={22: 16, 23: 17},
    )
    flat = list(done[10:14])
    firsts_out = [done[16], x_out, *moments[2::2]]
    seconds_out = [done[17], y_out, *moments[3::2]]
    fresh = [done[0], n_out, *done[2:10:2]]
    copied = [done[1], c_out, *done[3:10:2]]
    for place in range(6):
        entry = [firsts_out[place], seconds_out[place], fresh[place], copied[place]]
        if place == 2:
            entry = [flip(tensor) for tensor in entry]
        if place == 5:
            entry = [turn(tensor) for tensor in entry]
        flat += entry
    return (output.T, input_grad.T, *flat, done[14].T, done[15])


def solution(mesh):
    rows = P("dp", None)
    cells = P("dp", "chan")
    last = P(None, None, "chan")
    first = P("chan", None)
    middle = P(None, "chan", None)
    tensors = (last, first, middle, last, last, last)
    outs = [cells, cells] + [P("chan")] * 4
    for spec in tensors:
        outs += [spec] * 4
    return jax.shard_map(
        functools.partial(program, mesh.shape["dp"]),
        mesh=mesh,
        in_specs=(rows, cells, P("dp"), P(), *tensors, P("chan"), *tensors, P("chan"), *tensors),
        out_specs=(*outs, P(), P(None, "chan")),
        check_vma=False,
    )
```
